128 devices in a mesh: wide: 16 (over z, x_lo, core), shard: 8 (over x_hi, y).
Axes of the slice: x: 4 (x_hi: 2, x_lo: 2; x = x_hi * 2 + x_lo), y: 4, z: 4, core: 2. Of those that a mesh axis runs over, the one named last changes fastest.
Arguments:
- tokens: bfloat16 [49152, 1024], P(('wide', 'shard')), may hold values from -6 to 6
- cotangent: bfloat16 [49152, 1024], P(('wide', 'shard')), may hold values from -6 to 6
- lengths: int32 [128, 2], P(('wide', 'shard')), may hold values from 0 to 384, as said below
- joint_weight: float32 [1024, 3072], P('shard'), may hold values from -0.1875 to 0.1875
- joint_first: float32 [1024, 3072], P('shard'), may hold values from -80 to 80
- joint_second: float32 [1024, 3072], P('shard'), may hold values from 6 to 96
- output_weight: float32 [1024, 1024], P('shard'), may hold values from -0.5 to 0.5
- output_first: float32 [1024, 1024], P('shard'), may hold values from -40 to 40
- output_second: float32 [1024, 1024], P('shard'), may hold values from 3 to 48
- expand_weight: float32 [1024, 4096], P('shard'), may hold values from -0.1875 to 0.1875
- expand_first: float32 [1024, 4096], P('shard'), may hold values from -40 to 40
- expand_second: float32 [1024, 4096], P('shard'), may hold values from 1.5 to 24
- reduce_weight: float32 [4096, 1024], P('shard'), may hold values from -0.09375 to 0.09375
- reduce_first: float32 [4096, 1024], P('shard'), may hold values from -80 to 80
- reduce_second: float32 [4096, 1024], P('shard'), may hold values from 6 to 96
- vector_weight: float32 [12, 1024], P(None, 'shard'), may hold values from -0.5 to 1.3, as said below
- vector_first: float32 [12, 1024], P(None, 'shard'), may hold values from -160 to 160
- vector_second: float32 [12, 1024], P(None, 'shard'), may hold values from 12 to 192
Outputs:
- layer_out: bfloat16 [49152, 1024], P(('wide', 'shard'))
- input_grad: float32 [49152, 1024], P(('wide', 'shard'))
- joint_grad: float32 [1024, 3072], P('shard')
- output_grad: float32 [1024, 1024], P('shard')
- expand_grad: float32 [1024, 4096], P('shard')
- reduce_grad: float32 [4096, 1024], P('shard')
- vector_grad: float32 [12, 1024], P(None, 'shard')
- joint_mean: float32 [1024, 3072], P('shard')
- output_mean: float32 [1024, 1024], P('shard')
- expand_mean: float32 [1024, 4096], P('shard')
- reduce_mean: float32 [4096, 1024], P('shard')
- vector_mean: float32 [12, 1024], P(None, 'shard')
- joint_spread: float32 [1024, 3072], P('shard')
- output_spread: float32 [1024, 1024], P('shard')
- expand_spread: float32 [1024, 4096], P('shard')
- reduce_spread: float32 [4096, 1024], P('shard')
- vector_spread: float32 [12, 1024], P(None, 'shard')
- joint_next: float32 [1024, 3072], P('shard')
- output_next: float32 [1024, 1024], P('shard')
- expand_next: float32 [1024, 4096], P('shard')
- reduce_next: float32 [4096, 1024], P('shard')
- vector_next: float32 [12, 1024], P(None, 'shard')
The draws below stay inside these ranges and needn't reach their ends.
Inputs may be any that keep to these rules, and one draw needn't show every extreme that they name: Row i holds the lengths of the two sequences packed from slot 0 into the i-th block of 384 token rows: the first is 48 or more, the second may be 0, together they are at most 384; in every draw some block holds one sequence of all 384 slots. `vector_weight`: rows 0 and 5 lie within 0.7 to 1.3, the other rows within -0.5 to 0.5.
All inputs are finite; a program needn't handle non-finite values.
Results may differ from the reference program's by a relative error of at most 0.03.
Values may be sent and summed in bfloat16 or wider, within the bound.
No kernel may reach another device: no remote copies, remote signals or barrier semaphores. Data moves between devices by JAX's collectives and lax.ppermute only.
A program may use at most 256 MiB of HBM per device.

```python
import math
import jax
import jax.numpy as jnp
from jax import lax

D = 1024
HEAD_DIM = 64
FF = 4096
TOK_DEV = 384
STEP = 10
DEVS = 128
TOKENS = 49152


def draw_lengths(key, part):
    key = jax.random.fold_in(key, 17)
    key_first, key_second, key_full = jax.random.split(key, 3)
    opening = jax.random.randint(key_first, (DEVS,), TOK_DEV // 8, TOK_DEV + 1)
    chosen = jax.random.randint(key_full, (), 0, DEVS)
    opening = jnp.where(jnp.arange(DEVS) == chosen, TOK_DEV, opening)
    room = TOK_DEV - opening
    drawn = jax.random.randint(key_second, (DEVS,), 0, 1 << 20)
    second = drawn % (room + 1)
    return jnp.stack([opening, second], axis=1).astype(jnp.int32)


def draw_vector_weight(key, part):
    key = jax.random.fold_in(key, 29)
    key_gain, key_bias = jax.random.split(key)
    row_ids = jnp.arange(12)[:, None]
    gains = 1.0 + jax.random.uniform(key_gain, (12, D), jnp.float32, -0.3, 0.3)
    biases = jax.random.uniform(key_bias, (12, D), jnp.float32, -0.5, 0.5)
    is_gain = (row_ids == 0) | (row_ids == 5)
    return jnp.where(is_gain, gains, biases).astype(jnp.float32)


def block_scale(rng, shape, cuts, low, top_value):
    def one(dim, blocks):
        steps = jax.random.uniform(jax.random.fold_in(jax.random.fold_in(rng, 6), dim), (blocks,), jnp.float32, low / len(cuts), top_value / len(cuts))
        return jnp.repeat(jnp.exp(steps), shape[dim] // blocks).reshape((-1,) + (1,) * (len(shape) - dim - 1))

    level = one(*cuts[0])
    for cut in cuts[1:]:
        level = level * one(*cut)
    return level


def centred(key, extent, deviation, most, pieces=(), kind=jnp.bfloat16):
    values = deviation * jax.random.normal(key, extent, jnp.float32)
    if pieces:
        values = values * block_scale(key, extent, pieces, -0.22, 0.18)
    return jnp.clip(values, -most, most).astype(kind)


def setup_inputs(seed: int = 0) -> dict:
    key_list = jax.random.split(jax.random.key(seed), 19)
    tokens = centred(key_list[0], (TOKENS, D), 1.0, 6.0, ((0, 128),))
    cotangent = centred(key_list[1], (TOKENS, D), 1.0, 6.0, ((0, 128),))
    lengths = draw_lengths(jax.random.fold_in(key_list[18], 71), 0)
    joint_weight = centred(key_list[3], (D, 3 * D), D ** -0.5, 0.1875, ((0, 8),), jnp.float32)
    joint_first = centred(key_list[4], (D, 3 * D), (TOKENS ** 0.5 * 2 ** -4), 80.0, ((0, 8),), jnp.float32)
    joint_second = jnp.clip(jnp.exp(math.log(96.0) - 2.7725887 * jax.random.uniform(key_list[5], (D, 3 * D), jnp.float32) ** block_scale(key_list[5], (D, 3 * D), ((0, 8),), -0.2, 0.2)), 6.0, 96.0)
    output_weight = centred(key_list[6], (D, D), (D // 8) ** -0.5, 0.5, ((0, 8),), jnp.float32)
    output_first = centred(key_list[7], (D, D), (TOKENS ** 0.5 * 2 ** -5), 40.0, ((0, 8),), jnp.float32)
    output_second = jnp.clip(jnp.exp(math.log(48.0) - 2.7725887 * jax.random.uniform(key_list[8], (D, D), jnp.float32) ** block_scale(key_list[8], (D, D), ((0, 8),), -0.2, 0.2)), 3.0, 48.0)
    expand_weight = centred(key_list[9], (D, FF), D ** -0.5, 0.1875, ((0, 8),), jnp.float32)
    expand_first = centred(key_list[10], (D, FF), (TOKENS ** 0.5 * 2 ** -5), 40.0, ((0, 8),), jnp.float32)
    expand_second = jnp.clip(jnp.exp(math.log(24.0) - 2.7725887 * jax.random.uniform(key_list[11], (D, FF), jnp.float32) ** block_scale(key_list[11], (D, FF), ((0, 8),), -0.2, 0.2)), 1.5, 24.0)
    reduce_weight = centred(key_list[12], (FF, D), FF ** -0.5, 0.09375, ((0, 8),), jnp.float32)
    reduce_first = centred(key_list[13], (FF, D), (TOKENS ** 0.5 * 2 ** -4), 80.0, ((0, 8),), jnp.float32)
    reduce_second = jnp.clip(jnp.exp(math.log(96.0) - 2.7725887 * jax.random.uniform(key_list[14], (FF, D), jnp.float32) ** block_scale(key_list[14], (FF, D), ((0, 8),), -0.2, 0.2)), 6.0, 96.0)
    vector_weight = draw_vector_weight(jax.random.fold_in(key_list[18], 71), 0)
    vector_first = centred(key_list[16], (12, D), (TOKENS ** 0.5 * 2 ** -3), 160.0, ((1, 8),), jnp.float32)
    vector_second = jnp.clip(jnp.exp(math.log(192.0) - 2.7725887 * jax.random.uniform(key_list[17], (12, D), jnp.float32) ** block_scale(key_list[17], (12, D), ((1, 8),), -0.2, 0.2)), 12.0, 192.0)
    return dict(tokens=tokens, cotangent=cotangent, lengths=lengths, joint_weight=joint_weight, joint_first=joint_first, joint_second=joint_second, output_weight=output_weight, output_first=output_first, output_second=output_second, expand_weight=expand_weight, expand_first=expand_first, expand_second=expand_second, reduce_weight=reduce_weight, reduce_first=reduce_first, reduce_second=reduce_second, vector_weight=vector_weight, vector_first=vector_first, vector_second=vector_second)


@jax.custom_vjp
def low(v):
    return lax.optimization_barrier(v.astype(jnp.bfloat16)).astype(jnp.float32)

@jax.custom_vjp
def low_back(v):
    return v

def low_keep(v):
    return (low(v), None)

def low_pass(kept, grad):
    return (grad,)

def back_keep(v):
    return (v, None)

def back_low(kept, grad):
    return (low(grad),)
low.defvjp(low_keep, low_pass)
low_back.defvjp(back_keep, back_low)
HIGH = lax.Precision.HIGHEST
ROOT_TWO_PI = 0.7978845608028654
CUBIC = 0.044715
BETA_ONE = 0.9
BETA_TWO = 0.999
ADAM_EPS = 1e-08
MATRIX_RATE = 0.03
OUTPUT_RATE = 0.1
VECTOR_RATE = 0.2
MATRIX_DECAY = 0.1

def gelu_tanh(upward):
    return 0.5 * upward * (1.0 + jnp.tanh(ROOT_TWO_PI * (upward + CUBIC * upward * upward * upward)))

def layer_norm(values, gain, shift):
    center = values - lax.optimization_barrier(jnp.mean(values, axis=-1, keepdims=True))
    inverse = lax.rsqrt(lax.optimization_barrier(jnp.mean(center * center, axis=-1, keepdims=True)) + 1e-05)
    return center * inverse * gain + shift

def one_block(weights, inputs, pair):
    joint_mat, out_mat, up_mat, down_mat, vector_rows = weights
    count, width = inputs.shape
    heads = width // HEAD_DIM
    places = jnp.arange(count, dtype=jnp.int32)
    filled = pair[0] + pair[1]
    segment = jnp.where(places < pair[0], 0, jnp.where(places < filled, 1, places + 2))
    allowed = (segment[:, None] == segment[None, :]) & (places[:, None] >= places[None, :])
    normed_one = low(layer_norm(inputs, vector_rows[0], vector_rows[1]))
    joint = jnp.dot(normed_one, joint_mat, precision=HIGH)
    query = low(low_back(joint[:, :width] + vector_rows[2])).reshape(count, heads, HEAD_DIM)
    keys = low(low_back(joint[:, width:2 * width])).reshape(count, heads, HEAD_DIM)
    values = low(low_back(joint[:, 2 * width:] + vector_rows[3])).reshape(count, heads, HEAD_DIM)
    scores = low_back(jnp.einsum('qhd,khd->hqk', query, keys, precision=HIGH) * HEAD_DIM ** (-0.5))
    scores = jnp.where(allowed[None], scores, -1e+30)
    probs = low(jax.nn.softmax(scores, axis=-1))
    attended = jnp.einsum('hqk,khd->qhd', probs, values, precision=HIGH).reshape(count, width)
    attended = low(low_back(attended))
    branch = low_back(jnp.dot(attended, out_mat, precision=HIGH) + vector_rows[4])
    middle = inputs + branch
    normed_two = low(layer_norm(middle, vector_rows[5], vector_rows[6]))
    upward = low_back(jnp.dot(normed_two, up_mat, precision=HIGH) + vector_rows[7:11].reshape(-1))
    active = low(gelu_tanh(upward))
    return middle + jnp.dot(active, down_mat, precision=HIGH) + vector_rows[11]

def adam_step(weight, first, second, grad, rate, decay):
    first_new = BETA_ONE * first + (1.0 - BETA_ONE) * grad
    second_new = BETA_TWO * second + (1.0 - BETA_TWO) * grad * grad
    mean_hat = first_new / (1.0 - BETA_ONE ** STEP)
    square_hat = second_new / (1.0 - BETA_TWO ** STEP)
    fresh = weight - rate * (mean_hat / (jnp.sqrt(square_hat) + ADAM_EPS) + decay * weight)
    return (first_new, second_new, fresh)

def reference(tokens, cotangent, lengths, joint_weight, joint_first, joint_second, output_weight, output_first, output_second, expand_weight, expand_first, expand_second, reduce_weight, reduce_first, reduce_second, vector_weight, vector_first, vector_second):
    masters = (joint_weight, output_weight, expand_weight, reduce_weight, vector_weight)
    blocks = lengths.shape[0]
    width = tokens.shape[1]
    count = tokens.shape[0] // blocks
    stacked = tokens.astype(jnp.float32).reshape(blocks, count, width)

    def forward(master_set, inputs):
        rounded = tuple((low(item) for item in master_set))

        def per_block(bundle):
            return one_block(rounded, bundle[0], bundle[1])
        return lax.map(jax.checkpoint(per_block), (inputs, lengths))
    result, pullback = jax.vjp(forward, masters, stacked)
    places = jnp.arange(count, dtype=jnp.int32)
    filled = lengths[:, 0] + lengths[:, 1]
    live = (places[None, :] < filled[:, None]).astype(jnp.float32)
    arriving = cotangent.astype(jnp.float32).reshape(blocks, count, width) * live[:, :, None]
    grads, input_grad = pullback(arriving)
    firsts = (joint_first, output_first, expand_first, reduce_first, vector_first)
    seconds = (joint_second, output_second, expand_second, reduce_second, vector_second)
    rates = (MATRIX_RATE, OUTPUT_RATE, MATRIX_RATE, MATRIX_RATE, VECTOR_RATE)
    decays = (MATRIX_DECAY, MATRIX_DECAY, MATRIX_DECAY, MATRIX_DECAY, 0.0)
    means, spreads, nexts = ([], [], [])
    for index in range(5):
        first_new, second_new, fresh = adam_step(masters[index], firsts[index], seconds[index], grads[index], rates[index], decays[index])
        means.append(first_new)
        spreads.append(second_new)
        nexts.append(fresh)
    layer_out = result.reshape(-1, width).astype(jnp.bfloat16)
    return (layer_out, input_grad.reshape(-1, width), grads[0], grads[1], grads[2], grads[3], grads[4], means[0], means[1], means[2], means[3], means[4], spreads[0], spreads[1], spreads[2], spreads[3], spreads[4], nexts[0], nexts[1], nexts[2], nexts[3], nexts[4])
```

```python
import functools

import jax
import jax.numpy as jnp
from jax import lax
from jax.experimental import pallas as pl
from jax.experimental.pallas import tpu as pltpu
from jax.sharding import PartitionSpec as P

HEAD_DIM = 64
STEP = 10


ROOT_TWO_PI = 0.7978845608028654
CUBIC = 0.044715
BETA_ONE = 0.9
BETA_TWO = 0.999
ADAM_EPS = 1e-08
MATRIX_RATE = 0.03
OUTPUT_RATE = 0.1
VECTOR_RATE = 0.2
MATRIX_DECAY = 0.1

LOW = jnp.bfloat16
FULL = jnp.float32
AXES = ("wide", "shard")
SIZES = (4, 2, 2, 2, 4)
COLS = 512
VMEM_BYTES = 60 * 1024 * 1024


def coordinates():
    wide, shard = lax.axis_index("wide"), lax.axis_index("shard")
    z, xl, core = wide // 4, (wide // 2) % 2, wide % 2
    xh, y = shard // 4, shard % 4
    return {"z": z, "x": 2 * xh + xl, "y": y, "xl": xl, "xh": xh, "core": core}


def route(partner):
    pairs = []
    for source in range(128):
        rest, places = source, []
        for size in reversed(SIZES):
            places.append(rest % size)
            rest //= size
        y, xh, core, xl, z = places
        target = partner({"z": z, "x": 2 * xh + xl, "y": y, "core": core})
        flat = 0
        for place, size in zip(
            (target["z"], target["x"] % 2, target["core"], target["x"] // 2, target["y"]), SIZES
        ):
            flat = flat * size + place
        pairs.append((source, flat))
    return pairs


def flip(axis, bits):
    return route(lambda at: {**at, axis: at[axis] ^ bits})


def turn(axis, step):
    return route(lambda at: {**at, axis: at[axis] ^ (1 if (at["core"] + step) % 2 == 0 else 3)})


def send(value, pairs):
    return lax.ppermute(value, AXES, pairs)


def added(a, b):
    return (a.astype(FULL) + b.astype(FULL)).astype(LOW)


def orders(me, axis):
    here = me[axis]
    one = jnp.where(me["core"] == 0, 1, 3)
    return [here, here ^ one, here ^ (4 - one), here ^ 2]


def places_of(me):
    return jnp.stack(
        orders(me, "x") + orders(me, "y") + orders(me, "z") + [me["xh"]]
    ).astype(jnp.int32)


def after(value, *others):
    return lax.optimization_barrier((value, *others))[0]


def rows_of(*parts):
    return jnp.concatenate([p.reshape(-1, COLS) for p in parts])


def gather(me, along_x, along_y, along_z, out, follow=None):
    marks = []

    def wait(value, index):
        return value if follow is None else after(value, follow[index])

    half = lax.dynamic_index_in_dim(
        along_x.reshape(2, -1, COLS), me["xl"], 0, keepdims=False
    )
    quarter = lax.dynamic_index_in_dim(
        along_z.reshape(4, -1, COLS), me["z"], 0, keepdims=False
    )
    size_y, size_z = along_y.shape[0], quarter.shape[0]
    payload = [along_y, quarter]
    if out is not None:
        own_out = lax.dynamic_index_in_dim(out, me["z"], 0, keepdims=False)
        payload.append(own_out)
    other = send(wait(rows_of(*payload), 0), flip("x", 3))
    marks.append(other)
    pair_y = jnp.stack([along_y, other[:size_y]])
    pair_z = jnp.stack([quarter, other[size_y : size_y + size_z]])
    if out is not None:
        both = jnp.where(
            me["core"] == me["xh"], own_out.reshape(2, -1, COLS),
            other[size_y + size_z :].reshape(2, -1, COLS),
        )
        pair_z = jnp.concatenate([pair_z, both], axis=1)
    size_x = half.shape[0]
    first = wait(rows_of(half, pair_z), 1)
    second = send(first, turn("y", 0))
    marks.append(second)
    here = jnp.stack([first, second])
    there = send(wait(here, 2), turn("y", 1))
    marks.append(there)
    plane_x = jnp.concatenate([here[:, :size_x], there[:, :size_x]])
    plane_z = jnp.concatenate([here[:, size_x:], there[:, size_x:]]).reshape(
        (4,) + pair_z.shape
    )
    starts = [(plane_x, "x"), (pair_y, "y"), (plane_z, "z")]
    if follow is not None:
        starts = [(wait(a, 3), axis) for a, axis in starts]
    got = [send(a, turn(axis, 0)) for a, axis in starts]
    marks.append(got[0])
    held = [jnp.stack([a, b]) for (a, _), b in zip(starts, got)]
    far = [send(a, turn(axis, 1)) for a, (_, axis) in zip(held, starts)]
    return held, far, marks


def halved(keep, away, axis):
    near = added(keep, send(away, turn(axis, 1)))
    return added(near[0], send(near[1], turn(axis, 0)))


def total(me, raw, out_rows):
    along_x, along_y, along_z = (
        halved(raw[0], raw[1], "x"), halved(raw[2], raw[3], "y"), halved(raw[4], raw[5], "z"),
    )
    size_x, size_y = along_x.shape[1], along_y.shape[1]
    size_z = along_z.shape[2] - out_rows
    plane = jnp.concatenate([along_x, along_z.reshape(4, -1, COLS)], axis=1)
    plane = halved(plane[:2], plane[2:], "y")
    half, pair = plane[:size_x], plane[size_x:].reshape(2, size_z + out_rows, COLS)
    out = pair[:, size_z:]
    sums = rows_of(along_y[0], pair[0, :size_z], out)
    sums = added(sums, send(rows_of(along_y[1], pair[1, :size_z], out), flip("x", 3)))
    other = send(rows_of(sums, half), flip("x", 1))
    sums = added(sums, other[: sums.shape[0]])
    other = other[sums.shape[0] :]
    whole_x = jnp.where(
        me["xl"] == 0, jnp.concatenate([half, other]), jnp.concatenate([other, half])
    )
    flat = rows_of(whole_x, sums[:size_y])
    block = sums[size_y:]
    other = send(rows_of(flat, block), turn("z", 0))
    flat = added(flat, other[: flat.shape[0]])
    blocks = rows_of(block, other[flat.shape[0] :])
    other = send(rows_of(flat, blocks), turn("z", 1))
    flat = added(flat, other[: flat.shape[0]])
    blocks = rows_of(blocks, other[flat.shape[0] :]).reshape((4,) + block.shape)
    where = orders(me, "z")
    ordered = [
        sum(jnp.where(where[k] == place, blocks[k], 0) for k in range(4)) for place in range(4)
    ]
    ordered = jnp.stack([a.astype(LOW) for a in ordered])
    both = rows_of(flat, ordered)
    far = send(both, flip("core", 1))

    def parts(rows):
        x, y = rows[: 2 * size_x], rows[2 * size_x : 2 * size_x + size_y]
        z = rows[2 * size_x + size_y :].reshape(4, size_z + 2 * out_rows, COLS)
        return x, y, z[:, :size_z].reshape(-1, COLS), z[:, size_z:].reshape(
            4, 2, out_rows, COLS
        )

    return parts(both), parts(far)


def sum_all(value):
    for pairs in (
        flip("core", 1),
        turn("x", 0),
        turn("x", 1),
        turn("y", 0),
        turn("y", 1),
        turn("z", 0),
        turn("z", 1),
    ):
        value = value + send(value, pairs)
    return value


def copies(plan, places, arrays, shapes):
    def kernel(count, places_ref, *refs):
        inputs, outputs, sems = refs[: len(arrays)], refs[len(arrays) : -1], refs[-1]
        started = [
            pltpu.make_async_copy(a, b, sems.at[i])
            for i, (a, b) in enumerate(plan(places_ref, inputs, outputs))
        ]
        for copy in started:
            copy.start()
        for copy in started:
            copy.wait()

    class Any:
        @property
        def at(self):
            return self

        def __getitem__(self, index):
            return self

    count = len(plan([0] * 13, [Any()] * len(arrays), [Any()] * len(shapes)))
    moved = sum(s.size * 2 for s in shapes)
    call = pl.pallas_call(
        functools.partial(kernel, count),
        out_shape=shapes,
        in_specs=[pl.BlockSpec(memory_space=pltpu.SMEM)]
        + [pl.BlockSpec(memory_space=pl.ANY)] * len(arrays),
        out_specs=[pl.BlockSpec(memory_space=pl.ANY)] * len(shapes),
        scratch_shapes=[pltpu.SemaphoreType.DMA((count,))],
        cost_estimate=pl.CostEstimate(flops=0, bytes_accessed=2 * moved, transcendentals=0),
    )
    return list(call(places, *arrays))


def low_shape(*shape):
    return jax.ShapeDtypeStruct(shape, LOW)


def joint_plan(places, raw, mats):
    query, key, value, vectors = mats
    pairs = []
    for ky in range(4):
        y = places[4 + ky]
        for kx in range(4):
            x = places[kx]
            shard = (x // 2) * 4 + y
            pairs.append(
                (raw[0 + kx // 2].at[kx % 2, ky],
                 query.at[shard, pl.ds(pl.multiple_of((x % 2) * 64, 64), 64)])
            )
        for p in range(2):
            shard = (places[12] ^ p) * 4 + y
            source = raw[2 + ky // 2].at[ky % 2, p]
            pairs.append((source.at[pl.ds(0, 128)], key.at[shard]))
            if vectors is not None:
                pairs.append((source.at[pl.ds(128, 16)], vectors.at[shard]))
            for kz in range(4):
                pairs.append(
                    (raw[4 + kz // 2].at[kz % 2, ky, p],
                     value.at[shard, pl.ds(pl.multiple_of(places[8 + kz] * 32, 32), 32)])
                )
    return pairs


def rest_plan(places, raw, mats, out=True):
    up, down_one, down_two, output = mats
    pairs = []
    for ky in range(4):
        y = places[4 + ky]
        for kx in range(4):
            x = places[kx]
            shard = (x // 2) * 4 + y
            at = pl.ds(pl.multiple_of((x % 2) * 64, 64), 64)
            for j in range(3):
                pairs.append(
                    (raw[0 + kx // 2].at[kx % 2, ky, j], up.at[j, shard, at])
                )
        for p in range(2):
            shard = (places[12] ^ p) * 4 + y
            source = raw[2 + ky // 2].at[ky % 2, p]
            pairs.append((source.at[pl.ds(0, 128)], up.at[3, shard]))
            pairs.append((source.at[pl.ds(128, 256)], down_one.at[shard]))
            for kz in range(4):
                source = raw[4 + kz // 2].at[kz % 2, ky, p]
                at = pl.ds(pl.multiple_of(places[8 + kz] * 64, 64), 64)
                pairs.append((source.at[pl.ds(0, 64)], down_two.at[shard, at]))
                at = pl.ds(pl.multiple_of(places[8 + kz] * 32, 32), 32)
                pairs.append((source.at[pl.ds(64, 32)], output.at[p, y, at]))
    return pairs


def gelu_both(upward):
    square = upward * upward
    tangent = jnp.tanh(ROOT_TWO_PI * upward * (1.0 + CUBIC * square))
    half = 0.5 * (1.0 + tangent)
    slope = half + 0.5 * upward * (1.0 - tangent * tangent) * ROOT_TWO_PI * (
        1.0 + 3.0 * CUBIC * square
    )
    return upward * half, slope


def dot(a, b):
    return jnp.dot(a, b, preferred_element_type=FULL)


def dot_nt(a, b):
    return lax.dot_general(a, b, (((1,), (1,)), ((), ())), preferred_element_type=FULL)


def dot_tn(a, b):
    return lax.dot_general(a, b, (((0,), (0,)), ((), ())), preferred_element_type=FULL)


def forward_backward_kernel(
    normed, arriving, up, down_one, down_two, bias,
    up_grad, one_grad, two_grad, bias_grad, layer_own, layer_other, normed_grad,
    layer_sum, normed_sum, active, up_low,
):
    step, last = pl.program_id(0), pl.num_programs(0) - 1
    count = layer_own.shape[0]
    tile = 256

    @pl.when(step == 0)
    def _():
        layer_sum[...] = jnp.zeros_like(layer_sum)
        normed_sum[...] = jnp.zeros_like(normed_sum)

    bias_grad[...] = jnp.zeros_like(bias_grad)

    def rows_step(index, carry):
        rows = pl.ds(pl.multiple_of(index * tile, tile), tile)
        upward = dot(normed[rows, :], up[0]) + bias[...]
        act, slope = gelu_both(upward)
        act = act.astype(LOW)
        active[rows, :] = act
        layer_sum[rows, :COLS] += dot(act, down_one[...])
        layer_sum[rows, COLS:] += dot(act, down_two[...])
        grad = dot_nt(arriving[rows, :COLS], down_one[...])
        grad += dot_nt(arriving[rows, COLS:], down_two[...])
        low = (grad * slope).astype(LOW)
        up_low[rows, :] = low
        bias_grad[...] += jnp.sum(low.astype(FULL), axis=0, keepdims=True)
        normed_sum[rows, :] += dot_nt(low, up[0])
        return carry

    lax.fori_loop(0, normed.shape[0] // tile, rows_step, 0)
    one_grad[...] = dot_tn(active[...], arriving[:, :COLS]).astype(LOW)
    two_grad[...] = dot_tn(active[...], arriving[:, COLS:]).astype(LOW)
    up_grad[0] = dot_tn(normed[...], up_low[...]).astype(LOW)

    @pl.when(step == last)
    def _():
        layer_own[...] = layer_sum[:count]
        layer_other[...] = layer_sum[count:].astype(LOW)
        normed_grad[...] = normed_sum[...].astype(LOW)


def forward_backward(normed, arriving, up, down_one, down_two, bias):
    rows, width = normed.shape
    chunks = up.shape[0]
    hidden = chunks * COLS

    def whole(*shape):
        return pl.BlockSpec(shape, lambda j: (0,) * len(shape))

    def chunk(height):
        return pl.BlockSpec((height, COLS), lambda j: (j, 0))

    unit = pl.BlockSpec((1, width, COLS), lambda j: (j, 0, 0))
    across = pl.BlockSpec((1, COLS), lambda j: (0, j))
    shape = jax.ShapeDtypeStruct
    return pl.pallas_call(
        forward_backward_kernel,
        grid=(chunks,),
        in_specs=[whole(rows, width), whole(rows, width), unit, chunk(COLS), chunk(COLS), across],
        out_specs=[
            unit, chunk(COLS), chunk(COLS), across,
            whole(rows // 2, width), whole(rows // 2, width), whole(rows, width),
        ],
        out_shape=[
            low_shape(chunks, width, COLS), low_shape(hidden, COLS), low_shape(hidden, COLS),
            shape((1, hidden), FULL), shape((rows // 2, width), FULL),
            low_shape(rows // 2, width), low_shape(rows, width),
        ],
        scratch_shapes=[
            pltpu.VMEM((rows, width), FULL), pltpu.VMEM((rows, width), FULL),
            pltpu.VMEM((rows, COLS), LOW), pltpu.VMEM((rows, COLS), LOW),
        ],
        compiler_params=pltpu.CompilerParams(vmem_limit_bytes=VMEM_BYTES),
        cost_estimate=pl.CostEstimate(
            flops=12 * rows * width * hidden,
            bytes_accessed=8 * width * hidden + 8 * rows * width,
            transcendentals=rows * hidden,
        ),
    )(normed, arriving, up, down_one, down_two, bias)


def norm_forward(values, gain, shift):
    center = values - jnp.mean(values, axis=-1, keepdims=True)
    inverse = lax.rsqrt(jnp.mean(center * center, axis=-1, keepdims=True) + 1e-05)
    unit = center * inverse
    return (unit * gain + shift, unit, inverse)


def norm_backward(grad_out, unit, inverse, gain):
    scaled = grad_out * gain
    return inverse * (
        scaled
        - jnp.mean(scaled, axis=-1, keepdims=True)
        - unit * jnp.mean(scaled * unit, axis=-1, keepdims=True)
    )


def adam_step(weight, first, second, grad, rate, decay):
    first_new = BETA_ONE * first + (1.0 - BETA_ONE) * grad
    second_new = BETA_TWO * second + (1.0 - BETA_TWO) * grad * grad
    mean_hat = first_new / (1.0 - BETA_ONE**STEP)
    square_hat = second_new / (1.0 - BETA_TWO**STEP)
    fresh = weight - rate * (mean_hat / (jnp.sqrt(square_hat) + ADAM_EPS) + decay * weight)
    return (first_new, second_new, fresh)


def per_device(
    tokens,
    cotangent,
    lengths,
    joint_weight,
    joint_first,
    joint_second,
    output_weight,
    output_first,
    output_second,
    expand_weight,
    expand_first,
    expand_second,
    reduce_weight,
    reduce_first,
    reduce_second,
    vector_weight,
    vector_first,
    vector_second,
):
    me = coordinates()
    core = me["core"]
    places = places_of(me)
    across = flip("core", 1)
    count, width = tokens.shape
    local = width // 2
    heads = local // HEAD_DIM
    units = 256

    def mine(array, axis):
        return lax.dynamic_index_in_dim(array, core, axis, keepdims=False)

    joint_own = mine(joint_weight.reshape(128, 3, 2, local), 2).astype(LOW)
    vector_own = jnp.pad(vector_weight.astype(LOW).reshape(3, local), ((0, 13), (0, 0)))
    joint_held, joint_far, marks = gather(
        me,
        joint_own[:, 0],
        jnp.concatenate([joint_own[:, 1], vector_own]),
        joint_own[:, 2],
        None,
    )
    up_own = mine(expand_weight.reshape(128, 8, 2, units), 2).astype(LOW).reshape(128, 4, COLS)
    down_own = mine(reduce_weight.reshape(2, units, 2, COLS), 0).astype(LOW)
    out_own = (
        output_weight.astype(LOW).reshape(4, 32, 2, COLS).transpose(0, 2, 1, 3).reshape(4, 64, COLS)
    )
    rest_held, rest_far, _ = gather(
        me,
        rows_of(up_own[:, :3].reshape(2, 64, 3, COLS).transpose(0, 2, 1, 3)),
        rows_of(up_own[:, 3], down_own[:, 0]),
        down_own[:, 1],
        out_own,
        marks,
    )

    tokens = jnp.concatenate([tokens, send(tokens, across)])
    cotangent = jnp.concatenate([cotangent, send(cotangent, across)])
    lengths = jnp.concatenate([lengths, send(lengths, across)])

    raw = [a for pair in zip(joint_held, joint_far) for a in pair]
    query_mat, key_mat, value_mat, vectors = copies(
        joint_plan, places, raw, [low_shape(8, 128, COLS)] * 3 + [low_shape(8, 16, COLS)]
    )
    query_mat, key_mat, value_mat = (
        a.reshape(width, local) for a in (query_mat, key_mat, value_mat)
    )
    vector_rows = (
        vectors[:, :3].reshape(8, 12, 128).transpose(1, 0, 2).reshape(12, width)
    ).astype(FULL)
    raw = [a for pair in zip(rest_held, rest_far) for a in pair]
    raw[:2] = [a.reshape(2, 4, 3, 64, COLS) for a in raw[:2]]
    up_mat, one_mat, two_mat, out_mat = copies(
        rest_plan,
        places,
        raw,
        [
            low_shape(4, 8, 128, COLS),
            low_shape(8, units, COLS),
            low_shape(8, units, COLS),
            low_shape(2, 4, 128, COLS),
        ],
    )
    up_mat, out_mat = up_mat.reshape(4, width, COLS), out_mat.reshape(2, local, COLS)
    one_mat, two_mat = one_mat.reshape(4 * COLS, COLS), two_mat.reshape(4 * COLS, COLS)

    query_bias, value_bias = mine(vector_rows[2:4].reshape(2, 2, local), 1)
    up_bias = mine(vector_rows[7:11].reshape(8, 2, units), 1).reshape(1, -1)

    scale = HEAD_DIM ** (-0.5)
    slots = jnp.arange(count, dtype=jnp.int32)[None]
    opening = lengths[:, :1]
    filled = opening + lengths[:, 1:]
    segment = jnp.where(slots < opening, 0, jnp.where(slots < filled, 1, slots + 2))
    allowed = (segment[:, :, None] == segment[:, None, :]) & (
        slots[:, :, None] >= slots[:, None, :]
    )
    live = (slots < filled).astype(FULL).reshape(-1)
    gain_one, shift_one = (vector_rows[0], vector_rows[1])
    gain_two, shift_two = (vector_rows[5], vector_rows[6])

    def blocks(values):
        return values.reshape(2, count, heads, HEAD_DIM)

    inputs = tokens.astype(FULL)
    normed_one, unit_one, inverse_one = norm_forward(inputs, gain_one, shift_one)
    normed_one_low = normed_one.astype(LOW)
    query_low = blocks((dot(normed_one_low, query_mat) + query_bias).astype(LOW))
    key_low = blocks(dot(normed_one_low, key_mat).astype(LOW))
    value_low = blocks((dot(normed_one_low, value_mat) + value_bias).astype(LOW))
    scores = (
        jnp.einsum("bqhd,bkhd->bhqk", query_low, key_low, preferred_element_type=FULL) * scale
    )
    scores = jnp.where(allowed[:, None], scores, -1e30)
    probs = jax.nn.softmax(scores, axis=-1)
    probs_low = probs.astype(LOW)
    attended_low = (
        jnp.einsum("bhqk,bkhd->bqhd", probs_low, value_low, preferred_element_type=FULL)
        .reshape(2 * count, local)
        .astype(LOW)
    )

    def other_side(values):
        return jnp.concatenate([values[count:], values[:count]])

    branch = jnp.concatenate([dot(attended_low, out_mat[0]), dot(attended_low, out_mat[1])], axis=1)
    branch = branch.astype(LOW)
    branch_far = other_side(send(branch, across))
    middle = inputs + (branch.astype(FULL) + branch_far.astype(FULL)) + vector_rows[4]
    normed_two, unit_two, inverse_two = norm_forward(middle, gain_two, shift_two)
    arriving = cotangent.astype(FULL) * live[:, None]
    up_part, one_part, two_part, up_bias_grad, layer_own, layer_other, normed_two_part = (
        forward_backward(
            normed_two.astype(LOW), arriving.astype(LOW), up_mat, one_mat, two_mat, up_bias
        )
    )
    layer_far = send(layer_other, across)
    layer_out = (middle[:count] + layer_own + layer_far.astype(FULL) + vector_rows[11]).astype(LOW)

    normed_two_grad = normed_two_part.astype(FULL) + other_side(
        send(normed_two_part, across)
    ).astype(FULL)
    middle_grad = arriving + norm_backward(normed_two_grad, unit_two, inverse_two, gain_two)
    branch_low = middle_grad.astype(LOW)
    out_part = jnp.stack(
        [dot_tn(attended_low, branch_low[:, :COLS]), dot_tn(attended_low, branch_low[:, COLS:])]
    ).astype(LOW)

    pair_x, pair_y = low_shape(2, 4, 3, 64, COLS), low_shape(2, 2, 384, COLS)
    pair_z = low_shape(2, 4, 2, 96, COLS)
    raw = copies(
        lambda at, mats, arrays: [(b, a) for a, b in rest_plan(at, arrays, mats)],
        places,
        (
            up_part.reshape(4, 8, 128, COLS),
            one_part.reshape(8, units, COLS),
            two_part.reshape(8, units, COLS),
            out_part.reshape(2, 4, 128, COLS),
        ),
        [pair_x, pair_x, pair_y, pair_y, pair_z, pair_z],
    )
    raw[:2] = [a.reshape(2, 4, 192, COLS) for a in raw[:2]]
    rest_own, rest_other = total(me, raw, 32)

    attended_grad = blocks(
        (dot_nt(branch_low[:, :COLS], out_mat[0]) + dot_nt(branch_low[:, COLS:], out_mat[1])).astype(
            LOW
        )
    )
    prob_grad = jnp.einsum(
        "bqhd,bkhd->bhqk", attended_grad, value_low, preferred_element_type=FULL
    )
    value_grad = jnp.einsum(
        "bhqk,bqhd->bkhd", probs_low, attended_grad, preferred_element_type=FULL
    ).astype(LOW)
    score_low = (probs * (prob_grad - jnp.sum(probs * prob_grad, axis=-1, keepdims=True))).astype(
        LOW
    )
    query_grad = (
        jnp.einsum("bhqk,bkhd->bqhd", score_low, key_low, preferred_element_type=FULL) * scale
    ).astype(LOW)
    key_grad = (
        jnp.einsum("bhqk,bqhd->bkhd", score_low, query_low, preferred_element_type=FULL) * scale
    ).astype(LOW)
    query_grad = query_grad.reshape(2 * count, local)
    key_grad = key_grad.reshape(2 * count, local)
    value_grad = value_grad.reshape(2 * count, local)
    parts = [
        dot_tn(normed_one_low, grad).astype(LOW).reshape(8, 128, COLS)
        for grad in (query_grad, key_grad, value_grad)
    ]
    pair_x, pair_y = low_shape(2, 4, 64, COLS), low_shape(2, 2, 128, COLS)
    pair_z = low_shape(2, 4, 2, 32, COLS)
    raw = copies(
        lambda at, mats, arrays: [(b, a) for a, b in joint_plan(at, arrays, (*mats, None))],
        places,
        parts,
        [pair_x, pair_x, pair_y, pair_y, pair_z, pair_z],
    )
    joint_mine, joint_other = total(me, raw, 0)

    normed_one_part = (
        dot_nt(query_grad, query_mat) + dot_nt(key_grad, key_mat) + dot_nt(value_grad, value_mat)
    )
    normed_one_grad = normed_one_part[:count] + send(
        normed_one_part[count:].astype(LOW), across
    ).astype(FULL)
    unit_own = unit_one[:count]
    input_grad = middle_grad[:count] + norm_backward(
        normed_one_grad, unit_own, inverse_one[:count], gain_one
    )

    is_core = (jnp.arange(2) == core).astype(FULL)

    def own_half(values):
        return (is_core[:, None] * values[None]).reshape(-1)

    up_mine = is_core[None, :, None] * up_bias_grad.reshape(8, 1, units)
    two_own = normed_two_grad[:count]
    vector_local = jnp.concatenate(
        [
            jnp.stack(
                [
                    jnp.sum(normed_one_grad * unit_own, axis=0),
                    jnp.sum(normed_one_grad, axis=0),
                    own_half(jnp.sum(query_grad.astype(FULL), axis=0)),
                    own_half(jnp.sum(value_grad.astype(FULL), axis=0)),
                    jnp.sum(branch_low[:count].astype(FULL), axis=0),
                    jnp.sum(two_own * unit_two[:count], axis=0),
                    jnp.sum(two_own, axis=0),
                ]
            ),
            up_mine.reshape(4, width),
            jnp.sum(arriving[:count], axis=0)[None],
        ],
        axis=0,
    )
    vector_grad = lax.dynamic_slice(
        sum_all(vector_local), (0, 128 * lax.axis_index("shard")), (12, 128)
    )

    def joined(own, other, axis):
        return jnp.where(
            core == 0,
            jnp.concatenate([own, other], axis=axis),
            jnp.concatenate([other, own], axis=axis),
        )

    def joint_columns(parts):
        return jnp.stack(parts[:3], axis=1)

    joint_grad = joined(
        joint_columns(joint_mine)[:, :, None], joint_columns(joint_other)[:, :, None], 2
    ).reshape(128, 6 * COLS).astype(FULL)

    def up_columns(parts):
        along_x, along_y, _, _ = parts
        three = along_x.reshape(2, 3, 64, COLS).transpose(0, 2, 1, 3).reshape(128, 3 * COLS)
        return jnp.concatenate([three, along_y[:128]], axis=1).reshape(128, 8, 1, units)

    up_grad = joined(up_columns(rest_own), up_columns(rest_other), 2)
    up_grad = up_grad.reshape(128, 16 * units).astype(FULL)

    def down_columns(parts):
        return jnp.concatenate([parts[1][128:], parts[2]], axis=1)

    down_grad = joined(down_columns(rest_own), down_columns(rest_other), 0).astype(FULL)
    out_grad = jnp.where(core == me["xh"], rest_own[3], rest_other[3])
    out_grad = out_grad.transpose(0, 2, 1, 3).reshape(128, width).astype(FULL)

    shard_grads = (joint_grad, out_grad, up_grad, down_grad, vector_grad)
    masters = (joint_weight, output_weight, expand_weight, reduce_weight, vector_weight)
    firsts = (joint_first, output_first, expand_first, reduce_first, vector_first)
    seconds = (joint_second, output_second, expand_second, reduce_second, vector_second)
    rates = (MATRIX_RATE, OUTPUT_RATE, MATRIX_RATE, MATRIX_RATE, VECTOR_RATE)
    decays = (MATRIX_DECAY, MATRIX_DECAY, MATRIX_DECAY, MATRIX_DECAY, 0.0)
    means, spreads, nexts = ([], [], [])
    for index in range(5):
        first_new, second_new, fresh = adam_step(
            masters[index],
            firsts[index],
            seconds[index],
            shard_grads[index],
            rates[index],
            decays[index],
        )
        means.append(first_new)
        spreads.append(second_new)
        nexts.append(fresh)
    return (layer_out, input_grad, *shard_grads, *means, *spreads, *nexts)


def solution(mesh):
    rows, columns, split = P("shard", None), P(None, "shard"), P(("wide", "shard"), None)
    state = (rows, rows, rows, rows, columns)
    return jax.shard_map(
        per_device,
        mesh=mesh,
        in_specs=(split, split, split) + (rows,) * 12 + (columns,) * 3,
        out_specs=(split, split) + state * 4,
        check_vma=False,
    )
```

```python
import jax
import jax.numpy as jnp
from jax import lax
from jax.experimental import pallas as pl
from jax.experimental.pallas import tpu as pltpu
from jax.sharding import PartitionSpec as P

HEAD_DIM = 64
STEP = 10


ROOT_TWO_PI = 0.7978845608028654
CUBIC = 0.044715
BETA_ONE = 0.9
BETA_TWO = 0.999
ADAM_EPS = 1e-08
MATRIX_RATE = 0.03
OUTPUT_RATE = 0.1
VECTOR_RATE = 0.2
MATRIX_DECAY = 0.1

LOW = jnp.bfloat16
FULL = jnp.float32
AXES = ("wide", "shard")
SIZES = (4, 2, 2, 2, 4)
COLS = 512
VMEM_BYTES = 60 * 1024 * 1024


def coordinates():
    wide, shard = lax.axis_index("wide"), lax.axis_index("shard")
    z, xl, core = wide // 4, (wide // 2) % 2, wide % 2
    xh, y = shard // 4, shard % 4
    return {"z": z, "x": 2 * xh + xl, "y": y, "xl": xl, "xh": xh, "core": core}


def route(partner):
    pairs = []
    for source in range(128):
        rest, places = source, []
        for size in reversed(SIZES):
            places.append(rest % size)
            rest //= size
        y, xh, core, xl, z = places
        target = partner({"z": z, "x": 2 * xh + xl, "y": y, "core": core})
        flat = 0
        for place, size in zip(
            (target["z"], target["x"] % 2, target["core"], target["x"] // 2, target["y"]), SIZES
        ):
            flat = flat * size + place
        pairs.append((source, flat))
    return pairs


def flip(axis, bits):
    return route(lambda at: {**at, axis: at[axis] ^ bits})


def turn(axis, step):
    return route(lambda at: {**at, axis: at[axis] ^ (1 if (at["core"] + step) % 2 == 0 else 3)})


def send(value, pairs):
    return lax.ppermute(value, AXES, pairs)


def added(a, b):
    return (a.astype(FULL) + b.astype(FULL)).astype(LOW)


def orders(me, axis):
    here = me[axis]
    one = jnp.where(me["core"] == 0, 1, 3)
    return [here, here ^ one, here ^ (4 - one), here ^ 2]


def places_of(me):
    return jnp.stack(
        orders(me, "x") + orders(me, "y") + orders(me, "z") + [me["xh"], me["core"]]
    ).astype(jnp.int32)


def after(value, *others):
    return lax.optimization_barrier((value, *others))[0]


def rows_of(*parts):
    return jnp.concatenate([p.reshape(-1, COLS) for p in parts])


def gather(me, along_x, along_y, along_z, out, follow=None):
    marks = []

    def wait(value, index):
        return value if follow is None else after(value, follow[index])

    half = lax.dynamic_index_in_dim(
        along_x.reshape(2, -1, COLS), me["xl"], 0, keepdims=False
    )
    quarter = lax.dynamic_index_in_dim(
        along_z.reshape(4, -1, COLS), me["z"], 0, keepdims=False
    )
    size_y, size_z = along_y.shape[0], quarter.shape[0]
    payload = [along_y, quarter]
    if out is not None:
        own_out = lax.dynamic_index_in_dim(out, me["z"], 0, keepdims=False)
        payload.append(own_out)
    other = send(wait(rows_of(*payload), 0), flip("x", 3))
    marks.append(other)
    pair_y = jnp.stack([along_y, other[:size_y]])
    pair_z = jnp.stack([quarter, other[size_y : size_y + size_z]])
    if out is not None:
        both = jnp.where(
            me["core"] == me["xh"], own_out.reshape(2, -1, COLS),
            other[size_y + size_z :].reshape(2, -1, COLS),
        )
        pair_z = jnp.concatenate([pair_z, both], axis=1)
    size_x = half.shape[0]
    first = wait(rows_of(half, pair_z), 1)
    second = send(first, turn("y", 0))
    marks.append(second)
    here = jnp.stack([first, second])
    there = send(wait(here, 2), turn("y", 1))
    marks.append(there)
    plane_x = jnp.concatenate([here[:, :size_x], there[:, :size_x]])
    plane_z = jnp.concatenate([here[:, size_x:], there[:, size_x:]]).reshape(
        (4,) + pair_z.shape
    )
    starts = [(plane_x, "x"), (pair_y, "y"), (plane_z, "z")]
    if follow is not None:
        starts = [(wait(a, 3), axis) for a, axis in starts]
    got = [send(a, turn(axis, 0)) for a, axis in starts]
    marks.append(got[0])
    held = [jnp.stack([a, b]) for (a, _), b in zip(starts, got)]
    far = [send(a, turn(axis, 1)) for a, (_, axis) in zip(held, starts)]
    return held, far, marks


def halved(keep, away, axis):
    near = added(keep, send(away, turn(axis, 1)))
    return added(near[0], send(near[1], turn(axis, 0)))


def total(me, raw, out_rows):
    along_x, along_y, along_z = (
        halved(raw[0], raw[1], "x"), halved(raw[2], raw[3], "y"), halved(raw[4], raw[5], "z"),
    )
    size_x, size_y = along_x.shape[1], along_y.shape[1]
    size_z = along_z.shape[2] - out_rows
    plane = jnp.concatenate([along_x, along_z.reshape(4, -1, COLS)], axis=1)
    plane = halved(plane[:2], plane[2:], "y")
    half, pair = plane[:size_x], plane[size_x:].reshape(2, size_z + out_rows, COLS)
    out = pair[:, size_z:]
    sums = rows_of(along_y[0], pair[0, :size_z], out)
    sums = added(sums, send(rows_of(along_y[1], pair[1, :size_z], out), flip("x", 3)))
    other = send(rows_of(sums, half), flip("x", 1))
    sums = added(sums, other[: sums.shape[0]])
    other = other[sums.shape[0] :]
    whole_x = jnp.where(
        me["xl"] == 0, jnp.concatenate([half, other]), jnp.concatenate([other, half])
    )
    flat = rows_of(whole_x, sums[:size_y])
    block = sums[size_y:]
    other = send(rows_of(flat, block), turn("z", 0))
    flat = added(flat, other[: flat.shape[0]])
    blocks = rows_of(block, other[flat.shape[0] :])
    other = send(rows_of(flat, blocks), turn("z", 1))
    flat = added(flat, other[: flat.shape[0]])
    blocks = rows_of(blocks, other[flat.shape[0] :]).reshape((4,) + block.shape)
    where = orders(me, "z")
    ordered = [
        sum(jnp.where(where[k] == place, blocks[k], 0) for k in range(4)) for place in range(4)
    ]
    ordered = jnp.stack([a.astype(LOW) for a in ordered])
    both = rows_of(flat, ordered)
    far = send(both, flip("core", 1))

    def parts(rows):
        x, y = rows[: 2 * size_x], rows[2 * size_x : 2 * size_x + size_y]
        z = rows[2 * size_x + size_y :].reshape(4, size_z + 2 * out_rows, COLS)
        return x, y, z[:, :size_z].reshape(-1, COLS), z[:, size_z:].reshape(
            4, 2, out_rows, COLS
        )

    return parts(both), parts(far)


def sum_all(value):
    for pairs in (
        flip("core", 1),
        turn("x", 0),
        turn("x", 1),
        turn("y", 0),
        turn("y", 1),
        turn("z", 0),
        turn("z", 1),
    ):
        value = value + send(value, pairs)
    return value


def rows_at(start, size):
    return pl.ds(pl.multiple_of(start, size), size)


def joint_plan(places, raw, mats):
    query, key, value, vectors = mats
    pairs = []
    for ky in range(4):
        y = places[4 + ky]
        for kx in range(4):
            x = places[kx]
            start = ((x // 2) * 4 + y) * 128 + (x % 2) * 64
            pairs.append((raw[0 + kx // 2].at[kx % 2, ky], query.at[rows_at(start, 64)]))
        for p in range(2):
            shard = (places[12] ^ p) * 4 + y
            source = raw[2 + ky // 2].at[ky % 2, p]
            pairs.append((source.at[pl.ds(0, 128)], key.at[rows_at(shard * 128, 128)]))
            if vectors is not None:
                pairs.append(
                    (
                        source.at[pl.ds(128, 16), pl.ds(0, 128)],
                        vectors.at[:, rows_at(shard * 128, 128)],
                    )
                )
            for kz in range(4):
                start = shard * 128 + places[8 + kz] * 32
                pairs.append((raw[4 + kz // 2].at[kz % 2, ky, p], value.at[rows_at(start, 32)]))
    return pairs


def up_plan(places, raw, mats):
    up, down_one, down_two = mats
    pairs = []
    for ky in range(4):
        y = places[4 + ky]
        for kx in range(4):
            x = places[kx]
            start = ((x // 2) * 4 + y) * 128 + (x % 2) * 64
            for j in range(3):
                pairs.append(
                    (raw[0 + kx // 2].at[kx % 2, ky, j], up.at[j, rows_at(start, 64)])
                )
        for p in range(2):
            shard = (places[12] ^ p) * 4 + y
            source = raw[2 + ky // 2].at[ky % 2, p]
            pairs.append((source.at[pl.ds(0, 128)], up.at[3, rows_at(shard * 128, 128)]))
            pairs.append((source.at[pl.ds(128, 256)], down_one.at[rows_at(shard * 256, 256)]))
            for kz in range(4):
                source = raw[4 + kz // 2].at[kz % 2, ky, p]
                start = shard * 256 + places[8 + kz] * 64
                pairs.append((source.at[pl.ds(0, 64)], down_two.at[rows_at(start, 64)]))
    return pairs


def out_plan(places, raw, first, mat):
    pairs = []
    for ky in range(4):
        for kz in range(4):
            start = places[4 + ky] * 128 + places[8 + kz] * 32
            for p in range(2):
                source = raw[kz // 2].at[kz % 2, ky, p]
                pairs.append((source.at[pl.ds(first, 32)], mat.at[p, rows_at(start, 32)]))
    return pairs


def started(pairs, sems):
    all_of_them = [pltpu.make_async_copy(a, b, sems.at[i]) for i, (a, b) in enumerate(pairs)]
    for copy in all_of_them:
        copy.start()
    return all_of_them


def finished(all_of_them):
    for copy in all_of_them:
        copy.wait()


def turned(pairs):
    return [(b, a) for a, b in pairs]


def low_shape(*shape):
    return jax.ShapeDtypeStruct(shape, LOW)


def full_shape(*shape):
    return jax.ShapeDtypeStruct(shape, FULL)


SCALARS = pl.BlockSpec(memory_space=pltpu.SMEM)
INSIDE = pl.BlockSpec(memory_space=pltpu.VMEM)
OUTSIDE = pl.BlockSpec(memory_space=pl.ANY)


def call(kernel, in_specs, outs, scratch, flops, args):
    shapes, specs = [o[0] for o in outs], [o[1] for o in outs]
    moved = sum(a.size * a.dtype.itemsize for a in (*args, *shapes))
    return pl.pallas_call(
        kernel,
        out_shape=shapes,
        in_specs=in_specs,
        out_specs=specs,
        scratch_shapes=scratch,
        compiler_params=pltpu.CompilerParams(vmem_limit_bytes=VMEM_BYTES),
        cost_estimate=pl.CostEstimate(flops=flops, bytes_accessed=moved, transcendentals=0),
    )(*args)


def gelu_both(upward):
    square = upward * upward
    tangent = jnp.tanh(ROOT_TWO_PI * upward * (1.0 + CUBIC * square))
    half = 0.5 * (1.0 + tangent)
    slope = half + 0.5 * upward * (1.0 - tangent * tangent) * ROOT_TWO_PI * (
        1.0 + 3.0 * CUBIC * square
    )
    return upward * half, slope


def dot(a, b):
    return jnp.dot(a, b, preferred_element_type=FULL)


def dot_nt(a, b):
    return lax.dot_general(a, b, (((1,), (1,)), ((), ())), preferred_element_type=FULL)


def dot_tn(a, b):
    return lax.dot_general(a, b, (((0,), (0,)), ((), ())), preferred_element_type=FULL)


def unit_of(values):
    center = values - jnp.mean(values, axis=-1, keepdims=True)
    inverse = lax.rsqrt(jnp.mean(center * center, axis=-1, keepdims=True) + 1e-05)
    return center * inverse, inverse


def norm_backward(grad_out, unit, inverse, gain):
    scaled = grad_out * gain
    return inverse * (
        scaled
        - jnp.mean(scaled, axis=-1, keepdims=True)
        - unit * jnp.mean(scaled * unit, axis=-1, keepdims=True)
    )


def row_of(vectors, row):
    return vectors[row : row + 1, :].astype(FULL)


def own_columns(full, core, size):
    groups = full.shape[1] // (2 * size)
    first = jnp.concatenate(
        [full[:, (2 * g) * size : (2 * g + 1) * size] for g in range(groups)], axis=1
    )
    second = jnp.concatenate(
        [full[:, (2 * g + 1) * size : (2 * g + 2) * size] for g in range(groups)], axis=1
    )
    return jnp.where(core == 0, first, second)


def barred(lengths, block, first, height, span):
    shape = (height, span)
    rows = lax.broadcasted_iota(jnp.int32, shape, 0) + first
    keys = lax.broadcasted_iota(jnp.int32, shape, 1)
    opening = lengths[block, 0]
    filled = opening + lengths[block, 1]
    begin = jnp.where(rows < opening, 0, jnp.where(rows < filled, opening, rows))
    return jnp.where((keys <= rows) & (keys >= begin), 0.0, -1e30)


TILE = 128


def attention_kernel(
    places, lengths, own, other, *refs,
):
    raw, refs = refs[:6], refs[6:]
    (normed, query, key, value, attended, vectors, query_mat, key_mat, value_mat,
     mask, sems) = refs
    copies = started(joint_plan(places, raw, (query_mat, key_mat, value_mat, vectors)), sems)
    count = own.shape[0]
    spans = count // TILE
    for block in range(2):
        for i in range(spans):
            mask[block, i * TILE : (i + 1) * TILE, : (i + 1) * TILE] = barred(
                lengths, block, i * TILE, TILE, (i + 1) * TILE
            )
    finished(copies)
    gain, shift = row_of(vectors, 0), row_of(vectors, 1)
    core = places[13]
    query_bias = own_columns(row_of(vectors, 2), core, COLS)
    value_bias = own_columns(row_of(vectors, 3), core, COLS)
    for block, tokens in enumerate((own, other)):
        rows = pl.ds(block * count, count)
        unit, _ = unit_of(tokens[...].astype(FULL))
        low = (unit * gain + shift).astype(LOW)
        normed[rows, :] = low
        query[rows, :] = ((dot(low, query_mat[...]) + query_bias).astype(LOW) * 0.125).astype(LOW)
        key[rows, :] = dot(low, key_mat[...]).astype(LOW)
        value[rows, :] = (dot(low, value_mat[...]) + value_bias).astype(LOW)

    def two_heads(index, carry):
        block, cols = index // 4, rows_at((index % 4) * TILE, TILE)
        base = block * count
        lane = lax.broadcasted_iota(jnp.int32, (TILE, TILE), 1) < HEAD_DIM
        for i in range(spans):
            span = (i + 1) * TILE
            rows = rows_at(base + i * TILE, TILE)
            keys = rows_at(base, TILE)
            keys = pl.ds(keys.start, span)
            both = query[rows, cols]
            bar = mask[block, i * TILE : span, :span]
            outs = []
            for side in (lane, ~lane):
                scores = dot_nt(jnp.where(side, both, 0), key[keys, cols]) + bar
                probs = jnp.exp(scores - jnp.max(scores, axis=-1, keepdims=True))
                probs = probs * (1.0 / jnp.sum(probs, axis=-1, keepdims=True))
                outs.append(dot(probs.astype(LOW), value[keys, cols]))
            attended[rows, cols] = jnp.where(lane, outs[0], outs[1]).astype(LOW)
        return carry

    lax.fori_loop(0, 8, two_heads, 0)


def attention(places, lengths, own, other, raw):
    count, width = own.shape
    rows = 2 * count
    mat = (low_shape(width, COLS), INSIDE)
    half = (low_shape(rows, COLS), INSIDE)
    return call(
        attention_kernel,
        [SCALARS, SCALARS, INSIDE, INSIDE] + [OUTSIDE] * 6,
        [(low_shape(rows, width), INSIDE), half, half, half, half]
        + [(low_shape(16, width), INSIDE), mat, mat, mat],
        [pltpu.VMEM((2, count, count), FULL), pltpu.SemaphoreType.DMA((64,))],
        6 * rows * width * COLS + 4 * rows * count * COLS,
        (places, lengths, own, other, *raw),
    )


def output_kernel(places, attended, raw_one, raw_two, branch, out_mat, sems):
    finished(started(out_plan(places, (raw_one, raw_two), 64, out_mat), sems))
    for half in range(2):
        branch[:, half * COLS : (half + 1) * COLS] = dot(attended[...], out_mat[half]).astype(LOW)


def output(places, attended, raw):
    rows, local = attended.shape
    return call(
        output_kernel,
        [SCALARS, INSIDE, OUTSIDE, OUTSIDE],
        [(low_shape(rows, 2 * COLS), INSIDE), (low_shape(2, local, COLS), INSIDE)],
        [pltpu.SemaphoreType.DMA((32,))],
        4 * rows * local * COLS,
        (places, attended, *raw),
    )


def forward_backward_kernel(
    places, lengths, own, other, arriving_own, arriving_other, branch, branch_far, vectors, *refs
):
    raw, refs = refs[:6], refs[6:]
    sent, refs = refs[:6], refs[6:]
    (middle, layer_own, layer_other, normed_grad, bias_grad,
     up, down_one, down_two, up_grad, one_grad, two_grad,
     normed, arriving, layer_sum, normed_sum, active, up_low, sems) = refs
    copies = started(up_plan(places, raw, (up, down_one, down_two)), sems)
    count = own.shape[0]
    tile = 256
    gain, shift = row_of(vectors, 5), row_of(vectors, 6)
    for block, (tokens, cotangent) in enumerate(((own, arriving_own), (other, arriving_other))):
        rows, far = pl.ds(block * count, count), pl.ds((1 - block) * count, count)
        summed = branch[rows, :].astype(FULL) + branch_far[far, :].astype(FULL)
        held = tokens[...].astype(FULL) + summed + row_of(vectors, 4)
        middle[rows, :] = held
        unit, _ = unit_of(held)
        normed[rows, :] = (unit * gain + shift).astype(LOW)
        slots = lax.broadcasted_iota(jnp.int32, cotangent.shape, 0)
        live = slots < lengths[block, 0] + lengths[block, 1]
        arriving[rows, :] = jnp.where(live, cotangent[...], 0)
    layer_sum[...] = jnp.zeros_like(layer_sum)
    normed_sum[...] = jnp.zeros_like(normed_sum)
    bias_grad[...] = jnp.zeros_like(bias_grad)
    core = places[13]
    biases = jnp.concatenate(
        [own_columns(row_of(vectors, 7 + k), core, 256) for k in range(4)], axis=0
    )
    finished(copies)

    def chunk(j, carry):
        hidden = rows_at(j * COLS, COLS)
        bias = jnp.zeros((1, COLS), FULL)
        for k in range(4):
            bias = jnp.where(j == k, biases[k : k + 1], bias)

        def rows_step(index, carry):
            rows = rows_at(index * tile, tile)
            upward = dot(normed[rows, :], up[j]) + bias
            act, slope = gelu_both(upward)
            act = act.astype(LOW)
            active[rows, :] = act
            layer_sum[rows, :COLS] += dot(act, down_one[hidden, :])
            layer_sum[rows, COLS:] += dot(act, down_two[hidden, :])
            grad = dot_nt(arriving[rows, :COLS], down_one[hidden, :])
            grad += dot_nt(arriving[rows, COLS:], down_two[hidden, :])
            low = (grad * slope).astype(LOW)
            up_low[rows, :] = low
            bias_grad[pl.ds(j, 1), :] += jnp.sum(low.astype(FULL), axis=0, keepdims=True)
            normed_sum[rows, :] += dot_nt(low, up[j])
            return carry

        lax.fori_loop(0, normed.shape[0] // tile, rows_step, 0)
        one_grad[hidden, :] = dot_tn(active[...], arriving[:, :COLS]).astype(LOW)
        two_grad[hidden, :] = dot_tn(active[...], arriving[:, COLS:]).astype(LOW)
        up_grad[j] = dot_tn(normed[...], up_low[...]).astype(LOW)
        return carry

    lax.fori_loop(0, up.shape[0], chunk, 0)
    copies = started(turned(up_plan(places, sent, (up_grad, one_grad, two_grad))), sems)
    layer_own[...] = middle[:count, :] + layer_sum[:count, :] + row_of(vectors, 11)
    layer_other[...] = layer_sum[count:, :].astype(LOW)
    normed_grad[...] = normed_sum[...].astype(LOW)
    finished(copies)


def forward_backward(places, lengths, tokens, arriving, branch, branch_far, vectors, raw):
    count, width = tokens[0].shape
    rows, hidden = 2 * count, 4 * COLS
    sent = [low_shape(2, 4, 3, 64, COLS), low_shape(2, 2, 384, COLS), low_shape(2, 4, 2, 64, COLS)]
    inside = [
        full_shape(rows, width), full_shape(count, width), low_shape(count, width),
        low_shape(rows, width), full_shape(4, COLS),
    ]
    vmem = pltpu.VMEM
    mats = [vmem((4, width, COLS), LOW), vmem((hidden, COLS), LOW), vmem((hidden, COLS), LOW)]
    return call(
        forward_backward_kernel,
        [SCALARS, SCALARS] + [INSIDE] * 7 + [OUTSIDE] * 6,
        [(s, OUTSIDE) for s in sent for _ in range(2)] + [(s, INSIDE) for s in inside],
        mats + mats
        + [vmem((rows, width), LOW), vmem((rows, width), LOW)]
        + [vmem((rows, width), FULL), vmem((rows, width), FULL)]
        + [vmem((rows, COLS), LOW), vmem((rows, COLS), LOW), pltpu.SemaphoreType.DMA((96,))],
        12 * rows * width * hidden,
        (places, lengths, *tokens, *arriving, branch, branch_far, vectors, *raw),
    )


def output_backward_kernel(
    places, lengths, arriving_own, arriving_other, middle, part, part_far, vectors, attended,
    out_mat, sent_one, sent_two, middle_grad, attended_grad, sums, branch, out_grad, sems,
):
    count = arriving_own.shape[0]
    gain = row_of(vectors, 5)
    for block, cotangent in enumerate((arriving_own, arriving_other)):
        rows, far = pl.ds(block * count, count), pl.ds((1 - block) * count, count)
        unit, inverse = unit_of(middle[rows, :])
        grad = part[rows, :].astype(FULL) + part_far[far, :].astype(FULL)
        slots = lax.broadcasted_iota(jnp.int32, cotangent.shape, 0)
        live = slots < lengths[block, 0] + lengths[block, 1]
        arriving = jnp.where(live, cotangent[...].astype(FULL), 0.0)
        held = arriving + norm_backward(grad, unit, inverse, gain)
        low = held.astype(LOW)
        branch[rows, :] = low
        if block == 0:
            middle_grad[...] = held
            sums[...] = jnp.zeros_like(sums)
            sums[0:1, :] = jnp.sum(low.astype(FULL), axis=0, keepdims=True)
            sums[1:2, :] = jnp.sum(grad * unit, axis=0, keepdims=True)
            sums[2:3, :] = jnp.sum(grad, axis=0, keepdims=True)
            sums[3:4, :] = jnp.sum(arriving, axis=0, keepdims=True)
    for half in range(2):
        cols = slice(half * COLS, (half + 1) * COLS)
        out_grad[half] = dot_tn(attended[...], branch[:, cols]).astype(LOW)
    copies = started(turned(out_plan(places, (sent_one, sent_two), 0, out_grad)), sems)
    attended_grad[...] = (
        dot_nt(branch[:, :COLS], out_mat[0]) + dot_nt(branch[:, COLS:], out_mat[1])
    ).astype(LOW)
    finished(copies)


def output_backward(places, lengths, arriving, middle, part, part_far, vectors, attended, out_mat):
    rows, width = middle.shape
    sent = (low_shape(2, 4, 2, 32, COLS), OUTSIDE)
    inside = [full_shape(rows // 2, width), low_shape(rows, COLS), full_shape(8, width)]
    return call(
        output_backward_kernel,
        [SCALARS, SCALARS] + [INSIDE] * 8,
        [sent, sent] + [(s, INSIDE) for s in inside],
        [pltpu.VMEM((rows, width), LOW), pltpu.VMEM((2, COLS, COLS), LOW)]
        + [pltpu.SemaphoreType.DMA((32,))],
        8 * rows * width * COLS,
        (places, lengths, *arriving, middle, part, part_far, vectors, attended, out_mat),
    )


def attention_backward_kernel(
    places, lengths, query, key, value, grad_in, normed, *refs
):
    sent, refs = refs[:6], refs[6:]
    (query_grad, key_grad, value_grad, sums, mask, key_sum, value_sum,
     query_part, key_part, value_part, sems) = refs
    count = query.shape[0] // 2
    spans = count // TILE
    for block in range(2):
        for i in range(spans):
            mask[block, i * TILE : (i + 1) * TILE, : (i + 1) * TILE] = barred(
                lengths, block, i * TILE, TILE, (i + 1) * TILE
            )

    def two_heads(index, carry):
        block, cols = index // 4, rows_at((index % 4) * TILE, TILE)
        base = block * count
        lane = lax.broadcasted_iota(jnp.int32, (TILE, TILE), 1) < HEAD_DIM
        lanes = lax.broadcasted_iota(jnp.int32, (count, TILE), 1) < HEAD_DIM
        for i in range(spans):
            span = (i + 1) * TILE
            rows = rows_at(base + i * TILE, TILE)
            keys = rows_at(base, TILE)
            keys = pl.ds(keys.start, span)
            two_q, two_g = query[rows, cols], grad_in[rows, cols]
            two_k, two_v = key[keys, cols], value[keys, cols]
            bar = mask[block, i * TILE : span, :span]
            outs = []
            for h, side in enumerate((lane, ~lane)):
                scores = dot_nt(jnp.where(side, two_q, 0), two_k) + bar
                probs = jnp.exp(scores - jnp.max(scores, axis=-1, keepdims=True))
                probs = probs * (1.0 / jnp.sum(probs, axis=-1, keepdims=True))
                grad = dot_nt(jnp.where(side, two_g, 0), two_v)
                weighted = probs * grad
                grad = probs * (grad - jnp.sum(weighted, axis=-1, keepdims=True))
                low = grad.astype(LOW)
                outs.append(dot(low, two_k))
                key_now = dot_tn(low, two_q)
                value_now = dot_tn(probs.astype(LOW), two_g)
                if i == 0:
                    key_sum[h, :span] = key_now
                    value_sum[h, :span] = value_now
                else:
                    before = span - TILE
                    key_sum[h, :before] += key_now[:before]
                    value_sum[h, :before] += value_now[:before]
                    key_sum[h, before:span] = key_now[before:]
                    value_sum[h, before:span] = value_now[before:]
            query_grad[rows, cols] = (jnp.where(lane, outs[0], outs[1]) * 0.125).astype(LOW)
        rows = pl.ds(pl.multiple_of(base, TILE), count)
        key_grad[rows, cols] = jnp.where(lanes, key_sum[0], key_sum[1]).astype(LOW)
        value_grad[rows, cols] = jnp.where(lanes, value_sum[0], value_sum[1]).astype(LOW)
        return carry

    lax.fori_loop(0, 8, two_heads, 0)
    for grad, part in (
        (query_grad, query_part), (key_grad, key_part), (value_grad, value_part),
    ):
        part[...] = dot_tn(normed[...], grad[...]).astype(LOW)
    parts = (query_part, key_part, value_part, None)
    copies = started(turned(joint_plan(places, sent, parts)), sems)
    sums[...] = jnp.zeros_like(sums)
    sums[0:1, :] = jnp.sum(query_grad[...].astype(FULL), axis=0, keepdims=True)
    sums[1:2, :] = jnp.sum(value_grad[...].astype(FULL), axis=0, keepdims=True)
    finished(copies)


def attention_backward(places, lengths, query, key, value, grad_in, normed):
    rows, width = normed.shape
    count = rows // 2
    sent = [low_shape(2, 4, 64, COLS), low_shape(2, 2, 128, COLS), low_shape(2, 4, 2, 32, COLS)]
    half, vmem = (low_shape(rows, COLS), INSIDE), pltpu.VMEM
    return call(
        attention_backward_kernel,
        [SCALARS, SCALARS] + [INSIDE] * 5,
        [(s, OUTSIDE) for s in sent for _ in range(2)]
        + [half, half, half, (full_shape(8, COLS), INSIDE)],
        [vmem((2, count, count), FULL), vmem((2, count, TILE), FULL), vmem((2, count, TILE), FULL)]
        + [vmem((width, COLS), LOW)] * 3
        + [pltpu.SemaphoreType.DMA((56,))],
        6 * rows * width * COLS + 10 * rows * count * COLS,
        (places, lengths, query, key, value, grad_in, normed),
    )


def joint_backward_kernel(
    query_grad, key_grad, value_grad, query_mat, key_mat, value_mat, part_own, part_other
):
    count = part_own.shape[0]
    for block, out in enumerate((part_own, part_other)):
        rows = pl.ds(block * count, count)
        whole = dot_nt(query_grad[rows, :], query_mat[...])
        whole += dot_nt(key_grad[rows, :], key_mat[...])
        whole += dot_nt(value_grad[rows, :], value_mat[...])
        out[...] = whole.astype(out.dtype)


def joint_backward(grads, mats):
    rows, width = grads[0].shape[0], mats[0].shape[0]
    return call(
        joint_backward_kernel,
        [INSIDE] * 6,
        [(full_shape(rows // 2, width), INSIDE), (low_shape(rows // 2, width), INSIDE)],
        [],
        6 * rows * width * COLS,
        (*grads, *mats),
    )


def input_kernel(tokens, part, part_far, middle_grad, vectors, input_grad, sums):
    unit, inverse = unit_of(tokens[...].astype(FULL))
    grad = part[...] + part_far[...].astype(FULL)
    input_grad[...] = middle_grad[...] + norm_backward(grad, unit, inverse, row_of(vectors, 0))
    sums[...] = jnp.zeros_like(sums)
    sums[0:1, :] = jnp.sum(grad * unit, axis=0, keepdims=True)
    sums[1:2, :] = jnp.sum(grad, axis=0, keepdims=True)


def input_backward(tokens, part, part_far, middle_grad, vectors):
    return call(
        input_kernel,
        [INSIDE] * 5,
        [(full_shape(*part.shape), INSIDE), (full_shape(8, part.shape[1]), INSIDE)],
        [],
        20 * part.size,
        (tokens, part, part_far, middle_grad, vectors),
    )


def adam_step(weight, first, second, grad, rate, decay):
    first_new = BETA_ONE * first + (1.0 - BETA_ONE) * grad
    second_new = BETA_TWO * second + (1.0 - BETA_TWO) * grad * grad
    mean_hat = first_new / (1.0 - BETA_ONE**STEP)
    square_hat = second_new / (1.0 - BETA_TWO**STEP)
    fresh = weight - rate * (mean_hat / (jnp.sqrt(square_hat) + ADAM_EPS) + decay * weight)
    return (first_new, second_new, fresh)


def per_device(
    tokens,
    cotangent,
    lengths,
    joint_weight,
    joint_first,
    joint_second,
    output_weight,
    output_first,
    output_second,
    expand_weight,
    expand_first,
    expand_second,
    reduce_weight,
    reduce_first,
    reduce_second,
    vector_weight,
    vector_first,
    vector_second,
):
    me = coordinates()
    core = me["core"]
    places = places_of(me)
    across = flip("core", 1)
    width = tokens.shape[1]
    local = width // 2
    units = 256

    def mine(array, axis):
        return lax.dynamic_index_in_dim(array, core, axis, keepdims=False)

    joint_own = mine(joint_weight.reshape(128, 3, 2, local), 2).astype(LOW)
    vector_own = jnp.pad(vector_weight.astype(LOW), ((0, 4), (0, local - 128)))
    joint_held, joint_far, marks = gather(
        me,
        joint_own[:, 0],
        jnp.concatenate([joint_own[:, 1], vector_own]),
        joint_own[:, 2],
        None,
    )
    up_own = mine(expand_weight.reshape(128, 8, 2, units), 2).astype(LOW).reshape(128, 4, COLS)
    down_own = mine(reduce_weight.reshape(2, units, 2, COLS), 0).astype(LOW)
    out_own = (
        output_weight.astype(LOW).reshape(4, 32, 2, COLS).transpose(0, 2, 1, 3).reshape(4, 64, COLS)
    )
    rest_held, rest_far, _ = gather(
        me,
        rows_of(up_own[:, :3].reshape(2, 64, 3, COLS).transpose(0, 2, 1, 3)),
        rows_of(up_own[:, 3], down_own[:, 0]),
        down_own[:, 1],
        out_own,
        marks,
    )

    tokens = (tokens, send(tokens, across))
    cotangent = (cotangent, send(cotangent, across))
    lengths = jnp.concatenate([lengths, send(lengths, across)])

    raw = [a for pair in zip(joint_held, joint_far) for a in pair]
    normed_one, query, key, value, attended, vectors, *joint_mats = attention(
        places, lengths, *tokens, raw
    )
    raw = [a for pair in zip(rest_held, rest_far) for a in pair]
    raw[:2] = [a.reshape(2, 4, 3, 64, COLS) for a in raw[:2]]
    branch, out_mat = output(places, attended, raw[4:])
    branch_far = send(branch, across)
    *sent, middle, layer_own, layer_other, normed_two_part, up_bias_grad = forward_backward(
        places, lengths, tokens, cotangent, branch, branch_far, vectors, raw
    )
    part_far = send(normed_two_part, across)
    layer_out = (layer_own + send(layer_other, across).astype(FULL)).astype(LOW)

    out_one, out_two, middle_grad, attended_grad, two_sums = output_backward(
        places, lengths, cotangent, middle, normed_two_part, part_far, vectors, attended, out_mat
    )
    sent[:2] = [a.reshape(2, 4, 192, COLS) for a in sent[:2]]
    sent[4:] = [jnp.concatenate(a, axis=3) for a in zip(sent[4:], (out_one, out_two))]
    rest_own, rest_other = total(me, sent, 32)

    *sent, query_grad, key_grad, value_grad, head_sums = attention_backward(
        places, lengths, query, key, value, attended_grad, normed_one
    )
    joint_mine, joint_other = total(me, sent, 0)
    part_own, part_other = joint_backward((query_grad, key_grad, value_grad), joint_mats)
    input_grad, one_sums = input_backward(
        tokens[0], part_own, send(part_other, across), middle_grad, vectors
    )

    is_core = (jnp.arange(2) == core).astype(FULL)

    def own_half(values):
        return (is_core[:, None] * values[None]).reshape(1, -1)

    up_mine = is_core[None, :, None] * up_bias_grad.reshape(8, 1, units)
    vector_local = jnp.concatenate(
        [
            one_sums[:2],
            own_half(head_sums[0]),
            own_half(head_sums[1]),
            two_sums[:3],
            up_mine.reshape(4, width),
            two_sums[3:4],
        ],
        axis=0,
    )
    vector_grad = lax.dynamic_slice(
        sum_all(vector_local), (0, 128 * lax.axis_index("shard")), (12, 128)
    )

    def joined(own, other, axis):
        return jnp.where(
            core == 0,
            jnp.concatenate([own, other], axis=axis),
            jnp.concatenate([other, own], axis=axis),
        )

    def joint_columns(parts):
        return jnp.stack(parts[:3], axis=1)

    joint_grad = joined(
        joint_columns(joint_mine)[:, :, None], joint_columns(joint_other)[:, :, None], 2
    ).reshape(128, 6 * COLS).astype(FULL)

    def up_columns(parts):
        along_x, along_y, _, _ = parts
        three = along_x.reshape(2, 3, 64, COLS).transpose(0, 2, 1, 3).reshape(128, 3 * COLS)
        return jnp.concatenate([three, along_y[:128]], axis=1).reshape(128, 8, 1, units)

    up_grad = joined(up_columns(rest_own), up_columns(rest_other), 2)
    up_grad = up_grad.reshape(128, 16 * units).astype(FULL)

    def down_columns(parts):
        return jnp.concatenate([parts[1][128:], parts[2]], axis=1)

    down_grad = joined(down_columns(rest_own), down_columns(rest_other), 0).astype(FULL)
    out_grad = jnp.where(core == me["xh"], rest_own[3], rest_other[3])
    out_grad = out_grad.transpose(0, 2, 1, 3).reshape(128, width).astype(FULL)

    shard_grads = (joint_grad, out_grad, up_grad, down_grad, vector_grad)
    masters = (joint_weight, output_weight, expand_weight, reduce_weight, vector_weight)
    firsts = (joint_first, output_first, expand_first, reduce_first, vector_first)
    seconds = (joint_second, output_second, expand_second, reduce_second, vector_second)
    rates = (MATRIX_RATE, OUTPUT_RATE, MATRIX_RATE, MATRIX_RATE, VECTOR_RATE)
    decays = (MATRIX_DECAY, MATRIX_DECAY, MATRIX_DECAY, MATRIX_DECAY, 0.0)
    means, spreads, nexts = ([], [], [])
    for index in range(5):
        first_new, second_new, fresh = adam_step(
            masters[index],
            firsts[index],
            seconds[index],
            shard_grads[index],
            rates[index],
            decays[index],
        )
        means.append(first_new)
        spreads.append(second_new)
        nexts.append(fresh)
    return (layer_out, input_grad, *shard_grads, *means, *spreads, *nexts)


def solution(mesh):
    rows, columns, split = P("shard", None), P(None, "shard"), P(("wide", "shard"), None)
    state = (rows, rows, rows, rows, columns)
    return jax.shard_map(
        per_device,
        mesh=mesh,
        in_specs=(split, split, split) + (rows,) * 12 + (columns,) * 3,
        out_specs=(split, split) + state * 4,
        check_vma=False,
    )
```

```python
import jax
import jax.numpy as jnp
from jax import lax
from jax.experimental import pallas as pl
from jax.experimental.pallas import tpu as pltpu
from jax.sharding import PartitionSpec as P

HEAD_DIM = 64
STEP = 10


ROOT_TWO_PI = 0.7978845608028654
CUBIC = 0.044715
BETA_ONE = 0.9
BETA_TWO = 0.999
ADAM_EPS = 1e-08
MATRIX_RATE = 0.03
OUTPUT_RATE = 0.1
VECTOR_RATE = 0.2
MATRIX_DECAY = 0.1

LOW = jnp.bfloat16
FULL = jnp.float32
AXES = ("wide", "shard")
SIZES = (4, 2, 2, 2, 4)
COLS = 512
VMEM_BYTES = 60 * 1024 * 1024


def coordinates():
    wide, shard = lax.axis_index("wide"), lax.axis_index("shard")
    z, xl, core = wide // 4, (wide // 2) % 2, wide % 2
    xh, y = shard // 4, shard % 4
    return {"z": z, "x": 2 * xh + xl, "y": y, "xl": xl, "xh": xh, "core": core}


def route(partner):
    pairs = []
    for source in range(128):
        rest, places = source, []
        for size in reversed(SIZES):
            places.append(rest % size)
            rest //= size
        y, xh, core, xl, z = places
        target = partner({"z": z, "x": 2 * xh + xl, "y": y, "core": core})
        flat = 0
        for place, size in zip(
            (target["z"], target["x"] % 2, target["core"], target["x"] // 2, target["y"]), SIZES
        ):
            flat = flat * size + place
        pairs.append((source, flat))
    return pairs


def flip(axis, bits):
    return route(lambda at: {**at, axis: at[axis] ^ bits})


def turn(axis, step):
    return route(lambda at: {**at, axis: at[axis] ^ (1 if (at["core"] + step) % 2 == 0 else 3)})


def send(value, pairs):
    return lax.ppermute(value, AXES, pairs)


def added(a, b):
    return (a.astype(FULL) + b.astype(FULL)).astype(LOW)


def orders(me, axis):
    here = me[axis]
    one = jnp.where(me["core"] == 0, 1, 3)
    return [here, here ^ one, here ^ (4 - one), here ^ 2]


def places_of(me):
    return jnp.stack(
        orders(me, "x")
        + orders(me, "y")
        + orders(me, "z")
        + [me["xh"], me["core"], me["xl"], me["z"]]
    ).astype(jnp.int32)


def after(value, *others):
    return lax.optimization_barrier((value, *others))[0]


def rows_of(*parts):
    return jnp.concatenate([p.reshape(-1, COLS) for p in parts])


def main_phase(block, axis, gate=None):
    first, second = send(block, turn(axis, 0)), send(block, turn(axis, 1))
    passed = first if gate is None else after(first, gate)
    return [block, first, second, send(passed, turn(axis, 1))]


def gather_joint(half, block):
    other = send(block, flip("x", 3))
    here = jnp.stack([half, send(half, turn("y", 0))])
    there = send(here, turn("y", 1))
    along_y = main_phase(jnp.stack([block, other]), "y")
    along_x = main_phase(jnp.concatenate([here, there]), "x")
    return along_x, along_y, (other, along_y[1], along_x[1])


def gather_rest(me, half, block, marks):
    other = send(after(block, marks[0]), flip("x", 3))
    pair_y = jnp.stack([block[:384], other[:384]])
    wanted = jnp.where(me["core"] == me["xh"], block[448:], other[448:]).reshape(2, 32, COLS)
    pair_z = jnp.concatenate([jnp.stack([block[384:448], other[384:448]]), wanted], axis=1)
    size = half.shape[0]
    first = after(rows_of(half, pair_z), marks[1])
    here = jnp.stack([first, send(first, turn("y", 0))])
    there = send(after(here, marks[2]), turn("y", 1))
    plane_x = jnp.concatenate([here[:, :size], there[:, :size]])
    plane_z = jnp.concatenate([here[:, size:], there[:, size:]]).reshape(4, 2, 96, COLS)
    return plane_x, pair_y, plane_z


def halved(keep, away, axis, gates=(None, None)):
    far = send(away, turn(axis, 1))
    if gates[0] is not None:
        keep = after(keep, gates[0])
    near = added(keep, far)
    own, far = near[0], send(near[1], turn(axis, 0))
    if gates[1] is not None:
        own = after(own, gates[1])
    return added(own, far)


def total(me, raw, out_rows, units, gates=(None, None)):
    along_x, along_y, along_z = (
        halved(raw[0], raw[1], "x", gates),
        halved(raw[2], raw[3], "y", gates),
        halved(raw[4], raw[5], "z", gates),
    )
    size_x, size_y = along_x.shape[1], along_y.shape[1]
    size_z = along_z.shape[2] - out_rows
    plane = jnp.concatenate([along_x, along_z.reshape(4, -1, COLS)], axis=1)
    plane = halved(plane[:2], plane[2:], "y")
    half, pair = plane[:size_x], plane[size_x:].reshape(2, size_z + out_rows, COLS)
    out = pair[:, size_z:]
    sums = rows_of(along_y[0], pair[0, :size_z], out)
    sums = added(sums, send(rows_of(along_y[1], pair[1, :size_z], out), flip("x", 3)))
    other = send(rows_of(sums, half), flip("x", 1))
    sums = added(sums, other[: sums.shape[0]])
    half, other = half.reshape(units, -1, COLS), other[-size_x:].reshape(units, -1, COLS)
    whole_x = jnp.where(
        me["xl"] == 0, jnp.stack([half, other], axis=1), jnp.stack([other, half], axis=1)
    )
    flat = rows_of(whole_x, sums[:size_y])
    block = sums[size_y:]
    other = send(rows_of(flat, block), turn("z", 0))
    flat = added(flat, other[: flat.shape[0]])
    blocks = rows_of(block, other[flat.shape[0] :])
    other = send(rows_of(flat, blocks), turn("z", 1))
    flat = added(flat, other[: flat.shape[0]])
    blocks = rows_of(blocks, other[flat.shape[0] :]).reshape((4,) + block.shape)
    where = orders(me, "z")
    ordered = [
        sum(jnp.where(where[k] == place, blocks[k], 0) for k in range(4)) for place in range(4)
    ]
    both = rows_of(flat, *(a.astype(LOW) for a in ordered))
    return both, send(both, flip("core", 1))


def sum_all(value):
    for pairs in (
        flip("core", 1),
        turn("x", 0),
        turn("x", 1),
        turn("y", 0),
        turn("y", 1),
        turn("z", 0),
        turn("z", 1),
    ):
        value = value + send(value, pairs)
    return value


def rows_at(start, size):
    return pl.ds(pl.multiple_of(start, size), size)


def joint_plan(places, along_x, along_y, mats):
    query, key, value, vectors = mats
    pairs = []
    for ky in range(4):
        y = places[4 + ky]
        for kx in range(4):
            x = places[kx]
            shard, half = (x // 2) * 4 + y, x % 2
            source = along_x[kx].at[ky]
            pairs.append(
                (source.at[pl.ds(0, 64)], query.at[rows_at(shard * 128 + half * 64, 64)])
            )
            pairs.append(
                (source.at[pl.ds(64, 32)], value.at[rows_at(shard * 128 + half * 32, 32)])
            )
        for p in range(2):
            shard = (places[12] ^ p) * 4 + y
            source = along_y[ky].at[p]
            pairs.append((source.at[pl.ds(0, 128)], key.at[rows_at(shard * 128, 128)]))
            pairs.append((source.at[pl.ds(128, 64)], value.at[rows_at(shard * 128 + 64, 64)]))
            pairs.append(
                (
                    source.at[pl.ds(192, 16), pl.ds(0, 128)],
                    vectors.at[:, rows_at(shard * 128, 128)],
                )
            )
    return pairs


def joint_sent_plan(places, raw, parts):
    query, key, value = parts
    pairs = []
    for ky in range(4):
        y = places[4 + ky]
        for kx in range(4):
            x = places[kx]
            start = ((x // 2) * 4 + y) * 128 + (x % 2) * 64
            pairs.append((query.at[rows_at(start, 64)], raw[0 + kx // 2].at[kx % 2, ky]))
        for p in range(2):
            shard = (places[12] ^ p) * 4 + y
            pairs.append((key.at[rows_at(shard * 128, 128)], raw[2 + ky // 2].at[ky % 2, p]))
            for kz in range(4):
                start = shard * 128 + places[8 + kz] * 32
                pairs.append((value.at[rows_at(start, 32)], raw[4 + kz // 2].at[kz % 2, ky, p]))
    return pairs


def up_plan(places, at_x, at_y, at_z, mats):
    up, down_one, down_two = mats
    pairs = []
    for ky in range(4):
        y = places[4 + ky]
        for kx in range(4):
            x = places[kx]
            start = ((x // 2) * 4 + y) * 128 + (x % 2) * 64
            for j in range(3):
                source = at_x(kx).at[ky, pl.ds(64 * j, 64)]
                pairs.append((source, up.at[j, rows_at(start, 64)]))
        for p in range(2):
            shard = (places[12] ^ p) * 4 + y
            source = at_y(ky).at[p]
            pairs.append((source.at[pl.ds(0, 128)], up.at[3, rows_at(shard * 128, 128)]))
            pairs.append((source.at[pl.ds(128, 256)], down_one.at[rows_at(shard * 256, 256)]))
            for kz in range(4):
                start = shard * 256 + places[8 + kz] * 64
                source = at_z(kz).at[ky, p, pl.ds(0, 64)]
                pairs.append((source, down_two.at[rows_at(start, 64)]))
    return pairs


def out_plan(places, at_z, first, mat):
    pairs = []
    for ky in range(4):
        for kz in range(4):
            start = places[4 + ky] * 128 + places[8 + kz] * 32
            for p in range(2):
                source = at_z(kz).at[ky, p, pl.ds(first, 32)]
                pairs.append((source, mat.at[p, rows_at(start, 32)]))
    return pairs


def two_of(arrays):
    return lambda k: arrays[k // 2].at[k % 2]


def started(pairs, sems):
    all_of_them = [pltpu.make_async_copy(a, b, sems.at[i]) for i, (a, b) in enumerate(pairs)]
    for copy in all_of_them:
        copy.start()
    return all_of_them


def finished(all_of_them):
    for copy in all_of_them:
        copy.wait()


def turned(pairs):
    return [(b, a) for a, b in pairs]


def low_shape(*shape):
    return jax.ShapeDtypeStruct(shape, LOW)


def full_shape(*shape):
    return jax.ShapeDtypeStruct(shape, FULL)


SCALARS = pl.BlockSpec(memory_space=pltpu.SMEM)
INSIDE = pl.BlockSpec(memory_space=pltpu.VMEM)
OUTSIDE = pl.BlockSpec(memory_space=pl.ANY)


def call(kernel, in_specs, outs, scratch, flops, args, grid=()):
    shapes, specs = [o[0] for o in outs], [o[1] for o in outs]
    moved = sum(a.size * a.dtype.itemsize for a in (*args, *shapes))
    return pl.pallas_call(
        kernel,
        grid=grid,
        out_shape=shapes,
        in_specs=in_specs,
        out_specs=specs,
        scratch_shapes=scratch,
        compiler_params=pltpu.CompilerParams(vmem_limit_bytes=VMEM_BYTES),
        cost_estimate=pl.CostEstimate(flops=flops, bytes_accessed=moved, transcendentals=0),
    )(*args)


def gelu_both(upward):
    square = upward * upward
    tangent = jnp.tanh(ROOT_TWO_PI * upward * (1.0 + CUBIC * square))
    half = 0.5 * (1.0 + tangent)
    slope = half + 0.5 * upward * (1.0 - tangent * tangent) * ROOT_TWO_PI * (
        1.0 + 3.0 * CUBIC * square
    )
    return upward * half, slope


def dot(a, b):
    return jnp.dot(a, b, preferred_element_type=FULL)


def dot_nt(a, b):
    return lax.dot_general(a, b, (((1,), (1,)), ((), ())), preferred_element_type=FULL)


def dot_tn(a, b):
    return lax.dot_general(a, b, (((0,), (0,)), ((), ())), preferred_element_type=FULL)


def unit_of(values):
    center = values - jnp.mean(values, axis=-1, keepdims=True)
    inverse = lax.rsqrt(jnp.mean(center * center, axis=-1, keepdims=True) + 1e-05)
    return center * inverse, inverse


def norm_backward(grad_out, unit, inverse, gain):
    scaled = grad_out * gain
    return inverse * (
        scaled
        - jnp.mean(scaled, axis=-1, keepdims=True)
        - unit * jnp.mean(scaled * unit, axis=-1, keepdims=True)
    )


def row_of(vectors, row):
    return vectors[row : row + 1, :].astype(FULL)


def own_columns(full, core, size):
    groups = full.shape[1] // (2 * size)
    first = jnp.concatenate(
        [full[:, (2 * g) * size : (2 * g + 1) * size] for g in range(groups)], axis=1
    )
    second = jnp.concatenate(
        [full[:, (2 * g + 1) * size : (2 * g + 2) * size] for g in range(groups)], axis=1
    )
    return jnp.where(core == 0, first, second)


def barred(lengths, block, first, height, span):
    shape = (height, span)
    rows = lax.broadcasted_iota(jnp.int32, shape, 0) + first
    keys = lax.broadcasted_iota(jnp.int32, shape, 1)
    opening = lengths[block, 0]
    filled = opening + lengths[block, 1]
    begin = jnp.where(rows < opening, 0, jnp.where(rows < filled, opening, rows))
    return jnp.where((keys <= rows) & (keys >= begin), 0.0, -1e30)


TILE = 128


def joint_cast_kernel(places, weight, vector, half, block, held, padded, sems):
    core, xl = places[13], places[14]

    def cols(which):
        return rows_at(which * 2 * COLS + core * COLS, COLS)

    copies = started(
        [
            (weight.at[rows_at(xl * 64, 64), cols(0)], held.at[pl.ds(0, 64)]),
            (weight.at[rows_at(xl * 32, 32), cols(2)], held.at[pl.ds(64, 32)]),
            (weight.at[:, cols(1)], held.at[pl.ds(96, 128)]),
            (weight.at[pl.ds(64, 64), cols(2)], held.at[pl.ds(224, 64)]),
        ],
        sems,
    )
    padded[...] = jnp.zeros_like(padded)
    padded[: vector.shape[0], : vector.shape[1]] = vector[...]
    block[192:208, :] = padded[...].astype(LOW)
    finished(copies)
    half[...] = held[:96].astype(LOW)
    block[:192, :] = held[96:].astype(LOW)


def joint_cast(places, weight, vector):
    return call(
        joint_cast_kernel,
        [SCALARS, OUTSIDE, INSIDE],
        [(low_shape(96, COLS), INSIDE), (low_shape(208, COLS), INSIDE)],
        [pltpu.VMEM((288, COLS), FULL), pltpu.VMEM((16, COLS), FULL)]
        + [pltpu.SemaphoreType.DMA((4,))],
        0,
        (places, weight, vector),
    )


def rest_cast_kernel(places, expand, reduce, output, half, block, held, wide, sems):
    core, xl, z = places[13], places[14], places[15]
    pairs = []
    for s in range(8):
        j, right = s // 2, (s % 2) * 256
        cols = rows_at(s * 512 + core * 256, 256)
        rows, size = (rows_at(xl * 64, 64), 64) if j < 3 else (pl.ds(0, 128), 128)
        pairs.append((expand.at[rows, cols], held.at[pl.ds(64 * j, size), pl.ds(right, 256)]))
    pairs.append((reduce.at[rows_at(core * 256, 256), pl.ds(0, COLS)], held.at[pl.ds(320, 256)]))
    pairs.append(
        (reduce.at[rows_at(core * 256 + z * 64, 64), pl.ds(COLS, COLS)], held.at[pl.ds(576, 64)])
    )
    pairs.append((output.at[rows_at(z * 32, 32)], wide))
    finished(started(pairs, sems))
    half[...] = held[:192].astype(LOW)
    block[:448, :] = held[192:640].astype(LOW)
    block[448:480, :] = wide[:, :COLS].astype(LOW)
    block[480:512, :] = wide[:, COLS:].astype(LOW)


def rest_cast(places, expand, reduce, output):
    return call(
        rest_cast_kernel,
        [SCALARS, OUTSIDE, OUTSIDE, OUTSIDE],
        [(low_shape(192, COLS), INSIDE), (low_shape(512, COLS), INSIDE)],
        [pltpu.VMEM((640, COLS), FULL), pltpu.VMEM((32, 2 * COLS), FULL)]
        + [pltpu.SemaphoreType.DMA((11,))],
        0,
        (places, expand, reduce, output),
    )


def joint_kernel(places, own, other, *refs):
    along_x, along_y, refs = refs[:4], refs[4:8], refs[8:]
    normed, query, key, value, vectors, query_mat, key_mat, value_mat, sems = refs
    mats = (query_mat, key_mat, value_mat, vectors)
    finished(started(joint_plan(places, along_x, along_y, mats), sems))
    gain, shift = row_of(vectors, 0), row_of(vectors, 1)
    core = places[13]
    query_bias = own_columns(row_of(vectors, 2), core, COLS)
    value_bias = own_columns(row_of(vectors, 3), core, COLS)
    count = own.shape[0]
    for block, tokens in enumerate((own, other)):
        rows = pl.ds(block * count, count)
        unit, _ = unit_of(tokens[...].astype(FULL))
        low = (unit * gain + shift).astype(LOW)
        normed[rows, :] = low
        query[rows, :] = ((dot(low, query_mat[...]) + query_bias).astype(LOW) * 0.125).astype(LOW)
        key[rows, :] = dot(low, key_mat[...]).astype(LOW)
        value[rows, :] = (dot(low, value_mat[...]) + value_bias).astype(LOW)


def joint(places, own, other, along_x, along_y):
    count, width = own.shape
    rows = 2 * count
    mat, half = (low_shape(width, COLS), INSIDE), (low_shape(rows, COLS), INSIDE)
    return call(
        joint_kernel,
        [SCALARS, INSIDE, INSIDE] + [OUTSIDE] * 8,
        [(low_shape(rows, width), INSIDE), half, half, half]
        + [(low_shape(16, width), INSIDE), mat, mat, mat],
        [pltpu.SemaphoreType.DMA((56,))],
        6 * rows * width * COLS,
        (places, own, other, *along_x, *along_y),
    )


def attention_kernel(lengths, query, key, value, attended, mask):
    count = query.shape[0] // 2
    spans = count // TILE
    for block in range(2):
        for i in range(spans):
            mask[block, i * TILE : (i + 1) * TILE, : (i + 1) * TILE] = barred(
                lengths, block, i * TILE, TILE, (i + 1) * TILE
            )

    def two_heads(index, carry):
        block, cols = index // 4, rows_at((index % 4) * TILE, TILE)
        base = pl.multiple_of(block * count, TILE)
        lane = lax.broadcasted_iota(jnp.int32, (TILE, TILE), 1) < HEAD_DIM
        for i in range(spans):
            span = (i + 1) * TILE
            rows, keys = rows_at(base + i * TILE, TILE), pl.ds(base, span)
            both = query[rows, cols]
            bar = mask[block, i * TILE : span, :span]
            outs = []
            for side in (lane, ~lane):
                scores = dot_nt(jnp.where(side, both, 0), key[keys, cols]) + bar
                probs = jnp.exp(scores - jnp.max(scores, axis=-1, keepdims=True))
                probs = probs * (1.0 / jnp.sum(probs, axis=-1, keepdims=True))
                outs.append(dot(probs.astype(LOW), value[keys, cols]))
            attended[rows, cols] = jnp.where(lane, outs[0], outs[1]).astype(LOW)
        return carry

    lax.fori_loop(0, 8, two_heads, 0)


def attention(lengths, query, key, value):
    rows = query.shape[0]
    return call(
        attention_kernel,
        [SCALARS] + [INSIDE] * 3,
        [(low_shape(rows, COLS), INSIDE)],
        [pltpu.VMEM((2, rows // 2, rows // 2), FULL)],
        2 * rows * rows * COLS,
        (lengths, query, key, value),
    )[0]


def output_kernel(places, attended, *refs):
    raw, (branch, out_mat, sems) = refs[:4], refs[4:]
    finished(started(out_plan(places, lambda k: raw[k], 64, out_mat), sems))
    for half in range(2):
        branch[:, half * COLS : (half + 1) * COLS] = dot(attended[...], out_mat[half]).astype(LOW)


def output(places, attended, raw):
    rows, local = attended.shape
    return call(
        output_kernel,
        [SCALARS, INSIDE] + [OUTSIDE] * 4,
        [(low_shape(rows, 2 * COLS), INSIDE), (low_shape(2, local, COLS), INSIDE)],
        [pltpu.SemaphoreType.DMA((32,))],
        4 * rows * local * COLS,
        (places, attended, *raw),
    )


def forward_backward_kernel(
    places, lengths, own, other, arriving_own, arriving_other, branch, branch_far, vectors, *refs
):
    raw, refs = refs[:12], refs[12:]
    sent, refs = refs[:6], refs[6:]
    (middle, layer_own, layer_other, normed_grad, bias_grad,
     up, down_one, down_two, up_grad, one_grad, two_grad,
     normed, arriving, layer_sum, normed_sum, active, up_low, sems) = refs
    held = [lambda k, a=axis: raw[4 * a + k] for axis in range(3)]
    copies = started(up_plan(places, *held, (up, down_one, down_two)), sems)
    count = own.shape[0]
    tile = 256
    gain, shift = row_of(vectors, 5), row_of(vectors, 6)
    for block, (tokens, cotangent) in enumerate(((own, arriving_own), (other, arriving_other))):
        rows, far = pl.ds(block * count, count), pl.ds((1 - block) * count, count)
        summed = branch[rows, :].astype(FULL) + branch_far[far, :].astype(FULL)
        held = tokens[...].astype(FULL) + summed + row_of(vectors, 4)
        middle[rows, :] = held
        unit, _ = unit_of(held)
        normed[rows, :] = (unit * gain + shift).astype(LOW)
        slots = lax.broadcasted_iota(jnp.int32, cotangent.shape, 0)
        live = slots < lengths[block, 0] + lengths[block, 1]
        arriving[rows, :] = jnp.where(live, cotangent[...], 0)
    layer_sum[...] = jnp.zeros_like(layer_sum)
    normed_sum[...] = jnp.zeros_like(normed_sum)
    bias_grad[...] = jnp.zeros_like(bias_grad)
    core = places[13]
    biases = jnp.concatenate(
        [own_columns(row_of(vectors, 7 + k), core, 256) for k in range(4)], axis=0
    )
    finished(copies)

    def chunk(j, carry):
        hidden = rows_at(j * COLS, COLS)
        bias = jnp.zeros((1, COLS), FULL)
        for k in range(4):
            bias = jnp.where(j == k, biases[k : k + 1], bias)

        def rows_step(index, carry):
            rows = rows_at(index * tile, tile)
            upward = dot(normed[rows, :], up[j]) + bias
            act, slope = gelu_both(upward)
            act = act.astype(LOW)
            active[rows, :] = act
            layer_sum[rows, :COLS] += dot(act, down_one[hidden, :])
            layer_sum[rows, COLS:] += dot(act, down_two[hidden, :])
            grad = dot_nt(arriving[rows, :COLS], down_one[hidden, :])
            grad += dot_nt(arriving[rows, COLS:], down_two[hidden, :])
            low = (grad * slope).astype(LOW)
            up_low[rows, :] = low
            bias_grad[pl.ds(j, 1), :] += jnp.sum(low.astype(FULL), axis=0, keepdims=True)
            normed_sum[rows, :] += dot_nt(low, up[j])
            return carry

        lax.fori_loop(0, normed.shape[0] // tile, rows_step, 0)
        one_grad[hidden, :] = dot_tn(active[...], arriving[:, :COLS]).astype(LOW)
        two_grad[hidden, :] = dot_tn(active[...], arriving[:, COLS:]).astype(LOW)
        up_grad[j] = dot_tn(normed[...], up_low[...]).astype(LOW)
        return carry

    lax.fori_loop(0, up.shape[0], chunk, 0)
    held = [two_of(sent[2 * axis : 2 * axis + 2]) for axis in range(3)]
    copies = started(turned(up_plan(places, *held, (up_grad, one_grad, two_grad))), sems)
    layer_own[...] = middle[:count, :] + layer_sum[:count, :] + row_of(vectors, 11)
    layer_other[...] = layer_sum[count:, :].astype(LOW)
    normed_grad[...] = normed_sum[...].astype(LOW)
    finished(copies)


def forward_backward(places, lengths, tokens, arriving, branch, branch_far, vectors, raw):
    count, width = tokens[0].shape
    rows, hidden = 2 * count, 4 * COLS
    sent = [low_shape(2, 4, 192, COLS), low_shape(2, 2, 384, COLS), low_shape(2, 4, 2, 64, COLS)]
    inside = [
        full_shape(rows, width), full_shape(count, width), low_shape(count, width),
        low_shape(rows, width), full_shape(4, COLS),
    ]
    vmem = pltpu.VMEM
    mats = [vmem((4, width, COLS), LOW), vmem((hidden, COLS), LOW), vmem((hidden, COLS), LOW)]
    return call(
        forward_backward_kernel,
        [SCALARS, SCALARS] + [INSIDE] * 7 + [OUTSIDE] * 12,
        [(s, OUTSIDE) for s in sent for _ in range(2)] + [(s, INSIDE) for s in inside],
        mats + mats
        + [vmem((rows, width), LOW), vmem((rows, width), LOW)]
        + [vmem((rows, width), FULL), vmem((rows, width), FULL)]
        + [vmem((rows, COLS), LOW), vmem((rows, COLS), LOW), pltpu.SemaphoreType.DMA((96,))],
        12 * rows * width * hidden,
        (places, lengths, *tokens, *arriving, branch, branch_far, vectors, *raw),
    )


def output_backward_kernel(
    places, lengths, arriving_own, arriving_other, middle, part, part_far, vectors, attended,
    out_mat, sent_one, sent_two, middle_grad, attended_grad, sums, branch, out_grad, sems,
):
    count = arriving_own.shape[0]
    gain = row_of(vectors, 5)
    for block, cotangent in enumerate((arriving_own, arriving_other)):
        rows, far = pl.ds(block * count, count), pl.ds((1 - block) * count, count)
        unit, inverse = unit_of(middle[rows, :])
        grad = part[rows, :].astype(FULL) + part_far[far, :].astype(FULL)
        slots = lax.broadcasted_iota(jnp.int32, cotangent.shape, 0)
        live = slots < lengths[block, 0] + lengths[block, 1]
        arriving = jnp.where(live, cotangent[...].astype(FULL), 0.0)
        held = arriving + norm_backward(grad, unit, inverse, gain)
        low = held.astype(LOW)
        branch[rows, :] = low
        if block == 0:
            middle_grad[...] = held
            sums[...] = jnp.zeros_like(sums)
            sums[0:1, :] = jnp.sum(low.astype(FULL), axis=0, keepdims=True)
            sums[1:2, :] = jnp.sum(grad * unit, axis=0, keepdims=True)
            sums[2:3, :] = jnp.sum(grad, axis=0, keepdims=True)
            sums[3:4, :] = jnp.sum(arriving, axis=0, keepdims=True)
    for half in range(2):
        cols = slice(half * COLS, (half + 1) * COLS)
        out_grad[half] = dot_tn(attended[...], branch[:, cols]).astype(LOW)
    copies = started(turned(out_plan(places, two_of((sent_one, sent_two)), 0, out_grad)), sems)
    attended_grad[...] = (
        dot_nt(branch[:, :COLS], out_mat[0]) + dot_nt(branch[:, COLS:], out_mat[1])
    ).astype(LOW)
    finished(copies)


def output_backward(places, lengths, arriving, middle, part, part_far, vectors, attended, out_mat):
    rows, width = middle.shape
    sent = (low_shape(2, 4, 2, 32, COLS), OUTSIDE)
    inside = [full_shape(rows // 2, width), low_shape(rows, COLS), full_shape(8, width)]
    return call(
        output_backward_kernel,
        [SCALARS, SCALARS] + [INSIDE] * 8,
        [sent, sent] + [(s, INSIDE) for s in inside],
        [pltpu.VMEM((rows, width), LOW), pltpu.VMEM((2, COLS, COLS), LOW)]
        + [pltpu.SemaphoreType.DMA((32,))],
        8 * rows * width * COLS,
        (places, lengths, *arriving, middle, part, part_far, vectors, attended, out_mat),
    )


def attention_backward_kernel(
    block, lengths, query, key, value, grad_in, query_grad, key_grad, value_grad, sums,
    mask, key_sum, value_sum,
):
    count = query.shape[0]
    spans = count // TILE
    for i in range(spans):
        mask[i * TILE : (i + 1) * TILE, : (i + 1) * TILE] = barred(
            lengths, block, i * TILE, TILE, (i + 1) * TILE
        )

    def two_heads(index, carry):
        cols = rows_at(index * TILE, TILE)
        lane = lax.broadcasted_iota(jnp.int32, (TILE, TILE), 1) < HEAD_DIM
        lanes = lax.broadcasted_iota(jnp.int32, (count, TILE), 1) < HEAD_DIM
        for i in range(spans):
            before, span = i * TILE, (i + 1) * TILE
            two_q, two_g = query[before:span, cols], grad_in[before:span, cols]
            two_k, two_v = key[:span, cols], value[:span, cols]
            bar = mask[before:span, :span]
            outs = []
            for h, side in enumerate((lane, ~lane)):
                scores = dot_nt(jnp.where(side, two_q, 0), two_k) + bar
                probs = jnp.exp(scores - jnp.max(scores, axis=-1, keepdims=True))
                probs = probs * (1.0 / jnp.sum(probs, axis=-1, keepdims=True))
                grad = dot_nt(jnp.where(side, two_g, 0), two_v)
                weighted = probs * grad
                grad = probs * (grad - jnp.sum(weighted, axis=-1, keepdims=True))
                low = grad.astype(LOW)
                outs.append(dot(low, two_k))
                key_now = dot_tn(low, two_q)
                value_now = dot_tn(probs.astype(LOW), two_g)
                if i > 0:
                    key_sum[h, :before] += key_now[:before]
                    value_sum[h, :before] += value_now[:before]
                key_sum[h, before:span] = key_now[before:]
                value_sum[h, before:span] = value_now[before:]
            query_grad[before:span, cols] = (jnp.where(lane, outs[0], outs[1]) * 0.125).astype(LOW)
        key_grad[:, cols] = jnp.where(lanes, key_sum[0], key_sum[1]).astype(LOW)
        value_grad[:, cols] = jnp.where(lanes, value_sum[0], value_sum[1]).astype(LOW)
        return carry

    lax.fori_loop(0, COLS // TILE, two_heads, 0)
    sums[...] = jnp.zeros_like(sums)
    sums[0:1, :] = jnp.sum(query_grad[...].astype(FULL), axis=0, keepdims=True)
    sums[1:2, :] = jnp.sum(value_grad[...].astype(FULL), axis=0, keepdims=True)


def attention_backward(block, lengths, query, key, value, grad_in):
    count = query.shape[0] // 2
    vmem = pltpu.VMEM
    half = (low_shape(count, COLS), INSIDE)
    part = pl.BlockSpec((count, COLS), lambda i: (block, 0))
    return call(
        lambda *refs: attention_backward_kernel(block, *refs),
        [SCALARS] + [part] * 4,
        [half, half, half, (full_shape(8, COLS), INSIDE)],
        [vmem((count, count), FULL), vmem((2, count, TILE), FULL), vmem((2, count, TILE), FULL)],
        10 * count * count * COLS,
        (lengths, query, key, value, grad_in),
        grid=(1,),
    )


def joint_grad_kernel(places, normed, *refs):
    grads, sent, (query_part, key_part, value_part, sems) = refs[:6], refs[6:12], refs[12:]
    parts = (query_part, key_part, value_part)
    count = grads[0].shape[0]
    for part, own, other in zip(parts, grads[:3], grads[3:]):
        part[...] = (
            dot_tn(normed[:count, :], own[...]) + dot_tn(normed[count:, :], other[...])
        ).astype(LOW)
    finished(started(joint_sent_plan(places, sent, parts), sems))


def joint_grad_parts(places, normed, own, other):
    rows, width = normed.shape
    sent = [low_shape(2, 4, 64, COLS), low_shape(2, 2, 128, COLS), low_shape(2, 4, 2, 32, COLS)]
    return call(
        joint_grad_kernel,
        [SCALARS] + [INSIDE] * 7,
        [(s, OUTSIDE) for s in sent for _ in range(2)],
        [pltpu.VMEM((width, COLS), LOW)] * 3 + [pltpu.SemaphoreType.DMA((56,))],
        6 * rows * width * COLS,
        (places, normed, *own, *other),
    )


def joint_backward_kernel(*refs):
    own, other, mats, outs = refs[:3], refs[3:6], refs[6:9], refs[9:]
    for grads, out in zip((own, other), outs):
        whole = dot_nt(grads[0][...], mats[0][...])
        whole += dot_nt(grads[1][...], mats[1][...])
        whole += dot_nt(grads[2][...], mats[2][...])
        out[...] = whole.astype(out.dtype)


def joint_backward(own, other, mats):
    count, width = own[0].shape[0], mats[0].shape[0]
    return call(
        joint_backward_kernel,
        [INSIDE] * 9,
        [(full_shape(count, width), INSIDE), (low_shape(count, width), INSIDE)],
        [],
        12 * count * width * COLS,
        (*own, *other, *mats),
    )


def input_kernel(tokens, part, part_far, middle_grad, vectors, input_grad, sums):
    unit, inverse = unit_of(tokens[...].astype(FULL))
    grad = part[...] + part_far[...].astype(FULL)
    input_grad[...] = middle_grad[...] + norm_backward(grad, unit, inverse, row_of(vectors, 0))
    sums[...] = jnp.zeros_like(sums)
    sums[0:1, :] = jnp.sum(grad * unit, axis=0, keepdims=True)
    sums[1:2, :] = jnp.sum(grad, axis=0, keepdims=True)


def input_backward(tokens, part, part_far, middle_grad, vectors):
    return call(
        input_kernel,
        [INSIDE] * 5,
        [(full_shape(*part.shape), INSIDE), (full_shape(8, part.shape[1]), INSIDE)],
        [],
        20 * part.size,
        (tokens, part, part_far, middle_grad, vectors),
    )


def adam_step(weight, first, second, grad, rate, decay):
    first_new = BETA_ONE * first + (1.0 - BETA_ONE) * grad
    second_new = BETA_TWO * second + (1.0 - BETA_TWO) * grad * grad
    mean_hat = first_new / (1.0 - BETA_ONE**STEP)
    square_hat = second_new / (1.0 - BETA_TWO**STEP)
    fresh = weight - rate * (mean_hat / (jnp.sqrt(square_hat) + ADAM_EPS) + decay * weight)
    return (first_new, second_new, fresh)


def adam_kernel(grad_of, rate, places, weight, first, second, *refs):
    grads, outs = refs[:-4], refs[-4:]
    grad = grad_of(places, *(g[...].astype(FULL) for g in grads))
    outs[0][...] = grad
    outs[1][...], outs[2][...], outs[3][...] = adam_step(
        weight[...], first[...], second[...], grad, rate, MATRIX_DECAY
    )


def adam(grad_of, rate, grid, state, state_block, state_map, grads, places):
    spec = pl.BlockSpec(state_block, state_map)
    shape = full_shape(*state[0].shape)
    return pl.pallas_call(
        lambda *refs: adam_kernel(grad_of, rate, *refs),
        grid=grid,
        in_specs=[SCALARS] + [spec] * 3 + [pl.BlockSpec(g[1], g[2]) for g in grads],
        out_specs=[spec] * 4,
        out_shape=[shape] * 4,
        compiler_params=pltpu.CompilerParams(vmem_limit_bytes=VMEM_BYTES),
        cost_estimate=pl.CostEstimate(
            flops=20 * state[0].size, bytes_accessed=30 * state[0].size, transcendentals=0
        ),
    )(places, *state, *(g[0] for g in grads))


def by_core(places, both, far):
    own = places[13] == 0
    return jnp.where(own, both, far), jnp.where(own, far, both)


def adam_joint(places, state, sums):
    def grad_of(places, both, far):
        half = pl.program_id(0) % 2
        return jnp.where(half == places[13], both, far)

    block = (128, COLS)
    grads = [(a, block, lambda g: (g // 2, 0)) for a in sums]
    return adam(grad_of, MATRIX_RATE, (6,), state, block, lambda g: (0, g), grads, places)


def adam_expand(places, state, sums):
    def grad_of(places, both, far):
        zero, one = by_core(places, both, far)
        return jnp.concatenate(
            [zero[:, :256], one[:, :256], zero[:, 256:], one[:, 256:]], axis=1
        )

    grads = [(a, (128, COLS), lambda j: (j, 0)) for a in sums]
    return adam(
        grad_of, MATRIX_RATE, (4,), state, (128, 2 * COLS), lambda j: (0, j), grads, places
    )


def adam_reduce(places, state, sums):
    def grad_of(places, left, right, far_left, far_right):
        own = pl.program_id(0) // 4 == places[13]
        return jnp.concatenate(
            [jnp.where(own, left, far_left), jnp.where(own, right, far_right)], axis=1
        )

    block = (64, COLS)
    grads = []
    for a in sums:
        grads.append((a, block, lambda g: (8 + g % 4, 0)))
        grads.append((a, block, lambda g: (12 + 2 * (g % 4), 0)))
    return adam(
        grad_of, MATRIX_RATE, (8,), state, (64, 2 * COLS), lambda g: (g, 0), grads, places
    )


def adam_output(places, state, sums):
    def grad_of(places, both, far):
        grad = jnp.where(places[13] == places[12], both, far)
        return jnp.concatenate([grad[:32], grad[32:]], axis=1)

    grads = [(a, (64, COLS), lambda q: (13 + 2 * q, 0)) for a in sums]
    return adam(
        grad_of, OUTPUT_RATE, (4,), state, (32, 2 * COLS), lambda q: (q, 0), grads, places
    )


def per_device(
    tokens,
    cotangent,
    lengths,
    joint_weight,
    joint_first,
    joint_second,
    output_weight,
    output_first,
    output_second,
    expand_weight,
    expand_first,
    expand_second,
    reduce_weight,
    reduce_first,
    reduce_second,
    vector_weight,
    vector_first,
    vector_second,
):
    me = coordinates()
    core = me["core"]
    places = places_of(me)
    across = flip("core", 1)
    width = tokens.shape[1]
    units = 256

    half, block = joint_cast(places, joint_weight, vector_weight)
    joint_x, joint_y, marks = gather_joint(half, block)
    half, block = rest_cast(places, expand_weight, reduce_weight, output_weight)
    plane_x, pair_y, plane_z = gather_rest(me, half, block, marks)

    tokens = (tokens, send(tokens, across))
    cotangent = (cotangent, send(cotangent, across))
    lengths = jnp.concatenate([lengths, send(lengths, across)])

    normed_one, query, key, value, vectors, *joint_mats = joint(
        places, *tokens, joint_x, joint_y
    )
    raw = [
        *main_phase(plane_x, "x", query),
        *main_phase(pair_y, "y", query),
        *main_phase(plane_z, "z", query),
    ]
    attended = attention(lengths, query, key, value)
    branch, out_mat = output(places, attended, raw[8:])
    branch_far = send(branch, across)
    *sent, middle, layer_own, layer_other, normed_two_part, up_bias_grad = forward_backward(
        places, lengths, tokens, cotangent, branch, branch_far, vectors, raw
    )
    part_far = send(normed_two_part, across)
    layer_out = (layer_own + send(layer_other, across).astype(FULL)).astype(LOW)

    out_one, out_two, middle_grad, attended_grad, two_sums = output_backward(
        places, lengths, cotangent, middle, normed_two_part, part_far, vectors, attended, out_mat
    )
    *own_grads, own_sums = attention_backward(0, lengths, query, key, value, attended_grad)
    *other_grads, other_sums = attention_backward(1, lengths, query, key, value, attended_grad)
    sent[4:] = [jnp.concatenate(a, axis=3) for a in zip(sent[4:], (out_one, out_two))]
    rest_sums = total(me, sent, 32, 3, (own_grads[0], other_grads[0]))

    sent = joint_grad_parts(places, normed_one, own_grads, other_grads)
    joint_sums = total(me, sent, 0, 1)
    part_own, part_other = joint_backward(own_grads, other_grads, joint_mats)
    input_grad, one_sums = input_backward(
        tokens[0], part_own, send(part_other, across), middle_grad, vectors
    )

    is_core = (jnp.arange(2) == core).astype(FULL)

    def own_half(values):
        return (is_core[:, None] * values[None]).reshape(1, -1)

    head_sums = own_sums + other_sums
    up_mine = is_core[None, :, None] * up_bias_grad.reshape(8, 1, units)
    vector_local = jnp.concatenate(
        [
            one_sums[:2],
            own_half(head_sums[0]),
            own_half(head_sums[1]),
            two_sums[:3],
            up_mine.reshape(4, width),
            two_sums[3:4],
        ],
        axis=0,
    )
    vector_grad = lax.dynamic_slice(
        sum_all(vector_local), (0, 128 * lax.axis_index("shard")), (12, 128)
    )

    expand = adam_expand(places, (expand_weight, expand_first, expand_second), rest_sums)
    reduce = adam_reduce(places, (reduce_weight, reduce_first, reduce_second), rest_sums)
    output_state = adam_output(places, (output_weight, output_first, output_second), rest_sums)
    joint_state = adam_joint(places, (joint_weight, joint_first, joint_second), joint_sums)
    vector_state = (vector_grad,) + adam_step(
        vector_weight, vector_first, vector_second, vector_grad, VECTOR_RATE, 0.0
    )
    states = zip(joint_state, output_state, expand, reduce, vector_state)
    return (layer_out, input_grad, *(a for kind in states for a in kind))


def solution(mesh):
    rows, columns, split = P("shard", None), P(None, "shard"), P(("wide", "shard"), None)
    state = (rows, rows, rows, rows, columns)
    return jax.shard_map(
        per_device,
        mesh=mesh,
        in_specs=(split, split, split) + (rows,) * 12 + (columns,) * 3,
        out_specs=(split, split) + state * 4,
        check_vma=False,
    )
```

```python
import jax
import jax.numpy as jnp
from jax import lax
from jax.experimental import pallas as pl
from jax.experimental.pallas import tpu as pltpu
from jax.sharding import PartitionSpec as P

HEAD_DIM = 64
STEP = 10


ROOT_TWO_PI = 0.7978845608028654
CUBIC = 0.044715
BETA_ONE = 0.9
BETA_TWO = 0.999
ADAM_EPS = 1e-08
MATRIX_RATE = 0.03
OUTPUT_RATE = 0.1
VECTOR_RATE = 0.2
MATRIX_DECAY = 0.1

LOW = jnp.bfloat16
FULL = jnp.float32
AXES = ("wide", "shard")
SIZES = (4, 2, 2, 2, 4)
COLS = 512
VMEM_BYTES = 60 * 1024 * 1024


def coordinates():
    wide, shard = lax.axis_index("wide"), lax.axis_index("shard")
    z, xl, core = wide // 4, (wide // 2) % 2, wide % 2
    xh, y = shard // 4, shard % 4
    return {"z": z, "x": 2 * xh + xl, "y": y, "xl": xl, "xh": xh, "core": core}


def route(partner):
    pairs = []
    for source in range(128):
        rest, places = source, []
        for size in reversed(SIZES):
            places.append(rest % size)
            rest //= size
        y, xh, core, xl, z = places
        target = partner({"z": z, "x": 2 * xh + xl, "y": y, "core": core})
        flat = 0
        for place, size in zip(
            (target["z"], target["x"] % 2, target["core"], target["x"] // 2, target["y"]), SIZES
        ):
            flat = flat * size + place
        pairs.append((source, flat))
    return pairs


def flip(axis, bits):
    return route(lambda at: {**at, axis: at[axis] ^ bits})


def turn(axis, step):
    return route(lambda at: {**at, axis: at[axis] ^ (1 if (at["core"] + step) % 2 == 0 else 3)})


def send(value, pairs):
    return lax.ppermute(value, AXES, pairs)


def added(a, b):
    return (a.astype(FULL) + b.astype(FULL)).astype(LOW)


def orders(me, axis):
    here = me[axis]
    one = jnp.where(me["core"] == 0, 1, 3)
    return [here, here ^ one, here ^ (4 - one), here ^ 2]


def places_of(me):
    return jnp.stack(
        orders(me, "x")
        + orders(me, "y")
        + orders(me, "z")
        + [me["xh"], me["core"], me["xl"], me["z"]]
    ).astype(jnp.int32)


def after(value, *others):
    return lax.optimization_barrier((value, *others))[0]


def rows_of(*parts):
    return jnp.concatenate([p.reshape(-1, COLS) for p in parts])


def main_phase(block, axis, *gates):
    first, second = send(block, turn(axis, 0)), send(block, turn(axis, 1))
    return [block, first, second, send(after(first, second, *gates), turn(axis, 1))]


def gather_joint(half, block):
    other, second = lax.optimization_barrier((send(block, flip("x", 3)), send(half, turn("y", 0))))
    here, pair = jnp.stack([half, second]), jnp.stack([block, other])
    there, first_y = send(here, turn("y", 1)), send(pair, turn("y", 0))
    second_y = send(pair, turn("y", 1))
    there, first_y, second_y = lax.optimization_barrier((there, first_y, second_y))
    plane = jnp.concatenate([here, there])
    first_x, second_x = send(plane, turn("x", 0)), send(plane, turn("x", 1))
    third_y = send(first_y, turn("y", 1))
    first_x, second_x, third_y = lax.optimization_barrier((first_x, second_x, third_y))
    third_x = send(first_x, turn("x", 1))
    return (
        [plane, first_x, second_x, third_x],
        [pair, first_y, second_y, third_y],
        (other, first_x, third_x),
    )


def gather_rest(me, half, block, marks, kernel):
    other = send(after(block, marks[0]), flip("x", 3))
    pair_y = jnp.stack([block[:384], other[:384]])
    wanted = jnp.where(me["core"] == me["xh"], block[448:], other[448:]).reshape(2, 32, COLS)
    pair_z = jnp.concatenate([jnp.stack([block[384:448], other[384:448]]), wanted], axis=1)
    size = half.shape[0]
    first = after(rows_of(half, pair_z), marks[1])
    here = jnp.stack([first, send(first, turn("y", 0))])
    there = send(after(here, marks[2]), turn("y", 1))
    results = kernel(here)
    there = after(there, results[1])
    plane_x = jnp.concatenate([here[:, :size], there[:, :size]])
    plane_z = jnp.concatenate([here[:, size:], there[:, size:]]).reshape(4, 2, 96, COLS)
    return plane_x, after(pair_y, marks[2]), plane_z, results


def gated(value, gate):
    return value if gate is None else after(value, gate)


def total(me, raw, out_rows, units, extra_rows):
    axes = "xyz"
    far = [send(raw[2 * i + 1], turn(axis, 1)) for i, axis in enumerate(axes)]
    gate = yield
    near = [added(gated(raw[2 * i], gate), far[i]) for i in range(3)]
    near = lax.optimization_barrier(near)
    far = [send(near[i][1], turn(axis, 0)) for i, axis in enumerate(axes)]
    gate, extra = yield near[2]
    along_x, along_y, along_z = lax.optimization_barrier(
        [added(gated(near[i][0], gate), far[i]) for i in range(3)]
    )
    size_x, size_y = along_x.shape[1], along_y.shape[1] // 2
    size_z = (along_z.shape[2] - out_rows) // 2

    def with_extra(*parts):
        return rows_of(*parts, extra) if extra_rows else rows_of(*parts)

    def split(rows, *sizes):
        at, parts = 0, []
        for size in sizes:
            parts.append(rows[at : at + size])
            at += size
        return parts

    plane = jnp.concatenate([along_x, along_z.reshape(4, -1, COLS)], axis=1)
    size = plane.shape[1]
    far = send(with_extra(plane[2:]), turn("y", 1))
    gate = yield plane
    kept = gated(plane[:2], gate)
    near = added(kept, far[: 2 * size].reshape(2, size, COLS))
    if extra_rows:
        extra = added(extra, far[2 * size :])
    far = send(with_extra(near[1]), turn("y", 0))
    gate = yield near
    plane = added(gated(near[0], gate), far[:size])
    if extra_rows:
        extra = added(extra, far[size:])
    half, pair = plane[:size_x], plane[size_x:].reshape(2, 2 * size_z + out_rows, COLS)
    out = pair[:, 2 * size_z :].reshape(-1, COLS)
    pieces = jnp.concatenate(
        [along_y.reshape(4, size_y, COLS), pair[:, : 2 * size_z].reshape(4, size_z, COLS)], axis=1
    )
    size = size_y + size_z
    here = orders(me, "x")
    pieces = [
        lax.dynamic_index_in_dim(pieces, ((k // 2) ^ me["xh"]) * 2 + k % 2, 0, keepdims=False)
        for k in here
    ]
    far = send(with_extra(pieces[2], pieces[3], out), turn("x", 1))
    gate = yield plane
    sums, far_extra = split(far, 2 * size + 2 * out_rows, extra_rows)
    sums = added(gated(rows_of(pieces[0], pieces[1], out), gate), sums)
    if extra_rows:
        extra = added(extra, far_extra)
    piece, near, out = split(sums, size, size, 2 * out_rows)
    far = send(with_extra(near, out), turn("x", 0))
    gate = yield sums
    sums, far_extra = split(far, size + 2 * out_rows, extra_rows)
    sums = added(gated(rows_of(piece, out), gate), sums)
    if extra_rows:
        extra = added(extra, far_extra)
    flat, block = rows_of(half, sums[:size_y]), sums[size_y:]
    size, size_block = flat.shape[0], block.shape[0]
    far = send(with_extra(flat, block), turn("z", 0))
    gate = yield sums
    sums, other, far_extra = split(far, size, size_block, extra_rows)
    flat = added(gated(flat, gate), sums)
    if extra_rows:
        extra = added(extra, far_extra)
    blocks = rows_of(block, other)
    far = send(with_extra(flat, blocks), turn("z", 1))
    gate = yield flat
    sums, other, far_extra = split(far, size, 2 * size_block, extra_rows)
    flat = added(gated(flat, gate), sums)
    if extra_rows:
        extra = added(extra, far_extra)
    blocks = rows_of(blocks, other).reshape(4, size_block, COLS)
    where = orders(me, "z")
    ordered = jnp.stack(
        [
            sum(jnp.where(where[k] == place, blocks[k], 0) for k in range(4)).astype(LOW)
            for place in range(4)
        ]
    )
    mine = rows_of(flat, ordered[:, :size_z])
    far = send(mine, flip("x", 1))
    gate = yield mine
    mine = gated(mine, gate)

    def whole(groups, first, last):
        a, b = (rows[first:last].reshape(groups, -1, COLS) for rows in (mine, far))
        both = jnp.where(me["xl"] == 0, jnp.stack([a, b], axis=1), jnp.stack([b, a], axis=1))
        return both.reshape(-1, COLS)

    both = rows_of(
        whole(units, 0, size_x), whole(1, size_x, size), whole(4, size, mine.shape[0]),
        ordered[:, size_z:],
    )
    far = send(with_extra(both), flip("core", 1))
    yield both
    rows = both.shape[0]
    if extra_rows:
        extra = added(extra, far[rows:])
        far = far[:rows]
    yield both, far, extra


def rows_at(start, size):
    return pl.ds(pl.multiple_of(start, size), size)


def joint_plan(places, along_x, along_y, mats):
    query, key, value, vectors = mats
    pairs = []
    for ky in range(4):
        y = places[4 + ky]
        for kx in range(4):
            x = places[kx]
            shard, half = (x // 2) * 4 + y, x % 2
            source = along_x[kx].at[ky]
            pairs.append(
                (source.at[pl.ds(0, 64)], query.at[rows_at(shard * 128 + half * 64, 64)])
            )
            pairs.append(
                (source.at[pl.ds(64, 32)], value.at[rows_at(shard * 128 + half * 32, 32)])
            )
        for p in range(2):
            shard = (places[12] ^ p) * 4 + y
            source = along_y[ky].at[p]
            pairs.append((source.at[pl.ds(0, 128)], key.at[rows_at(shard * 128, 128)]))
            pairs.append((source.at[pl.ds(128, 64)], value.at[rows_at(shard * 128 + 64, 64)]))
            pairs.append(
                (
                    source.at[pl.ds(192, 16), pl.ds(0, 128)],
                    vectors.at[:, rows_at(shard * 128, 128)],
                )
            )
    return pairs


def joint_sent_plan(places, raw, parts):
    query, key, value = parts
    pairs = []
    for ky in range(4):
        y = places[4 + ky]
        for kx in range(4):
            x = places[kx]
            start = ((x // 2) * 4 + y) * 128 + (x % 2) * 64
            pairs.append((query.at[rows_at(start, 64)], raw[0 + kx // 2].at[kx % 2, ky]))
        for p in range(2):
            shard = (places[12] ^ p) * 4 + y
            pairs.append((key.at[rows_at(shard * 128, 128)], raw[2 + ky // 2].at[ky % 2, p]))
            for kz in range(4):
                start = shard * 128 + places[8 + kz] * 32
                pairs.append((value.at[rows_at(start, 32)], raw[4 + kz // 2].at[kz % 2, ky, p]))
    return pairs


def up_plan(places, at_x, at_y, at_z, mats):
    up, down_one, down_two = mats
    pairs = []
    for ky in range(4):
        y = places[4 + ky]
        for kx in range(4):
            x = places[kx]
            start = ((x // 2) * 4 + y) * 128 + (x % 2) * 64
            for j in range(3):
                source = at_x(kx).at[ky, pl.ds(64 * j, 64)]
                pairs.append((source, up.at[j, rows_at(start, 64)]))
        for p in range(2):
            shard = (places[12] ^ p) * 4 + y
            source = at_y(ky).at[p]
            pairs.append((source.at[pl.ds(0, 128)], up.at[3, rows_at(shard * 128, 128)]))
            pairs.append((source.at[pl.ds(128, 256)], down_one.at[rows_at(shard * 256, 256)]))
            for kz in range(4):
                start = shard * 256 + places[8 + kz] * 64
                source = at_z(kz).at[ky, p, pl.ds(0, 64)]
                pairs.append((source, down_two.at[rows_at(start, 64)]))
    return pairs


def out_plan(places, at_z, first, mat):
    pairs = []
    for ky in range(4):
        for kz in range(4):
            start = places[4 + ky] * 128 + places[8 + kz] * 32
            for p in range(2):
                source = at_z(kz).at[ky, p, pl.ds(first, 32)]
                pairs.append((source, mat.at[p, rows_at(start, 32)]))
    return pairs


def two_of(arrays):
    return lambda k: arrays[k // 2].at[k % 2]


def started(pairs, sems):
    all_of_them = [pltpu.make_async_copy(a, b, sems.at[i]) for i, (a, b) in enumerate(pairs)]
    for copy in all_of_them:
        copy.start()
    return all_of_them


def finished(all_of_them):
    for copy in all_of_them:
        copy.wait()


def turned(pairs):
    return [(b, a) for a, b in pairs]


def low_shape(*shape):
    return jax.ShapeDtypeStruct(shape, LOW)


def full_shape(*shape):
    return jax.ShapeDtypeStruct(shape, FULL)


SCALARS = pl.BlockSpec(memory_space=pltpu.SMEM)
INSIDE = pl.BlockSpec(memory_space=pltpu.VMEM)
OUTSIDE = pl.BlockSpec(memory_space=pl.ANY)


def call(kernel, in_specs, outs, scratch, flops, args, grid=()):
    shapes, specs = [o[0] for o in outs], [o[1] for o in outs]
    moved = sum(a.size * a.dtype.itemsize for a in (*args, *shapes))
    return pl.pallas_call(
        kernel,
        grid=grid,
        out_shape=shapes,
        in_specs=in_specs,
        out_specs=specs,
        scratch_shapes=scratch,
        compiler_params=pltpu.CompilerParams(vmem_limit_bytes=VMEM_BYTES),
        cost_estimate=pl.CostEstimate(flops=flops, bytes_accessed=moved, transcendentals=0),
    )(*args)


def gelu_both(upward):
    square = upward * upward
    tangent = jnp.tanh(ROOT_TWO_PI * upward * (1.0 + CUBIC * square))
    half = 0.5 * (1.0 + tangent)
    slope = half + 0.5 * upward * (1.0 - tangent * tangent) * ROOT_TWO_PI * (
        1.0 + 3.0 * CUBIC * square
    )
    return upward * half, slope


def dot(a, b):
    return jnp.dot(a, b, preferred_element_type=FULL)


def dot_nt(a, b):
    return lax.dot_general(a, b, (((1,), (1,)), ((), ())), preferred_element_type=FULL)


def dot_tn(a, b):
    return lax.dot_general(a, b, (((0,), (0,)), ((), ())), preferred_element_type=FULL)


def unit_of(values):
    center = values - jnp.mean(values, axis=-1, keepdims=True)
    inverse = lax.rsqrt(jnp.mean(center * center, axis=-1, keepdims=True) + 1e-05)
    return center * inverse, inverse


def norm_backward(grad_out, unit, inverse, gain):
    scaled = grad_out * gain
    return inverse * (
        scaled
        - jnp.mean(scaled, axis=-1, keepdims=True)
        - unit * jnp.mean(scaled * unit, axis=-1, keepdims=True)
    )


def row_of(vectors, row):
    return vectors[row : row + 1, :].astype(FULL)


def own_columns(full, core, size):
    groups = full.shape[1] // (2 * size)
    first = jnp.concatenate(
        [full[:, (2 * g) * size : (2 * g + 1) * size] for g in range(groups)], axis=1
    )
    second = jnp.concatenate(
        [full[:, (2 * g + 1) * size : (2 * g + 2) * size] for g in range(groups)], axis=1
    )
    return jnp.where(core == 0, first, second)


def barred(lengths, block, first, height, span):
    shape = (height, span)
    rows = lax.broadcasted_iota(jnp.int32, shape, 0) + first
    keys = lax.broadcasted_iota(jnp.int32, shape, 1)
    opening = lengths[block, 0]
    filled = opening + lengths[block, 1]
    begin = jnp.where(rows < opening, 0, jnp.where(rows < filled, opening, rows))
    return jnp.where((keys <= rows) & (keys >= begin), 0.0, -1e30)


TILE = 128


def joint_cast_kernel(places, weight, vector, half, block, held, padded, sems):
    core, xl = places[13], places[14]

    def cols(which):
        return rows_at(which * 2 * COLS + core * COLS, COLS)

    copies = started(
        [
            (weight.at[rows_at(xl * 64, 64), cols(0)], held.at[pl.ds(0, 64)]),
            (weight.at[rows_at(xl * 32, 32), cols(2)], held.at[pl.ds(64, 32)]),
            (weight.at[:, cols(1)], held.at[pl.ds(96, 128)]),
            (weight.at[pl.ds(64, 64), cols(2)], held.at[pl.ds(224, 64)]),
        ],
        sems,
    )
    padded[...] = jnp.zeros_like(padded)
    padded[: vector.shape[0], : vector.shape[1]] = vector[...]
    block[192:208, :] = padded[...].astype(LOW)
    finished(copies)
    half[...] = held[:96].astype(LOW)
    block[:192, :] = held[96:].astype(LOW)


def joint_cast(places, weight, vector):
    return call(
        joint_cast_kernel,
        [SCALARS, OUTSIDE, INSIDE],
        [(low_shape(96, COLS), INSIDE), (low_shape(208, COLS), INSIDE)],
        [pltpu.VMEM((288, COLS), FULL), pltpu.VMEM((16, COLS), FULL)]
        + [pltpu.SemaphoreType.DMA((4,))],
        0,
        (places, weight, vector),
    )


def rest_cast_kernel(places, expand, reduce, output, half, block, held, wide, sems):
    core, xl, z = places[13], places[14], places[15]
    pairs = []
    for s in range(8):
        j, right = s // 2, (s % 2) * 256
        cols = rows_at(s * 512 + core * 256, 256)
        rows, size = (rows_at(xl * 64, 64), 64) if j < 3 else (pl.ds(0, 128), 128)
        pairs.append((expand.at[rows, cols], held.at[pl.ds(64 * j, size), pl.ds(right, 256)]))
    pairs.append((reduce.at[rows_at(core * 256, 256), pl.ds(0, COLS)], held.at[pl.ds(320, 256)]))
    pairs.append(
        (reduce.at[rows_at(core * 256 + z * 64, 64), pl.ds(COLS, COLS)], held.at[pl.ds(576, 64)])
    )
    pairs.append((output.at[rows_at(z * 32, 32)], wide))
    finished(started(pairs, sems))
    half[...] = held[:192].astype(LOW)
    block[:448, :] = held[192:640].astype(LOW)
    block[448:480, :] = wide[:, :COLS].astype(LOW)
    block[480:512, :] = wide[:, COLS:].astype(LOW)


def rest_cast(places, expand, reduce, output):
    return call(
        rest_cast_kernel,
        [SCALARS, OUTSIDE, OUTSIDE, OUTSIDE],
        [(low_shape(192, COLS), INSIDE), (low_shape(512, COLS), INSIDE)],
        [pltpu.VMEM((640, COLS), FULL), pltpu.VMEM((32, 2 * COLS), FULL)]
        + [pltpu.SemaphoreType.DMA((11,))],
        0,
        (places, expand, reduce, output),
    )


def joint_kernel(places, own, other, *refs):
    along_x, along_y, refs = refs[:4], refs[4:8], refs[8:]
    normed, query, key, value, vectors, query_mat, key_mat, value_mat, sems = refs
    mats = (query_mat, key_mat, value_mat, vectors)
    finished(started(joint_plan(places, along_x, along_y, mats), sems))
    gain, shift = row_of(vectors, 0), row_of(vectors, 1)
    core = places[13]
    query_bias = own_columns(row_of(vectors, 2), core, COLS)
    value_bias = own_columns(row_of(vectors, 3), core, COLS)
    count = own.shape[0]
    for block, tokens in enumerate((own, other)):
        rows = pl.ds(block * count, count)
        unit, _ = unit_of(tokens[...].astype(FULL))
        low = (unit * gain + shift).astype(LOW)
        normed[rows, :] = low
        query[rows, :] = ((dot(low, query_mat[...]) + query_bias).astype(LOW) * 0.125).astype(LOW)
        key[rows, :] = dot(low, key_mat[...]).astype(LOW)
        value[rows, :] = (dot(low, value_mat[...]) + value_bias).astype(LOW)


def joint(places, own, other, along_x, along_y):
    count, width = own.shape
    rows = 2 * count
    mat, half = (low_shape(width, COLS), INSIDE), (low_shape(rows, COLS), INSIDE)
    return call(
        joint_kernel,
        [SCALARS, INSIDE, INSIDE] + [OUTSIDE] * 8,
        [(low_shape(rows, width), INSIDE), half, half, half]
        + [(low_shape(16, width), INSIDE), mat, mat, mat],
        [pltpu.SemaphoreType.DMA((56,))],
        6 * rows * width * COLS,
        (places, own, other, *along_x, *along_y),
    )


def attention_kernel(block, lengths, query, key, value, attended, mask):
    count = query.shape[0]
    spans = count // TILE
    for i in range(spans):
        mask[i * TILE : (i + 1) * TILE, : (i + 1) * TILE] = barred(
            lengths, block, i * TILE, TILE, (i + 1) * TILE
        )

    def two_heads(index, carry):
        cols = rows_at(index * TILE, TILE)
        lane = lax.broadcasted_iota(jnp.int32, (TILE, TILE), 1) < HEAD_DIM
        for i in range(spans):
            before, span = i * TILE, (i + 1) * TILE
            both = query[before:span, cols]
            bar = mask[before:span, :span]
            outs = []
            for side in (lane, ~lane):
                scores = dot_nt(jnp.where(side, both, 0), key[:span, cols]) + bar
                probs = jnp.exp(scores - jnp.max(scores, axis=-1, keepdims=True))
                probs = probs * (1.0 / jnp.sum(probs, axis=-1, keepdims=True))
                outs.append(dot(probs.astype(LOW), value[:span, cols]))
            attended[before:span, cols] = jnp.where(lane, outs[0], outs[1]).astype(LOW)
        return carry

    lax.fori_loop(0, COLS // TILE, two_heads, 0)


def attention(block, lengths, query, key, value):
    count = query.shape[0] // 2
    return call(
        lambda *refs: attention_kernel(block, *refs),
        [SCALARS] + [pl.BlockSpec((count, COLS), lambda i: (block, 0))] * 3,
        [(low_shape(count, COLS), INSIDE)],
        [pltpu.VMEM((count, count), FULL)],
        4 * count * count * COLS,
        (lengths, query, key, value),
        grid=(1,),
    )[0]


def output_kernel(places, own, other, *refs):
    raw, (branch, out_mat, sems) = refs[:4], refs[4:]
    finished(started(out_plan(places, lambda k: raw[k], 64, out_mat), sems))
    count = own.shape[0]
    for block, attended in enumerate((own, other)):
        for half in range(2):
            branch[block * count : (block + 1) * count, half * COLS : (half + 1) * COLS] = dot(
                attended[...], out_mat[half]
            ).astype(LOW)


def output(places, own, other, raw):
    rows, local = 2 * own.shape[0], own.shape[1]
    return call(
        output_kernel,
        [SCALARS, INSIDE, INSIDE] + [OUTSIDE] * 4,
        [(low_shape(rows, 2 * COLS), INSIDE), (low_shape(2, local, COLS), INSIDE)],
        [pltpu.SemaphoreType.DMA((32,))],
        4 * rows * local * COLS,
        (places, own, other, *raw),
    )


def forward_backward_kernel(
    places, lengths, own, other, arriving_own, arriving_other, branch, branch_far, vectors, *refs
):
    raw, refs = refs[:12], refs[12:]
    sent, refs = refs[:6], refs[6:]
    (middle, layer_own, layer_other, normed_grad, bias_grad,
     up, down_one, down_two, up_grad, one_grad, two_grad,
     normed, arriving, layer_sum, normed_sum, active, up_low, sems) = refs
    held = [lambda k, a=axis: raw[4 * a + k] for axis in range(3)]
    copies = started(up_plan(places, *held, (up, down_one, down_two)), sems)
    count = own.shape[0]
    tile = 256
    gain, shift = row_of(vectors, 5), row_of(vectors, 6)
    for block, (tokens, cotangent) in enumerate(((own, arriving_own), (other, arriving_other))):
        rows, far = pl.ds(block * count, count), pl.ds((1 - block) * count, count)
        summed = branch[rows, :].astype(FULL) + branch_far[far, :].astype(FULL)
        held = tokens[...].astype(FULL) + summed + row_of(vectors, 4)
        middle[rows, :] = held
        unit, _ = unit_of(held)
        normed[rows, :] = (unit * gain + shift).astype(LOW)
        slots = lax.broadcasted_iota(jnp.int32, cotangent.shape, 0)
        live = slots < lengths[block, 0] + lengths[block, 1]
        arriving[rows, :] = jnp.where(live, cotangent[...], 0)
    layer_sum[...] = jnp.zeros_like(layer_sum)
    normed_sum[...] = jnp.zeros_like(normed_sum)
    bias_grad[...] = jnp.zeros_like(bias_grad)
    core = places[13]
    biases = jnp.concatenate(
        [own_columns(row_of(vectors, 7 + k), core, 256) for k in range(4)], axis=0
    )
    finished(copies)

    def chunk(j, carry):
        hidden = rows_at(j * COLS, COLS)
        bias = jnp.zeros((1, COLS), FULL)
        for k in range(4):
            bias = jnp.where(j == k, biases[k : k + 1], bias)

        def rows_step(index, carry):
            rows = rows_at(index * tile, tile)
            upward = dot(normed[rows, :], up[j]) + bias
            act, slope = gelu_both(upward)
            act = act.astype(LOW)
            active[rows, :] = act
            layer_sum[rows, :COLS] += dot(act, down_one[hidden, :])
            layer_sum[rows, COLS:] += dot(act, down_two[hidden, :])
            grad = dot_nt(arriving[rows, :COLS], down_one[hidden, :])
            grad += dot_nt(arriving[rows, COLS:], down_two[hidden, :])
            low = (grad * slope).astype(LOW)
            up_low[rows, :] = low
            bias_grad[pl.ds(j, 1), :] += jnp.sum(low.astype(FULL), axis=0, keepdims=True)
            normed_sum[rows, :] += dot_nt(low, up[j])
            return carry

        lax.fori_loop(0, normed.shape[0] // tile, rows_step, 0)
        one_grad[hidden, :] = dot_tn(active[...], arriving[:, :COLS]).astype(LOW)
        two_grad[hidden, :] = dot_tn(active[...], arriving[:, COLS:]).astype(LOW)
        up_grad[j] = dot_tn(normed[...], up_low[...]).astype(LOW)
        return carry

    lax.fori_loop(0, up.shape[0], chunk, 0)
    held = [two_of(sent[2 * axis : 2 * axis + 2]) for axis in range(3)]
    copies = started(turned(up_plan(places, *held, (up_grad, one_grad, two_grad))), sems)
    layer_own[...] = middle[:count, :] + layer_sum[:count, :] + row_of(vectors, 11)
    layer_other[...] = layer_sum[count:, :].astype(LOW)
    normed_grad[...] = normed_sum[...].astype(LOW)
    finished(copies)


def forward_backward(places, lengths, tokens, arriving, branch, branch_far, vectors, raw):
    count, width = tokens[0].shape
    rows, hidden = 2 * count, 4 * COLS
    sent = [low_shape(2, 4, 192, COLS), low_shape(2, 2, 384, COLS), low_shape(2, 4, 2, 64, COLS)]
    inside = [
        full_shape(rows, width), full_shape(count, width), low_shape(count, width),
        low_shape(rows, width), full_shape(4, COLS),
    ]
    vmem = pltpu.VMEM
    mats = [vmem((4, width, COLS), LOW), vmem((hidden, COLS), LOW), vmem((hidden, COLS), LOW)]
    return call(
        forward_backward_kernel,
        [SCALARS, SCALARS] + [INSIDE] * 7 + [OUTSIDE] * 12,
        [(s, OUTSIDE) for s in sent for _ in range(2)] + [(s, INSIDE) for s in inside],
        mats + mats
        + [vmem((rows, width), LOW), vmem((rows, width), LOW)]
        + [vmem((rows, width), FULL), vmem((rows, width), FULL)]
        + [vmem((rows, COLS), LOW), vmem((rows, COLS), LOW), pltpu.SemaphoreType.DMA((96,))],
        12 * rows * width * hidden,
        (places, lengths, *tokens, *arriving, branch, branch_far, vectors, *raw),
    )


def output_backward_kernel(
    places, lengths, arriving_own, arriving_other, middle, part, part_far, vectors, own, other,
    out_mat, sent_one, sent_two, middle_grad, attended_grad, sums, branch, out_grad, sems,
):
    count = arriving_own.shape[0]
    gain = row_of(vectors, 5)
    for block, cotangent in enumerate((arriving_own, arriving_other)):
        rows, far = pl.ds(block * count, count), pl.ds((1 - block) * count, count)
        unit, inverse = unit_of(middle[rows, :])
        grad = part[rows, :].astype(FULL) + part_far[far, :].astype(FULL)
        slots = lax.broadcasted_iota(jnp.int32, cotangent.shape, 0)
        live = slots < lengths[block, 0] + lengths[block, 1]
        arriving = jnp.where(live, cotangent[...].astype(FULL), 0.0)
        held = arriving + norm_backward(grad, unit, inverse, gain)
        low = held.astype(LOW)
        branch[rows, :] = low
        if block == 0:
            middle_grad[...] = held
            sums[...] = jnp.zeros_like(sums)
            sums[0:1, :] = jnp.sum(low.astype(FULL), axis=0, keepdims=True)
            sums[1:2, :] = jnp.sum(grad * unit, axis=0, keepdims=True)
            sums[2:3, :] = jnp.sum(grad, axis=0, keepdims=True)
            sums[3:4, :] = jnp.sum(arriving, axis=0, keepdims=True)
    for half in range(2):
        cols = slice(half * COLS, (half + 1) * COLS)
        out_grad[half] = (
            dot_tn(own[...], branch[:count, cols]) + dot_tn(other[...], branch[count:, cols])
        ).astype(LOW)
    copies = started(turned(out_plan(places, two_of((sent_one, sent_two)), 0, out_grad)), sems)
    attended_grad[...] = (
        dot_nt(branch[:, :COLS], out_mat[0]) + dot_nt(branch[:, COLS:], out_mat[1])
    ).astype(LOW)
    finished(copies)


def output_backward(
    places, lengths, arriving, middle, part, part_far, vectors, attended, out_mat
):
    rows, width = middle.shape
    sent = (low_shape(2, 4, 2, 32, COLS), OUTSIDE)
    inside = [full_shape(rows // 2, width), low_shape(rows, COLS), full_shape(8, width)]
    return call(
        output_backward_kernel,
        [SCALARS, SCALARS] + [INSIDE] * 9,
        [sent, sent] + [(s, INSIDE) for s in inside],
        [pltpu.VMEM((rows, width), LOW), pltpu.VMEM((2, COLS, COLS), LOW)]
        + [pltpu.SemaphoreType.DMA((32,))],
        8 * rows * width * COLS,
        (places, lengths, *arriving, middle, part, part_far, vectors, *attended, out_mat),
    )


def attention_backward_kernel(
    block, lengths, query, key, value, grad_in, query_grad, key_grad, value_grad, sums,
    mask, key_sum, value_sum,
):
    count = query.shape[0]
    spans = count // TILE
    for i in range(spans):
        mask[i * TILE : (i + 1) * TILE, : (i + 1) * TILE] = barred(
            lengths, block, i * TILE, TILE, (i + 1) * TILE
        )

    def two_heads(index, carry):
        cols = rows_at(index * TILE, TILE)
        lane = lax.broadcasted_iota(jnp.int32, (TILE, TILE), 1) < HEAD_DIM
        lanes = lax.broadcasted_iota(jnp.int32, (count, TILE), 1) < HEAD_DIM
        for i in range(spans):
            before, span = i * TILE, (i + 1) * TILE
            two_q, two_g = query[before:span, cols], grad_in[before:span, cols]
            two_k, two_v = key[:span, cols], value[:span, cols]
            bar = mask[before:span, :span]
            outs = []
            for h, side in enumerate((lane, ~lane)):
                scores = dot_nt(jnp.where(side, two_q, 0), two_k) + bar
                probs = jnp.exp(scores - jnp.max(scores, axis=-1, keepdims=True))
                probs = probs * (1.0 / jnp.sum(probs, axis=-1, keepdims=True))
                grad = dot_nt(jnp.where(side, two_g, 0), two_v)
                weighted = probs * grad
                grad = probs * (grad - jnp.sum(weighted, axis=-1, keepdims=True))
                low = grad.astype(LOW)
                outs.append(dot(low, two_k))
                key_now = dot_tn(low, two_q)
                value_now = dot_tn(probs.astype(LOW), two_g)
                if i > 0:
                    key_sum[h, :before] += key_now[:before]
                    value_sum[h, :before] += value_now[:before]
                key_sum[h, before:span] = key_now[before:]
                value_sum[h, before:span] = value_now[before:]
            query_grad[before:span, cols] = (jnp.where(lane, outs[0], outs[1]) * 0.125).astype(LOW)
        key_grad[:, cols] = jnp.where(lanes, key_sum[0], key_sum[1]).astype(LOW)
        value_grad[:, cols] = jnp.where(lanes, value_sum[0], value_sum[1]).astype(LOW)
        return carry

    lax.fori_loop(0, COLS // TILE, two_heads, 0)
    sums[...] = jnp.zeros_like(sums)
    sums[0:1, :] = jnp.sum(query_grad[...].astype(FULL), axis=0, keepdims=True)
    sums[1:2, :] = jnp.sum(value_grad[...].astype(FULL), axis=0, keepdims=True)


def attention_backward(block, lengths, query, key, value, grad_in):
    count = query.shape[0] // 2
    vmem = pltpu.VMEM
    half = (low_shape(count, COLS), INSIDE)
    part = pl.BlockSpec((count, COLS), lambda i: (block, 0))
    return call(
        lambda *refs: attention_backward_kernel(block, *refs),
        [SCALARS] + [part] * 4,
        [half, half, half, (full_shape(8, COLS), INSIDE)],
        [vmem((count, count), FULL), vmem((2, count, TILE), FULL), vmem((2, count, TILE), FULL)],
        10 * count * count * COLS,
        (lengths, query, key, value, grad_in),
        grid=(1,),
    )


def joint_grad_kernel(places, normed, *refs):
    grads, sent, (query_part, key_part, value_part, sems) = refs[:6], refs[6:12], refs[12:]
    parts = (query_part, key_part, value_part)
    count = grads[0].shape[0]
    for part, own, other in zip(parts, grads[:3], grads[3:]):
        part[...] = (
            dot_tn(normed[:count, :], own[...]) + dot_tn(normed[count:, :], other[...])
        ).astype(LOW)
    finished(started(joint_sent_plan(places, sent, parts), sems))


def joint_grad_parts(places, normed, own, other):
    rows, width = normed.shape
    sent = [low_shape(2, 4, 64, COLS), low_shape(2, 2, 128, COLS), low_shape(2, 4, 2, 32, COLS)]
    return call(
        joint_grad_kernel,
        [SCALARS] + [INSIDE] * 7,
        [(s, OUTSIDE) for s in sent for _ in range(2)],
        [pltpu.VMEM((width, COLS), LOW)] * 3 + [pltpu.SemaphoreType.DMA((56,))],
        6 * rows * width * COLS,
        (places, normed, *own, *other),
    )


def joint_backward_kernel(*refs):
    own, other, mats, outs = refs[:3], refs[3:6], refs[6:9], refs[9:]
    for grads, out in zip((own, other), outs):
        whole = dot_nt(grads[0][...], mats[0][...])
        whole += dot_nt(grads[1][...], mats[1][...])
        whole += dot_nt(grads[2][...], mats[2][...])
        out[...] = whole.astype(out.dtype)


def joint_backward(own, other, mats):
    count, width = own[0].shape[0], mats[0].shape[0]
    return call(
        joint_backward_kernel,
        [INSIDE] * 9,
        [(full_shape(count, width), INSIDE), (low_shape(count, width), INSIDE)],
        [],
        12 * count * width * COLS,
        (*own, *other, *mats),
    )


def input_kernel(tokens, part, part_far, middle_grad, vectors, input_grad, sums):
    unit, inverse = unit_of(tokens[...].astype(FULL))
    grad = part[...] + part_far[...].astype(FULL)
    input_grad[...] = middle_grad[...] + norm_backward(grad, unit, inverse, row_of(vectors, 0))
    sums[...] = jnp.zeros_like(sums)
    sums[0:1, :] = jnp.sum(grad * unit, axis=0, keepdims=True)
    sums[1:2, :] = jnp.sum(grad, axis=0, keepdims=True)


def input_backward(tokens, part, part_far, middle_grad, vectors):
    return call(
        input_kernel,
        [INSIDE] * 5,
        [(full_shape(*part.shape), INSIDE), (full_shape(8, part.shape[1]), INSIDE)],
        [],
        20 * part.size,
        (tokens, part, part_far, middle_grad, vectors),
    )


def adam_step(weight, first, second, grad, rate, decay):
    first_new = BETA_ONE * first + (1.0 - BETA_ONE) * grad
    second_new = BETA_TWO * second + (1.0 - BETA_TWO) * grad * grad
    mean_hat = first_new / (1.0 - BETA_ONE**STEP)
    square_hat = second_new / (1.0 - BETA_TWO**STEP)
    fresh = weight - rate * (mean_hat / (jnp.sqrt(square_hat) + ADAM_EPS) + decay * weight)
    return (first_new, second_new, fresh)


def adam_kernel(grad_of, rate, places, weight, first, second, *refs):
    grads, outs = refs[:-4], refs[-4:]
    grad = grad_of(places, *(g[...].astype(FULL) for g in grads))
    outs[0][...] = grad
    outs[1][...], outs[2][...], outs[3][...] = adam_step(
        weight[...], first[...], second[...], grad, rate, MATRIX_DECAY
    )


def adam(grad_of, rate, grid, state, state_block, state_map, grads, places):
    spec = pl.BlockSpec(state_block, state_map)
    shape = full_shape(*state[0].shape)
    return pl.pallas_call(
        lambda *refs: adam_kernel(grad_of, rate, *refs),
        grid=grid,
        in_specs=[SCALARS] + [spec] * 3 + [pl.BlockSpec(g[1], g[2]) for g in grads],
        out_specs=[spec] * 4,
        out_shape=[shape] * 4,
        compiler_params=pltpu.CompilerParams(vmem_limit_bytes=VMEM_BYTES),
        cost_estimate=pl.CostEstimate(
            flops=20 * state[0].size, bytes_accessed=30 * state[0].size, transcendentals=0
        ),
    )(places, *state, *(g[0] for g in grads))


def by_core(places, both, far):
    own = places[13] == 0
    return jnp.where(own, both, far), jnp.where(own, far, both)


def adam_joint(places, state, sums):
    def grad_of(places, both, far):
        half = pl.program_id(0) % 2
        return jnp.where(half == places[13], both, far)

    block = (128, COLS)
    grads = [(a, block, lambda g: (g // 2, 0)) for a in sums]
    return adam(grad_of, MATRIX_RATE, (6,), state, block, lambda g: (0, g), grads, places)


def adam_expand(places, state, sums):
    def grad_of(places, both, far):
        zero, one = by_core(places, both, far)
        return jnp.concatenate(
            [zero[:, :256], one[:, :256], zero[:, 256:], one[:, 256:]], axis=1
        )

    grads = [(a, (128, COLS), lambda j: (j, 0)) for a in sums]
    return adam(
        grad_of, MATRIX_RATE, (4,), state, (128, 2 * COLS), lambda j: (0, j), grads, places
    )


def adam_reduce(places, state, sums):
    def grad_of(places, left, right, far_left, far_right):
        own = pl.program_id(0) // 4 == places[13]
        return jnp.concatenate(
            [jnp.where(own, left, far_left), jnp.where(own, right, far_right)], axis=1
        )

    block = (64, COLS)
    grads = []
    for a in sums:
        grads.append((a, block, lambda g: (8 + g % 4, 0)))
        grads.append((a, block, lambda g: (12 + g % 4, 0)))
    return adam(
        grad_of, MATRIX_RATE, (8,), state, (64, 2 * COLS), lambda g: (g, 0), grads, places
    )


def adam_output(places, state, sums):
    def grad_of(places, both, far):
        grad = jnp.where(places[13] == places[12], both, far)
        return jnp.concatenate([grad[:32], grad[32:]], axis=1)

    grads = [(a, (64, COLS), lambda q: (16 + q, 0)) for a in sums]
    return adam(
        grad_of, OUTPUT_RATE, (4,), state, (32, 2 * COLS), lambda q: (q, 0), grads, places
    )


def per_device(
    tokens,
    cotangent,
    lengths,
    joint_weight,
    joint_first,
    joint_second,
    output_weight,
    output_first,
    output_second,
    expand_weight,
    expand_first,
    expand_second,
    reduce_weight,
    reduce_first,
    reduce_second,
    vector_weight,
    vector_first,
    vector_second,
):
    me = coordinates()
    core = me["core"]
    places = places_of(me)
    across = flip("core", 1)
    width = tokens.shape[1]
    units = 256

    half, block = joint_cast(places, joint_weight, vector_weight)
    joint_x, joint_y, marks = gather_joint(half, block)
    half, block = rest_cast(places, expand_weight, reduce_weight, output_weight)

    tokens = (tokens, send(tokens, across))
    cotangent = (cotangent, send(cotangent, across))
    lengths = jnp.concatenate([lengths, send(lengths, across)])

    plane_x, pair_y, plane_z, results = gather_rest(
        me, half, block, marks, lambda gate: joint(places, *tokens, joint_x, joint_y)
    )
    normed_one, query, key, value, vectors, *joint_mats = results
    along_y = main_phase(pair_y, "y", query)
    own = attention(0, lengths, after(query, *along_y[1:3]), key, value)
    along_z = main_phase(plane_z, "z", own)
    along_x = main_phase(plane_x, "x", own)
    other = attention(1, lengths, after(query, *along_z[1:3], *along_x[1:3]), key, value)
    attended = (own, other)
    branch, out_mat = output(places, own, after(other, along_x[3], along_y[3]), along_z)
    branch_far = send(branch, across)
    *sent, middle, layer_own, layer_other, normed_two_part, up_bias_grad = forward_backward(
        places, lengths, tokens, cotangent, branch, branch_far, vectors,
        [*along_x, *along_y, *along_z],
    )
    part_far = send(normed_two_part, across)
    layer_out = (layer_own + send(layer_other, across).astype(FULL)).astype(LOW)

    out_one, out_two, middle_grad, attended_grad, two_sums = output_backward(
        places, lengths, cotangent, middle, normed_two_part, part_far, vectors, attended, out_mat
    )
    sent[4:] = [jnp.concatenate(a, axis=3) for a in zip(sent[4:], (out_one, out_two))]
    rest = total(me, sent, 32, 3, 0)
    next(rest)
    *own_grads, own_sums = attention_backward(0, lengths, query, key, value, attended_grad)
    mark = rest.send(own_grads[0])
    *other_grads, other_sums = attention_backward(
        1, lengths, query, key, value, after(attended_grad, mark)
    )
    mark = rest.send((other_grads[0], None))
    sent = joint_grad_parts(places, after(normed_one, mark), own_grads, other_grads)
    joint_rows = total(me, sent, 0, 1, 32)
    next(joint_rows)
    mark = rest.send(sent[0])
    part_own, part_other = joint_backward(
        (after(own_grads[0], mark), *own_grads[1:]), other_grads, joint_mats
    )
    part_far = send(part_other, across)
    mark = rest.send(part_own)
    mark = joint_rows.send(mark)
    input_grad, one_sums = input_backward(
        tokens[0], after(part_own, mark), part_far, middle_grad, vectors
    )

    is_core = (jnp.arange(2) == core).astype(FULL)

    def own_half(values):
        return (is_core[:, None] * values[None]).reshape(1, -1)

    head_sums = own_sums + other_sums
    up_mine = is_core[None, :, None] * up_bias_grad.reshape(8, 1, units)
    vector_local = jnp.concatenate(
        [
            one_sums[:2],
            own_half(head_sums[0]),
            own_half(head_sums[1]),
            two_sums[:3],
            up_mine.reshape(4, width),
            two_sums[3:4],
            jnp.zeros((4, width), FULL),
        ],
        axis=0,
    ).astype(LOW)
    vector_local = rows_of(vector_local[:, :COLS], vector_local[:, COLS:])

    mark = rest.send(one_sums)
    mark = joint_rows.send((mark, vector_local))
    for _ in range(3):
        mark = rest.send(mark)
        mark = joint_rows.send(mark)
    mark = rest.send(mark)
    *rest_sums, _ = next(rest)
    expand = adam_expand(places, (expand_weight, expand_first, expand_second), rest_sums)
    mark = joint_rows.send(mark)
    mark = joint_rows.send(expand[0])
    reduce = adam_reduce(places, (reduce_weight, reduce_first, reduce_second), rest_sums)
    mark = joint_rows.send(reduce[0])
    output_state = adam_output(places, (output_weight, output_first, output_second), rest_sums)
    mark = joint_rows.send(output_state[0])
    *joint_sums, extra = next(joint_rows)
    joint_state = adam_joint(places, (joint_weight, joint_first, joint_second), joint_sums)
    vector_grad = lax.dynamic_slice(
        jnp.concatenate([extra[:12], extra[16:28]], axis=1).astype(FULL),
        (0, 128 * lax.axis_index("shard")),
        (12, 128),
    )
    vector_state = (vector_grad,) + adam_step(
        vector_weight, vector_first, vector_second, vector_grad, VECTOR_RATE, 0.0
    )
    states = zip(joint_state, output_state, expand, reduce, vector_state)
    return (layer_out, input_grad, *(a for kind in states for a in kind))


def solution(mesh):
    rows, columns, split = P("shard", None), P(None, "shard"), P(("wide", "shard"), None)
    state = (rows, rows, rows, rows, columns)
    return jax.shard_map(
        per_device,
        mesh=mesh,
        in_specs=(split, split, split) + (rows,) * 12 + (columns,) * 3,
        out_specs=(split, split) + state * 4,
        check_vma=False,
    )
```

```python
import jax
import jax.numpy as jnp
from jax import lax
from jax.experimental import pallas as pl
from jax.experimental.pallas import tpu as pltpu
from jax.sharding import PartitionSpec as P

HEAD_DIM = 64
STEP = 10


ROOT_TWO_PI = 0.7978845608028654
CUBIC = 0.044715
BETA_ONE = 0.9
BETA_TWO = 0.999
ADAM_EPS = 1e-08
MATRIX_RATE = 0.03
OUTPUT_RATE = 0.1
VECTOR_RATE = 0.2
MATRIX_DECAY = 0.1

LOW = jnp.bfloat16
FULL = jnp.float32
AXES = ("wide", "shard")
SIZES = (4, 2, 2, 2, 4)
COLS = 512
VMEM_BYTES = 60 * 1024 * 1024
FLOPS_PER_US = 1_150_000_000


def coordinates():
    wide, shard = lax.axis_index("wide"), lax.axis_index("shard")
    z, xl, core = wide // 4, (wide // 2) % 2, wide % 2
    xh, y = shard // 4, shard % 4
    return {"z": z, "x": 2 * xh + xl, "y": y, "xl": xl, "xh": xh, "core": core}


def route(partner):
    pairs = []
    for source in range(128):
        rest, places = source, []
        for size in reversed(SIZES):
            places.append(rest % size)
            rest //= size
        y, xh, core, xl, z = places
        target = partner({"z": z, "x": 2 * xh + xl, "y": y, "core": core})
        flat = 0
        for place, size in zip(
            (target["z"], target["x"] % 2, target["core"], target["x"] // 2, target["y"]), SIZES
        ):
            flat = flat * size + place
        pairs.append((source, flat))
    return pairs


def flip(axis, bits):
    return route(lambda at: {**at, axis: at[axis] ^ bits})


def turn(axis, step):
    return route(lambda at: {**at, axis: at[axis] ^ (1 if (at["core"] + step) % 2 == 0 else 3)})


def send(value, pairs):
    return lax.ppermute(value, AXES, pairs)


def added(*terms):
    return sum(term.astype(FULL) for term in terms).astype(LOW)


def orders(me, axis):
    here = me[axis]
    one = jnp.where(me["core"] == 0, 1, 3)
    return [here, here ^ one, here ^ (4 - one), here ^ 2]


def places_of(me):
    return jnp.stack(
        orders(me, "x")
        + orders(me, "y")
        + orders(me, "z")
        + [me["xh"], me["core"], me["xl"], me["z"]]
    ).astype(jnp.int32)


def after(value, *others):
    return lax.optimization_barrier((value, *others))[0]


def rows_of(*parts):
    return jnp.concatenate([p.reshape(-1, COLS) for p in parts])


def main_phase(block, axis, *gates):
    first, second = send(block, turn(axis, 0)), send(block, turn(axis, 1))
    return [block, first, second, send(after(first, second, *gates), turn(axis, 1))]


def gather_joint(half, block, *beside):
    size, size_y = half.shape[0], 2 * block.shape[0]
    other, second, *early = lax.optimization_barrier(
        (send(block, flip("x", 3)), send(half, turn("y", 0)), *beside[0])
    )
    pair, both = rows_of(block, other), rows_of(block, other, half, second)
    first_y, second_y = lax.optimization_barrier((send(pair, turn("y", 0)), send(both, turn("y", 1))))
    plane = rows_of(half, second, second_y[size_y:]).reshape(4, size, COLS)
    first_x, second_x = send(plane, turn("x", 0)), send(plane, turn("x", 1))
    third_y = send(first_y, turn("y", 1))
    first_x, second_x, third_y, *late = lax.optimization_barrier(
        (first_x, second_x, third_y, *beside[1])
    )
    third_x = send(first_x, turn("x", 1))
    return (
        [plane, first_x, second_x, third_x],
        [pair, first_y, second_y, third_y],
        (other, first_x, third_x),
        early,
        late,
    )


def gather_rest(me, half, block, marks):
    other = send(after(block, marks[0]), flip("x", 3))
    pair_y = jnp.stack([block[:384], other[:384]])
    wanted = jnp.where(me["core"] == me["xh"], block[448:], other[448:]).reshape(2, 32, COLS)
    pair_z = jnp.concatenate([jnp.stack([block[384:448], other[384:448]]), wanted], axis=1)
    first = after(rows_of(half, pair_z), marks[1])
    here = jnp.stack([first, send(first, turn("y", 0))])
    there = send(after(here, marks[2]), turn("y", 1))
    return here, there, pair_y, send(after(pair_y, here, marks[2]), turn("y", 0))


def gated(value, gate):
    return value if gate is None else after(value, gate)


def total(me, raw, out_rows, units, extra_rows):
    axes = "xyz"
    parts = [raw[:2], raw[2:4], *(raw[k : k + 2] for k in range(4, len(raw), 2))]
    axes += "z" * (len(parts) - 3)
    far = [send(away, turn(axis, 1)) for (_, away), axis in zip(parts, axes)]
    gate = yield
    far = list(far if gate is None else lax.optimization_barrier((*far, gate))[:-1])
    keeps = [keep for keep, _ in parts]
    near = lax.optimization_barrier([added(k[1], f[1]) for k, f in zip(keeps, far)])
    again = [send(n, turn(axis, 0)) for n, axis in zip(near, axes)]
    gate, extra = yield near[2]
    again = lax.optimization_barrier((*again, gate))[:-1]
    along_x, along_y, *along_z = lax.optimization_barrier(
        [added(k[0], f[0], a) for k, f, a in zip(keeps, far, again)]
    )
    along_z = jnp.concatenate(along_z, axis=2) if len(along_z) > 1 else along_z[0]
    size_x, size_y = along_x.shape[1], along_y.shape[1] // 2
    size_z = (along_z.shape[2] - out_rows) // 2

    def with_extra(*parts):
        return rows_of(*parts, extra) if extra_rows else rows_of(*parts)

    def split(rows, *sizes):
        at, parts = 0, []
        for size in sizes:
            parts.append(rows[at : at + size])
            at += size
        return parts

    plane = jnp.concatenate([along_x, along_z.reshape(4, -1, COLS)], axis=1)
    size = plane.shape[1]
    far = send(with_extra(plane[2:]), turn("y", 1))
    gate = yield plane
    kept = gated(plane[:2], gate)
    near = added(kept[1], far[size : 2 * size])
    if extra_rows:
        extra = added(extra, far[2 * size :])
    again = send(with_extra(near), turn("y", 0))
    gate = yield near
    plane = added(gated(kept[0], gate), far[:size], again[:size])
    if extra_rows:
        extra = added(extra, again[size:])
    half, pair = plane[:size_x], plane[size_x:].reshape(2, 2 * size_z + out_rows, COLS)
    out = pair[:, 2 * size_z :].reshape(-1, COLS)
    pieces = jnp.concatenate(
        [along_y.reshape(4, size_y, COLS), pair[:, : 2 * size_z].reshape(4, size_z, COLS)], axis=1
    )
    size = size_y + size_z
    pieces = [
        lax.dynamic_index_in_dim(pieces, ((k // 2) ^ me["xh"]) * 2 + k % 2, 0, keepdims=False)
        for k in orders(me, "x")
    ]
    far = send(with_extra(pieces[2], pieces[3], out), turn("x", 1))
    gate = yield plane
    first, second, far_out, far_extra = split(far, size, size, 2 * out_rows, extra_rows)
    sums = added(gated(rows_of(pieces[1], out), gate), rows_of(second, far_out))
    if extra_rows:
        extra = added(extra, far_extra)
    again = send(with_extra(sums), turn("x", 0))
    gate = yield sums
    near, out, far_extra = split(again, size, 2 * out_rows, extra_rows)
    sums = rows_of(
        added(gated(pieces[0], gate), first, near), added(sums[size:], out)
    )
    if extra_rows:
        extra = added(extra, far_extra)
    flat, block = rows_of(half, sums[:size_y]), sums[size_y:]
    size, size_block = flat.shape[0], block.shape[0]
    far = send(with_extra(flat, block), turn("z", 0))
    gate = yield sums
    sums, other, far_extra = split(far, size, size_block, extra_rows)
    flat = added(gated(flat, gate), sums)
    if extra_rows:
        extra = added(extra, far_extra)
    blocks = rows_of(block, other)
    far = send(with_extra(flat, blocks), turn("z", 1))
    gate = yield flat
    sums, other, far_extra = split(far, size, 2 * size_block, extra_rows)
    flat = added(gated(flat, gate), sums)
    if extra_rows:
        extra = added(extra, far_extra)
    blocks = rows_of(blocks, other).reshape(4, size_block, COLS)
    where = orders(me, "z")
    ordered = jnp.stack(
        [
            sum(jnp.where(where[k] == place, blocks[k], 0) for k in range(4)).astype(LOW)
            for place in range(4)
        ]
    )
    mine = rows_of(flat, ordered[:, :size_z])
    far = send(mine, flip("x", 1))
    gate = yield mine
    mine = gated(mine, gate)

    def whole(groups, first, last):
        a, b = (rows[first:last].reshape(groups, -1, COLS) for rows in (mine, far))
        both = jnp.where(me["xl"] == 0, jnp.stack([a, b], axis=1), jnp.stack([b, a], axis=1))
        return both.reshape(-1, COLS)

    both = rows_of(
        whole(units, 0, size_x), whole(1, size_x, size), whole(4, size, mine.shape[0]),
        ordered[:, size_z:],
    )
    far = send(with_extra(both), flip("core", 1))
    yield both
    rows = both.shape[0]
    if extra_rows:
        extra = added(extra, far[rows:])
        far = far[:rows]
    yield both, far, extra


def rows_at(start, size):
    return pl.ds(pl.multiple_of(start, size), size)


def joint_plan(places, along_x, along_y, mats):
    query, key, value, vectors = mats
    pairs = []
    for ky in range(4):
        y = places[4 + ky]
        for kx in range(4):
            x = places[kx]
            shard, half = (x // 2) * 4 + y, x % 2
            source = along_x[kx].at[ky]
            pairs.append(
                (source.at[pl.ds(0, 64)], query.at[rows_at(shard * 128 + half * 64, 64)])
            )
            pairs.append(
                (source.at[pl.ds(64, 32)], value.at[rows_at(shard * 128 + half * 32, 32)])
            )
        for p in range(2):
            shard = (places[12] ^ p) * 4 + y
            source, at = along_y[ky], p * 208
            pairs.append((source.at[pl.ds(at, 128)], key.at[rows_at(shard * 128, 128)]))
            pairs.append((source.at[pl.ds(at + 128, 64)], value.at[rows_at(shard * 128 + 64, 64)]))
            pairs.append(
                (
                    source.at[pl.ds(at + 192, 16), pl.ds(0, 128)],
                    vectors.at[:, rows_at(shard * 128, 128)],
                )
            )
    return pairs


def joint_sent_plan(places, raw, parts):
    query, key, value = parts
    pairs = []
    for ky in range(4):
        y = places[4 + ky]
        for kx in range(4):
            x = places[kx]
            start = ((x // 2) * 4 + y) * 128 + (x % 2) * 64
            pairs.append((query.at[rows_at(start, 64)], raw[0 + kx // 2].at[kx % 2, ky]))
        for p in range(2):
            shard = (places[12] ^ p) * 4 + y
            pairs.append((key.at[rows_at(shard * 128, 128)], raw[2 + ky // 2].at[ky % 2, p]))
            for kz in range(4):
                start = shard * 128 + places[8 + kz] * 32
                pairs.append((value.at[rows_at(start, 32)], raw[4 + kz // 2].at[kz % 2, ky, p]))
    return pairs


def up_plan(places, at_x, at_y, at_z, mats):
    up, down_one, down_two = mats
    pairs = []
    for ky in range(4):
        y = places[4 + ky]
        for kx in range(4):
            x = places[kx]
            start = ((x // 2) * 4 + y) * 128 + (x % 2) * 64
            for j in range(3):
                source = at_x(kx).at[ky, pl.ds(64 * j, 64)]
                pairs.append((source, up.at[j, rows_at(start, 64)]))
        for p in range(2):
            shard = (places[12] ^ p) * 4 + y
            source = at_y(ky).at[p]
            pairs.append((source.at[pl.ds(0, 128)], up.at[3, rows_at(shard * 128, 128)]))
            pairs.append((source.at[pl.ds(128, 256)], down_one.at[rows_at(shard * 256, 256)]))
            for kz in range(4):
                start = shard * 256 + places[8 + kz] * 64
                source = at_z(kz).at[ky, p, pl.ds(0, 64)]
                pairs.append((source, down_two.at[rows_at(start, 64)]))
    return pairs


def up_kind(index):
    index %= 24
    if index < 12:
        return index % 3
    return 3 if (index - 12) % 6 == 0 else None


def up_shard(places, index):
    ky, index = divmod(index, 24)
    return (places[12] ^ ((index - 12) // 6)) * 4 + places[4 + ky]


def out_plan(places, at_z, first, mat):
    pairs = []
    for ky in range(4):
        for kz in range(4):
            start = places[4 + ky] * 128 + places[8 + kz] * 32
            for p in range(2):
                source = at_z(kz).at[ky, p, pl.ds(first, 32)]
                pairs.append((source, mat.at[p, rows_at(start, 32)]))
    return pairs


def two_of(arrays):
    return lambda k: arrays[k // 2].at[k % 2]


def started(pairs, sems):
    all_of_them = [pltpu.make_async_copy(a, b, sems.at[i]) for i, (a, b) in enumerate(pairs)]
    for copy in all_of_them:
        copy.start()
    return all_of_them


def finished(all_of_them):
    for copy in all_of_them:
        copy.wait()


def turned(pairs):
    return [(b, a) for a, b in pairs]


def low_shape(*shape):
    return jax.ShapeDtypeStruct(shape, LOW)


def full_shape(*shape):
    return jax.ShapeDtypeStruct(shape, FULL)


SCALARS = pl.BlockSpec(memory_space=pltpu.SMEM)
INSIDE = pl.BlockSpec(memory_space=pltpu.VMEM)
OUTSIDE = pl.BlockSpec(memory_space=pl.ANY)


def call(kernel, in_specs, outs, scratch, length, args, grid=()):
    shapes, specs = [o[0] for o in outs], [o[1] for o in outs]
    moved = sum(a.size * a.dtype.itemsize for a in (*args, *shapes))
    return pl.pallas_call(
        kernel,
        grid=grid,
        out_shape=shapes,
        in_specs=in_specs,
        out_specs=specs,
        scratch_shapes=scratch,
        compiler_params=pltpu.CompilerParams(vmem_limit_bytes=VMEM_BYTES),
        cost_estimate=pl.CostEstimate(
            flops=length * FLOPS_PER_US, bytes_accessed=moved, transcendentals=0
        ),
    )(*args)


def gelu_both(upward):
    square = upward * upward
    tangent = jnp.tanh(ROOT_TWO_PI * upward * (1.0 + CUBIC * square))
    half = 0.5 * (1.0 + tangent)
    slope = half + 0.5 * upward * (1.0 - tangent * tangent) * ROOT_TWO_PI * (
        1.0 + 3.0 * CUBIC * square
    )
    return upward * half, slope


def dot(a, b):
    return jnp.dot(a, b, preferred_element_type=FULL)


def dot_nt(a, b):
    return lax.dot_general(a, b, (((1,), (1,)), ((), ())), preferred_element_type=FULL)


def dot_tn(a, b):
    return lax.dot_general(a, b, (((0,), (0,)), ((), ())), preferred_element_type=FULL)


def unit_of(values):
    center = values - jnp.mean(values, axis=-1, keepdims=True)
    inverse = lax.rsqrt(jnp.mean(center * center, axis=-1, keepdims=True) + 1e-05)
    return center * inverse, inverse


def norm_backward(grad_out, unit, inverse, gain):
    scaled = grad_out * gain
    return inverse * (
        scaled
        - jnp.mean(scaled, axis=-1, keepdims=True)
        - unit * jnp.mean(scaled * unit, axis=-1, keepdims=True)
    )


def row_of(vectors, row):
    return vectors[row : row + 1, :].astype(FULL)


def own_columns(full, core, size):
    groups = full.shape[1] // (2 * size)
    first = jnp.concatenate(
        [full[:, (2 * g) * size : (2 * g + 1) * size] for g in range(groups)], axis=1
    )
    second = jnp.concatenate(
        [full[:, (2 * g + 1) * size : (2 * g + 2) * size] for g in range(groups)], axis=1
    )
    return jnp.where(core == 0, first, second)


def barred(lengths, block, first, height, span):
    shape = (height, span)
    rows = lax.broadcasted_iota(jnp.int32, shape, 0) + first
    keys = lax.broadcasted_iota(jnp.int32, shape, 1)
    opening = lengths[block, 0]
    filled = opening + lengths[block, 1]
    begin = jnp.where(rows < opening, 0, jnp.where(rows < filled, opening, rows))
    return jnp.where((keys <= rows) & (keys >= begin), 0.0, -1e30)


TILE = 128


def joint_cast_kernel(places, weight, vector, half, block, held, padded, sems):
    core, xl = places[13], places[14]

    def cols(which):
        return rows_at(which * 2 * COLS + core * COLS, COLS)

    copies = started(
        [
            (weight.at[rows_at(xl * 64, 64), cols(0)], held.at[pl.ds(0, 64)]),
            (weight.at[rows_at(xl * 32, 32), cols(2)], held.at[pl.ds(64, 32)]),
            (weight.at[:, cols(1)], held.at[pl.ds(96, 128)]),
            (weight.at[pl.ds(64, 64), cols(2)], held.at[pl.ds(224, 64)]),
        ],
        sems,
    )
    padded[...] = jnp.zeros_like(padded)
    padded[: vector.shape[0], : vector.shape[1]] = vector[...]
    block[192:208, :] = padded[...].astype(LOW)
    finished(copies)
    half[...] = held[:96].astype(LOW)
    block[:192, :] = held[96:].astype(LOW)


def joint_cast(places, weight, vector):
    return call(
        joint_cast_kernel,
        [SCALARS, OUTSIDE, INSIDE],
        [(low_shape(96, COLS), INSIDE), (low_shape(208, COLS), INSIDE)],
        [pltpu.VMEM((288, COLS), FULL), pltpu.VMEM((16, COLS), FULL)]
        + [pltpu.SemaphoreType.DMA((4,))],
        2,
        (places, weight, vector),
    )


def rest_cast_kernel(places, expand, reduce, output, half, block, held, wide, sems):
    core, xl, z = places[13], places[14], places[15]
    pairs = []
    for s in range(8):
        j, right = s // 2, (s % 2) * 256
        cols = rows_at(s * 512 + core * 256, 256)
        rows, size = (rows_at(xl * 64, 64), 64) if j < 3 else (pl.ds(0, 128), 128)
        pairs.append((expand.at[rows, cols], held.at[pl.ds(64 * j, size), pl.ds(right, 256)]))
    pairs.append((reduce.at[rows_at(core * 256, 256), pl.ds(0, COLS)], held.at[pl.ds(320, 256)]))
    pairs.append(
        (reduce.at[rows_at(core * 256 + z * 64, 64), pl.ds(COLS, COLS)], held.at[pl.ds(576, 64)])
    )
    pairs.append((output.at[rows_at(z * 32, 32)], wide))
    finished(started(pairs, sems))
    half[...] = held[:192].astype(LOW)
    block[:448, :] = held[192:640].astype(LOW)
    block[448:480, :] = wide[:, :COLS].astype(LOW)
    block[480:512, :] = wide[:, COLS:].astype(LOW)


def rest_cast(places, expand, reduce, output):
    return call(
        rest_cast_kernel,
        [SCALARS, OUTSIDE, OUTSIDE, OUTSIDE],
        [(low_shape(192, COLS), INSIDE), (low_shape(512, COLS), INSIDE)],
        [pltpu.VMEM((640, COLS), FULL), pltpu.VMEM((32, 2 * COLS), FULL)]
        + [pltpu.SemaphoreType.DMA((11,))],
        3,
        (places, expand, reduce, output),
    )


def joint_kernel(places, own, other, *refs):
    along_x, along_y, refs = refs[:4], refs[4:8], refs[8:]
    normed, query, key, value, vectors, query_mat, key_mat, value_mat, sems = refs
    mats = (query_mat, key_mat, value_mat, vectors)
    finished(started(joint_plan(places, along_x, along_y, mats), sems))
    gain, shift = row_of(vectors, 0), row_of(vectors, 1)
    core = places[13]
    query_bias = own_columns(row_of(vectors, 2), core, COLS)
    value_bias = own_columns(row_of(vectors, 3), core, COLS)
    count = own.shape[0]
    for block, tokens in enumerate((own, other)):
        rows = pl.ds(block * count, count)
        unit, _ = unit_of(tokens[...].astype(FULL))
        low = (unit * gain + shift).astype(LOW)
        normed[rows, :] = low
        query[rows, :] = ((dot(low, query_mat[...]) + query_bias).astype(LOW) * 0.125).astype(LOW)
        key[rows, :] = dot(low, key_mat[...]).astype(LOW)
        value[rows, :] = (dot(low, value_mat[...]) + value_bias).astype(LOW)


def joint(places, own, other, along_x, along_y):
    count, width = own.shape
    rows = 2 * count
    mat, half = (low_shape(width, COLS), INSIDE), (low_shape(rows, COLS), INSIDE)
    return call(
        joint_kernel,
        [SCALARS, INSIDE, INSIDE] + [OUTSIDE] * 8,
        [(low_shape(rows, width), INSIDE), half, half, half]
        + [(low_shape(16, width), INSIDE), mat, mat, mat],
        [pltpu.SemaphoreType.DMA((56,))],
        8,
        (places, own, other, *along_x, *along_y),
    )


def two_by_two(values, lane):
    return jnp.concatenate([jnp.where(lane, values, 0), jnp.where(lane, 0, values)], axis=0)


def probabilities(stacked, keys, bar):
    scores = dot_nt(stacked, keys) + jnp.concatenate([bar, bar], axis=0)
    probs = jnp.exp(scores - jnp.max(scores, axis=-1, keepdims=True))
    return probs * (1.0 / jnp.sum(probs, axis=-1, keepdims=True))


def attention_kernel(block, lengths, query, key, value, attended, mask):
    count = query.shape[0]
    mask[...] = barred(lengths, block, 0, count, count)
    lane = lax.broadcasted_iota(jnp.int32, (count, TILE), 1) < HEAD_DIM
    for index in range(COLS // TILE):
        cols = pl.ds(index * TILE, TILE)
        probs = probabilities(two_by_two(query[:, cols], lane), key[:, cols], mask[...])
        out = dot(probs.astype(LOW), value[:, cols])
        attended[:, cols] = jnp.where(lane, out[:count], out[count:]).astype(LOW)


def attention(block, lengths, query, key, value):
    count = query.shape[0] // 2
    return call(
        lambda *refs: attention_kernel(block, *refs),
        [SCALARS] + [pl.BlockSpec((count, COLS), lambda i: (block, 0))] * 3,
        [(low_shape(count, COLS), INSIDE)],
        [pltpu.VMEM((count, count), FULL)],
        5,
        (lengths, query, key, value),
        grid=(1,),
    )[0]


def output_kernel(places, own, other, *refs):
    raw, (branch, out_mat, sems) = refs[:4], refs[4:]
    finished(started(out_plan(places, lambda k: raw[k], 64, out_mat), sems))
    count = own.shape[0]
    for block, attended in enumerate((own, other)):
        for half in range(2):
            branch[block * count : (block + 1) * count, half * COLS : (half + 1) * COLS] = dot(
                attended[...], out_mat[half]
            ).astype(LOW)


def output(places, own, other, raw):
    rows, local = 2 * own.shape[0], own.shape[1]
    return call(
        output_kernel,
        [SCALARS, INSIDE, INSIDE] + [OUTSIDE] * 4,
        [(low_shape(rows, 2 * COLS), INSIDE), (low_shape(2, local, COLS), INSIDE)],
        [pltpu.SemaphoreType.DMA((32,))],
        5,
        (places, own, other, *raw),
    )


def forward_backward_kernel(
    places, lengths, own, other, arriving_own, arriving_other, branch, branch_far, vectors, *refs
):
    raw, refs = refs[:12], refs[12:]
    sent, refs = refs[:6], refs[6:]
    (middle, layer_own, layer_other, normed_grad, bias_grad,
     up, down_one, down_two, up_grad, one_grad, two_grad,
     tokens, near, far, held, normed, arriving, layer_sum, normed_sum, active, up_low,
     row_sems, sems, sems_out) = refs
    count = own.shape[0]
    blocks = [pl.ds(0, count), pl.ds(count, count)]
    rows_in = []
    for block, (token, cotangent) in enumerate(((own, arriving_own), (other, arriving_other))):
        here, there = blocks[block], blocks[1 - block]
        pairs = [
            (token, tokens.at[here]),
            (branch.at[here], near.at[here]),
            (branch_far.at[there], far.at[here]),
            (cotangent, arriving.at[here]),
        ]
        rows_in.append(started(pairs, row_sems.at[pl.ds(4 * block, 4)]))
    views = [lambda k, a=axis: raw[4 * a + k] for axis in range(3)]
    plan = up_plan(places, *views, (up, down_one, down_two))
    copies = [pltpu.make_async_copy(a, b, sems.at[i]) for i, (a, b) in enumerate(plan)]
    kinds = [up_kind(index) for index in range(len(copies))]
    for wanted in (0, None, 1, 2, 3):
        for copy, kind in zip(copies, kinds):
            if kind == wanted:
                copy.start()
    gain, shift = row_of(vectors, 5), row_of(vectors, 6)
    rows_out = []
    for block, here in enumerate(blocks):
        finished(rows_in[block])
        summed = near[here, :].astype(FULL) + far[here, :].astype(FULL)
        value = tokens[here, :].astype(FULL) + summed + row_of(vectors, 4)
        held[here, :] = value
        rows_out += started([(held.at[here], middle.at[here])], row_sems.at[pl.ds(8 + block, 1)])
        unit, _ = unit_of(value)
        normed[here, :] = (unit * gain + shift).astype(LOW)
        slots = lax.broadcasted_iota(jnp.int32, value.shape, 0)
        live = slots < lengths[block, 0] + lengths[block, 1]
        arriving[here, :] = jnp.where(live, arriving[here, :], 0)
    core = places[13]
    biases = jnp.concatenate(
        [own_columns(row_of(vectors, 7 + k), core, 256) for k in range(4)], axis=0
    )
    views = [two_of(sent[2 * axis : 2 * axis + 2]) for axis in range(3)]
    plan = turned(up_plan(places, *views, (up_grad, one_grad, two_grad)))
    copies_out = [pltpu.make_async_copy(a, b, sems_out.at[i]) for i, (a, b) in enumerate(plan)]

    def of_chunk(j, action, list_of_copies):
        for index, (copy, kind) in enumerate(zip(list_of_copies, kinds)):
            if kind == j:
                action(copy)
            elif kind is None:

                @pl.when(up_shard(places, index) // 2 == j)
                def _(copy=copy):
                    action(copy)

    for j in range(up.shape[0]):
        hidden = pl.ds(j * COLS, COLS)
        of_chunk(j, lambda copy: copy.wait(), copies)
        upward = dot(normed[...], up[j]) + biases[j : j + 1]
        act, slope = gelu_both(upward)
        active[...] = act.astype(LOW)
        layer_one, layer_two = dot(active[...], down_one[hidden, :]), dot(active[...], down_two[hidden, :])
        grad = dot_nt(arriving[:, :COLS], down_one[hidden, :])
        grad += dot_nt(arriving[:, COLS:], down_two[hidden, :])
        low = (grad * slope).astype(LOW)
        up_low[...] = low
        bias_grad[j : j + 1, :] = jnp.sum(low.astype(FULL), axis=0, keepdims=True)
        normed_part = dot_nt(up_low[...], up[j])
        if j == 0:
            layer_sum[:, :COLS], layer_sum[:, COLS:] = layer_one, layer_two
            normed_sum[...] = normed_part
        else:
            layer_sum[:, :COLS] += layer_one
            layer_sum[:, COLS:] += layer_two
            normed_sum[...] += normed_part
        whole = dot_tn(active[...], arriving[...]).astype(LOW)
        one_grad[hidden, :] = whole[:, :COLS]
        two_grad[hidden, :] = whole[:, COLS:]
        up_grad[j] = dot_tn(normed[...], up_low[...]).astype(LOW)
        of_chunk(j, lambda copy: copy.start(), copies_out)
    layer_own[...] = held[:count, :] + layer_sum[:count, :] + row_of(vectors, 11)
    layer_other[...] = layer_sum[count:, :].astype(LOW)
    normed_grad[...] = normed_sum[...].astype(LOW)
    finished(rows_out)
    finished(copies_out)


def forward_backward(places, lengths, tokens, arriving, branch, branch_far, vectors, raw):
    count, width = tokens[0].shape
    rows, hidden = 2 * count, 4 * COLS
    sent = [low_shape(2, 4, 192, COLS), low_shape(2, 2, 384, COLS), low_shape(2, 4, 2, 64, COLS)]
    inside = [
        full_shape(count, width), low_shape(count, width), low_shape(rows, width),
        full_shape(4, COLS),
    ]
    vmem = pltpu.VMEM
    mats = [vmem((4, width, COLS), LOW), vmem((hidden, COLS), LOW), vmem((hidden, COLS), LOW)]
    low, full = vmem((rows, width), LOW), vmem((rows, width), FULL)
    return call(
        forward_backward_kernel,
        [SCALARS, SCALARS] + [OUTSIDE] * 6 + [INSIDE] + [OUTSIDE] * 12,
        [(s, OUTSIDE) for s in sent for _ in range(2)]
        + [(full_shape(rows, width), OUTSIDE)]
        + [(s, INSIDE) for s in inside],
        mats + mats + [low, low, low, full, low, low, full, full]
        + [vmem((rows, COLS), LOW), vmem((rows, COLS), LOW)]
        + [pltpu.SemaphoreType.DMA((n,)) for n in (10, 96, 96)],
        33,
        (places, lengths, *tokens, *arriving, branch, branch_far, vectors, *raw),
    )


def output_backward_kernel(
    places, lengths, arriving_own, arriving_other, middle, part, part_far, vectors, own, other,
    out_mat, sent_one, sent_two, middle_grad, attended_grad, sums,
    held, near, far, arriving, branch, out_grad, row_sems, sems,
):
    count = arriving_own.shape[0]
    blocks = [pl.ds(0, count), pl.ds(count, count)]
    rows_in = []
    for block, cotangent in enumerate((arriving_own, arriving_other)):
        here, there = blocks[block], blocks[1 - block]
        pairs = [
            (middle.at[here], held.at[here]),
            (part.at[here], near.at[here]),
            (part_far.at[there], far.at[here]),
            (cotangent, arriving.at[here]),
        ]
        rows_in.append(started(pairs, row_sems.at[pl.ds(4 * block, 4)]))
    gain = row_of(vectors, 5)
    for block, rows in enumerate(blocks):
        finished(rows_in[block])
        unit, inverse = unit_of(held[rows, :])
        grad = near[rows, :].astype(FULL) + far[rows, :].astype(FULL)
        slots = lax.broadcasted_iota(jnp.int32, grad.shape, 0)
        live = slots < lengths[block, 0] + lengths[block, 1]
        coming = jnp.where(live, arriving[rows, :].astype(FULL), 0.0)
        result = coming + norm_backward(grad, unit, inverse, gain)
        low = result.astype(LOW)
        branch[rows, :] = low
        if block == 0:
            middle_grad[...] = result
            sums[...] = jnp.zeros_like(sums)
            sums[0:1, :] = jnp.sum(low.astype(FULL), axis=0, keepdims=True)
            sums[1:2, :] = jnp.sum(grad * unit, axis=0, keepdims=True)
            sums[2:3, :] = jnp.sum(grad, axis=0, keepdims=True)
            sums[3:4, :] = jnp.sum(coming, axis=0, keepdims=True)
    whole = dot_tn(own[...], branch[:count, :]) + dot_tn(other[...], branch[count:, :])
    out_grad[0] = whole[:, :COLS].astype(LOW)
    out_grad[1] = whole[:, COLS:].astype(LOW)
    copies = started(turned(out_plan(places, two_of((sent_one, sent_two)), 0, out_grad)), sems)
    attended_grad[...] = (
        dot_nt(branch[:, :COLS], out_mat[0]) + dot_nt(branch[:, COLS:], out_mat[1])
    ).astype(LOW)
    finished(copies)


def output_backward(
    places, lengths, arriving, middle, part, part_far, vectors, attended, out_mat
):
    rows, width = middle.shape
    sent = (low_shape(2, 4, 2, 32, COLS), OUTSIDE)
    inside = [full_shape(rows // 2, width), low_shape(rows, COLS), full_shape(8, width)]
    low = pltpu.VMEM((rows, width), LOW)
    return call(
        output_backward_kernel,
        [SCALARS, SCALARS] + [OUTSIDE] * 5 + [INSIDE] * 4,
        [sent, sent] + [(s, INSIDE) for s in inside],
        [pltpu.VMEM((rows, width), FULL), low, low, low, low, pltpu.VMEM((2, COLS, COLS), LOW)]
        + [pltpu.SemaphoreType.DMA((8,)), pltpu.SemaphoreType.DMA((32,))],
        10,
        (places, lengths, *arriving, middle, part, part_far, vectors, *attended, out_mat),
    )


def attention_backward_kernel(
    block, lengths, query, key, value, grad_in, query_grad, key_grad, value_grad, sums, mask
):
    count = query.shape[0]
    mask[...] = barred(lengths, block, 0, count, count)
    lane = lax.broadcasted_iota(jnp.int32, (count, TILE), 1) < HEAD_DIM
    for index in range(COLS // TILE):
        cols = pl.ds(index * TILE, TILE)
        stacked, given = two_by_two(query[:, cols], lane), two_by_two(grad_in[:, cols], lane)
        probs = probabilities(stacked, key[:, cols], mask[...])
        weighted = probs * dot_nt(given, value[:, cols])
        grad = (weighted - probs * jnp.sum(weighted, axis=-1, keepdims=True)).astype(LOW)
        out = dot(grad, key[:, cols])
        query_grad[:, cols] = (jnp.where(lane, out[:count], out[count:]) * 0.125).astype(LOW)
        key_grad[:, cols] = dot_tn(grad, stacked).astype(LOW)
        value_grad[:, cols] = dot_tn(probs.astype(LOW), given).astype(LOW)
    sums[...] = jnp.zeros_like(sums)
    sums[0:1, :] = jnp.sum(query_grad[...].astype(FULL), axis=0, keepdims=True)
    sums[1:2, :] = jnp.sum(value_grad[...].astype(FULL), axis=0, keepdims=True)


def attention_backward(block, lengths, query, key, value, grad_in):
    count = query.shape[0] // 2
    vmem = pltpu.VMEM
    half = (low_shape(count, COLS), INSIDE)
    part = pl.BlockSpec((count, COLS), lambda i: (block, 0))
    return call(
        lambda *refs: attention_backward_kernel(block, *refs),
        [SCALARS] + [part] * 4,
        [half, half, half, (full_shape(8, COLS), INSIDE)],
        [vmem((count, count), FULL)],
        8,
        (lengths, query, key, value, grad_in),
        grid=(1,),
    )


def joint_grad_kernel(places, normed, *refs):
    grads, sent, (query_part, key_part, value_part, sems) = refs[:6], refs[6:12], refs[12:]
    parts = (query_part, key_part, value_part)
    count = grads[0].shape[0]
    sides = [jnp.concatenate([g[...] for g in grads[i : i + 3]], axis=1) for i in (0, 3)]
    whole = dot_tn(normed[:count, :], sides[0]) + dot_tn(normed[count:, :], sides[1])
    for index, part in enumerate(parts):
        part[...] = whole[:, index * COLS : (index + 1) * COLS].astype(LOW)
    finished(started(joint_sent_plan(places, sent, parts), sems))


def joint_grad_parts(places, normed, own, other):
    rows, width = normed.shape
    sent = [low_shape(2, 4, 64, COLS), low_shape(2, 2, 128, COLS), low_shape(2, 4, 2, 32, COLS)]
    return call(
        joint_grad_kernel,
        [SCALARS] + [INSIDE] * 7,
        [(s, OUTSIDE) for s in sent for _ in range(2)],
        [pltpu.VMEM((width, COLS), LOW)] * 3 + [pltpu.SemaphoreType.DMA((56,))],
        8,
        (places, normed, *own, *other),
    )


def joint_backward_kernel(*refs):
    own, other, mats, outs = refs[:3], refs[3:6], refs[6:9], refs[9:]
    for grads, out in zip((own, other), outs):
        whole = dot_nt(grads[0][...], mats[0][...])
        whole += dot_nt(grads[1][...], mats[1][...])
        whole += dot_nt(grads[2][...], mats[2][...])
        out[...] = whole.astype(out.dtype)


def joint_backward(own, other, mats):
    count, width = own[0].shape[0], mats[0].shape[0]
    return call(
        joint_backward_kernel,
        [INSIDE] * 9,
        [(full_shape(count, width), INSIDE), (low_shape(count, width), INSIDE)],
        [],
        6,
        (*own, *other, *mats),
    )


def input_kernel(tokens, part, part_far, middle_grad, vectors, input_grad, sums):
    unit, inverse = unit_of(tokens[...].astype(FULL))
    grad = part[...] + part_far[...].astype(FULL)
    input_grad[...] = middle_grad[...] + norm_backward(grad, unit, inverse, row_of(vectors, 0))
    sums[...] = jnp.zeros_like(sums)
    sums[0:1, :] = jnp.sum(grad * unit, axis=0, keepdims=True)
    sums[1:2, :] = jnp.sum(grad, axis=0, keepdims=True)


def input_backward(tokens, part, part_far, middle_grad, vectors):
    return call(
        input_kernel,
        [INSIDE] * 5,
        [(full_shape(*part.shape), INSIDE), (full_shape(8, part.shape[1]), INSIDE)],
        [],
        5,
        (tokens, part, part_far, middle_grad, vectors),
    )


def adam_step(weight, first, second, grad, rate, decay):
    first_new = BETA_ONE * first + (1.0 - BETA_ONE) * grad
    second_new = BETA_TWO * second + (1.0 - BETA_TWO) * grad * grad
    mean_hat = first_new / (1.0 - BETA_ONE**STEP)
    square_hat = second_new / (1.0 - BETA_TWO**STEP)
    fresh = weight - rate * (mean_hat / (jnp.sqrt(square_hat) + ADAM_EPS) + decay * weight)
    return (first_new, second_new, fresh)


def adam_kernel(grad_of, rate, places, weight, first, second, *refs):
    grads, outs = refs[:-4], refs[-4:]
    grad = grad_of(places, *(g[...].astype(FULL) for g in grads))
    outs[0][...] = grad
    outs[1][...], outs[2][...], outs[3][...] = adam_step(
        weight[...], first[...], second[...], grad, rate, MATRIX_DECAY
    )


def adam(grad_of, rate, grid, state, state_block, state_map, grads, places):
    spec = pl.BlockSpec(state_block, state_map)
    shape = full_shape(*state[0].shape)
    return pl.pallas_call(
        lambda *refs: adam_kernel(grad_of, rate, *refs),
        grid=grid,
        in_specs=[SCALARS] + [spec] * 3 + [pl.BlockSpec(g[1], g[2]) for g in grads],
        out_specs=[spec] * 4,
        out_shape=[shape] * 4,
        compiler_params=pltpu.CompilerParams(vmem_limit_bytes=VMEM_BYTES),
        cost_estimate=pl.CostEstimate(
            flops=7 * FLOPS_PER_US, bytes_accessed=30 * state[0].size, transcendentals=0
        ),
    )(places, *state, *(g[0] for g in grads))


def by_core(places, both, far):
    own = places[13] == 0
    return jnp.where(own, both, far), jnp.where(own, far, both)


def adam_joint(places, state, sums):
    def grad_of(places, both, far):
        half = pl.program_id(0) % 2
        return jnp.where(half == places[13], both, far)

    block = (128, COLS)
    grads = [(a, block, lambda g: (g // 2, 0)) for a in sums]
    return adam(grad_of, MATRIX_RATE, (6,), state, block, lambda g: (0, g), grads, places)


def adam_expand(places, state, sums):
    def grad_of(places, both, far):
        zero, one = by_core(places, both, far)
        return jnp.concatenate(
            [zero[:, :256], one[:, :256], zero[:, 256:], one[:, 256:]], axis=1
        )

    grads = [(a, (128, COLS), lambda j: (j, 0)) for a in sums]
    return adam(
        grad_of, MATRIX_RATE, (4,), state, (128, 2 * COLS), lambda j: (0, j), grads, places
    )


def adam_reduce(places, state, sums):
    def grad_of(places, left, right, far_left, far_right):
        own = pl.program_id(0) // 4 == places[13]
        return jnp.concatenate(
            [jnp.where(own, left, far_left), jnp.where(own, right, far_right)], axis=1
        )

    block = (64, COLS)
    grads = []
    for a in sums:
        grads.append((a, block, lambda g: (8 + g % 4, 0)))
        grads.append((a, block, lambda g: (12 + g % 4, 0)))
    return adam(
        grad_of, MATRIX_RATE, (8,), state, (64, 2 * COLS), lambda g: (g, 0), grads, places
    )


def adam_output(places, state, sums):
    def grad_of(places, both, far):
        grad = jnp.where(places[13] == places[12], both, far)
        return jnp.concatenate([grad[:32], grad[32:]], axis=1)

    grads = [(a, (64, COLS), lambda q: (16 + q, 0)) for a in sums]
    return adam(
        grad_of, OUTPUT_RATE, (4,), state, (32, 2 * COLS), lambda q: (q, 0), grads, places
    )


def per_device(
    tokens,
    cotangent,
    lengths,
    joint_weight,
    joint_first,
    joint_second,
    output_weight,
    output_first,
    output_second,
    expand_weight,
    expand_first,
    expand_second,
    reduce_weight,
    reduce_first,
    reduce_second,
    vector_weight,
    vector_first,
    vector_second,
):
    me = coordinates()
    core = me["core"]
    places = places_of(me)
    across = flip("core", 1)
    width = tokens.shape[1]
    units = 256

    half, block = joint_cast(places, joint_weight, vector_weight)
    joint_x, joint_y, marks, rest_block, far = gather_joint(
        half,
        block,
        rest_cast(places, expand_weight, reduce_weight, output_weight),
        [send(a, across) for a in (tokens, cotangent, lengths)],
    )
    here, there, pair_y, first_y = gather_rest(me, *rest_block, marks)
    tokens, cotangent = (tokens, far[0]), (cotangent, far[1])
    lengths = jnp.concatenate([lengths, far[2]])

    normed_one, query, key, value, vectors, *joint_mats = joint(
        places, *tokens, joint_x, joint_y
    )
    there = after(there, query)
    plane_x = jnp.concatenate([here[:, :192], there[:, :192]])
    plane_z = jnp.concatenate([here[:, 192:], there[:, 192:]]).reshape(4, 2, 96, COLS)
    along_y = [
        pair_y,
        first_y,
        send(after(pair_y, there), turn("y", 1)),
        send(after(first_y, there), turn("y", 1)),
    ]
    own = attention(0, lengths, after(query, first_y), key, value)
    along_z = main_phase(plane_z, "z", own)
    along_x = main_phase(plane_x, "x", own)
    other = attention(1, lengths, after(query, along_y[2], *along_z[1:3], *along_x[1:3]), key, value)
    attended = (own, other)
    branch, out_mat = output(places, own, after(other, along_x[3], along_y[3]), along_z)
    branch_far = send(branch, across)
    *sent, middle, layer_own, layer_other, normed_two_part, up_bias_grad = forward_backward(
        places, lengths, tokens, cotangent, branch, branch_far, vectors,
        [*along_x, *along_y, *along_z],
    )
    part_far = send(normed_two_part, across)
    layer_out = (layer_own + send(layer_other, across).astype(FULL)).astype(LOW)

    out_one, out_two, middle_grad, attended_grad, two_sums = output_backward(
        places, lengths, cotangent, middle, normed_two_part, part_far, vectors, attended, out_mat
    )
    rest = total(me, [*sent, out_one, out_two], 32, 3, 0)
    next(rest)
    *own_grads, own_sums = attention_backward(0, lengths, query, key, value, attended_grad)
    mark = rest.send(own_grads[0])
    *other_grads, other_sums = attention_backward(
        1, lengths, query, key, value, after(attended_grad, mark)
    )
    mark = rest.send((other_grads[0], None))
    sent = joint_grad_parts(places, after(normed_one, mark), own_grads, other_grads)
    joint_rows = total(me, sent, 0, 1, 32)
    next(joint_rows)
    mark = rest.send(sent[0])
    part_own, part_other = joint_backward(
        (after(own_grads[0], mark), *own_grads[1:]), other_grads, joint_mats
    )
    part_far = send(part_other, across)
    mark = rest.send(part_own)
    mark = joint_rows.send(mark)
    input_grad, one_sums = input_backward(
        tokens[0], after(part_own, mark), part_far, middle_grad, vectors
    )

    is_core = (jnp.arange(2) == core).astype(FULL)

    def own_half(values):
        return (is_core[:, None] * values[None]).reshape(1, -1)

    head_sums = own_sums + other_sums
    up_mine = is_core[None, :, None] * up_bias_grad.reshape(8, 1, units)
    vector_local = jnp.concatenate(
        [
            one_sums[:2],
            own_half(head_sums[0]),
            own_half(head_sums[1]),
            two_sums[:3],
            up_mine.reshape(4, width),
            two_sums[3:4],
            jnp.zeros((4, width), FULL),
        ],
        axis=0,
    ).astype(LOW)
    vector_local = rows_of(vector_local[:, :COLS], vector_local[:, COLS:])

    mark = rest.send(one_sums)
    mark = joint_rows.send((mark, vector_local))
    for _ in range(3):
        mark = rest.send(mark)
        mark = joint_rows.send(mark)
    mark = joint_rows.send(mark)
    mark = rest.send(mark)
    mark = joint_rows.send(mark)
    one, two, _ = next(rest)
    expand = adam_expand(places, (expand_weight, expand_first, expand_second), (one, two))
    mark = joint_rows.send(expand[0])
    output_state = adam_output(
        places, (output_weight, output_first, output_second), (after(one, mark), two)
    )
    mark = joint_rows.send(output_state[0])
    reduce = adam_reduce(
        places, (reduce_weight, reduce_first, reduce_second), (after(one, mark), two)
    )
    one, two, extra = next(joint_rows)
    joint_state = adam_joint(
        places, (joint_weight, joint_first, joint_second), (after(one, reduce[0]), two)
    )
    vector_grad = lax.dynamic_slice(
        jnp.concatenate([extra[:12], extra[16:28]], axis=1).astype(FULL),
        (0, 128 * lax.axis_index("shard")),
        (12, 128),
    )
    vector_state = (vector_grad,) + adam_step(
        vector_weight, vector_first, vector_second, vector_grad, VECTOR_RATE, 0.0
    )
    states = zip(joint_state, output_state, expand, reduce, vector_state)
    return (layer_out, input_grad, *(a for kind in states for a in kind))


def solution(mesh):
    rows, columns, split = P("shard", None), P(None, "shard"), P(("wide", "shard"), None)
    state = (rows, rows, rows, rows, columns)
    return jax.shard_map(
        per_device,
        mesh=mesh,
        in_specs=(split, split, split) + (rows,) * 12 + (columns,) * 3,
        out_specs=(split, split) + state * 4,
        check_vma=False,
    )
```

```python
import jax
import jax.numpy as jnp
from jax import lax
from jax.experimental import pallas as pl
from jax.experimental.pallas import tpu as pltpu
from jax.sharding import PartitionSpec as P

HEAD_DIM = 64
STEP = 10


ROOT_TWO_PI = 0.7978845608028654
CUBIC = 0.044715
BETA_ONE = 0.9
BETA_TWO = 0.999
ADAM_EPS = 1e-08
MATRIX_RATE = 0.03
OUTPUT_RATE = 0.1
VECTOR_RATE = 0.2
MATRIX_DECAY = 0.1

LOW = jnp.bfloat16
FULL = jnp.float32
AXES = ("wide", "shard")
SIZES = (4, 2, 2, 2, 4)
COLS = 512
FLOPS_PER_US = 1_150_000_000


def coordinates():
    wide, shard = lax.axis_index("wide"), lax.axis_index("shard")
    z, xl, core = wide // 4, (wide // 2) % 2, wide % 2
    xh, y = shard // 4, shard % 4
    return {"z": z, "x": 2 * xh + xl, "y": y, "xl": xl, "xh": xh, "core": core}


def route(partner):
    pairs = []
    for source in range(128):
        rest, places = source, []
        for size in reversed(SIZES):
            places.append(rest % size)
            rest //= size
        y, xh, core, xl, z = places
        target = partner({"z": z, "x": 2 * xh + xl, "y": y, "core": core})
        flat = 0
        for place, size in zip(
            (target["z"], target["x"] % 2, target["core"], target["x"] // 2, target["y"]), SIZES
        ):
            flat = flat * size + place
        pairs.append((source, flat))
    return pairs


def flip(axis, bits):
    return route(lambda at: {**at, axis: at[axis] ^ bits})


def turn(axis, step):
    return route(lambda at: {**at, axis: at[axis] ^ (1 if (at["core"] + step) % 2 == 0 else 3)})


def send(value, pairs):
    return lax.ppermute(value, AXES, pairs)


def added(*terms):
    return sum(term.astype(FULL) for term in terms).astype(LOW)


def orders(me, axis):
    here = me[axis]
    one = jnp.where(me["core"] == 0, 1, 3)
    return [here, here ^ one, here ^ (4 - one), here ^ 2]


def places_of(me):
    return jnp.stack(
        orders(me, "x")
        + orders(me, "y")
        + orders(me, "z")
        + [me["xh"], me["core"], me["xl"], me["z"]]
    ).astype(jnp.int32)


def after(value, *others):
    return lax.optimization_barrier((value, *others))[0]


def rows_of(*parts):
    return jnp.concatenate([p.reshape(-1, COLS) for p in parts])


def main_phase(block, axis, gate, late=False):
    first, second = send(block, turn(axis, 0)), send(gated(block, gate if late else None), turn(axis, 1))
    return [block, first, second, send(after(first, gate), turn(axis, 1))]


def gather_joint(half, block, *beside):
    size, size_y = half.shape[0], 2 * block.shape[0]
    other, second, *early = lax.optimization_barrier(
        (send(block, flip("x", 3)), send(half, turn("y", 0)), *beside[0])
    )
    pair, both = rows_of(block, other), rows_of(block, other, half, second)
    first_y, second_y = lax.optimization_barrier((send(pair, turn("y", 0)), send(both, turn("y", 1))))
    plane = rows_of(half, second, second_y[size_y:]).reshape(4, size, COLS)
    first_x, second_x = send(plane, turn("x", 0)), send(plane, turn("x", 1))
    third_y = send(first_y, turn("y", 1))
    first_x, second_x, third_y, *late = lax.optimization_barrier(
        (first_x, second_x, third_y, *beside[1])
    )
    third_x = send(first_x, turn("x", 1))
    return (
        [plane, first_x, second_x, third_x],
        [pair, first_y, second_y, third_y],
        (other, first_x, third_x),
        early,
        late,
    )


def gather_rest(me, half, block, marks):
    other = send(after(block, marks[0]), flip("x", 3))
    pair_y = jnp.stack([block[:384], other[:384]])
    wanted = jnp.where(me["core"] == me["xh"], block[448:], other[448:]).reshape(2, 32, COLS)
    pair_z = jnp.concatenate([jnp.stack([block[384:448], other[384:448]]), wanted], axis=1)
    first = after(rows_of(half, pair_z), marks[1])
    here = jnp.stack([first, send(first, turn("y", 0))])
    return here, send(after(here, marks[2]), turn("y", 1)), pair_y


def added_all(sums, steps=2):
    terms, specs, outs, out_specs = [], [], [], []
    for group in sums:
        rows = min(a.size for a, _ in group) // COLS
        rows = rows // 2 if len(group) == 2 else rows
        for array, which in group:
            terms.append(array.reshape(-1, COLS))
            specs.append(
                pl.BlockSpec((rows // steps, COLS), lambda i, at=which * steps: (at + i, 0))
            )
        outs.append(low_shape(rows, COLS))
        out_specs.append(pl.BlockSpec((rows // steps, COLS), lambda i: (i, 0)))

    def kernel(*refs):
        at = 0
        for group, out in zip(sums, refs[len(terms) :]):
            out[...] = added(*(ref[...] for ref in refs[at : at + len(group)]))
            at += len(group)

    return pl.pallas_call(
        kernel,
        grid=(steps,),
        in_specs=specs,
        out_specs=out_specs,
        out_shape=outs,
        compiler_params=pltpu.CompilerParams(vmem_limit_bytes=12 << 20),
        cost_estimate=pl.CostEstimate(
            flops=3 * FLOPS_PER_US, bytes_accessed=6 * sum(o.size for o in outs), transcendentals=0
        ),
    )(*terms)


def gated(value, gate):
    return value if gate is None else after(value, gate)


def total(me, raw, out_rows, units, extra_rows):
    axes = "xyz"
    parts = [raw[:2], raw[2:4], *(raw[k : k + 2] for k in range(4, len(raw), 2))]
    axes += "z" * (len(parts) - 3)
    far = [send(away, turn(axis, 1)) for (_, away), axis in zip(parts, axes)]
    gate = yield
    far = list(far if gate is None else lax.optimization_barrier((*far, gate))[:-1])
    keeps = [keep for keep, _ in parts]
    near = added_all([[(k, 1), (f, 1)] for k, f in zip(keeps, far)])
    near = lax.optimization_barrier([n.reshape(k.shape[1:]) for n, k in zip(near, keeps)])
    again = [send(n, turn(axis, 0)) for n, axis in zip(near, axes)]
    gate, extra = yield near[2]
    again = lax.optimization_barrier((*again, gate))[:-1]
    along = added_all([[(k, 0), (f, 0), (a, 0)] for k, f, a in zip(keeps, far, again)])
    along_x, along_y, *along_z = lax.optimization_barrier(
        [a.reshape(k.shape[1:]) for a, k in zip(along, keeps)]
    )
    along_z = jnp.concatenate(along_z, axis=2) if len(along_z) > 1 else along_z[0]
    size_x, size_y = along_x.shape[1], along_y.shape[1] // 2
    size_z = (along_z.shape[2] - out_rows) // 2

    def with_extra(*parts):
        return rows_of(*parts, extra) if extra_rows else rows_of(*parts)

    def split(rows, *sizes):
        at, parts = 0, []
        for size in sizes:
            parts.append(rows[at : at + size])
            at += size
        return parts

    plane = jnp.concatenate([along_x, along_z.reshape(4, -1, COLS)], axis=1)
    size = plane.shape[1]
    far = send(with_extra(plane[2:]), turn("y", 1))
    gate = yield plane
    far, kept = gated(far, gate), plane[:2]
    near = added(kept[1], far[size : 2 * size])
    if extra_rows:
        extra = added(extra, far[2 * size :])
    again = send(with_extra(near), turn("y", 0))
    gate = yield near
    again = gated(again, gate)
    plane = added(kept[0], far[:size], again[:size])
    if extra_rows:
        extra = added(extra, again[size:])
    half, pair = plane[:size_x], plane[size_x:].reshape(2, 2 * size_z + out_rows, COLS)
    out = pair[:, 2 * size_z :].reshape(-1, COLS)
    pieces = jnp.concatenate(
        [along_y.reshape(4, size_y, COLS), pair[:, : 2 * size_z].reshape(4, size_z, COLS)], axis=1
    )
    size = size_y + size_z
    pieces = [
        lax.dynamic_index_in_dim(pieces, ((k // 2) ^ me["xh"]) * 2 + k % 2, 0, keepdims=False)
        for k in orders(me, "x")
    ]
    far = send(with_extra(pieces[2], pieces[3], out), turn("x", 1))
    gate = yield plane
    far = gated(far, gate)
    first, second, far_out, far_extra = split(far, size, size, 2 * out_rows, extra_rows)
    sums = added(rows_of(pieces[1], out), rows_of(second, far_out))
    if extra_rows:
        extra = added(extra, far_extra)
    again = send(with_extra(sums), turn("x", 0))
    gate = yield sums
    near, out, far_extra = split(gated(again, gate), size, 2 * out_rows, extra_rows)
    sums = rows_of(added(pieces[0], first, near), added(sums[size:], out))
    if extra_rows:
        extra = added(extra, far_extra)
    flat, block = rows_of(half, sums[:size_y]), sums[size_y:]
    size, size_block = flat.shape[0], block.shape[0]
    far = send(with_extra(flat, block), turn("z", 0))
    gate = yield sums
    sums, other, far_extra = split(gated(far, gate), size, size_block, extra_rows)
    flat = added(flat, sums)
    if extra_rows:
        extra = added(extra, far_extra)
    blocks = rows_of(block, other)
    far = send(with_extra(flat, blocks), turn("z", 1))
    gate = yield flat
    sums, other, far_extra = split(gated(far, gate), size, 2 * size_block, extra_rows)
    flat = added(flat, sums)
    if extra_rows:
        extra = added(extra, far_extra)
    blocks = rows_of(blocks, other).reshape(4, size_block, COLS)
    where = orders(me, "z")
    ordered = jnp.stack(
        [
            sum(jnp.where(where[k] == place, blocks[k], 0) for k in range(4)).astype(LOW)
            for place in range(4)
        ]
    )
    mine = rows_of(flat, ordered[:, :size_z])
    far = send(mine, flip("x", 1))
    gate = yield mine
    far = gated(far, gate)

    def whole(groups, first, last):
        a, b = (rows[first:last].reshape(groups, -1, COLS) for rows in (mine, far))
        both = jnp.where(me["xl"] == 0, jnp.stack([a, b], axis=1), jnp.stack([b, a], axis=1))
        return both.reshape(-1, COLS)

    both = rows_of(
        whole(units, 0, size_x), whole(1, size_x, size), whole(4, size, mine.shape[0]),
        ordered[:, size_z:],
    )
    far = send(with_extra(both), flip("core", 1))
    yield both
    rows = both.shape[0]
    if extra_rows:
        extra = added(extra, far[rows:])
        far = far[:rows]
    yield both, far, extra


def rows_at(start, size):
    return pl.ds(pl.multiple_of(start, size), size)


def joint_plan(places, along_x, along_y, mats):
    query, key, value, vectors = mats
    pairs = []
    for ky in range(4):
        y = places[4 + ky]
        for kx in range(4):
            x = places[kx]
            shard, half = (x // 2) * 4 + y, x % 2
            source = along_x[kx].at[ky]
            pairs.append(
                (source.at[pl.ds(0, 64)], query.at[rows_at(shard * 128 + half * 64, 64)])
            )
            pairs.append(
                (source.at[pl.ds(64, 32)], value.at[rows_at(shard * 128 + half * 32, 32)])
            )
        for p in range(2):
            shard = (places[12] ^ p) * 4 + y
            source, at = along_y[ky], p * 208
            pairs.append((source.at[pl.ds(at, 128)], key.at[rows_at(shard * 128, 128)]))
            pairs.append((source.at[pl.ds(at + 128, 64)], value.at[rows_at(shard * 128 + 64, 64)]))
            pairs.append(
                (
                    source.at[pl.ds(at + 192, 16), pl.ds(0, 128)],
                    vectors.at[:, rows_at(shard * 128, 128)],
                )
            )
    return pairs


def joint_sent_plan(places, raw, parts):
    query, key, value = parts
    pairs = []
    for ky in range(4):
        y = places[4 + ky]
        for kx in range(4):
            x = places[kx]
            start = ((x // 2) * 4 + y) * 128 + (x % 2) * 64
            pairs.append((query.at[rows_at(start, 64)], raw[0 + kx // 2].at[kx % 2, ky]))
        for p in range(2):
            shard = (places[12] ^ p) * 4 + y
            pairs.append((key.at[rows_at(shard * 128, 128)], raw[2 + ky // 2].at[ky % 2, p]))
            for kz in range(4):
                start = shard * 128 + places[8 + kz] * 32
                pairs.append((value.at[rows_at(start, 32)], raw[4 + kz // 2].at[kz % 2, ky, p]))
    return pairs


def up_plan(places, at_x, at_y, at_z, mats):
    up, down_one, down_two = mats
    pairs = []
    for ky in range(4):
        y = places[4 + ky]
        for kx in range(4):
            x = places[kx]
            start = ((x // 2) * 4 + y) * 128 + (x % 2) * 64
            for j in range(3):
                source = at_x(kx).at[ky, pl.ds(64 * j, 64)]
                pairs.append((source, up.at[j, rows_at(start, 64)]))
        for p in range(2):
            shard = (places[12] ^ p) * 4 + y
            source = at_y(ky).at[p]
            pairs.append((source.at[pl.ds(0, 128)], up.at[3, rows_at(shard * 128, 128)]))
            pairs.append((source.at[pl.ds(128, 256)], down_one.at[rows_at(shard * 256, 256)]))
            for kz in range(4):
                start = shard * 256 + places[8 + kz] * 64
                source = at_z(kz).at[ky, p, pl.ds(0, 64)]
                pairs.append((source, down_two.at[rows_at(start, 64)]))
    return pairs


def up_kind(index):
    index %= 24
    if index < 12:
        return index % 3
    return 3 if (index - 12) % 6 == 0 else None


def up_shard(places, index):
    ky, index = divmod(index, 24)
    return (places[12] ^ ((index - 12) // 6)) * 4 + places[4 + ky]


def out_plan(places, at_z, first, mat):
    pairs = []
    for ky in range(4):
        for kz in range(4):
            start = places[4 + ky] * 128 + places[8 + kz] * 32
            for p in range(2):
                source = at_z(kz).at[ky, p, pl.ds(first, 32)]
                pairs.append((source, mat.at[p, rows_at(start, 32)]))
    return pairs


def two_of(arrays):
    return lambda k: arrays[k // 2].at[k % 2]


def started(pairs, sems):
    all_of_them = [pltpu.make_async_copy(a, b, sems.at[i]) for i, (a, b) in enumerate(pairs)]
    for copy in all_of_them:
        copy.start()
    return all_of_them


def finished(all_of_them):
    for copy in all_of_them:
        copy.wait()


def turned(pairs):
    return [(b, a) for a, b in pairs]


def low_shape(*shape):
    return jax.ShapeDtypeStruct(shape, LOW)


def full_shape(*shape):
    return jax.ShapeDtypeStruct(shape, FULL)


SCALARS = pl.BlockSpec(memory_space=pltpu.SMEM)
INSIDE = pl.BlockSpec(memory_space=pltpu.VMEM)
OUTSIDE = pl.BlockSpec(memory_space=pl.ANY)


def call(kernel, in_specs, outs, scratch, length, args, grid=(), vmem=60):
    shapes, specs = [o[0] for o in outs], [o[1] for o in outs]
    moved = sum(a.size * a.dtype.itemsize for a in (*args, *shapes))
    return pl.pallas_call(
        kernel,
        grid=grid,
        out_shape=shapes,
        in_specs=in_specs,
        out_specs=specs,
        scratch_shapes=scratch,
        compiler_params=pltpu.CompilerParams(vmem_limit_bytes=vmem << 20),
        cost_estimate=pl.CostEstimate(
            flops=length * FLOPS_PER_US, bytes_accessed=moved, transcendentals=0
        ),
    )(*args)


def gelu_both(upward):
    square = upward * upward
    tangent = jnp.tanh(ROOT_TWO_PI * upward * (1.0 + CUBIC * square))
    half = 0.5 * (1.0 + tangent)
    slope = half + 0.5 * upward * (1.0 - tangent * tangent) * ROOT_TWO_PI * (
        1.0 + 3.0 * CUBIC * square
    )
    return upward * half, slope


def dot(a, b):
    return jnp.dot(a, b, preferred_element_type=FULL)


def dot_nt(a, b):
    return lax.dot_general(a, b, (((1,), (1,)), ((), ())), preferred_element_type=FULL)


def dot_tn(a, b):
    return lax.dot_general(a, b, (((0,), (0,)), ((), ())), preferred_element_type=FULL)


def unit_of(values):
    center = values - jnp.mean(values, axis=-1, keepdims=True)
    inverse = lax.rsqrt(jnp.mean(center * center, axis=-1, keepdims=True) + 1e-05)
    return center * inverse, inverse


def norm_backward(grad_out, unit, inverse, gain):
    scaled = grad_out * gain
    return inverse * (
        scaled
        - jnp.mean(scaled, axis=-1, keepdims=True)
        - unit * jnp.mean(scaled * unit, axis=-1, keepdims=True)
    )


def row_of(vectors, row):
    return vectors[row : row + 1, :].astype(FULL)


def own_columns(full, core, size):
    groups = full.shape[1] // (2 * size)
    first = jnp.concatenate(
        [full[:, (2 * g) * size : (2 * g + 1) * size] for g in range(groups)], axis=1
    )
    second = jnp.concatenate(
        [full[:, (2 * g + 1) * size : (2 * g + 2) * size] for g in range(groups)], axis=1
    )
    return jnp.where(core == 0, first, second)


def barred(lengths, block, first, height, span):
    shape = (height, span)
    rows = lax.broadcasted_iota(jnp.int32, shape, 0) + first
    keys = lax.broadcasted_iota(jnp.int32, shape, 1)
    opening = lengths[block, 0]
    filled = opening + lengths[block, 1]
    begin = jnp.where(rows < opening, 0, jnp.where(rows < filled, opening, rows))
    return jnp.where((keys <= rows) & (keys >= begin), 0.0, -1e30)


TILE = 128


def joint_cast_kernel(places, weight, vector, half, block, held, padded, sems):
    core, xl = places[13], places[14]

    def cols(which):
        return rows_at(which * 2 * COLS + core * COLS, COLS)

    copies = started(
        [
            (weight.at[rows_at(xl * 64, 64), cols(0)], held.at[pl.ds(0, 64)]),
            (weight.at[rows_at(xl * 32, 32), cols(2)], held.at[pl.ds(64, 32)]),
            (weight.at[:, cols(1)], held.at[pl.ds(96, 128)]),
            (weight.at[pl.ds(64, 64), cols(2)], held.at[pl.ds(224, 64)]),
        ],
        sems,
    )
    padded[...] = jnp.zeros_like(padded)
    padded[: vector.shape[0], : vector.shape[1]] = vector[...]
    block[192:208, :] = padded[...].astype(LOW)
    finished(copies)
    half[...] = held[:96].astype(LOW)
    block[:192, :] = held[96:].astype(LOW)


def joint_cast(places, weight, vector):
    return call(
        joint_cast_kernel,
        [SCALARS, OUTSIDE, INSIDE],
        [(low_shape(96, COLS), INSIDE), (low_shape(208, COLS), INSIDE)],
        [pltpu.VMEM((288, COLS), FULL), pltpu.VMEM((16, COLS), FULL)]
        + [pltpu.SemaphoreType.DMA((4,))],
        2,
        (places, weight, vector),
        vmem=8,
    )


def rest_cast_kernel(places, expand, reduce, output, half, block, held, wide, sems):
    core, xl, z = places[13], places[14], places[15]
    pairs = []
    for s in range(8):
        j, right = s // 2, (s % 2) * 256
        cols = rows_at(s * 512 + core * 256, 256)
        rows, size = (rows_at(xl * 64, 64), 64) if j < 3 else (pl.ds(0, 128), 128)
        pairs.append((expand.at[rows, cols], held.at[pl.ds(64 * j, size), pl.ds(right, 256)]))
    pairs.append((reduce.at[rows_at(core * 256, 256), pl.ds(0, COLS)], held.at[pl.ds(320, 256)]))
    pairs.append(
        (reduce.at[rows_at(core * 256 + z * 64, 64), pl.ds(COLS, COLS)], held.at[pl.ds(576, 64)])
    )
    pairs.append((output.at[rows_at(z * 32, 32)], wide))
    finished(started(pairs, sems))
    half[...] = held[:192].astype(LOW)
    block[:448, :] = held[192:640].astype(LOW)
    block[448:480, :] = wide[:, :COLS].astype(LOW)
    block[480:512, :] = wide[:, COLS:].astype(LOW)


def rest_cast(places, expand, reduce, output):
    return call(
        rest_cast_kernel,
        [SCALARS, OUTSIDE, OUTSIDE, OUTSIDE],
        [(low_shape(192, COLS), INSIDE), (low_shape(512, COLS), INSIDE)],
        [pltpu.VMEM((640, COLS), FULL), pltpu.VMEM((32, 2 * COLS), FULL)]
        + [pltpu.SemaphoreType.DMA((11,))],
        3,
        (places, expand, reduce, output),
        vmem=8,
    )


def joint_kernel(places, own, other, *refs):
    along_x, along_y, refs = refs[:4], refs[4:8], refs[8:]
    normed, query, key, value, vectors, query_mat, key_mat, value_mat, sems = refs
    mats = (query_mat, key_mat, value_mat, vectors)
    finished(started(joint_plan(places, along_x, along_y, mats), sems))
    gain, shift = row_of(vectors, 0), row_of(vectors, 1)
    core = places[13]
    query_bias = own_columns(row_of(vectors, 2), core, COLS)
    value_bias = own_columns(row_of(vectors, 3), core, COLS)
    count = own.shape[0]
    for block, tokens in enumerate((own, other)):
        rows = pl.ds(block * count, count)
        unit, _ = unit_of(tokens[...].astype(FULL))
        low = (unit * gain + shift).astype(LOW)
        normed[rows, :] = low
        query[rows, :] = ((dot(low, query_mat[...]) + query_bias).astype(LOW) * 0.125).astype(LOW)
        key[rows, :] = dot(low, key_mat[...]).astype(LOW)
        value[rows, :] = (dot(low, value_mat[...]) + value_bias).astype(LOW)


def joint(places, own, other, along_x, along_y):
    count, width = own.shape
    rows = 2 * count
    mat, half = (low_shape(width, COLS), INSIDE), (low_shape(rows, COLS), INSIDE)
    return call(
        joint_kernel,
        [SCALARS, INSIDE, INSIDE] + [OUTSIDE] * 8,
        [(low_shape(rows, width), INSIDE), half, half, half]
        + [(low_shape(16, width), INSIDE), mat, mat, mat],
        [pltpu.SemaphoreType.DMA((56,))],
        8,
        (places, own, other, *along_x, *along_y),
        vmem=24,
    )


def two_by_two(values, lane):
    return jnp.concatenate([jnp.where(lane, values, 0), jnp.where(lane, 0, values)], axis=0)


def probabilities(stacked, keys, bar):
    scores = dot_nt(stacked, keys) + jnp.concatenate([bar, bar], axis=0)
    probs = jnp.exp(scores - jnp.max(scores, axis=-1, keepdims=True))
    return probs * (1.0 / jnp.sum(probs, axis=-1, keepdims=True))


def attention_kernel(block, lengths, query, key, value, attended, mask):
    count = query.shape[0]
    mask[...] = barred(lengths, block, 0, count, count)
    lane = lax.broadcasted_iota(jnp.int32, (count, TILE), 1) < HEAD_DIM
    for index in range(COLS // TILE):
        cols = pl.ds(index * TILE, TILE)
        probs = probabilities(two_by_two(query[:, cols], lane), key[:, cols], mask[...])
        out = dot(probs.astype(LOW), value[:, cols])
        attended[:, cols] = jnp.where(lane, out[:count], out[count:]).astype(LOW)


def attention(block, lengths, query, key, value):
    count = query.shape[0] // 2
    return call(
        lambda *refs: attention_kernel(block, *refs),
        [SCALARS] + [pl.BlockSpec((count, COLS), lambda i: (block, 0))] * 3,
        [(low_shape(count, COLS), INSIDE)],
        [pltpu.VMEM((count, count), FULL)],
        5,
        (lengths, query, key, value),
        grid=(1,),
        vmem=20,
    )[0]


def output_kernel(places, own, other, *refs):
    raw, (branch, out_mat, sems) = refs[:4], refs[4:]
    finished(started(out_plan(places, lambda k: raw[k], 64, out_mat), sems))
    count = own.shape[0]
    for block, attended in enumerate((own, other)):
        for half in range(2):
            branch[block * count : (block + 1) * count, half * COLS : (half + 1) * COLS] = dot(
                attended[...], out_mat[half]
            ).astype(LOW)


def output(places, own, other, raw):
    rows, local = 2 * own.shape[0], own.shape[1]
    return call(
        output_kernel,
        [SCALARS, INSIDE, INSIDE] + [OUTSIDE] * 4,
        [(low_shape(rows, 2 * COLS), INSIDE), (low_shape(2, local, COLS), INSIDE)],
        [pltpu.SemaphoreType.DMA((32,))],
        5,
        (places, own, other, *raw),
        vmem=14,
    )


def forward_backward_kernel(
    places, lengths, own, other, arriving_own, arriving_other, branch, branch_far, vectors, *refs
):
    raw, refs = refs[:12], refs[12:]
    sent, refs = refs[:6], refs[6:]
    (middle, layer_own, layer_other, normed_grad, bias_grad,
     up, down_one, down_two, up_grad, one_grad, two_grad,
     tokens, near, far, held, normed, arriving, layer_sum, normed_sum, active, up_low,
     row_sems, sems, sems_out) = refs
    count = own.shape[0]
    blocks = [pl.ds(0, count), pl.ds(count, count)]
    rows_in = []
    for block, (token, cotangent) in enumerate(((own, arriving_own), (other, arriving_other))):
        here, there = blocks[block], blocks[1 - block]
        pairs = [
            (token, tokens.at[here]),
            (branch.at[here], near.at[here]),
            (branch_far.at[there], far.at[here]),
            (cotangent, arriving.at[here]),
        ]
        rows_in.append(started(pairs, row_sems.at[pl.ds(4 * block, 4)]))
    views = [lambda k, a=axis: raw[4 * a + k] for axis in range(3)]
    plan = up_plan(places, *views, (up, down_one, down_two))
    copies = [pltpu.make_async_copy(a, b, sems.at[i]) for i, (a, b) in enumerate(plan)]
    kinds = [up_kind(index) for index in range(len(copies))]
    for wanted in (0, None, 1, 2, 3):
        for copy, kind in zip(copies, kinds):
            if kind == wanted:
                copy.start()
    gain, shift = row_of(vectors, 5), row_of(vectors, 6)
    rows_out = []
    for block, here in enumerate(blocks):
        finished(rows_in[block])
        summed = near[here, :].astype(FULL) + far[here, :].astype(FULL)
        value = tokens[here, :].astype(FULL) + summed + row_of(vectors, 4)
        held[here, :] = value
        rows_out += started([(held.at[here], middle.at[here])], row_sems.at[pl.ds(8 + block, 1)])
        unit, _ = unit_of(value)
        normed[here, :] = (unit * gain + shift).astype(LOW)
        slots = lax.broadcasted_iota(jnp.int32, value.shape, 0)
        live = slots < lengths[block, 0] + lengths[block, 1]
        arriving[here, :] = jnp.where(live, arriving[here, :], 0)
    core = places[13]
    biases = jnp.concatenate(
        [own_columns(row_of(vectors, 7 + k), core, 256) for k in range(4)], axis=0
    )
    finished(copies)
    views = [two_of(sent[2 * axis : 2 * axis + 2]) for axis in range(3)]
    plan = turned(up_plan(places, *views, (up_grad, one_grad, two_grad)))
    copies_out = [pltpu.make_async_copy(a, b, sems_out.at[i]) for i, (a, b) in enumerate(plan)]

    def of_chunk(j, action, list_of_copies):
        for index, (copy, kind) in enumerate(zip(list_of_copies, kinds)):
            if kind == j:
                action(copy)
            elif kind is None:

                @pl.when(up_shard(places, index) // 2 == j)
                def _(copy=copy):
                    action(copy)

    for j in range(up.shape[0]):
        hidden = pl.ds(j * COLS, COLS)
        upward = dot(normed[...], up[j]) + biases[j : j + 1]
        act, slope = gelu_both(upward)
        active[...] = act.astype(LOW)
        layer_one, layer_two = dot(active[...], down_one[hidden, :]), dot(active[...], down_two[hidden, :])
        grad = dot_nt(arriving[:, :COLS], down_one[hidden, :])
        grad += dot_nt(arriving[:, COLS:], down_two[hidden, :])
        low = (grad * slope).astype(LOW)
        up_low[...] = low
        bias_grad[j : j + 1, :] = jnp.sum(low.astype(FULL), axis=0, keepdims=True)
        normed_part = dot_nt(up_low[...], up[j])
        if j == 0:
            layer_sum[:, :COLS], layer_sum[:, COLS:] = layer_one, layer_two
            normed_sum[...] = normed_part
        else:
            layer_sum[:, :COLS] += layer_one
            layer_sum[:, COLS:] += layer_two
            normed_sum[...] += normed_part
        whole = dot_tn(active[...], arriving[...]).astype(LOW)
        one_grad[hidden, :] = whole[:, :COLS]
        two_grad[hidden, :] = whole[:, COLS:]
        up_grad[j] = dot_tn(normed[...], up_low[...]).astype(LOW)
        of_chunk(j, lambda copy: copy.start(), copies_out)
    layer_own[...] = held[:count, :] + layer_sum[:count, :] + row_of(vectors, 11)
    layer_other[...] = layer_sum[count:, :].astype(LOW)
    normed_grad[...] = normed_sum[...].astype(LOW)
    finished(rows_out)
    finished(copies_out)


def forward_backward(places, lengths, tokens, arriving, branch, branch_far, vectors, raw):
    count, width = tokens[0].shape
    rows, hidden = 2 * count, 4 * COLS
    sent = [low_shape(2, 4, 192, COLS), low_shape(2, 2, 384, COLS), low_shape(2, 4, 2, 64, COLS)]
    inside = [
        full_shape(count, width), low_shape(count, width), low_shape(rows, width),
        full_shape(4, COLS),
    ]
    vmem = pltpu.VMEM
    mats = [vmem((4, width, COLS), LOW), vmem((hidden, COLS), LOW), vmem((hidden, COLS), LOW)]
    low, full = vmem((rows, width), LOW), vmem((rows, width), FULL)
    return call(
        forward_backward_kernel,
        [SCALARS, SCALARS] + [OUTSIDE] * 6 + [INSIDE] + [OUTSIDE] * 12,
        [(s, OUTSIDE) for s in sent for _ in range(2)]
        + [(full_shape(rows, width), OUTSIDE)]
        + [(s, INSIDE) for s in inside],
        mats + mats + [low, low, low, full, low, low, full, full]
        + [vmem((rows, COLS), LOW), vmem((rows, COLS), LOW)]
        + [pltpu.SemaphoreType.DMA((n,)) for n in (10, 96, 96)],
        33,
        (places, lengths, *tokens, *arriving, branch, branch_far, vectors, *raw),
    )


def output_backward_kernel(
    places, lengths, arriving_own, arriving_other, middle, part, part_far, vectors, own, other,
    out_mat, sent_one, sent_two, middle_grad, attended_grad, sums,
    held, near, far, arriving, branch, out_grad, row_sems, sems,
):
    count = arriving_own.shape[0]
    blocks = [pl.ds(0, count), pl.ds(count, count)]
    rows_in = []
    for block, cotangent in enumerate((arriving_own, arriving_other)):
        here, there = blocks[block], blocks[1 - block]
        pairs = [
            (middle.at[here], held.at[here]),
            (part.at[here], near.at[here]),
            (part_far.at[there], far.at[here]),
            (cotangent, arriving.at[here]),
        ]
        rows_in.append(started(pairs, row_sems.at[pl.ds(4 * block, 4)]))
    gain = row_of(vectors, 5)
    for block, rows in enumerate(blocks):
        finished(rows_in[block])
        unit, inverse = unit_of(held[rows, :])
        grad = near[rows, :].astype(FULL) + far[rows, :].astype(FULL)
        slots = lax.broadcasted_iota(jnp.int32, grad.shape, 0)
        live = slots < lengths[block, 0] + lengths[block, 1]
        coming = jnp.where(live, arriving[rows, :].astype(FULL), 0.0)
        result = coming + norm_backward(grad, unit, inverse, gain)
        low = result.astype(LOW)
        branch[rows, :] = low
        if block == 0:
            middle_grad[...] = result
            sums[...] = jnp.zeros_like(sums)
            sums[0:1, :] = jnp.sum(low.astype(FULL), axis=0, keepdims=True)
            sums[1:2, :] = jnp.sum(grad * unit, axis=0, keepdims=True)
            sums[2:3, :] = jnp.sum(grad, axis=0, keepdims=True)
            sums[3:4, :] = jnp.sum(coming, axis=0, keepdims=True)
    whole = dot_tn(own[...], branch[:count, :]) + dot_tn(other[...], branch[count:, :])
    out_grad[0] = whole[:, :COLS].astype(LOW)
    out_grad[1] = whole[:, COLS:].astype(LOW)
    copies = started(turned(out_plan(places, two_of((sent_one, sent_two)), 0, out_grad)), sems)
    attended_grad[...] = (
        dot_nt(branch[:, :COLS], out_mat[0]) + dot_nt(branch[:, COLS:], out_mat[1])
    ).astype(LOW)
    finished(copies)


def output_backward(
    places, lengths, arriving, middle, part, part_far, vectors, attended, out_mat
):
    rows, width = middle.shape
    sent = (low_shape(2, 4, 2, 32, COLS), OUTSIDE)
    inside = [full_shape(rows // 2, width), low_shape(rows, COLS), full_shape(8, width)]
    low = pltpu.VMEM((rows, width), LOW)
    return call(
        output_backward_kernel,
        [SCALARS, SCALARS] + [OUTSIDE] * 5 + [INSIDE] * 4,
        [sent, sent] + [(s, INSIDE) for s in inside],
        [pltpu.VMEM((rows, width), FULL), low, low, low, low, pltpu.VMEM((2, COLS, COLS), LOW)]
        + [pltpu.SemaphoreType.DMA((8,)), pltpu.SemaphoreType.DMA((32,))],
        10,
        (places, lengths, *arriving, middle, part, part_far, vectors, *attended, out_mat),
        vmem=32,
    )


def attention_backward_kernel(
    block, lengths, query, key, value, grad_in, query_grad, key_grad, value_grad, sums, mask
):
    count = query.shape[0]
    mask[...] = barred(lengths, block, 0, count, count)
    lane = lax.broadcasted_iota(jnp.int32, (count, TILE), 1) < HEAD_DIM
    for index in range(COLS // TILE):
        cols = pl.ds(index * TILE, TILE)
        stacked, given = two_by_two(query[:, cols], lane), two_by_two(grad_in[:, cols], lane)
        probs = probabilities(stacked, key[:, cols], mask[...])
        weighted = probs * dot_nt(given, value[:, cols])
        grad = (weighted - probs * jnp.sum(weighted, axis=-1, keepdims=True)).astype(LOW)
        out = dot(grad, key[:, cols])
        query_grad[:, cols] = (jnp.where(lane, out[:count], out[count:]) * 0.125).astype(LOW)
        key_grad[:, cols] = dot_tn(grad, stacked).astype(LOW)
        value_grad[:, cols] = dot_tn(probs.astype(LOW), given).astype(LOW)
    sums[...] = jnp.zeros_like(sums)
    sums[0:1, :] = jnp.sum(query_grad[...].astype(FULL), axis=0, keepdims=True)
    sums[1:2, :] = jnp.sum(value_grad[...].astype(FULL), axis=0, keepdims=True)


def attention_backward(block, lengths, query, key, value, grad_in):
    count = query.shape[0] // 2
    vmem = pltpu.VMEM
    half = (low_shape(count, COLS), INSIDE)
    part = pl.BlockSpec((count, COLS), lambda i: (block, 0))
    return call(
        lambda *refs: attention_backward_kernel(block, *refs),
        [SCALARS] + [part] * 4,
        [half, half, half, (full_shape(8, COLS), INSIDE)],
        [vmem((count, count), FULL)],
        8,
        (lengths, query, key, value, grad_in),
        grid=(1,),
        vmem=20,
    )


def joint_grad_kernel(places, normed, *refs):
    grads, sent, (query_part, key_part, value_part, sems) = refs[:6], refs[6:12], refs[12:]
    parts = (query_part, key_part, value_part)
    count = grads[0].shape[0]
    sides = [jnp.concatenate([g[...] for g in grads[i : i + 3]], axis=1) for i in (0, 3)]
    whole = dot_tn(normed[:count, :], sides[0]) + dot_tn(normed[count:, :], sides[1])
    for index, part in enumerate(parts):
        part[...] = whole[:, index * COLS : (index + 1) * COLS].astype(LOW)
    finished(started(joint_sent_plan(places, sent, parts), sems))


def joint_grad_parts(places, normed, own, other):
    rows, width = normed.shape
    sent = [low_shape(2, 4, 64, COLS), low_shape(2, 2, 128, COLS), low_shape(2, 4, 2, 32, COLS)]
    return call(
        joint_grad_kernel,
        [SCALARS] + [INSIDE] * 7,
        [(s, OUTSIDE) for s in sent for _ in range(2)],
        [pltpu.VMEM((width, COLS), LOW)] * 3 + [pltpu.SemaphoreType.DMA((56,))],
        8,
        (places, normed, *own, *other),
        vmem=30,
    )


def joint_backward_kernel(*refs):
    own, other, mats, outs = refs[:3], refs[3:6], refs[6:9], refs[9:]
    for grads, out in zip((own, other), outs):
        whole = dot_nt(grads[0][...], mats[0][...])
        whole += dot_nt(grads[1][...], mats[1][...])
        whole += dot_nt(grads[2][...], mats[2][...])
        out[...] = whole.astype(out.dtype)


def joint_backward(own, other, mats):
    count, width = own[0].shape[0], mats[0].shape[0]
    return call(
        joint_backward_kernel,
        [INSIDE] * 9,
        [(full_shape(count, width), INSIDE), (low_shape(count, width), INSIDE)],
        [],
        6,
        (*own, *other, *mats),
        vmem=20,
    )


def input_kernel(tokens, part, part_far, middle_grad, vectors, input_grad, sums):
    unit, inverse = unit_of(tokens[...].astype(FULL))
    grad = part[...] + part_far[...].astype(FULL)
    input_grad[...] = middle_grad[...] + norm_backward(grad, unit, inverse, row_of(vectors, 0))
    sums[...] = jnp.zeros_like(sums)
    sums[0:1, :] = jnp.sum(grad * unit, axis=0, keepdims=True)
    sums[1:2, :] = jnp.sum(grad, axis=0, keepdims=True)


def input_backward(tokens, part, part_far, middle_grad, vectors):
    return call(
        input_kernel,
        [INSIDE] * 5,
        [(full_shape(*part.shape), INSIDE), (full_shape(8, part.shape[1]), INSIDE)],
        [],
        5,
        (tokens, part, part_far, middle_grad, vectors),
        vmem=20,
    )


def adam_step(weight, first, second, grad, rate, decay):
    first_new = BETA_ONE * first + (1.0 - BETA_ONE) * grad
    second_new = BETA_TWO * second + (1.0 - BETA_TWO) * grad * grad
    mean_hat = first_new / (1.0 - BETA_ONE**STEP)
    square_hat = second_new / (1.0 - BETA_TWO**STEP)
    fresh = weight - rate * (mean_hat / (jnp.sqrt(square_hat) + ADAM_EPS) + decay * weight)
    return (first_new, second_new, fresh)


def adam_kernel(grad_of, rate, chunks, places, *refs):
    state, refs = refs[:3], refs[3:]
    grads, refs = refs[:-8], refs[-8:]
    outs, (held, results, sems_in, sems_out) = refs[:4], refs[4:]
    coming = [
        started([(a.at[at], held.at[(i, *at)]) for i, a in enumerate(state)], sems_in.at[n])
        for n, at in enumerate(chunks)
    ]
    going = []
    for n, at in enumerate(chunks):
        grad = grad_of(n, places, *grads)
        finished(coming[n])
        results[(0, *at)] = grad
        weight, first, second = (held[(i, *at)] for i in range(3))
        new = adam_step(weight, first, second, grad, rate, MATRIX_DECAY)
        for i, value in enumerate(new):
            results[(1 + i, *at)] = value
        going += started(
            [(results.at[(i, *at)], out.at[at]) for i, out in enumerate(outs)], sems_out.at[n]
        )
    finished(going)


def adam(grad_of, rate, chunks, state, grads, places):
    shape = state[0].shape
    return pl.pallas_call(
        lambda *refs: adam_kernel(grad_of, rate, chunks, *refs),
        grid=(1,),
        in_specs=[SCALARS]
        + [OUTSIDE] * 3
        + [pl.BlockSpec((g[1], COLS), lambda i, at=g[2]: (at, 0)) for g in grads],
        out_specs=[OUTSIDE] * 4,
        out_shape=[full_shape(*shape)] * 4,
        scratch_shapes=[pltpu.VMEM((3, *shape), FULL), pltpu.VMEM((4, *shape), FULL)]
        + [pltpu.SemaphoreType.DMA((len(chunks), 3)), pltpu.SemaphoreType.DMA((len(chunks), 4))],
        compiler_params=pltpu.CompilerParams(vmem_limit_bytes=24 << 20),
        cost_estimate=pl.CostEstimate(
            flops=6 * FLOPS_PER_US, bytes_accessed=30 * state[0].size, transcendentals=0
        ),
    )(places, *state, *(g[0] for g in grads))


def by_core(places, both, far):
    own = places[13] == 0
    both, far = both.astype(FULL), far.astype(FULL)
    return jnp.where(own, both, far), jnp.where(own, far, both)


def columns_of(width, count):
    return [(slice(None), slice(n * width, (n + 1) * width)) for n in range(count)]


def rows_each(height, count):
    return [(slice(n * height, (n + 1) * height), slice(None)) for n in range(count)]


def adam_joint(places, state, sums):
    def grad_of(n, places, both, far):
        rows = slice(128 * n, 128 * (n + 1))
        return jnp.concatenate(by_core(places, both[rows, :], far[rows, :]), axis=1)

    grads = [(a, 384, 0) for a in sums]
    return adam(grad_of, MATRIX_RATE, columns_of(2 * COLS, 3), state, grads, places)


def adam_expand(places, state, sums):
    def grad_of(n, places, both, far):
        rows = slice(128 * n, 128 * (n + 1))
        zero, one = by_core(places, both[rows, :], far[rows, :])
        return jnp.concatenate(
            [zero[:, :256], one[:, :256], zero[:, 256:], one[:, 256:]], axis=1
        )

    grads = [(a, 512, 0) for a in sums]
    return adam(grad_of, MATRIX_RATE, columns_of(2 * COLS, 4), state, grads, places)


def adam_reduce(places, state, sums):
    def grad_of(n, places, left, right, far_left, far_right):
        rows = slice(128 * (n % 2), 128 * (n % 2 + 1))
        own = places[13] == n // 2
        return jnp.concatenate(
            [
                jnp.where(own, left[rows, :].astype(FULL), far_left[rows, :].astype(FULL)),
                jnp.where(own, right[rows, :].astype(FULL), far_right[rows, :].astype(FULL)),
            ],
            axis=1,
        )

    grads = [(a, 256, at) for a in sums for at in (2, 3)]
    return adam(grad_of, MATRIX_RATE, rows_each(128, 4), state, grads, places)


def adam_output(places, state, sums):
    def grad_of(n, places, both, far):
        def rows(a):
            return jnp.concatenate(
                [
                    jnp.concatenate([a[64 * q : 64 * q + 32, :], a[64 * q + 32 : 64 * q + 64, :]], axis=1)
                    for q in (2 * n, 2 * n + 1)
                ]
            ).astype(FULL)

        return jnp.where(places[13] == places[12], rows(both), rows(far))

    grads = [(a, 256, 4) for a in sums]
    return adam(grad_of, OUTPUT_RATE, rows_each(64, 2), state, grads, places)


def per_device(
    tokens,
    cotangent,
    lengths,
    joint_weight,
    joint_first,
    joint_second,
    output_weight,
    output_first,
    output_second,
    expand_weight,
    expand_first,
    expand_second,
    reduce_weight,
    reduce_first,
    reduce_second,
    vector_weight,
    vector_first,
    vector_second,
):
    me = coordinates()
    core = me["core"]
    places = places_of(me)
    across = flip("core", 1)
    width = tokens.shape[1]
    units = 256

    half, block = joint_cast(places, joint_weight, vector_weight)
    joint_x, joint_y, marks, rest_block, far = gather_joint(
        half,
        block,
        rest_cast(places, expand_weight, reduce_weight, output_weight),
        [send(a, across) for a in (tokens, cotangent, lengths)],
    )
    here, there, pair_y = gather_rest(me, *rest_block, marks)
    tokens, cotangent = (tokens, far[0]), (cotangent, far[1])
    lengths = jnp.concatenate([lengths, far[2]])

    normed_one, query, key, value, vectors, *joint_mats = joint(
        places, *tokens, joint_x, joint_y
    )
    there = after(there, query)
    plane_x = jnp.concatenate([here[:, :192], there[:, :192]])
    plane_z = jnp.concatenate([here[:, 192:], there[:, 192:]]).reshape(4, 2, 96, COLS)
    pair_y = after(pair_y, there)
    own = attention(0, lengths, query, key, value)
    along_x, along_y = main_phase(plane_x, "x", own), main_phase(pair_y, "y", own)
    along_z = main_phase(plane_z, "z", own, late=True)
    other = attention(1, lengths, after(query, *along_x[1:3], *along_y[1:3], along_z[1]), key, value)
    attended = (own, other)
    branch, out_mat = output(places, own, after(other, along_x[3], along_y[3]), along_z)
    branch_far = send(branch, across)
    *sent, middle, layer_own, layer_other, normed_two_part, up_bias_grad = forward_backward(
        places, lengths, tokens, cotangent, branch, branch_far, vectors,
        [*along_x, *along_y, *along_z],
    )
    part_far = send(normed_two_part, across)
    layer_out = (layer_own + send(layer_other, across).astype(FULL)).astype(LOW)

    out_one, out_two, middle_grad, attended_grad, two_sums = output_backward(
        places, lengths, cotangent, middle, normed_two_part, part_far, vectors, attended, out_mat
    )
    rest = total(me, [*sent, out_one, out_two], 32, 3, 0)
    next(rest)
    *own_grads, own_sums = attention_backward(0, lengths, query, key, value, attended_grad)
    mark = rest.send(own_grads[0])
    *other_grads, other_sums = attention_backward(
        1, lengths, query, key, value, after(attended_grad, mark)
    )
    mark = rest.send((other_grads[0], None))
    sent = joint_grad_parts(places, after(normed_one, mark), own_grads, other_grads)
    joint_rows = total(me, sent, 0, 1, 32)
    next(joint_rows)
    mark = rest.send(sent[0])
    part_own, part_other = joint_backward(
        (after(own_grads[0], mark), *own_grads[1:]), other_grads, joint_mats
    )
    part_far = send(part_other, across)
    mark = rest.send(part_own)
    mark = joint_rows.send(mark)
    input_grad, one_sums = input_backward(
        tokens[0], after(part_own, mark), part_far, middle_grad, vectors
    )

    is_core = (jnp.arange(2) == core).astype(FULL)

    def own_half(values):
        return (is_core[:, None] * values[None]).reshape(1, -1)

    head_sums = own_sums + other_sums
    up_mine = is_core[None, :, None] * up_bias_grad.reshape(8, 1, units)
    vector_local = jnp.concatenate(
        [
            one_sums[:2],
            own_half(head_sums[0]),
            own_half(head_sums[1]),
            two_sums[:3],
            up_mine.reshape(4, width),
            two_sums[3:4],
            jnp.zeros((4, width), FULL),
        ],
        axis=0,
    ).astype(LOW)
    vector_local = rows_of(vector_local[:, :COLS], vector_local[:, COLS:])

    mark = rest.send(one_sums)
    mark = joint_rows.send((mark, vector_local))
    for _ in range(3):
        mark = rest.send(mark)
        mark = joint_rows.send(mark)
    mark = joint_rows.send(mark)
    mark = rest.send(mark)
    mark = joint_rows.send(mark)
    one, two, _ = next(rest)
    expand = adam_expand(places, (expand_weight, expand_first, expand_second), (one, two))
    mark = joint_rows.send(expand[0])
    output_state = adam_output(
        places, (output_weight, output_first, output_second), (after(one, mark), two)
    )
    mark = joint_rows.send(output_state[0])
    reduce = adam_reduce(
        places, (reduce_weight, reduce_first, reduce_second), (after(one, mark), two)
    )
    one, two, extra = next(joint_rows)
    joint_state = adam_joint(
        places, (joint_weight, joint_first, joint_second), (after(one, reduce[0]), two)
    )
    vector_grad = lax.dynamic_slice(
        jnp.concatenate([extra[:12], extra[16:28]], axis=1).astype(FULL),
        (0, 128 * lax.axis_index("shard")),
        (12, 128),
    )
    vector_state = (vector_grad,) + adam_step(
        vector_weight, vector_first, vector_second, vector_grad, VECTOR_RATE, 0.0
    )
    states = zip(joint_state, output_state, expand, reduce, vector_state)
    return (layer_out, input_grad, *(a for kind in states for a in kind))


def solution(mesh):
    rows, columns, split = P("shard", None), P(None, "shard"), P(("wide", "shard"), None)
    state = (rows, rows, rows, rows, columns)
    return jax.shard_map(
        per_device,
        mesh=mesh,
        in_specs=(split, split, split) + (rows,) * 12 + (columns,) * 3,
        out_specs=(split, split) + state * 4,
        check_vma=False,
    )
```

```python
import jax
import jax.numpy as jnp
from jax import lax
from jax.experimental import pallas as pl
from jax.experimental.pallas import tpu as pltpu
from jax.sharding import PartitionSpec as P

HEAD_DIM = 64
STEP = 10


ROOT_TWO_PI = 0.7978845608028654
CUBIC = 0.044715
BETA_ONE = 0.9
BETA_TWO = 0.999
ADAM_EPS = 1e-08
MATRIX_RATE = 0.03
OUTPUT_RATE = 0.1
VECTOR_RATE = 0.2
MATRIX_DECAY = 0.1

LOW = jnp.bfloat16
FULL = jnp.float32
AXES = ("wide", "shard")
SIZES = (4, 2, 2, 2, 4)
COLS = 512
FLOPS_PER_US = 1_150_000_000


def coordinates():
    wide, shard = lax.axis_index("wide"), lax.axis_index("shard")
    z, xl, core = wide // 4, (wide // 2) % 2, wide % 2
    xh, y = shard // 4, shard % 4
    return {"z": z, "x": 2 * xh + xl, "y": y, "xl": xl, "xh": xh, "core": core}


def route(partner):
    pairs = []
    for source in range(128):
        rest, places = source, []
        for size in reversed(SIZES):
            places.append(rest % size)
            rest //= size
        y, xh, core, xl, z = places
        target = partner({"z": z, "x": 2 * xh + xl, "y": y, "core": core})
        flat = 0
        for place, size in zip(
            (target["z"], target["x"] % 2, target["core"], target["x"] // 2, target["y"]), SIZES
        ):
            flat = flat * size + place
        pairs.append((source, flat))
    return pairs


def flip(axis, bits):
    return route(lambda at: {**at, axis: at[axis] ^ bits})


def turn(axis, step):
    return route(lambda at: {**at, axis: at[axis] ^ (1 if (at["core"] + step) % 2 == 0 else 3)})


def send(value, pairs):
    return lax.ppermute(value, AXES, pairs)


def added(*terms):
    return sum(term.astype(FULL) for term in terms).astype(LOW)


def orders(me, axis):
    here = me[axis]
    one = jnp.where(me["core"] == 0, 1, 3)
    return [here, here ^ one, here ^ (4 - one), here ^ 2]


def places_of(me):
    return jnp.stack(
        orders(me, "x")
        + orders(me, "y")
        + orders(me, "z")
        + [me["xh"], me["core"], me["xl"], me["z"]]
    ).astype(jnp.int32)


def after(value, *others):
    return lax.optimization_barrier((value, *others))[0]


def rows_of(*parts):
    return jnp.concatenate([p.reshape(-1, COLS) for p in parts])


def main_phase(block, axis, gate, late=False):
    first, second = send(block, turn(axis, 0)), send(gated(block, gate if late else None), turn(axis, 1))
    return [block, first, second, send(after(first, gate), turn(axis, 1))]


def gather_first(me, half, block, rest_half, rest_y, exchanged):
    size = half.shape[0]
    other, second = lax.optimization_barrier((send(block, flip("x", 3)), send(half, turn("y", 0))))
    joint_pair = rows_of(block[:208], other[:208])
    wanted = jnp.where(me["core"] == me["xh"], block[272:], other[272:])
    pair_z = rows_of(block[208:272], wanted[:32], other[208:272], wanted[32:])
    first_y = send(rows_of(joint_pair, pair_z), turn("y", 0))
    second_y = send(rows_of(joint_pair, half, second), turn("y", 1))
    rest_other = send(after(rest_y, other), flip("x", 3))
    first_y, second_y, rest_other = lax.optimization_barrier((first_y, second_y, rest_other))
    plane = rows_of(half, second, second_y[416:]).reshape(4, size, COLS)
    first_x, second_x = send(plane, turn("x", 0)), send(plane, turn("x", 1))
    third_y = send(rows_of(first_y[:416], pair_z, first_y[416:]), turn("y", 1))
    rest_near = send(after(rest_half, first_y), turn("y", 0))
    first_x, second_x, third_y, rest_near, *exchanged = lax.optimization_barrier(
        (first_x, second_x, third_y, rest_near, *exchanged)
    )
    third_x = send(first_x, turn("x", 1))
    here = rows_of(rest_half, rest_near)
    there = send(here, turn("y", 1))
    plane_z = rows_of(pair_z, first_y[416:], third_y[416:]).reshape(4, 2, 96, COLS)
    pair_y = jnp.stack([rest_y, rest_other])
    along_z = [plane_z, send(plane_z, turn("z", 0)), send(plane_z, turn("z", 1))]
    along_y = [pair_y, send(after(pair_y, third_y), turn("y", 0))]
    third_x, there = lax.optimization_barrier((third_x, there))
    plane_x = rows_of(here, there).reshape(4, -1, COLS)
    along_x = [plane_x, send(plane_x, turn("x", 0)), send(plane_x, turn("x", 1))]
    joint_x = [plane, first_x, second_x, third_x]
    joint_y = [joint_pair, first_y, second_y, third_y]
    return joint_x, joint_y, along_x, along_y, along_z, exchanged


def added_all(sums, steps=2):
    terms, specs, outs, out_specs = [], [], [], []
    for group in sums:
        rows = min(a.size for a, _ in group) // COLS
        rows = rows // 2 if len(group) == 2 else rows
        for array, which in group:
            terms.append(array.reshape(-1, COLS))
            specs.append(
                pl.BlockSpec((rows // steps, COLS), lambda i, at=which * steps: (at + i, 0))
            )
        outs.append(low_shape(rows, COLS))
        out_specs.append(pl.BlockSpec((rows // steps, COLS), lambda i: (i, 0)))

    def kernel(*refs):
        at = 0
        for group, out in zip(sums, refs[len(terms) :]):
            out[...] = added(*(ref[...] for ref in refs[at : at + len(group)]))
            at += len(group)

    return pl.pallas_call(
        kernel,
        grid=(steps,),
        in_specs=specs,
        out_specs=out_specs,
        out_shape=outs,
        compiler_params=pltpu.CompilerParams(vmem_limit_bytes=12 << 20),
        cost_estimate=pl.CostEstimate(
            flops=3 * FLOPS_PER_US, bytes_accessed=6 * sum(o.size for o in outs), transcendentals=0
        ),
    )(*terms)


def gated(value, gate):
    return value if gate is None else after(value, gate)


def total(me, raw, out_rows, units, extra_rows):
    axes = "xyz"
    parts = [raw[:2], raw[2:4], *(raw[k : k + 2] for k in range(4, len(raw), 2))]
    axes += "z" * (len(parts) - 3)
    far = [send(away, turn(axis, 1)) for (_, away), axis in zip(parts, axes)]
    gate = yield
    far = list(far if gate is None else lax.optimization_barrier((*far, gate))[:-1])
    keeps = [keep for keep, _ in parts]
    near = added_all([[(k, 1), (f, 1)] for k, f in zip(keeps, far)])
    near = lax.optimization_barrier([n.reshape(k.shape[1:]) for n, k in zip(near, keeps)])
    again = [send(n, turn(axis, 0)) for n, axis in zip(near, axes)]
    gate, extra = yield near[2]
    again = lax.optimization_barrier((*again, gate))[:-1]
    along = added_all([[(k, 0), (f, 0), (a, 0)] for k, f, a in zip(keeps, far, again)])
    along_x, along_y, *along_z = lax.optimization_barrier(
        [a.reshape(k.shape[1:]) for a, k in zip(along, keeps)]
    )
    along_z = jnp.concatenate(along_z, axis=2) if len(along_z) > 1 else along_z[0]
    size_x, size_y = along_x.shape[1], along_y.shape[1] // 2
    size_z = (along_z.shape[2] - out_rows) // 2

    def with_extra(*parts):
        return rows_of(*parts, extra) if extra_rows else rows_of(*parts)

    def split(rows, *sizes):
        at, parts = 0, []
        for size in sizes:
            parts.append(rows[at : at + size])
            at += size
        return parts

    plane = jnp.concatenate([along_x, along_z.reshape(4, -1, COLS)], axis=1)
    size = plane.shape[1]
    far = send(with_extra(plane[2:]), turn("y", 1))
    gate = yield plane
    far, kept = gated(far, gate), plane[:2]
    near = added(kept[1], far[size : 2 * size])
    if extra_rows:
        extra = added(extra, far[2 * size :])
    again = send(with_extra(near), turn("y", 0))
    gate = yield near
    again = gated(again, gate)
    plane = added(kept[0], far[:size], again[:size])
    if extra_rows:
        extra = added(extra, again[size:])
    half, pair = plane[:size_x], plane[size_x:].reshape(2, 2 * size_z + out_rows, COLS)
    out = pair[:, 2 * size_z :].reshape(-1, COLS)
    pieces = jnp.concatenate(
        [along_y.reshape(4, size_y, COLS), pair[:, : 2 * size_z].reshape(4, size_z, COLS)], axis=1
    )
    size = size_y + size_z
    pieces = [
        lax.dynamic_index_in_dim(pieces, ((k // 2) ^ me["xh"]) * 2 + k % 2, 0, keepdims=False)
        for k in orders(me, "x")
    ]
    far = send(with_extra(pieces[2], pieces[3], out), turn("x", 1))
    gate = yield plane
    far = gated(far, gate)
    first, second, far_out, far_extra = split(far, size, size, 2 * out_rows, extra_rows)
    sums = added(rows_of(pieces[1], out), rows_of(second, far_out))
    if extra_rows:
        extra = added(extra, far_extra)
    again = send(with_extra(sums), turn("x", 0))
    gate = yield sums
    near, out, far_extra = split(gated(again, gate), size, 2 * out_rows, extra_rows)
    sums = rows_of(added(pieces[0], first, near), added(sums[size:], out))
    if extra_rows:
        extra = added(extra, far_extra)
    flat, block = rows_of(half, sums[:size_y]), sums[size_y:]
    size, size_block = flat.shape[0], block.shape[0]
    far = send(with_extra(flat, block), turn("z", 0))
    gate = yield sums
    sums, other, far_extra = split(gated(far, gate), size, size_block, extra_rows)
    flat = added(flat, sums)
    if extra_rows:
        extra = added(extra, far_extra)
    blocks = rows_of(block, other)
    far = send(with_extra(flat, blocks), turn("z", 1))
    gate = yield flat
    sums, other, far_extra = split(gated(far, gate), size, 2 * size_block, extra_rows)
    flat = added(flat, sums)
    if extra_rows:
        extra = added(extra, far_extra)
    blocks = rows_of(blocks, other).reshape(4, size_block, COLS)
    where = orders(me, "z")
    ordered = jnp.stack(
        [
            sum(jnp.where(where[k] == place, blocks[k], 0) for k in range(4)).astype(LOW)
            for place in range(4)
        ]
    )
    mine = rows_of(flat, ordered[:, :size_z])
    far = send(mine, flip("x", 1))
    gate = yield mine
    far = gated(far, gate)

    def whole(groups, first, last):
        a, b = (rows[first:last].reshape(groups, -1, COLS) for rows in (mine, far))
        both = jnp.where(me["xl"] == 0, jnp.stack([a, b], axis=1), jnp.stack([b, a], axis=1))
        return both.reshape(-1, COLS)

    both = rows_of(
        whole(units, 0, size_x), whole(1, size_x, size), whole(4, size, mine.shape[0]),
        ordered[:, size_z:],
    )
    far = send(with_extra(both), flip("core", 1))
    yield both
    rows = both.shape[0]
    if extra_rows:
        extra = added(extra, far[rows:])
        far = far[:rows]
    yield both, far, extra


def rows_at(start, size):
    return pl.ds(pl.multiple_of(start, size), size)


def joint_plan(places, along_x, along_y, mats):
    query, key, value, vectors = mats
    pairs = []
    for ky in range(4):
        y = places[4 + ky]
        for kx in range(4):
            x = places[kx]
            shard, half = (x // 2) * 4 + y, x % 2
            source = along_x[kx].at[ky]
            pairs.append(
                (source.at[pl.ds(0, 64)], query.at[rows_at(shard * 128 + half * 64, 64)])
            )
            pairs.append(
                (source.at[pl.ds(64, 32)], value.at[rows_at(shard * 128 + half * 32, 32)])
            )
        for p in range(2):
            shard = (places[12] ^ p) * 4 + y
            source, at = along_y[ky], p * 208
            pairs.append((source.at[pl.ds(at, 128)], key.at[rows_at(shard * 128, 128)]))
            pairs.append((source.at[pl.ds(at + 128, 64)], value.at[rows_at(shard * 128 + 64, 64)]))
            pairs.append(
                (
                    source.at[pl.ds(at + 192, 16), pl.ds(0, 128)],
                    vectors.at[:, rows_at(shard * 128, 128)],
                )
            )
    return pairs


def joint_sent_plan(places, raw, parts):
    query, key, value = parts
    pairs = []
    for ky in range(4):
        y = places[4 + ky]
        for kx in range(4):
            x = places[kx]
            start = ((x // 2) * 4 + y) * 128 + (x % 2) * 64
            pairs.append((query.at[rows_at(start, 64)], raw[0 + kx // 2].at[kx % 2, ky]))
        for p in range(2):
            shard = (places[12] ^ p) * 4 + y
            pairs.append((key.at[rows_at(shard * 128, 128)], raw[2 + ky // 2].at[ky % 2, p]))
            for kz in range(4):
                start = shard * 128 + places[8 + kz] * 32
                pairs.append((value.at[rows_at(start, 32)], raw[4 + kz // 2].at[kz % 2, ky, p]))
    return pairs


def up_plan(places, at_x, at_y, at_z, mats):
    up, down_one, down_two = mats
    pairs = []
    for ky in range(4):
        y = places[4 + ky]
        for kx in range(4):
            x = places[kx]
            start = ((x // 2) * 4 + y) * 128 + (x % 2) * 64
            for j in range(3):
                source = at_x(kx).at[ky, pl.ds(64 * j, 64)]
                pairs.append((source, up.at[j, rows_at(start, 64)]))
        for p in range(2):
            shard = (places[12] ^ p) * 4 + y
            source = at_y(ky).at[p]
            pairs.append((source.at[pl.ds(0, 128)], up.at[3, rows_at(shard * 128, 128)]))
            pairs.append((source.at[pl.ds(128, 256)], down_one.at[rows_at(shard * 256, 256)]))
            for kz in range(4):
                start = shard * 256 + places[8 + kz] * 64
                source = at_z(kz).at[ky, p, pl.ds(0, 64)]
                pairs.append((source, down_two.at[rows_at(start, 64)]))
    return pairs


def up_kind(index):
    index %= 24
    if index < 12:
        return index % 3
    return 3 if (index - 12) % 6 == 0 else None


def up_shard(places, index):
    ky, index = divmod(index, 24)
    return (places[12] ^ ((index - 12) // 6)) * 4 + places[4 + ky]


def out_plan(places, at_z, first, mat):
    pairs = []
    for ky in range(4):
        for kz in range(4):
            start = places[4 + ky] * 128 + places[8 + kz] * 32
            for p in range(2):
                source = at_z(kz).at[ky, p, pl.ds(first, 32)]
                pairs.append((source, mat.at[p, rows_at(start, 32)]))
    return pairs


def two_of(arrays):
    return lambda k: arrays[k // 2].at[k % 2]


def started(pairs, sems):
    all_of_them = [pltpu.make_async_copy(a, b, sems.at[i]) for i, (a, b) in enumerate(pairs)]
    for copy in all_of_them:
        copy.start()
    return all_of_them


def finished(all_of_them):
    for copy in all_of_them:
        copy.wait()


def turned(pairs):
    return [(b, a) for a, b in pairs]


def low_shape(*shape):
    return jax.ShapeDtypeStruct(shape, LOW)


def full_shape(*shape):
    return jax.ShapeDtypeStruct(shape, FULL)


SCALARS = pl.BlockSpec(memory_space=pltpu.SMEM)
INSIDE = pl.BlockSpec(memory_space=pltpu.VMEM)
OUTSIDE = pl.BlockSpec(memory_space=pl.ANY)


def call(kernel, in_specs, outs, scratch, length, args, grid=(), vmem=60):
    shapes, specs = [o[0] for o in outs], [o[1] for o in outs]
    moved = sum(a.size * a.dtype.itemsize for a in (*args, *shapes))
    return pl.pallas_call(
        kernel,
        grid=grid,
        out_shape=shapes,
        in_specs=in_specs,
        out_specs=specs,
        scratch_shapes=scratch,
        compiler_params=pltpu.CompilerParams(vmem_limit_bytes=vmem << 20),
        cost_estimate=pl.CostEstimate(
            flops=length * FLOPS_PER_US, bytes_accessed=moved, transcendentals=0
        ),
    )(*args)


def gelu_both(upward):
    square = upward * upward
    tangent = jnp.tanh(ROOT_TWO_PI * upward * (1.0 + CUBIC * square))
    half = 0.5 * (1.0 + tangent)
    slope = half + 0.5 * upward * (1.0 - tangent * tangent) * ROOT_TWO_PI * (
        1.0 + 3.0 * CUBIC * square
    )
    return upward * half, slope


def dot(a, b):
    return jnp.dot(a, b, preferred_element_type=FULL)


def dot_nt(a, b):
    return lax.dot_general(a, b, (((1,), (1,)), ((), ())), preferred_element_type=FULL)


def dot_tn(a, b):
    return lax.dot_general(a, b, (((0,), (0,)), ((), ())), preferred_element_type=FULL)


def unit_of(values):
    center = values - jnp.mean(values, axis=-1, keepdims=True)
    inverse = lax.rsqrt(jnp.mean(center * center, axis=-1, keepdims=True) + 1e-05)
    return center * inverse, inverse


def norm_backward(grad_out, unit, inverse, gain):
    scaled = grad_out * gain
    return inverse * (
        scaled
        - jnp.mean(scaled, axis=-1, keepdims=True)
        - unit * jnp.mean(scaled * unit, axis=-1, keepdims=True)
    )


def row_of(vectors, row):
    return vectors[row : row + 1, :].astype(FULL)


def own_columns(full, core, size):
    groups = full.shape[1] // (2 * size)
    first = jnp.concatenate(
        [full[:, (2 * g) * size : (2 * g + 1) * size] for g in range(groups)], axis=1
    )
    second = jnp.concatenate(
        [full[:, (2 * g + 1) * size : (2 * g + 2) * size] for g in range(groups)], axis=1
    )
    return jnp.where(core == 0, first, second)


def barred(lengths, block, first, height, span):
    shape = (height, span)
    rows = lax.broadcasted_iota(jnp.int32, shape, 0) + first
    keys = lax.broadcasted_iota(jnp.int32, shape, 1)
    opening = lengths[block, 0]
    filled = opening + lengths[block, 1]
    begin = jnp.where(rows < opening, 0, jnp.where(rows < filled, opening, rows))
    return jnp.where((keys <= rows) & (keys >= begin), 0.0, -1e30)


TILE = 128


def cast_kernel(
    places, weight, vector, expand, reduce, output, half, block, rest_half, rest_y,
    held, rest, wide, padded, sems,
):
    core, xl, z = places[13], places[14], places[15]

    def cols(which):
        return rows_at(which * 2 * COLS + core * COLS, COLS)

    first = [
        (weight.at[rows_at(xl * 64, 64), cols(0)], held.at[pl.ds(0, 64)]),
        (weight.at[rows_at(xl * 32, 32), cols(2)], held.at[pl.ds(64, 32)]),
        (weight.at[:, cols(1)], held.at[pl.ds(96, 128)]),
        (weight.at[pl.ds(64, 64), cols(2)], held.at[pl.ds(224, 64)]),
        (
            reduce.at[rows_at(core * 256 + z * 64, 64), pl.ds(COLS, COLS)],
            held.at[pl.ds(288, 64)],
        ),
        (output.at[rows_at(z * 32, 32)], wide),
    ]
    second = [(reduce.at[rows_at(core * 256, 256), pl.ds(0, COLS)], rest.at[pl.ds(320, 256)])]
    for s in range(8):
        j, right = s // 2, (s % 2) * 256
        at = rows_at(s * 512 + core * 256, 256)
        rows, size = (rows_at(xl * 64, 64), 64) if j < 3 else (pl.ds(0, 128), 128)
        second.append((expand.at[rows, at], rest.at[pl.ds(64 * j, size), pl.ds(right, 256)]))
    first = started(first, sems.at[pl.ds(0, 6)])
    second = started(second, sems.at[pl.ds(6, 9)])
    padded[...] = jnp.zeros_like(padded)
    padded[: vector.shape[0], : vector.shape[1]] = vector[...]
    block[192:208, :] = padded[...].astype(LOW)
    finished(first)
    half[...] = held[:96].astype(LOW)
    block[:192, :] = held[96:288].astype(LOW)
    block[208:272, :] = held[288:].astype(LOW)
    block[272:304, :] = wide[:, :COLS].astype(LOW)
    block[304:336, :] = wide[:, COLS:].astype(LOW)
    finished(second)
    rest_half[...] = rest[:192].astype(LOW)
    rest_y[...] = rest[192:].astype(LOW)


def cast(places, *arrays):
    outs = [low_shape(96, COLS), low_shape(336, COLS), low_shape(192, COLS), low_shape(384, COLS)]
    vmem = pltpu.VMEM
    return call(
        cast_kernel,
        [SCALARS, OUTSIDE, INSIDE, OUTSIDE, OUTSIDE, OUTSIDE],
        [(shape, INSIDE) for shape in outs],
        [vmem((352, COLS), FULL), vmem((576, COLS), FULL), vmem((32, 2 * COLS), FULL)]
        + [vmem((16, COLS), FULL), pltpu.SemaphoreType.DMA((15,))],
        3,
        (places, *arrays),
        vmem=8,
    )


def joint_kernel(places, own, other, *refs):
    along_x, along_y, refs = refs[:4], refs[4:8], refs[8:]
    normed, query, key, value, vectors, query_mat, key_mat, value_mat, sems = refs
    mats = (query_mat, key_mat, value_mat, vectors)
    finished(started(joint_plan(places, along_x, along_y, mats), sems))
    gain, shift = row_of(vectors, 0), row_of(vectors, 1)
    core = places[13]
    query_bias = own_columns(row_of(vectors, 2), core, COLS)
    value_bias = own_columns(row_of(vectors, 3), core, COLS)
    count = own.shape[0]
    for block, tokens in enumerate((own, other)):
        rows = pl.ds(block * count, count)
        unit, _ = unit_of(tokens[...].astype(FULL))
        low = (unit * gain + shift).astype(LOW)
        normed[rows, :] = low
        query[rows, :] = ((dot(low, query_mat[...]) + query_bias).astype(LOW) * 0.125).astype(LOW)
        key[rows, :] = dot(low, key_mat[...]).astype(LOW)
        value[rows, :] = (dot(low, value_mat[...]) + value_bias).astype(LOW)


def joint(places, own, other, along_x, along_y):
    count, width = own.shape
    rows = 2 * count
    mat, half = (low_shape(width, COLS), INSIDE), (low_shape(rows, COLS), INSIDE)
    return call(
        joint_kernel,
        [SCALARS, INSIDE, INSIDE] + [OUTSIDE] * 8,
        [(low_shape(rows, width), INSIDE), half, half, half]
        + [(low_shape(16, width), INSIDE), mat, mat, mat],
        [pltpu.SemaphoreType.DMA((56,))],
        8,
        (places, own, other, *along_x, *along_y),
        vmem=24,
    )


def two_by_two(values, lane):
    return jnp.concatenate([jnp.where(lane, values, 0), jnp.where(lane, 0, values)], axis=0)


def probabilities(stacked, keys, bar):
    scores = dot_nt(stacked, keys) + jnp.concatenate([bar, bar], axis=0)
    probs = jnp.exp(scores - jnp.max(scores, axis=-1, keepdims=True))
    return probs * (1.0 / jnp.sum(probs, axis=-1, keepdims=True))


def attention_kernel(block, lengths, query, key, value, attended, mask):
    count = query.shape[0]
    mask[...] = barred(lengths, block, 0, count, count)
    lane = lax.broadcasted_iota(jnp.int32, (count, TILE), 1) < HEAD_DIM
    for index in range(COLS // TILE):
        cols = pl.ds(index * TILE, TILE)
        probs = probabilities(two_by_two(query[:, cols], lane), key[:, cols], mask[...])
        out = dot(probs.astype(LOW), value[:, cols])
        attended[:, cols] = jnp.where(lane, out[:count], out[count:]).astype(LOW)


def attention(block, lengths, query, key, value):
    count = query.shape[0] // 2
    return call(
        lambda *refs: attention_kernel(block, *refs),
        [SCALARS] + [pl.BlockSpec((count, COLS), lambda i: (block, 0))] * 3,
        [(low_shape(count, COLS), INSIDE)],
        [pltpu.VMEM((count, count), FULL)],
        5,
        (lengths, query, key, value),
        grid=(1,),
        vmem=20,
    )[0]


def output_kernel(places, own, other, *refs):
    raw, (branch, out_mat, sems) = refs[:4], refs[4:]
    finished(started(out_plan(places, lambda k: raw[k], 64, out_mat), sems))
    count = own.shape[0]
    for block, attended in enumerate((own, other)):
        for half in range(2):
            branch[block * count : (block + 1) * count, half * COLS : (half + 1) * COLS] = dot(
                attended[...], out_mat[half]
            ).astype(LOW)


def output(places, own, other, raw):
    rows, local = 2 * own.shape[0], own.shape[1]
    return call(
        output_kernel,
        [SCALARS, INSIDE, INSIDE] + [OUTSIDE] * 4,
        [(low_shape(rows, 2 * COLS), INSIDE), (low_shape(2, local, COLS), INSIDE)],
        [pltpu.SemaphoreType.DMA((32,))],
        5,
        (places, own, other, *raw),
        vmem=14,
    )


def forward_backward_kernel(
    places, lengths, own, other, arriving_own, arriving_other, branch, branch_far, vectors, *refs
):
    raw, refs = refs[:12], refs[12:]
    sent, refs = refs[:6], refs[6:]
    (middle, layer_own, layer_other, normed_grad, bias_grad,
     up, down_one, down_two, up_grad, one_grad, two_grad,
     tokens, near, far, held, normed, arriving, layer_sum, normed_sum, active, up_low,
     row_sems, sems, sems_out) = refs
    count = own.shape[0]
    blocks = [pl.ds(0, count), pl.ds(count, count)]
    rows_in = []
    for block, (token, cotangent) in enumerate(((own, arriving_own), (other, arriving_other))):
        here, there = blocks[block], blocks[1 - block]
        pairs = [
            (token, tokens.at[here]),
            (branch.at[here], near.at[here]),
            (branch_far.at[there], far.at[here]),
            (cotangent, arriving.at[here]),
        ]
        rows_in.append(started(pairs, row_sems.at[pl.ds(4 * block, 4)]))
    views = [lambda k, a=axis: raw[4 * a + k] for axis in range(3)]
    plan = up_plan(places, *views, (up, down_one, down_two))
    copies = [pltpu.make_async_copy(a, b, sems.at[i]) for i, (a, b) in enumerate(plan)]
    kinds = [up_kind(index) for index in range(len(copies))]
    for wanted in (0, None, 1, 2, 3):
        for copy, kind in zip(copies, kinds):
            if kind == wanted:
                copy.start()
    gain, shift = row_of(vectors, 5), row_of(vectors, 6)
    rows_out = []
    for block, here in enumerate(blocks):
        finished(rows_in[block])
        summed = near[here, :].astype(FULL) + far[here, :].astype(FULL)
        value = tokens[here, :].astype(FULL) + summed + row_of(vectors, 4)
        held[here, :] = value
        rows_out += started([(held.at[here], middle.at[here])], row_sems.at[pl.ds(8 + block, 1)])
        unit, _ = unit_of(value)
        normed[here, :] = (unit * gain + shift).astype(LOW)
        slots = lax.broadcasted_iota(jnp.int32, value.shape, 0)
        live = slots < lengths[block, 0] + lengths[block, 1]
        arriving[here, :] = jnp.where(live, arriving[here, :], 0)
    core = places[13]
    biases = jnp.concatenate(
        [own_columns(row_of(vectors, 7 + k), core, 256) for k in range(4)], axis=0
    )
    finished(copies)
    views = [two_of(sent[2 * axis : 2 * axis + 2]) for axis in range(3)]
    plan = turned(up_plan(places, *views, (up_grad, one_grad, two_grad)))
    copies_out = [pltpu.make_async_copy(a, b, sems_out.at[i]) for i, (a, b) in enumerate(plan)]

    def of_chunk(j, action, list_of_copies):
        for index, (copy, kind) in enumerate(zip(list_of_copies, kinds)):
            if kind == j:
                action(copy)
            elif kind is None:

                @pl.when(up_shard(places, index) // 2 == j)
                def _(copy=copy):
                    action(copy)

    for j in range(up.shape[0]):
        hidden = pl.ds(j * COLS, COLS)
        upward = dot(normed[...], up[j]) + biases[j : j + 1]
        act, slope = gelu_both(upward)
        active[...] = act.astype(LOW)
        layer_one, layer_two = dot(active[...], down_one[hidden, :]), dot(active[...], down_two[hidden, :])
        grad = dot_nt(arriving[:, :COLS], down_one[hidden, :])
        grad += dot_nt(arriving[:, COLS:], down_two[hidden, :])
        low = (grad * slope).astype(LOW)
        up_low[...] = low
        bias_grad[j : j + 1, :] = jnp.sum(low.astype(FULL), axis=0, keepdims=True)
        normed_part = dot_nt(up_low[...], up[j])
        if j == 0:
            layer_sum[:, :COLS], layer_sum[:, COLS:] = layer_one, layer_two
            normed_sum[...] = normed_part
        else:
            layer_sum[:, :COLS] += layer_one
            layer_sum[:, COLS:] += layer_two
            normed_sum[...] += normed_part
        whole = dot_tn(active[...], arriving[...]).astype(LOW)
        one_grad[hidden, :] = whole[:, :COLS]
        two_grad[hidden, :] = whole[:, COLS:]
        up_grad[j] = dot_tn(normed[...], up_low[...]).astype(LOW)
        of_chunk(j, lambda copy: copy.start(), copies_out)
    layer_own[...] = held[:count, :] + layer_sum[:count, :] + row_of(vectors, 11)
    layer_other[...] = layer_sum[count:, :].astype(LOW)
    normed_grad[...] = normed_sum[...].astype(LOW)
    finished(rows_out)
    finished(copies_out)


def forward_backward(places, lengths, tokens, arriving, branch, branch_far, vectors, raw):
    count, width = tokens[0].shape
    rows, hidden = 2 * count, 4 * COLS
    sent = [low_shape(2, 4, 192, COLS), low_shape(2, 2, 384, COLS), low_shape(2, 4, 2, 64, COLS)]
    inside = [
        full_shape(count, width), low_shape(count, width), low_shape(rows, width),
        full_shape(4, COLS),
    ]
    vmem = pltpu.VMEM
    mats = [vmem((4, width, COLS), LOW), vmem((hidden, COLS), LOW), vmem((hidden, COLS), LOW)]
    low, full = vmem((rows, width), LOW), vmem((rows, width), FULL)
    return call(
        forward_backward_kernel,
        [SCALARS, SCALARS] + [OUTSIDE] * 6 + [INSIDE] + [OUTSIDE] * 12,
        [(s, OUTSIDE) for s in sent for _ in range(2)]
        + [(full_shape(rows, width), OUTSIDE)]
        + [(s, INSIDE) for s in inside],
        mats + mats + [low, low, low, full, low, low, full, full]
        + [vmem((rows, COLS), LOW), vmem((rows, COLS), LOW)]
        + [pltpu.SemaphoreType.DMA((n,)) for n in (10, 96, 96)],
        33,
        (places, lengths, *tokens, *arriving, branch, branch_far, vectors, *raw),
        vmem=50,
    )


def output_backward_kernel(
    places, lengths, arriving_own, arriving_other, middle, part, part_far, vectors, own, other,
    out_mat, sent_one, sent_two, middle_grad, attended_grad, sums,
    held, near, far, arriving, branch, out_grad, row_sems, sems,
):
    count = arriving_own.shape[0]
    blocks = [pl.ds(0, count), pl.ds(count, count)]
    rows_in = []
    for block, cotangent in enumerate((arriving_own, arriving_other)):
        here, there = blocks[block], blocks[1 - block]
        pairs = [
            (middle.at[here], held.at[here]),
            (part.at[here], near.at[here]),
            (part_far.at[there], far.at[here]),
            (cotangent, arriving.at[here]),
        ]
        rows_in.append(started(pairs, row_sems.at[pl.ds(4 * block, 4)]))
    gain = row_of(vectors, 5)
    for block, rows in enumerate(blocks):
        finished(rows_in[block])
        unit, inverse = unit_of(held[rows, :])
        grad = near[rows, :].astype(FULL) + far[rows, :].astype(FULL)
        slots = lax.broadcasted_iota(jnp.int32, grad.shape, 0)
        live = slots < lengths[block, 0] + lengths[block, 1]
        coming = jnp.where(live, arriving[rows, :].astype(FULL), 0.0)
        result = coming + norm_backward(grad, unit, inverse, gain)
        low = result.astype(LOW)
        branch[rows, :] = low
        if block == 0:
            middle_grad[...] = result
            sums[...] = jnp.zeros_like(sums)
            sums[0:1, :] = jnp.sum(low.astype(FULL), axis=0, keepdims=True)
            sums[1:2, :] = jnp.sum(grad * unit, axis=0, keepdims=True)
            sums[2:3, :] = jnp.sum(grad, axis=0, keepdims=True)
            sums[3:4, :] = jnp.sum(coming, axis=0, keepdims=True)
    whole = dot_tn(own[...], branch[:count, :]) + dot_tn(other[...], branch[count:, :])
    out_grad[0] = whole[:, :COLS].astype(LOW)
    out_grad[1] = whole[:, COLS:].astype(LOW)
    copies = started(turned(out_plan(places, two_of((sent_one, sent_two)), 0, out_grad)), sems)
    attended_grad[...] = (
        dot_nt(branch[:, :COLS], out_mat[0]) + dot_nt(branch[:, COLS:], out_mat[1])
    ).astype(LOW)
    finished(copies)


def output_backward(
    places, lengths, arriving, middle, part, part_far, vectors, attended, out_mat
):
    rows, width = middle.shape
    sent = (low_shape(2, 4, 2, 32, COLS), OUTSIDE)
    inside = [full_shape(rows // 2, width), low_shape(rows, COLS), full_shape(8, width)]
    low = pltpu.VMEM((rows, width), LOW)
    return call(
        output_backward_kernel,
        [SCALARS, SCALARS] + [OUTSIDE] * 5 + [INSIDE] * 4,
        [sent, sent] + [(s, INSIDE) for s in inside],
        [pltpu.VMEM((rows, width), FULL), low, low, low, low, pltpu.VMEM((2, COLS, COLS), LOW)]
        + [pltpu.SemaphoreType.DMA((8,)), pltpu.SemaphoreType.DMA((32,))],
        10,
        (places, lengths, *arriving, middle, part, part_far, vectors, *attended, out_mat),
        vmem=32,
    )


def attention_backward_kernel(
    block, lengths, query, key, value, grad_in, query_grad, key_grad, value_grad, sums, mask
):
    count = query.shape[0]
    mask[...] = barred(lengths, block, 0, count, count)
    lane = lax.broadcasted_iota(jnp.int32, (count, TILE), 1) < HEAD_DIM
    for index in range(COLS // TILE):
        cols = pl.ds(index * TILE, TILE)
        stacked, given = two_by_two(query[:, cols], lane), two_by_two(grad_in[:, cols], lane)
        probs = probabilities(stacked, key[:, cols], mask[...])
        weighted = probs * dot_nt(given, value[:, cols])
        grad = (weighted - probs * jnp.sum(weighted, axis=-1, keepdims=True)).astype(LOW)
        out = dot(grad, key[:, cols])
        query_grad[:, cols] = (jnp.where(lane, out[:count], out[count:]) * 0.125).astype(LOW)
        key_grad[:, cols] = dot_tn(grad, stacked).astype(LOW)
        value_grad[:, cols] = dot_tn(probs.astype(LOW), given).astype(LOW)
    sums[...] = jnp.zeros_like(sums)
    sums[0:1, :] = jnp.sum(query_grad[...].astype(FULL), axis=0, keepdims=True)
    sums[1:2, :] = jnp.sum(value_grad[...].astype(FULL), axis=0, keepdims=True)


def attention_backward(block, lengths, query, key, value, grad_in):
    count = query.shape[0] // 2
    vmem = pltpu.VMEM
    half = (low_shape(count, COLS), INSIDE)
    part = pl.BlockSpec((count, COLS), lambda i: (block, 0))
    return call(
        lambda *refs: attention_backward_kernel(block, *refs),
        [SCALARS] + [part] * 4,
        [half, half, half, (full_shape(8, COLS), INSIDE)],
        [vmem((count, count), FULL)],
        8,
        (lengths, query, key, value, grad_in),
        grid=(1,),
        vmem=20,
    )


def joint_grad_kernel(places, normed, *refs):
    grads, sent, (query_part, key_part, value_part, sems) = refs[:6], refs[6:12], refs[12:]
    parts = (query_part, key_part, value_part)
    count = grads[0].shape[0]
    sides = [jnp.concatenate([g[...] for g in grads[i : i + 3]], axis=1) for i in (0, 3)]
    whole = dot_tn(normed[:count, :], sides[0]) + dot_tn(normed[count:, :], sides[1])
    for index, part in enumerate(parts):
        part[...] = whole[:, index * COLS : (index + 1) * COLS].astype(LOW)
    finished(started(joint_sent_plan(places, sent, parts), sems))


def joint_grad_parts(places, normed, own, other):
    rows, width = normed.shape
    sent = [low_shape(2, 4, 64, COLS), low_shape(2, 2, 128, COLS), low_shape(2, 4, 2, 32, COLS)]
    return call(
        joint_grad_kernel,
        [SCALARS] + [INSIDE] * 7,
        [(s, OUTSIDE) for s in sent for _ in range(2)],
        [pltpu.VMEM((width, COLS), LOW)] * 3 + [pltpu.SemaphoreType.DMA((56,))],
        8,
        (places, normed, *own, *other),
        vmem=30,
    )


def joint_backward_kernel(*refs):
    own, other, mats, outs = refs[:3], refs[3:6], refs[6:9], refs[9:]
    for grads, out in zip((own, other), outs):
        whole = dot_nt(grads[0][...], mats[0][...])
        whole += dot_nt(grads[1][...], mats[1][...])
        whole += dot_nt(grads[2][...], mats[2][...])
        out[...] = whole.astype(out.dtype)


def joint_backward(own, other, mats):
    count, width = own[0].shape[0], mats[0].shape[0]
    return call(
        joint_backward_kernel,
        [INSIDE] * 9,
        [(full_shape(count, width), INSIDE), (low_shape(count, width), INSIDE)],
        [],
        6,
        (*own, *other, *mats),
        vmem=20,
    )


def input_kernel(tokens, part, part_far, middle_grad, vectors, input_grad, sums):
    unit, inverse = unit_of(tokens[...].astype(FULL))
    grad = part[...] + part_far[...].astype(FULL)
    input_grad[...] = middle_grad[...] + norm_backward(grad, unit, inverse, row_of(vectors, 0))
    sums[...] = jnp.zeros_like(sums)
    sums[0:1, :] = jnp.sum(grad * unit, axis=0, keepdims=True)
    sums[1:2, :] = jnp.sum(grad, axis=0, keepdims=True)


def input_backward(tokens, part, part_far, middle_grad, vectors):
    return call(
        input_kernel,
        [INSIDE] * 5,
        [(full_shape(*part.shape), INSIDE), (full_shape(8, part.shape[1]), INSIDE)],
        [],
        5,
        (tokens, part, part_far, middle_grad, vectors),
        vmem=20,
    )


def adam_step(weight, first, second, grad, rate, decay):
    first_new = BETA_ONE * first + (1.0 - BETA_ONE) * grad
    second_new = BETA_TWO * second + (1.0 - BETA_TWO) * grad * grad
    mean_hat = first_new / (1.0 - BETA_ONE**STEP)
    square_hat = second_new / (1.0 - BETA_TWO**STEP)
    fresh = weight - rate * (mean_hat / (jnp.sqrt(square_hat) + ADAM_EPS) + decay * weight)
    return (first_new, second_new, fresh)


def adam_kernel(grad_of, rate, chunks, places, *refs):
    state, refs = refs[:3], refs[3:]
    grads, refs = refs[:-8], refs[-8:]
    outs, (held, results, sems_in, sems_out) = refs[:4], refs[4:]
    coming = [
        started([(a.at[at], held.at[(i, *at)]) for i, a in enumerate(state)], sems_in.at[n])
        for n, at in enumerate(chunks)
    ]
    going = []
    for n, at in enumerate(chunks):
        grad = grad_of(n, places, *grads)
        finished(coming[n])
        results[(0, *at)] = grad
        weight, first, second = (held[(i, *at)] for i in range(3))
        new = adam_step(weight, first, second, grad, rate, MATRIX_DECAY)
        for i, value in enumerate(new):
            results[(1 + i, *at)] = value
        going += started(
            [(results.at[(i, *at)], out.at[at]) for i, out in enumerate(outs)], sems_out.at[n]
        )
    finished(going)


def adam(grad_of, rate, chunks, state, grads, places):
    shape = state[0].shape
    return pl.pallas_call(
        lambda *refs: adam_kernel(grad_of, rate, chunks, *refs),
        grid=(1,),
        in_specs=[SCALARS]
        + [OUTSIDE] * 3
        + [pl.BlockSpec((g[1], COLS), lambda i, at=g[2]: (at, 0)) for g in grads],
        out_specs=[OUTSIDE] * 4,
        out_shape=[full_shape(*shape)] * 4,
        scratch_shapes=[pltpu.VMEM((3, *shape), FULL), pltpu.VMEM((4, *shape), FULL)]
        + [pltpu.SemaphoreType.DMA((len(chunks), 3)), pltpu.SemaphoreType.DMA((len(chunks), 4))],
        compiler_params=pltpu.CompilerParams(vmem_limit_bytes=24 << 20),
        cost_estimate=pl.CostEstimate(
            flops=6 * FLOPS_PER_US, bytes_accessed=30 * state[0].size, transcendentals=0
        ),
    )(places, *state, *(g[0] for g in grads))


def by_core(places, both, far):
    own = places[13] == 0
    both, far = both.astype(FULL), far.astype(FULL)
    return jnp.where(own, both, far), jnp.where(own, far, both)


def columns_of(width, count):
    return [(slice(None), slice(n * width, (n + 1) * width)) for n in range(count)]


def rows_each(height, count):
    return [(slice(n * height, (n + 1) * height), slice(None)) for n in range(count)]


def adam_joint(places, state, sums):
    def grad_of(n, places, both, far):
        rows = slice(128 * n, 128 * (n + 1))
        return jnp.concatenate(by_core(places, both[rows, :], far[rows, :]), axis=1)

    grads = [(a, 384, 0) for a in sums]
    return adam(grad_of, MATRIX_RATE, columns_of(2 * COLS, 3), state, grads, places)


def adam_expand(places, state, sums):
    def grad_of(n, places, both, far):
        rows = slice(128 * n, 128 * (n + 1))
        zero, one = by_core(places, both[rows, :], far[rows, :])
        return jnp.concatenate(
            [zero[:, :256], one[:, :256], zero[:, 256:], one[:, 256:]], axis=1
        )

    grads = [(a, 512, 0) for a in sums]
    return adam(grad_of, MATRIX_RATE, columns_of(2 * COLS, 4), state, grads, places)


def adam_reduce(places, state, sums):
    def grad_of(n, places, left, right, far_left, far_right):
        rows = slice(128 * (n % 2), 128 * (n % 2 + 1))
        own = places[13] == n // 2
        return jnp.concatenate(
            [
                jnp.where(own, left[rows, :].astype(FULL), far_left[rows, :].astype(FULL)),
                jnp.where(own, right[rows, :].astype(FULL), far_right[rows, :].astype(FULL)),
            ],
            axis=1,
        )

    grads = [(a, 256, at) for a in sums for at in (2, 3)]
    return adam(grad_of, MATRIX_RATE, rows_each(128, 4), state, grads, places)


def adam_output(places, state, sums):
    def grad_of(n, places, both, far):
        def rows(a):
            return jnp.concatenate(
                [
                    jnp.concatenate([a[64 * q : 64 * q + 32, :], a[64 * q + 32 : 64 * q + 64, :]], axis=1)
                    for q in (2 * n, 2 * n + 1)
                ]
            ).astype(FULL)

        return jnp.where(places[13] == places[12], rows(both), rows(far))

    grads = [(a, 256, 4) for a in sums]
    return adam(grad_of, OUTPUT_RATE, rows_each(64, 2), state, grads, places)


def per_device(
    tokens,
    cotangent,
    lengths,
    joint_weight,
    joint_first,
    joint_second,
    output_weight,
    output_first,
    output_second,
    expand_weight,
    expand_first,
    expand_second,
    reduce_weight,
    reduce_first,
    reduce_second,
    vector_weight,
    vector_first,
    vector_second,
):
    me = coordinates()
    core = me["core"]
    places = places_of(me)
    across = flip("core", 1)
    width = tokens.shape[1]
    units = 256

    half, block, rest_half, rest_y = cast(
        places, joint_weight, vector_weight, expand_weight, reduce_weight, output_weight
    )
    joint_x, joint_y, along_x, along_y, along_z, far = gather_first(
        me, half, block, rest_half, rest_y, [send(a, across) for a in (tokens, cotangent, lengths)]
    )
    tokens, cotangent = (tokens, far[0]), (cotangent, far[1])
    lengths = jnp.concatenate([lengths, far[2]])

    normed_one, query, key, value, vectors, *joint_mats = joint(
        places, *tokens, joint_x, joint_y
    )
    along_z.append(send(after(along_z[1], query), turn("z", 1)))
    along_y.append(send(after(along_y[0], query), turn("y", 1)))
    own = attention(0, lengths, after(query, along_y[1], *along_z[1:3]), key, value)
    along_x.append(send(after(along_x[1], own), turn("x", 1)))
    along_y.append(send(after(along_y[1], own), turn("y", 1)))
    other = attention(1, lengths, after(query, along_x[1]), key, value)
    attended = (own, other)
    branch, out_mat = output(places, own, after(other, *along_x[2:], *along_y[2:]), along_z)
    branch_far = send(branch, across)
    *sent, middle, layer_own, layer_other, normed_two_part, up_bias_grad = forward_backward(
        places, lengths, tokens, cotangent, branch, branch_far, vectors,
        [*along_x, *along_y, *along_z],
    )
    part_far = send(normed_two_part, across)
    layer_out = (layer_own + send(layer_other, across).astype(FULL)).astype(LOW)

    out_one, out_two, middle_grad, attended_grad, two_sums = output_backward(
        places, lengths, cotangent, middle, normed_two_part, part_far, vectors, attended, out_mat
    )
    rest = total(me, [*sent, out_one, out_two], 32, 3, 0)
    next(rest)
    *own_grads, own_sums = attention_backward(0, lengths, query, key, value, attended_grad)
    mark = rest.send(own_grads[0])
    *other_grads, other_sums = attention_backward(
        1, lengths, query, key, value, after(attended_grad, mark)
    )
    mark = rest.send((other_grads[0], None))
    sent = joint_grad_parts(places, after(normed_one, mark), own_grads, other_grads)
    joint_rows = total(me, sent, 0, 1, 32)
    next(joint_rows)
    mark = rest.send(sent[0])
    part_own, part_other = joint_backward(
        (after(own_grads[0], mark), *own_grads[1:]), other_grads, joint_mats
    )
    part_far = send(part_other, across)
    mark = rest.send(part_own)
    mark = joint_rows.send(mark)
    input_grad, one_sums = input_backward(
        tokens[0], after(part_own, mark), part_far, middle_grad, vectors
    )

    is_core = (jnp.arange(2) == core).astype(FULL)

    def own_half(values):
        return (is_core[:, None] * values[None]).reshape(1, -1)

    head_sums = own_sums + other_sums
    up_mine = is_core[None, :, None] * up_bias_grad.reshape(8, 1, units)
    vector_local = jnp.concatenate(
        [
            one_sums[:2],
            own_half(head_sums[0]),
            own_half(head_sums[1]),
            two_sums[:3],
            up_mine.reshape(4, width),
            two_sums[3:4],
            jnp.zeros((4, width), FULL),
        ],
        axis=0,
    ).astype(LOW)
    vector_local = rows_of(vector_local[:, :COLS], vector_local[:, COLS:])

    mark = joint_rows.send((one_sums, vector_local))
    mark = rest.send(mark)
    for _ in range(3):
        mark = rest.send(mark)
        mark = joint_rows.send(mark)
    mark = joint_rows.send(mark)
    mark = rest.send(mark)
    mark = joint_rows.send(mark)
    one, two, _ = next(rest)
    expand = adam_expand(places, (expand_weight, expand_first, expand_second), (one, two))
    mark = joint_rows.send(expand[0])
    output_state = adam_output(
        places, (output_weight, output_first, output_second), (after(one, mark), two)
    )
    mark = joint_rows.send(output_state[0])
    reduce = adam_reduce(
        places, (reduce_weight, reduce_first, reduce_second), (after(one, mark), two)
    )
    one, two, extra = next(joint_rows)
    joint_state = adam_joint(
        places, (joint_weight, joint_first, joint_second), (after(one, reduce[0]), two)
    )
    vector_grad = lax.dynamic_slice(
        jnp.concatenate([extra[:12], extra[16:28]], axis=1).astype(FULL),
        (0, 128 * lax.axis_index("shard")),
        (12, 128),
    )
    vector_state = (vector_grad,) + adam_step(
        vector_weight, vector_first, vector_second, vector_grad, VECTOR_RATE, 0.0
    )
    states = zip(joint_state, output_state, expand, reduce, vector_state)
    return (layer_out, input_grad, *(a for kind in states for a in kind))


def solution(mesh):
    rows, columns, split = P("shard", None), P(None, "shard"), P(("wide", "shard"), None)
    state = (rows, rows, rows, rows, columns)
    return jax.shard_map(
        per_device,
        mesh=mesh,
        in_specs=(split, split, split) + (rows,) * 12 + (columns,) * 3,
        out_specs=(split, split) + state * 4,
        check_vma=False,
    )
```

```python
import jax
import jax.numpy as jnp
from jax import lax
from jax.experimental import pallas as pl
from jax.experimental.pallas import tpu as pltpu
from jax.sharding import PartitionSpec as P

HEAD_DIM = 64
STEP = 10


ROOT_TWO_PI = 0.7978845608028654
CUBIC = 0.044715
BETA_ONE = 0.9
BETA_TWO = 0.999
ADAM_EPS = 1e-08
MATRIX_RATE = 0.03
OUTPUT_RATE = 0.1
VECTOR_RATE = 0.2
MATRIX_DECAY = 0.1

LOW = jnp.bfloat16
FULL = jnp.float32
AXES = ("wide", "shard")
SIZES = (4, 2, 2, 2, 4)
COLS = 512
FLOPS_PER_US = 1_150_000_000


def coordinates():
    wide, shard = lax.axis_index("wide"), lax.axis_index("shard")
    z, xl, core = wide // 4, (wide // 2) % 2, wide % 2
    xh, y = shard // 4, shard % 4
    return {"z": z, "x": 2 * xh + xl, "y": y, "xl": xl, "xh": xh, "core": core}


def route(partner):
    pairs = []
    for source in range(128):
        rest, places = source, []
        for size in reversed(SIZES):
            places.append(rest % size)
            rest //= size
        y, xh, core, xl, z = places
        target = partner({"z": z, "x": 2 * xh + xl, "y": y, "core": core})
        flat = 0
        for place, size in zip(
            (target["z"], target["x"] % 2, target["core"], target["x"] // 2, target["y"]), SIZES
        ):
            flat = flat * size + place
        pairs.append((source, flat))
    return pairs


def flip(axis, bits):
    return route(lambda at: {**at, axis: at[axis] ^ bits})


def turn(axis, step):
    return route(lambda at: {**at, axis: at[axis] ^ (1 if (at["core"] + step) % 2 == 0 else 3)})


def send(value, pairs):
    return lax.ppermute(value, AXES, pairs)


def added(*terms):
    return sum(term.astype(FULL) for term in terms).astype(LOW)


def orders(me, axis):
    here = me[axis]
    one = jnp.where(me["core"] == 0, 1, 3)
    return [here, here ^ one, here ^ (4 - one), here ^ 2]


def places_of(me):
    return jnp.stack(
        orders(me, "x")
        + orders(me, "y")
        + orders(me, "z")
        + [me["xh"], me["core"], me["xl"], me["z"]]
    ).astype(jnp.int32)


def after(value, *others):
    return lax.optimization_barrier((value, *others))[0]


def rows_of(*parts):
    return jnp.concatenate([p.reshape(-1, COLS) for p in parts])


def main_phase(block, axis, gate, late=False):
    first, second = send(block, turn(axis, 0)), send(gated(block, gate if late else None), turn(axis, 1))
    return [block, first, second, send(after(first, gate), turn(axis, 1))]


def pack_kernel(places, block, other, half, second, first, again):
    for out in (first, again):
        out[:208, :] = block[:208, :]
        out[208:416, :] = other[:208, :]
    again[416:512, :] = half[...]
    again[512:608, :] = second[...]
    own = places[13] == places[12]
    for p, held in enumerate((block, other)):
        at = 416 + 96 * p
        first[at : at + 64, :] = held[208:272, :]
        rows = slice(272 + 32 * p, 304 + 32 * p)
        first[at + 64 : at + 96, :] = jnp.where(own, block[rows, :], other[rows, :])


def pack(places, *arrays):
    return call(
        pack_kernel,
        [SCALARS] + [INSIDE] * 4,
        [(low_shape(608, COLS), INSIDE)] * 2,
        [],
        1,
        (places, *arrays),
        vmem=8,
    )


def gather_first(places, half, block, rest_half, rest_y, exchanged):
    size = half.shape[0]
    other, second, *early = lax.optimization_barrier(
        (send(block, flip("x", 3)), send(half, turn("y", 0)), *exchanged[:2])
    )
    own_y, both = pack(places, block, other, half, second)
    first_y, second_y = send(own_y, turn("y", 0)), send(both, turn("y", 1))
    rest_other = send(after(rest_y, other), flip("x", 3))
    first_y, second_y, rest_other, *late = lax.optimization_barrier(
        (first_y, second_y, rest_other, *exchanged[2:])
    )
    plane = rows_of(half, second, second_y[416:]).reshape(4, size, COLS)
    first_x, second_x = send(plane, turn("x", 0)), send(plane, turn("x", 1))
    third_y = send(rows_of(first_y[:416], own_y[416:], first_y[416:]), turn("y", 1))
    rest_near = send(after(rest_half, first_y), turn("y", 0))
    first_x, second_x, third_y, rest_near = lax.optimization_barrier(
        (first_x, second_x, third_y, rest_near)
    )
    third_x = send(first_x, turn("x", 1))
    here = rows_of(rest_half, rest_near)
    there = send(here, turn("y", 1))
    plane_z = rows_of(own_y[416:], first_y[416:], third_y[416:]).reshape(4, 2, 96, COLS)
    pair_y = jnp.stack([rest_y, rest_other])
    along_z = [plane_z, send(plane_z, turn("z", 0)), send(plane_z, turn("z", 1))]
    along_y = [pair_y, send(after(pair_y, third_y), turn("y", 0))]
    third_x, there = lax.optimization_barrier((third_x, there))
    plane_x = rows_of(here, there).reshape(4, -1, COLS)
    along_x = [plane_x, send(plane_x, turn("x", 0)), send(plane_x, turn("x", 1))]
    joint_x = [plane, first_x, second_x, third_x]
    joint_y = [own_y, first_y, second_y, third_y]
    return joint_x, joint_y, along_x, along_y, along_z, early + late


def added_all(sums, steps=2):
    terms, specs, outs, out_specs = [], [], [], []
    for group in sums:
        rows = min(a.size for a, _ in group) // COLS
        rows = rows // 2 if len(group) == 2 else rows
        for array, which in group:
            terms.append(array.reshape(-1, COLS))
            specs.append(
                pl.BlockSpec((rows // steps, COLS), lambda i, at=which * steps: (at + i, 0))
            )
        outs.append(low_shape(rows, COLS))
        out_specs.append(pl.BlockSpec((rows // steps, COLS), lambda i: (i, 0)))

    def kernel(*refs):
        at = 0
        for group, out in zip(sums, refs[len(terms) :]):
            out[...] = added(*(ref[...] for ref in refs[at : at + len(group)]))
            at += len(group)

    return pl.pallas_call(
        kernel,
        grid=(steps,),
        in_specs=specs,
        out_specs=out_specs,
        out_shape=outs,
        compiler_params=pltpu.CompilerParams(vmem_limit_bytes=60 << 20),
        cost_estimate=pl.CostEstimate(
            flops=3 * FLOPS_PER_US, bytes_accessed=6 * sum(o.size for o in outs), transcendentals=0
        ),
    )(*terms)


def gated(value, gate):
    return value if gate is None else after(value, gate)


def total(me, raw, out_rows, units, extra_rows):
    axes = "xyz"
    parts = [raw[:2], raw[2:4], raw[4:]]
    far = [send(away, turn(axis, 1)) for (_, away), axis in zip(parts, axes)]
    gate = yield
    far = list(far if gate is None else lax.optimization_barrier((*far, gate))[:-1])
    keeps = [keep for keep, _ in parts]
    near = added_all([[(k, 1), (f, 1)] for k, f in zip(keeps, far)])
    near = lax.optimization_barrier([n.reshape(k.shape[1:]) for n, k in zip(near, keeps)])
    again = [send(n, turn(axis, 0)) for n, axis in zip(near, axes)]
    gate, extra, out = yield near[2]
    again = lax.optimization_barrier((*again, gate))[:-1]
    along = added_all([[(k, 0), (f, 0), (a, 0)] for k, f, a in zip(keeps, far, again)])
    along_x, along_y, along_z = lax.optimization_barrier(
        [a.reshape(k.shape[1:]) for a, k in zip(along, keeps)]
    )
    if out_rows:
        along_z = jnp.concatenate([along_z, out], axis=2)
    size_x, size_y = along_x.shape[1], along_y.shape[1] // 2
    size_z = (along_z.shape[2] - out_rows) // 2

    def with_extra(*parts):
        return rows_of(*parts, extra) if extra_rows else rows_of(*parts)

    def split(rows, *sizes):
        at, parts = 0, []
        for size in sizes:
            parts.append(rows[at : at + size])
            at += size
        return parts

    plane = jnp.concatenate([along_x, along_z.reshape(4, -1, COLS)], axis=1)
    size = plane.shape[1]
    far = send(with_extra(plane[2:]), turn("y", 1))
    gate = yield plane
    far, kept = gated(far, gate), plane[:2]
    near = added(kept[1], far[size : 2 * size])
    if extra_rows:
        extra = added(extra, far[2 * size :])
    again = send(with_extra(near), turn("y", 0))
    gate = yield near
    again = gated(again, gate)
    plane = added(kept[0], far[:size], again[:size])
    if extra_rows:
        extra = added(extra, again[size:])
    half, pair = plane[:size_x], plane[size_x:].reshape(2, 2 * size_z + out_rows, COLS)
    out = pair[:, 2 * size_z :].reshape(-1, COLS)
    pieces = jnp.concatenate(
        [along_y.reshape(4, size_y, COLS), pair[:, : 2 * size_z].reshape(4, size_z, COLS)], axis=1
    )
    size = size_y + size_z
    pieces = [
        lax.dynamic_index_in_dim(pieces, ((k // 2) ^ me["xh"]) * 2 + k % 2, 0, keepdims=False)
        for k in orders(me, "x")
    ]
    far = send(with_extra(pieces[2], pieces[3], out), turn("x", 1))
    gate = yield plane
    far = gated(far, gate)
    first, second, far_out, far_extra = split(far, size, size, 2 * out_rows, extra_rows)
    sums = added(rows_of(pieces[1], out), rows_of(second, far_out))
    if extra_rows:
        extra = added(extra, far_extra)
    again = send(with_extra(sums), turn("x", 0))
    gate = yield sums
    near, out, far_extra = split(gated(again, gate), size, 2 * out_rows, extra_rows)
    sums = rows_of(added(pieces[0], first, near), added(sums[size:], out))
    if extra_rows:
        extra = added(extra, far_extra)
    flat, block = rows_of(half, sums[:size_y]), sums[size_y:]
    size, size_block = flat.shape[0], block.shape[0]
    far = send(with_extra(flat, block), turn("z", 0))
    gate = yield sums
    sums, other, far_extra = split(gated(far, gate), size, size_block, extra_rows)
    flat = added(flat, sums)
    if extra_rows:
        extra = added(extra, far_extra)
    blocks = rows_of(block, other)
    far = send(with_extra(flat, blocks), turn("z", 1))
    gate = yield flat
    sums, other, far_extra = split(gated(far, gate), size, 2 * size_block, extra_rows)
    flat = added(flat, sums)
    if extra_rows:
        extra = added(extra, far_extra)
    blocks = rows_of(blocks, other).reshape(4, size_block, COLS)
    where = orders(me, "z")
    ordered = jnp.stack(
        [
            sum(jnp.where(where[k] == place, blocks[k], 0) for k in range(4)).astype(LOW)
            for place in range(4)
        ]
    )
    mine = rows_of(flat, ordered[:, :size_z])
    far = send(mine, flip("x", 1))
    gate = yield mine
    far = gated(far, gate)

    def whole(groups, first, last):
        a, b = (rows[first:last].reshape(groups, -1, COLS) for rows in (mine, far))
        both = jnp.where(me["xl"] == 0, jnp.stack([a, b], axis=1), jnp.stack([b, a], axis=1))
        return both.reshape(-1, COLS)

    both = rows_of(
        whole(units, 0, size_x), whole(1, size_x, size), whole(4, size, mine.shape[0]),
        ordered[:, size_z:],
    )
    far = send(with_extra(both), flip("core", 1))
    yield both
    rows = both.shape[0]
    if extra_rows:
        extra = added(extra, far[rows:])
        far = far[:rows]
    yield both, far, extra


def rows_at(start, size):
    return pl.ds(pl.multiple_of(start, size), size)


def joint_plan(places, along_x, along_y, mats):
    query, key, value, vectors = mats
    pairs = []
    for ky in range(4):
        y = places[4 + ky]
        for kx in range(4):
            x = places[kx]
            shard, half = (x // 2) * 4 + y, x % 2
            source = along_x[kx].at[ky]
            pairs.append(
                (source.at[pl.ds(0, 64)], query.at[rows_at(shard * 128 + half * 64, 64)])
            )
            pairs.append(
                (source.at[pl.ds(64, 32)], value.at[rows_at(shard * 128 + half * 32, 32)])
            )
        for p in range(2):
            shard = (places[12] ^ p) * 4 + y
            source, at = along_y[ky], p * 208
            pairs.append((source.at[pl.ds(at, 128)], key.at[rows_at(shard * 128, 128)]))
            pairs.append((source.at[pl.ds(at + 128, 64)], value.at[rows_at(shard * 128 + 64, 64)]))
            pairs.append(
                (
                    source.at[pl.ds(at + 192, 16), pl.ds(0, 128)],
                    vectors.at[:, rows_at(shard * 128, 128)],
                )
            )
    return pairs


def joint_sent_plan(places, raw, parts):
    query, key, value = parts
    pairs = []
    for ky in range(4):
        y = places[4 + ky]
        for kx in range(4):
            x = places[kx]
            start = ((x // 2) * 4 + y) * 128 + (x % 2) * 64
            pairs.append((query.at[rows_at(start, 64)], raw[0 + kx // 2].at[kx % 2, ky]))
        for p in range(2):
            shard = (places[12] ^ p) * 4 + y
            pairs.append((key.at[rows_at(shard * 128, 128)], raw[2 + ky // 2].at[ky % 2, p]))
            for kz in range(4):
                start = shard * 128 + places[8 + kz] * 32
                pairs.append((value.at[rows_at(start, 32)], raw[4 + kz // 2].at[kz % 2, ky, p]))
    return pairs


def up_plan(places, at_x, at_y, at_z, mats):
    up, down_one, down_two = mats
    pairs = []
    for ky in range(4):
        y = places[4 + ky]
        for kx in range(4):
            x = places[kx]
            start = ((x // 2) * 4 + y) * 128 + (x % 2) * 64
            for j in range(3):
                source = at_x(kx).at[ky, pl.ds(64 * j, 64)]
                pairs.append((source, up.at[j, rows_at(start, 64)]))
        for p in range(2):
            shard = (places[12] ^ p) * 4 + y
            source = at_y(ky).at[p]
            pairs.append((source.at[pl.ds(0, 128)], up.at[3, rows_at(shard * 128, 128)]))
            pairs.append((source.at[pl.ds(128, 256)], down_one.at[rows_at(shard * 256, 256)]))
            for kz in range(4):
                start = shard * 256 + places[8 + kz] * 64
                source = at_z(kz).at[ky, p, pl.ds(0, 64)]
                pairs.append((source, down_two.at[rows_at(start, 64)]))
    return pairs


def up_kind(index):
    index %= 24
    if index < 12:
        return index % 3
    return 3 if (index - 12) % 6 == 0 else None


def up_shard(places, index):
    ky, index = divmod(index, 24)
    return (places[12] ^ ((index - 12) // 6)) * 4 + places[4 + ky]


def out_plan(places, at_z, first, mat):
    pairs = []
    for ky in range(4):
        for kz in range(4):
            start = places[4 + ky] * 128 + places[8 + kz] * 32
            for p in range(2):
                source = at_z(kz).at[ky, p, pl.ds(first, 32)]
                pairs.append((source, mat.at[p, rows_at(start, 32)]))
    return pairs


def two_of(arrays):
    return lambda k: arrays[k // 2].at[k % 2]


def started(pairs, sems):
    all_of_them = [pltpu.make_async_copy(a, b, sems.at[i]) for i, (a, b) in enumerate(pairs)]
    for copy in all_of_them:
        copy.start()
    return all_of_them


def finished(all_of_them):
    for copy in all_of_them:
        copy.wait()


def turned(pairs):
    return [(b, a) for a, b in pairs]


def low_shape(*shape):
    return jax.ShapeDtypeStruct(shape, LOW)


def full_shape(*shape):
    return jax.ShapeDtypeStruct(shape, FULL)


SCALARS = pl.BlockSpec(memory_space=pltpu.SMEM)
INSIDE = pl.BlockSpec(memory_space=pltpu.VMEM)
OUTSIDE = pl.BlockSpec(memory_space=pl.ANY)


def call(kernel, in_specs, outs, scratch, length, args, grid=(), vmem=60):
    shapes, specs = [o[0] for o in outs], [o[1] for o in outs]
    moved = sum(a.size * a.dtype.itemsize for a in (*args, *shapes))
    return pl.pallas_call(
        kernel,
        grid=grid,
        out_shape=shapes,
        in_specs=in_specs,
        out_specs=specs,
        scratch_shapes=scratch,
        compiler_params=pltpu.CompilerParams(vmem_limit_bytes=vmem << 20),
        cost_estimate=pl.CostEstimate(
            flops=length * FLOPS_PER_US, bytes_accessed=moved, transcendentals=0
        ),
    )(*args)


def gelu_both(upward):
    square = upward * upward
    tangent = jnp.tanh(ROOT_TWO_PI * upward * (1.0 + CUBIC * square))
    half = 0.5 * (1.0 + tangent)
    slope = half + 0.5 * upward * (1.0 - tangent * tangent) * ROOT_TWO_PI * (
        1.0 + 3.0 * CUBIC * square
    )
    return upward * half, slope


def dot(a, b):
    return jnp.dot(a, b, preferred_element_type=FULL)


def dot_nt(a, b):
    return lax.dot_general(a, b, (((1,), (1,)), ((), ())), preferred_element_type=FULL)


def dot_tn(a, b):
    return lax.dot_general(a, b, (((0,), (0,)), ((), ())), preferred_element_type=FULL)


def unit_of(values):
    center = values - jnp.mean(values, axis=-1, keepdims=True)
    inverse = lax.rsqrt(jnp.mean(center * center, axis=-1, keepdims=True) + 1e-05)
    return center * inverse, inverse


def norm_backward(grad_out, unit, inverse, gain):
    scaled = grad_out * gain
    return inverse * (
        scaled
        - jnp.mean(scaled, axis=-1, keepdims=True)
        - unit * jnp.mean(scaled * unit, axis=-1, keepdims=True)
    )


def row_of(vectors, row):
    return vectors[row : row + 1, :].astype(FULL)


def own_columns(full, core, size):
    groups = full.shape[1] // (2 * size)
    first = jnp.concatenate(
        [full[:, (2 * g) * size : (2 * g + 1) * size] for g in range(groups)], axis=1
    )
    second = jnp.concatenate(
        [full[:, (2 * g + 1) * size : (2 * g + 2) * size] for g in range(groups)], axis=1
    )
    return jnp.where(core == 0, first, second)


def barred(lengths, block, first, height, span):
    shape = (height, span)
    rows = lax.broadcasted_iota(jnp.int32, shape, 0) + first
    keys = lax.broadcasted_iota(jnp.int32, shape, 1)
    opening = lengths[block, 0]
    filled = opening + lengths[block, 1]
    begin = jnp.where(rows < opening, 0, jnp.where(rows < filled, opening, rows))
    return jnp.where((keys <= rows) & (keys >= begin), 0.0, -1e30)


TILE = 128


def cast_kernel(
    places, weight, vector, expand, reduce, output, half, block, rest_half, rest_y,
    held, rest, wide, padded, sems,
):
    core, xl, z = places[13], places[14], places[15]

    def cols(which):
        return rows_at(which * 2 * COLS + core * COLS, COLS)

    first = [
        (weight.at[rows_at(xl * 64, 64), cols(0)], held.at[pl.ds(0, 64)]),
        (weight.at[rows_at(xl * 32, 32), cols(2)], held.at[pl.ds(64, 32)]),
        (weight.at[:, cols(1)], held.at[pl.ds(96, 128)]),
        (weight.at[pl.ds(64, 64), cols(2)], held.at[pl.ds(224, 64)]),
        (
            reduce.at[rows_at(core * 256 + z * 64, 64), pl.ds(COLS, COLS)],
            held.at[pl.ds(288, 64)],
        ),
        (output.at[rows_at(z * 32, 32)], wide),
    ]
    second = [(reduce.at[rows_at(core * 256, 256), pl.ds(0, COLS)], rest.at[pl.ds(320, 256)])]
    for s in range(8):
        j, right = s // 2, (s % 2) * 256
        at = rows_at(s * 512 + core * 256, 256)
        rows, size = (rows_at(xl * 64, 64), 64) if j < 3 else (pl.ds(0, 128), 128)
        second.append((expand.at[rows, at], rest.at[pl.ds(64 * j, size), pl.ds(right, 256)]))
    first = started(first, sems.at[pl.ds(0, 6)])
    second = started(second, sems.at[pl.ds(6, 9)])
    padded[...] = jnp.zeros_like(padded)
    padded[: vector.shape[0], : vector.shape[1]] = vector[...]
    block[192:208, :] = padded[...].astype(LOW)
    finished(first)
    half[...] = held[:96].astype(LOW)
    block[:192, :] = held[96:288].astype(LOW)
    block[208:272, :] = held[288:].astype(LOW)
    block[272:304, :] = wide[:, :COLS].astype(LOW)
    block[304:336, :] = wide[:, COLS:].astype(LOW)
    finished(second)
    rest_half[...] = rest[:192].astype(LOW)
    rest_y[...] = rest[192:].astype(LOW)


def cast(places, *arrays):
    outs = [low_shape(96, COLS), low_shape(336, COLS), low_shape(192, COLS), low_shape(384, COLS)]
    vmem = pltpu.VMEM
    return call(
        cast_kernel,
        [SCALARS, OUTSIDE, INSIDE, OUTSIDE, OUTSIDE, OUTSIDE],
        [(shape, INSIDE) for shape in outs],
        [vmem((352, COLS), FULL), vmem((576, COLS), FULL), vmem((32, 2 * COLS), FULL)]
        + [vmem((16, COLS), FULL), pltpu.SemaphoreType.DMA((15,))],
        3,
        (places, *arrays),
        vmem=60,
    )


def joint_kernel(places, own, other, *refs):
    along_x, along_y, refs = refs[:4], refs[4:8], refs[8:]
    normed, query, key, value, vectors, query_mat, key_mat, value_mat, sems = refs
    mats = (query_mat, key_mat, value_mat, vectors)
    finished(started(joint_plan(places, along_x, along_y, mats), sems))
    gain, shift = row_of(vectors, 0), row_of(vectors, 1)
    core = places[13]
    query_bias = own_columns(row_of(vectors, 2), core, COLS)
    value_bias = own_columns(row_of(vectors, 3), core, COLS)
    count = own.shape[0]
    for block, tokens in enumerate((own, other)):
        rows = pl.ds(block * count, count)
        unit, _ = unit_of(tokens[...].astype(FULL))
        low = (unit * gain + shift).astype(LOW)
        normed[rows, :] = low
        query[rows, :] = ((dot(low, query_mat[...]) + query_bias).astype(LOW) * 0.125).astype(LOW)
        key[rows, :] = dot(low, key_mat[...]).astype(LOW)
        value[rows, :] = (dot(low, value_mat[...]) + value_bias).astype(LOW)


def joint(places, own, other, along_x, along_y):
    count, width = own.shape
    rows = 2 * count
    mat, half = (low_shape(width, COLS), INSIDE), (low_shape(rows, COLS), INSIDE)
    return call(
        joint_kernel,
        [SCALARS, INSIDE, INSIDE] + [OUTSIDE] * 8,
        [(low_shape(rows, width), INSIDE), half, half, half]
        + [(low_shape(16, width), INSIDE), mat, mat, mat],
        [pltpu.SemaphoreType.DMA((56,))],
        8,
        (places, own, other, *along_x, *along_y),
        vmem=24,
    )


def two_by_two(values, lane):
    return jnp.concatenate([jnp.where(lane, values, 0), jnp.where(lane, 0, values)], axis=0)


def probabilities(stacked, keys, bar):
    scores = dot_nt(stacked, keys) + jnp.concatenate([bar, bar], axis=0)
    probs = jnp.exp(scores - jnp.max(scores, axis=-1, keepdims=True))
    return probs * (1.0 / jnp.sum(probs, axis=-1, keepdims=True))


def attention_kernel(block, lengths, query, key, value, attended, mask):
    count = query.shape[0]
    mask[...] = barred(lengths, block, 0, count, count)
    lane = lax.broadcasted_iota(jnp.int32, (count, TILE), 1) < HEAD_DIM
    for index in range(COLS // TILE):
        cols = pl.ds(index * TILE, TILE)
        probs = probabilities(two_by_two(query[:, cols], lane), key[:, cols], mask[...])
        out = dot(probs.astype(LOW), value[:, cols])
        attended[:, cols] = jnp.where(lane, out[:count], out[count:]).astype(LOW)


def attention(block, lengths, query, key, value):
    count = query.shape[0] // 2
    return call(
        lambda *refs: attention_kernel(block, *refs),
        [SCALARS] + [pl.BlockSpec((count, COLS), lambda i: (block, 0))] * 3,
        [(low_shape(count, COLS), INSIDE)],
        [pltpu.VMEM((count, count), FULL)],
        5,
        (lengths, query, key, value),
        grid=(1,),
        vmem=20,
    )[0]


def output_kernel(places, own, other, *refs):
    raw, (branch, out_mat, sems) = refs[:4], refs[4:]
    finished(started(out_plan(places, lambda k: raw[k], 64, out_mat), sems))
    count = own.shape[0]
    for block, attended in enumerate((own, other)):
        for half in range(2):
            branch[block * count : (block + 1) * count, half * COLS : (half + 1) * COLS] = dot(
                attended[...], out_mat[half]
            ).astype(LOW)


def output(places, own, other, raw):
    rows, local = 2 * own.shape[0], own.shape[1]
    return call(
        output_kernel,
        [SCALARS, INSIDE, INSIDE] + [OUTSIDE] * 4,
        [(low_shape(rows, 2 * COLS), INSIDE), (low_shape(2, local, COLS), INSIDE)],
        [pltpu.SemaphoreType.DMA((32,))],
        5,
        (places, own, other, *raw),
        vmem=14,
    )


def forward_backward_kernel(
    places, lengths, own, other, arriving_own, arriving_other, branch, branch_far, vectors, *refs
):
    raw, refs = refs[:12], refs[12:]
    sent, refs = refs[:6], refs[6:]
    (middle, layer_own, layer_other, normed_grad, bias_grad,
     up, down_one, down_two, up_grad, one_grad, two_grad,
     tokens, near, far, held, normed, arriving, layer_sum, normed_sum, active, up_low,
     row_sems, sems, sems_out) = refs
    count = own.shape[0]
    blocks = [pl.ds(0, count), pl.ds(count, count)]
    rows_in = []
    for block, (token, cotangent) in enumerate(((own, arriving_own), (other, arriving_other))):
        here, there = blocks[block], blocks[1 - block]
        pairs = [
            (token, tokens.at[here]),
            (branch.at[here], near.at[here]),
            (branch_far.at[there], far.at[here]),
            (cotangent, arriving.at[here]),
        ]
        rows_in.append(started(pairs, row_sems.at[pl.ds(4 * block, 4)]))
    views = [lambda k, a=axis: raw[4 * a + k] for axis in range(3)]
    plan = up_plan(places, *views, (up, down_one, down_two))
    copies = [pltpu.make_async_copy(a, b, sems.at[i]) for i, (a, b) in enumerate(plan)]
    kinds = [up_kind(index) for index in range(len(copies))]
    for wanted in (0, None, 1, 2, 3):
        for copy, kind in zip(copies, kinds):
            if kind == wanted:
                copy.start()
    gain, shift = row_of(vectors, 5), row_of(vectors, 6)
    rows_out = []
    for block, here in enumerate(blocks):
        finished(rows_in[block])
        summed = near[here, :].astype(FULL) + far[here, :].astype(FULL)
        value = tokens[here, :].astype(FULL) + summed + row_of(vectors, 4)
        held[here, :] = value
        rows_out += started([(held.at[here], middle.at[here])], row_sems.at[pl.ds(8 + block, 1)])
        unit, _ = unit_of(value)
        normed[here, :] = (unit * gain + shift).astype(LOW)
        slots = lax.broadcasted_iota(jnp.int32, value.shape, 0)
        live = slots < lengths[block, 0] + lengths[block, 1]
        arriving[here, :] = jnp.where(live, arriving[here, :], 0)
    core = places[13]
    biases = jnp.concatenate(
        [own_columns(row_of(vectors, 7 + k), core, 256) for k in range(4)], axis=0
    )
    finished(copies)
    views = [two_of(sent[2 * axis : 2 * axis + 2]) for axis in range(3)]
    plan = turned(up_plan(places, *views, (up_grad, one_grad, two_grad)))
    copies_out = [pltpu.make_async_copy(a, b, sems_out.at[i]) for i, (a, b) in enumerate(plan)]

    def of_chunk(j, action, list_of_copies):
        for index, (copy, kind) in enumerate(zip(list_of_copies, kinds)):
            if kind == j:
                action(copy)
            elif kind is None:

                @pl.when(up_shard(places, index) // 2 == j)
                def _(copy=copy):
                    action(copy)

    for j in range(up.shape[0]):
        hidden = pl.ds(j * COLS, COLS)
        upward = dot(normed[...], up[j]) + biases[j : j + 1]
        act, slope = gelu_both(upward)
        active[...] = act.astype(LOW)
        layer_one, layer_two = dot(active[...], down_one[hidden, :]), dot(active[...], down_two[hidden, :])
        grad = dot_nt(arriving[:, :COLS], down_one[hidden, :])
        grad += dot_nt(arriving[:, COLS:], down_two[hidden, :])
        low = (grad * slope).astype(LOW)
        up_low[...] = low
        bias_grad[j : j + 1, :] = jnp.sum(low.astype(FULL), axis=0, keepdims=True)
        normed_part = dot_nt(up_low[...], up[j])
        if j == 0:
            layer_sum[:, :COLS], layer_sum[:, COLS:] = layer_one, layer_two
            normed_sum[...] = normed_part
        else:
            layer_sum[:, :COLS] += layer_one
            layer_sum[:, COLS:] += layer_two
            normed_sum[...] += normed_part
        whole = dot_tn(active[...], arriving[...]).astype(LOW)
        one_grad[hidden, :] = whole[:, :COLS]
        two_grad[hidden, :] = whole[:, COLS:]
        up_grad[j] = dot_tn(normed[...], up_low[...]).astype(LOW)
        of_chunk(j, lambda copy: copy.start(), copies_out)
    layer_own[...] = held[:count, :] + layer_sum[:count, :] + row_of(vectors, 11)
    layer_other[...] = layer_sum[count:, :].astype(LOW)
    normed_grad[...] = normed_sum[...].astype(LOW)
    finished(rows_out)
    finished(copies_out)


def forward_backward(places, lengths, tokens, arriving, branch, branch_far, vectors, raw):
    count, width = tokens[0].shape
    rows, hidden = 2 * count, 4 * COLS
    sent = [low_shape(2, 4, 192, COLS), low_shape(2, 2, 384, COLS), low_shape(2, 4, 2, 64, COLS)]
    inside = [
        full_shape(count, width), low_shape(count, width), low_shape(rows, width),
        full_shape(4, COLS),
    ]
    vmem = pltpu.VMEM
    mats = [vmem((4, width, COLS), LOW), vmem((hidden, COLS), LOW), vmem((hidden, COLS), LOW)]
    low, full = vmem((rows, width), LOW), vmem((rows, width), FULL)
    return call(
        forward_backward_kernel,
        [SCALARS, SCALARS] + [OUTSIDE] * 6 + [INSIDE] + [OUTSIDE] * 12,
        [(s, OUTSIDE) for s in sent for _ in range(2)]
        + [(full_shape(rows, width), OUTSIDE)]
        + [(s, INSIDE) for s in inside],
        mats + mats + [low, low, low, full, low, low, full, full]
        + [vmem((rows, COLS), LOW), vmem((rows, COLS), LOW)]
        + [pltpu.SemaphoreType.DMA((n,)) for n in (10, 96, 96)],
        33,
        (places, lengths, *tokens, *arriving, branch, branch_far, vectors, *raw),
        vmem=50,
    )


def output_backward_kernel(
    places, lengths, arriving_own, arriving_other, middle, part, part_far, vectors, own, other,
    out_mat, sent_one, sent_two, middle_grad, attended_grad, sums,
    held, near, far, arriving, branch, out_grad, row_sems, sems,
):
    count = arriving_own.shape[0]
    blocks = [pl.ds(0, count), pl.ds(count, count)]
    rows_in = []
    for block, cotangent in enumerate((arriving_own, arriving_other)):
        here, there = blocks[block], blocks[1 - block]
        pairs = [
            (middle.at[here], held.at[here]),
            (part.at[here], near.at[here]),
            (part_far.at[there], far.at[here]),
            (cotangent, arriving.at[here]),
        ]
        rows_in.append(started(pairs, row_sems.at[pl.ds(4 * block, 4)]))
    gain = row_of(vectors, 5)
    for block, rows in enumerate(blocks):
        finished(rows_in[block])
        unit, inverse = unit_of(held[rows, :])
        grad = near[rows, :].astype(FULL) + far[rows, :].astype(FULL)
        slots = lax.broadcasted_iota(jnp.int32, grad.shape, 0)
        live = slots < lengths[block, 0] + lengths[block, 1]
        coming = jnp.where(live, arriving[rows, :].astype(FULL), 0.0)
        result = coming + norm_backward(grad, unit, inverse, gain)
        low = result.astype(LOW)
        branch[rows, :] = low
        if block == 0:
            middle_grad[...] = result
            sums[...] = jnp.zeros_like(sums)
            sums[0:1, :] = jnp.sum(low.astype(FULL), axis=0, keepdims=True)
            sums[1:2, :] = jnp.sum(grad * unit, axis=0, keepdims=True)
            sums[2:3, :] = jnp.sum(grad, axis=0, keepdims=True)
            sums[3:4, :] = jnp.sum(coming, axis=0, keepdims=True)
    whole = dot_tn(own[...], branch[:count, :]) + dot_tn(other[...], branch[count:, :])
    out_grad[0] = whole[:, :COLS].astype(LOW)
    out_grad[1] = whole[:, COLS:].astype(LOW)
    copies = started(turned(out_plan(places, two_of((sent_one, sent_two)), 0, out_grad)), sems)
    attended_grad[...] = (
        dot_nt(branch[:, :COLS], out_mat[0]) + dot_nt(branch[:, COLS:], out_mat[1])
    ).astype(LOW)
    finished(copies)


def output_backward(
    places, lengths, arriving, middle, part, part_far, vectors, attended, out_mat
):
    rows, width = middle.shape
    sent = (low_shape(2, 4, 2, 32, COLS), OUTSIDE)
    inside = [full_shape(rows // 2, width), low_shape(rows, COLS), full_shape(8, width)]
    low = pltpu.VMEM((rows, width), LOW)
    return call(
        output_backward_kernel,
        [SCALARS, SCALARS] + [OUTSIDE] * 5 + [INSIDE] * 4,
        [sent, sent] + [(s, INSIDE) for s in inside],
        [pltpu.VMEM((rows, width), FULL), low, low, low, low, pltpu.VMEM((2, COLS, COLS), LOW)]
        + [pltpu.SemaphoreType.DMA((8,)), pltpu.SemaphoreType.DMA((32,))],
        10,
        (places, lengths, *arriving, middle, part, part_far, vectors, *attended, out_mat),
        vmem=60,
    )


def attention_backward_kernel(
    block, lengths, query, key, value, grad_in, query_grad, key_grad, value_grad, sums, mask
):
    count = query.shape[0]
    mask[...] = barred(lengths, block, 0, count, count)
    lane = lax.broadcasted_iota(jnp.int32, (count, TILE), 1) < HEAD_DIM
    for index in range(COLS // TILE):
        cols = pl.ds(index * TILE, TILE)
        stacked, given = two_by_two(query[:, cols], lane), two_by_two(grad_in[:, cols], lane)
        probs = probabilities(stacked, key[:, cols], mask[...])
        weighted = probs * dot_nt(given, value[:, cols])
        grad = (weighted - probs * jnp.sum(weighted, axis=-1, keepdims=True)).astype(LOW)
        out = dot(grad, key[:, cols])
        query_grad[:, cols] = (jnp.where(lane, out[:count], out[count:]) * 0.125).astype(LOW)
        key_grad[:, cols] = dot_tn(grad, stacked).astype(LOW)
        value_grad[:, cols] = dot_tn(probs.astype(LOW), given).astype(LOW)
    sums[...] = jnp.zeros_like(sums)
    sums[0:1, :] = jnp.sum(query_grad[...].astype(FULL), axis=0, keepdims=True)
    sums[1:2, :] = jnp.sum(value_grad[...].astype(FULL), axis=0, keepdims=True)


def attention_backward(block, lengths, query, key, value, grad_in):
    count = query.shape[0] // 2
    vmem = pltpu.VMEM
    half = (low_shape(count, COLS), INSIDE)
    part = pl.BlockSpec((count, COLS), lambda i: (block, 0))
    return call(
        lambda *refs: attention_backward_kernel(block, *refs),
        [SCALARS] + [part] * 4,
        [half, half, half, (full_shape(8, COLS), INSIDE)],
        [vmem((count, count), FULL)],
        8,
        (lengths, query, key, value, grad_in),
        grid=(1,),
        vmem=60,
    )


def joint_grad_kernel(places, normed, *refs):
    grads, sent, (query_part, key_part, value_part, sems) = refs[:6], refs[6:12], refs[12:]
    parts = (query_part, key_part, value_part)
    count = grads[0].shape[0]
    sides = [jnp.concatenate([g[...] for g in grads[i : i + 3]], axis=1) for i in (0, 3)]
    whole = dot_tn(normed[:count, :], sides[0]) + dot_tn(normed[count:, :], sides[1])
    for index, part in enumerate(parts):
        part[...] = whole[:, index * COLS : (index + 1) * COLS].astype(LOW)
    finished(started(joint_sent_plan(places, sent, parts), sems))


def joint_grad_parts(places, normed, own, other):
    rows, width = normed.shape
    sent = [low_shape(2, 4, 64, COLS), low_shape(2, 2, 128, COLS), low_shape(2, 4, 2, 32, COLS)]
    return call(
        joint_grad_kernel,
        [SCALARS] + [INSIDE] * 7,
        [(s, OUTSIDE) for s in sent for _ in range(2)],
        [pltpu.VMEM((width, COLS), LOW)] * 3 + [pltpu.SemaphoreType.DMA((56,))],
        8,
        (places, normed, *own, *other),
        vmem=60,
    )


def joint_backward_kernel(*refs):
    own, other, mats, outs = refs[:3], refs[3:6], refs[6:9], refs[9:]
    for grads, out in zip((own, other), outs):
        whole = dot_nt(grads[0][...], mats[0][...])
        whole += dot_nt(grads[1][...], mats[1][...])
        whole += dot_nt(grads[2][...], mats[2][...])
        out[...] = whole.astype(out.dtype)


def joint_backward(own, other, mats):
    count, width = own[0].shape[0], mats[0].shape[0]
    return call(
        joint_backward_kernel,
        [INSIDE] * 9,
        [(full_shape(count, width), INSIDE), (low_shape(count, width), INSIDE)],
        [],
        6,
        (*own, *other, *mats),
        vmem=20,
    )


def input_kernel(
    places, tokens, part, part_far, middle_grad, vectors, two_sums, own_sums, other_sums, up_sums,
    layer_own, layer_far, input_grad, sums, layer_out, rows,
):
    unit, inverse = unit_of(tokens[...].astype(FULL))
    grad = part[...] + part_far[...].astype(FULL)
    input_grad[...] = middle_grad[...] + norm_backward(grad, unit, inverse, row_of(vectors, 0))
    layer_out[...] = (layer_own[...] + layer_far[...].astype(FULL)).astype(LOW)
    first = places[13] == 0

    def own_side(values):
        none = jnp.zeros_like(values)
        return jnp.concatenate(
            [jnp.where(first, values, none), jnp.where(first, none, values)], axis=1
        )

    rows[...] = jnp.zeros_like(rows)
    rows[0:1, :] = jnp.sum(grad * unit, axis=0, keepdims=True)
    rows[1:2, :] = jnp.sum(grad, axis=0, keepdims=True)
    for k in range(2):
        rows[2 + k : 3 + k, :] = own_side(own_sums[k : k + 1, :] + other_sums[k : k + 1, :])
    rows[4:7, :] = two_sums[0:3, :]
    for k in range(4):
        hidden = up_sums[k : k + 1, :]
        rows[7 + k : 8 + k, :] = jnp.concatenate(
            [own_side(hidden[:, :256]), own_side(hidden[:, 256:])], axis=1
        )
    rows[11:12, :] = two_sums[3:4, :]
    sums[:16, :] = rows[:, :COLS].astype(LOW)
    sums[16:, :] = rows[:, COLS:].astype(LOW)


def input_backward(places, *arrays):
    count, width = arrays[0].shape
    return call(
        input_kernel,
        [SCALARS] + [INSIDE] * 11,
        [(full_shape(count, width), INSIDE), (low_shape(32, COLS), INSIDE)]
        + [(low_shape(count, width), INSIDE)],
        [pltpu.VMEM((16, width), FULL)],
        4,
        (places, *arrays),
        vmem=20,
    )


def adam_step(weight, first, second, grad, rate, decay):
    first_new = BETA_ONE * first + (1.0 - BETA_ONE) * grad
    second_new = BETA_TWO * second + (1.0 - BETA_TWO) * grad * grad
    mean_hat = first_new / (1.0 - BETA_ONE**STEP)
    square_hat = second_new / (1.0 - BETA_TWO**STEP)
    fresh = weight - rate * (mean_hat / (jnp.sqrt(square_hat) + ADAM_EPS) + decay * weight)
    return (first_new, second_new, fresh)


def adam_kernel(grad_of, rate, chunks, places, *refs):
    state, refs = refs[:3], refs[3:]
    grads, refs = refs[:-8], refs[-8:]
    outs, (held, results, sems_in, sems_out) = refs[:4], refs[4:]
    coming = [
        started([(a.at[at], held.at[(i, *at)]) for i, a in enumerate(state)], sems_in.at[n])
        for n, at in enumerate(chunks)
    ]
    going = []
    for n, at in enumerate(chunks):
        grad = grad_of(n, places, *grads)
        finished(coming[n])
        results[(0, *at)] = grad
        weight, first, second = (held[(i, *at)] for i in range(3))
        new = adam_step(weight, first, second, grad, rate, MATRIX_DECAY)
        for i, value in enumerate(new):
            results[(1 + i, *at)] = value
        going += started(
            [(results.at[(i, *at)], out.at[at]) for i, out in enumerate(outs)], sems_out.at[n]
        )
    finished(going)


def adam(grad_of, rate, chunks, state, grads, places):
    shape = state[0].shape
    return pl.pallas_call(
        lambda *refs: adam_kernel(grad_of, rate, chunks, *refs),
        grid=(1,),
        in_specs=[SCALARS]
        + [OUTSIDE] * 3
        + [pl.BlockSpec((g[1], COLS), lambda i, at=g[2]: (at, 0)) for g in grads],
        out_specs=[OUTSIDE] * 4,
        out_shape=[full_shape(*shape)] * 4,
        scratch_shapes=[pltpu.VMEM((3, *shape), FULL), pltpu.VMEM((4, *shape), FULL)]
        + [pltpu.SemaphoreType.DMA((len(chunks), 3)), pltpu.SemaphoreType.DMA((len(chunks), 4))],
        compiler_params=pltpu.CompilerParams(vmem_limit_bytes=24 << 20),
        cost_estimate=pl.CostEstimate(
            flops=6 * FLOPS_PER_US, bytes_accessed=30 * state[0].size, transcendentals=0
        ),
    )(places, *state, *(g[0] for g in grads))


def by_core(places, both, far):
    own = places[13] == 0
    both, far = both.astype(FULL), far.astype(FULL)
    return jnp.where(own, both, far), jnp.where(own, far, both)


def columns_of(width, count):
    return [(slice(None), slice(n * width, (n + 1) * width)) for n in range(count)]


def rows_each(height, count):
    return [(slice(n * height, (n + 1) * height), slice(None)) for n in range(count)]


def adam_joint(places, state, sums):
    def grad_of(n, places, both, far):
        rows = slice(128 * n, 128 * (n + 1))
        return jnp.concatenate(by_core(places, both[rows, :], far[rows, :]), axis=1)

    grads = [(a, 384, 0) for a in sums]
    return adam(grad_of, MATRIX_RATE, columns_of(2 * COLS, 3), state, grads, places)


def adam_expand(places, state, sums):
    def grad_of(n, places, both, far):
        rows = slice(128 * n, 128 * (n + 1))
        zero, one = by_core(places, both[rows, :], far[rows, :])
        return jnp.concatenate(
            [zero[:, :256], one[:, :256], zero[:, 256:], one[:, 256:]], axis=1
        )

    grads = [(a, 512, 0) for a in sums]
    return adam(grad_of, MATRIX_RATE, columns_of(2 * COLS, 4), state, grads, places)


def adam_reduce(places, state, sums):
    def grad_of(n, places, left, right, far_left, far_right):
        rows = slice(128 * (n % 2), 128 * (n % 2 + 1))
        own = places[13] == n // 2
        return jnp.concatenate(
            [
                jnp.where(own, left[rows, :].astype(FULL), far_left[rows, :].astype(FULL)),
                jnp.where(own, right[rows, :].astype(FULL), far_right[rows, :].astype(FULL)),
            ],
            axis=1,
        )

    grads = [(a, 256, at) for a in sums for at in (2, 3)]
    return adam(grad_of, MATRIX_RATE, rows_each(128, 4), state, grads, places)


def adam_output(places, state, sums):
    def grad_of(n, places, *grads):
        both, far = grads[n], grads[2 + n]

        def rows(a):
            return jnp.concatenate(
                [
                    jnp.concatenate([a[64 * q : 64 * q + 32, :], a[64 * q + 32 : 64 * q + 64, :]], axis=1)
                    for q in (0, 1)
                ]
            ).astype(FULL)

        return jnp.where(places[13] == places[12], rows(both), rows(far))

    grads = [(a, 128, at) for a in sums for at in (3, 4)]
    return adam(grad_of, OUTPUT_RATE, rows_each(64, 2), state, grads, places)


def per_device(
    tokens,
    cotangent,
    lengths,
    joint_weight,
    joint_first,
    joint_second,
    output_weight,
    output_first,
    output_second,
    expand_weight,
    expand_first,
    expand_second,
    reduce_weight,
    reduce_first,
    reduce_second,
    vector_weight,
    vector_first,
    vector_second,
):
    me = coordinates()
    places = places_of(me)
    across = flip("core", 1)

    half, block, rest_half, rest_y = cast(
        places, joint_weight, vector_weight, expand_weight, reduce_weight, output_weight
    )
    joint_x, joint_y, along_x, along_y, along_z, far = gather_first(
        places, half, block, rest_half, rest_y, [send(a, across) for a in (lengths, tokens, cotangent)]
    )
    tokens, cotangent = (tokens, far[1]), (cotangent, far[2])
    lengths = jnp.concatenate([lengths, far[0]])

    normed_one, query, key, value, vectors, *joint_mats = joint(
        places, *tokens, joint_x, joint_y
    )
    along_z.append(send(after(along_z[1], query), turn("z", 1)))
    along_y.append(send(after(along_y[0], query), turn("y", 1)))
    along_y.append(send(after(along_y[1], query), turn("y", 1)))
    own = attention(0, lengths, after(query, along_y[1], *along_z[1:3]), key, value)
    along_x.append(send(after(along_x[1], own), turn("x", 1)))
    other = attention(1, lengths, after(query, along_x[1]), key, value)
    attended = (own, other)
    branch, out_mat = output(places, own, after(other, *along_x[2:], *along_y[2:]), along_z)
    branch_far = send(branch, across)
    *sent, middle, layer_own, layer_other, normed_two_part, up_bias_grad = forward_backward(
        places, lengths, tokens, cotangent, branch, branch_far, vectors,
        [*along_x, *along_y, *along_z],
    )
    part_far = send(normed_two_part, across)
    layer_far = send(layer_other, across)

    out_one, out_two, middle_grad, attended_grad, two_sums = output_backward(
        places, lengths, cotangent, middle, normed_two_part, part_far, vectors, attended, out_mat
    )
    rest = total(me, sent, 0, 3, 0)
    next(rest)
    out_far = send(out_two, turn("z", 1))
    *own_grads, own_sums = attention_backward(0, lengths, query, key, value, attended_grad)
    *other_grads, other_sums = attention_backward(1, lengths, query, key, value, attended_grad)
    mark = rest.send(other_grads[0])
    sent = joint_grad_parts(places, after(normed_one, mark), own_grads, other_grads)
    joint_rows = total(me, sent, 32, 1, 32)
    next(joint_rows)
    mark = rest.send((sent[0], None, None))
    (out_near,) = added_all([[(out_one, 1), (after(out_far, mark), 1)]])
    out_near = out_near.reshape(out_one.shape[1:])
    out_again = send(out_near, turn("z", 0))
    part_own, part_other = joint_backward(
        (after(own_grads[0], out_near), *own_grads[1:]), other_grads, joint_mats
    )
    part_far = send(part_other, across)
    mark = joint_rows.send(part_own)
    mark = rest.send(mark)
    input_grad, vector_local, layer_out = input_backward(
        places, tokens[0], after(part_own, mark), part_far, middle_grad, vectors, two_sums,
        own_sums, other_sums, up_bias_grad, layer_own, layer_far,
    )
    (out_along,) = added_all(
        [[(out_one, 0), (out_far, 0), (after(out_again, vector_local), 0)]]
    )
    out_along = out_along.reshape(out_one.shape[1:])

    mark = joint_rows.send((vector_local, vector_local, out_along))
    for _ in range(4):
        mark = rest.send(mark)
        mark = joint_rows.send(mark)
    mark = rest.send(mark)
    mark = joint_rows.send(mark)
    mark = joint_rows.send(mark)
    mark = rest.send(mark)
    mark = joint_rows.send(mark)
    one, two, extra = next(joint_rows)
    joint_state = adam_joint(
        places, (joint_weight, joint_first, joint_second), (after(one, mark), two)
    )
    output_state = adam_output(
        places, (output_weight, output_first, output_second), (after(one, mark), two)
    )
    one, two, _ = next(rest)
    one = after(one, joint_state[0], output_state[0])
    expand = adam_expand(places, (expand_weight, expand_first, expand_second), (one, two))
    reduce = adam_reduce(places, (reduce_weight, reduce_first, reduce_second), (one, two))
    vector_grad = lax.dynamic_slice(
        jnp.concatenate([extra[:12], extra[16:28]], axis=1).astype(FULL),
        (0, 128 * lax.axis_index("shard")),
        (12, 128),
    )
    vector_state = (vector_grad,) + adam_step(
        vector_weight, vector_first, vector_second, vector_grad, VECTOR_RATE, 0.0
    )
    states = zip(joint_state, output_state, expand, reduce, vector_state)
    return (layer_out, input_grad, *(a for kind in states for a in kind))


def solution(mesh):
    rows, columns, split = P("shard", None), P(None, "shard"), P(("wide", "shard"), None)
    state = (rows, rows, rows, rows, columns)
    return jax.shard_map(
        per_device,
        mesh=mesh,
        in_specs=(split, split, split) + (rows,) * 12 + (columns,) * 3,
        out_specs=(split, split) + state * 4,
        check_vma=False,
    )
```

```python
import jax
import jax.numpy as jnp
from jax import lax
from jax.experimental import pallas as pl
from jax.experimental.pallas import tpu as pltpu
from jax.sharding import PartitionSpec as P

HEAD_DIM = 64
STEP = 10


ROOT_TWO_PI = 0.7978845608028654
CUBIC = 0.044715
BETA_ONE = 0.9
BETA_TWO = 0.999
ADAM_EPS = 1e-08
MATRIX_RATE = 0.03
OUTPUT_RATE = 0.1
VECTOR_RATE = 0.2
MATRIX_DECAY = 0.1

LOW = jnp.bfloat16
FULL = jnp.float32
AXES = ("wide", "shard")
SIZES = (4, 2, 2, 2, 4)
COLS = 512
FLOPS_PER_US = 1_150_000_000


def coordinates():
    wide, shard = lax.axis_index("wide"), lax.axis_index("shard")
    z, xl, core = wide // 4, (wide // 2) % 2, wide % 2
    xh, y = shard // 4, shard % 4
    return {"z": z, "x": 2 * xh + xl, "y": y, "xl": xl, "xh": xh, "core": core}


def route(partner):
    pairs = []
    for source in range(128):
        rest, places = source, []
        for size in reversed(SIZES):
            places.append(rest % size)
            rest //= size
        y, xh, core, xl, z = places
        target = partner({"z": z, "x": 2 * xh + xl, "y": y, "core": core})
        flat = 0
        for place, size in zip(
            (target["z"], target["x"] % 2, target["core"], target["x"] // 2, target["y"]), SIZES
        ):
            flat = flat * size + place
        pairs.append((source, flat))
    return pairs


def flip(axis, bits):
    return route(lambda at: {**at, axis: at[axis] ^ bits})


def turn(axis, step):
    return route(lambda at: {**at, axis: at[axis] ^ (1 if (at["core"] + step) % 2 == 0 else 3)})


def send(value, pairs):
    return lax.ppermute(value, AXES, pairs)


def added(*terms):
    return sum(term.astype(FULL) for term in terms).astype(LOW)


def orders(me, axis):
    here = me[axis]
    one = jnp.where(me["core"] == 0, 1, 3)
    return [here, here ^ one, here ^ (4 - one), here ^ 2]


def places_of(me):
    return jnp.stack(
        orders(me, "x")
        + orders(me, "y")
        + orders(me, "z")
        + [me["xh"], me["core"], me["xl"], me["z"]]
    ).astype(jnp.int32)


def after(value, *others):
    return lax.optimization_barrier((value, *others))[0]


def rows_of(*parts):
    return jnp.concatenate([p.reshape(-1, COLS) for p in parts])


def main_phase(block, axis, gate, late=False):
    first, second = send(block, turn(axis, 0)), send(gated(block, gate if late else None), turn(axis, 1))
    return [block, first, second, send(after(first, gate), turn(axis, 1))]


def pack_kernel(places, block, other, half, second, first, again):
    for out in (first, again):
        out[:208, :] = block[:208, :]
        out[208:416, :] = other[:208, :]
    again[416:512, :] = half[...]
    again[512:608, :] = second[...]
    own = places[13] == places[12]
    for p, held in enumerate((block, other)):
        at = 416 + 96 * p
        first[at : at + 64, :] = held[208:272, :]
        rows = slice(272 + 32 * p, 304 + 32 * p)
        first[at + 64 : at + 96, :] = jnp.where(own, block[rows, :], other[rows, :])


def pack(places, *arrays):
    return call(
        pack_kernel,
        [SCALARS] + [INSIDE] * 4,
        [(low_shape(608, COLS), INSIDE)] * 2,
        [],
        1,
        (places, *arrays),
        vmem=8,
    )


def gather_first(places, half, block, rest_half, rest_y, exchanged):
    size = half.shape[0]
    other, second, *early = lax.optimization_barrier(
        (send(block, flip("x", 3)), send(half, turn("y", 0)), *exchanged[:2])
    )
    own_y, both = pack(places, block, other, half, second)
    first_y, second_y = send(own_y, turn("y", 0)), send(both, turn("y", 1))
    rest_other = send(after(rest_y, other), flip("x", 3))
    first_y, second_y, rest_other, *late = lax.optimization_barrier(
        (first_y, second_y, rest_other, *exchanged[2:])
    )
    plane = rows_of(half, second, second_y[416:]).reshape(4, size, COLS)
    first_x, second_x = send(plane, turn("x", 0)), send(plane, turn("x", 1))
    third_y = send(rows_of(first_y[:416], own_y[416:], first_y[416:]), turn("y", 1))
    rest_near = send(after(rest_half, first_y), turn("y", 0))
    first_x, second_x, third_y, rest_near = lax.optimization_barrier(
        (first_x, second_x, third_y, rest_near)
    )
    third_x = send(first_x, turn("x", 1))
    here = rows_of(rest_half, rest_near)
    there = send(here, turn("y", 1))
    plane_z = rows_of(own_y[416:], first_y[416:], third_y[416:]).reshape(4, 2, 96, COLS)
    pair_y = jnp.stack([rest_y, rest_other])
    along_z = [plane_z, send(plane_z, turn("z", 0)), send(plane_z, turn("z", 1))]
    along_y = [pair_y, send(after(pair_y, third_y), turn("y", 0))]
    third_x, there = lax.optimization_barrier((third_x, there))
    plane_x = rows_of(here, there).reshape(4, -1, COLS)
    along_x = [plane_x, send(plane_x, turn("x", 0)), send(plane_x, turn("x", 1))]
    joint_x = [plane, first_x, second_x, third_x]
    joint_y = [own_y, first_y, second_y, third_y]
    return joint_x, joint_y, along_x, along_y, along_z, early + late


def added_all(sums, steps=2):
    terms, specs, outs, out_specs = [], [], [], []
    for group in sums:
        rows = min(a.size for a, _ in group) // COLS
        rows = rows // 2 if len(group) == 2 else rows
        for array, which in group:
            terms.append(array.reshape(-1, COLS))
            specs.append(
                pl.BlockSpec((rows // steps, COLS), lambda i, at=which * steps: (at + i, 0))
            )
        outs.append(low_shape(rows, COLS))
        out_specs.append(pl.BlockSpec((rows // steps, COLS), lambda i: (i, 0)))

    def kernel(*refs):
        at = 0
        for group, out in zip(sums, refs[len(terms) :]):
            out[...] = added(*(ref[...] for ref in refs[at : at + len(group)]))
            at += len(group)

    return pl.pallas_call(
        kernel,
        grid=(steps,),
        in_specs=specs,
        out_specs=out_specs,
        out_shape=outs,
        compiler_params=pltpu.CompilerParams(vmem_limit_bytes=12 << 20),
        cost_estimate=pl.CostEstimate(
            flops=3 * FLOPS_PER_US, bytes_accessed=6 * sum(o.size for o in outs), transcendentals=0
        ),
    )(*terms)


def assembled(me, mine, far, behind, pieces):
    behind = [a.reshape(-1, COLS) for a in behind]
    rows = 2 * mine.shape[0] + sum(a.shape[0] for a in behind)

    def kernel(right, mine, far, *refs):
        behind, out = refs[:-1], refs[-1]
        first = right[0] == 0
        source = target = 0
        for count, size in pieces:
            for _ in range(count):
                a, b = mine[source : source + size, :], far[source : source + size, :]
                out[target : target + size, :] = jnp.where(first, a, b)
                out[target + size : target + 2 * size, :] = jnp.where(first, b, a)
                source, target = source + size, target + 2 * size
        for part in behind:
            out[target : target + part.shape[0], :] = part[...]
            target += part.shape[0]

    return pl.pallas_call(
        kernel,
        out_shape=low_shape(rows, COLS),
        in_specs=[pl.BlockSpec(memory_space=pltpu.SMEM)]
        + [pl.BlockSpec(memory_space=pltpu.VMEM)] * (2 + len(behind)),
        out_specs=pl.BlockSpec(memory_space=pltpu.VMEM),
        compiler_params=pltpu.CompilerParams(vmem_limit_bytes=8 << 20),
        cost_estimate=pl.CostEstimate(
            flops=FLOPS_PER_US, bytes_accessed=4 * rows * COLS, transcendentals=0
        ),
    )(me["xl"].reshape(1).astype(jnp.int32), mine, far, *behind)


def gated(value, gate):
    return value if gate is None else after(value, *(gate if isinstance(gate, tuple) else (gate,)))


def total(me, raw, out_rows, units, extra_rows):
    axes = "xyz"
    parts = [raw[:2], raw[2:4], raw[4:]]
    far = [send(away, turn(axis, 1)) for (_, away), axis in zip(parts, axes)]
    gate = yield
    far = list(far if gate is None else lax.optimization_barrier((*far, gate))[:-1])
    keeps = [keep for keep, _ in parts]
    near = added_all([[(k, 1), (f, 1)] for k, f in zip(keeps, far)])
    near = lax.optimization_barrier([n.reshape(k.shape[1:]) for n, k in zip(near, keeps)])
    again = [send(n, turn(axis, 0)) for n, axis in zip(near, axes)]
    gate, extra, out = yield near[2]
    again = lax.optimization_barrier((*again, gate))[:-1]
    along = added_all([[(k, 0), (f, 0), (a, 0)] for k, f, a in zip(keeps, far, again)])
    along_x, along_y, along_z = lax.optimization_barrier(
        [a.reshape(k.shape[1:]) for a, k in zip(along, keeps)]
    )
    if out_rows:
        along_z = jnp.concatenate([along_z, out], axis=2)
    size_x, size_y = along_x.shape[1], along_y.shape[1] // 2
    size_z = (along_z.shape[2] - out_rows) // 2

    def with_extra(*parts):
        return rows_of(*parts, extra) if extra_rows else rows_of(*parts)

    def split(rows, *sizes):
        at, parts = 0, []
        for size in sizes:
            parts.append(rows[at : at + size])
            at += size
        return parts

    plane = jnp.concatenate([along_x, along_z.reshape(4, -1, COLS)], axis=1)
    size = plane.shape[1]
    far = send(with_extra(plane[2:]), turn("y", 1))
    gate = yield plane
    far, kept = gated(far, gate), plane[:2]
    near = added(kept[1], far[size : 2 * size])
    if extra_rows:
        extra = added(extra, far[2 * size :])
    again = send(with_extra(near), turn("y", 0))
    gate = yield near
    again = gated(again, gate)
    plane = added(kept[0], far[:size], again[:size])
    if extra_rows:
        extra = added(extra, again[size:])
    half, pair = plane[:size_x], plane[size_x:].reshape(2, 2 * size_z + out_rows, COLS)
    out = pair[:, 2 * size_z :].reshape(-1, COLS)
    pieces = jnp.concatenate(
        [along_y.reshape(4, size_y, COLS), pair[:, : 2 * size_z].reshape(4, size_z, COLS)], axis=1
    )
    size = size_y + size_z
    pieces = [
        lax.dynamic_index_in_dim(pieces, ((k // 2) ^ me["xh"]) * 2 + k % 2, 0, keepdims=False)
        for k in orders(me, "x")
    ]
    far = send(with_extra(pieces[2], pieces[3], out), turn("x", 1))
    gate = yield plane
    far = gated(far, gate)
    first, second, far_out, far_extra = split(far, size, size, 2 * out_rows, extra_rows)
    sums = added(rows_of(pieces[1], out), rows_of(second, far_out))
    if extra_rows:
        extra = added(extra, far_extra)
    again = send(with_extra(sums), turn("x", 0))
    gate = yield sums
    near, out, far_extra = split(gated(again, gate), size, 2 * out_rows, extra_rows)
    sums = rows_of(added(pieces[0], first, near), added(sums[size:], out))
    if extra_rows:
        extra = added(extra, far_extra)
    flat, block = rows_of(half, sums[:size_y]), sums[size_y:]
    size, size_block = flat.shape[0], block.shape[0]
    far = send(with_extra(flat, block), turn("z", 0))
    gate = yield sums
    sums, other, far_extra = split(gated(far, gate), size, size_block, extra_rows)
    flat = added(flat, sums)
    if extra_rows:
        extra = added(extra, far_extra)
    blocks = rows_of(block, other)
    far = send(with_extra(flat, blocks), turn("z", 1))
    gate = yield flat
    sums, other, far_extra = split(gated(far, gate), size, 2 * size_block, extra_rows)
    flat = added(flat, sums)
    if extra_rows:
        extra = added(extra, far_extra)
    blocks = rows_of(blocks, other).reshape(4, size_block, COLS)
    where = orders(me, "z")
    ordered = jnp.stack(
        [
            sum(jnp.where(where[k] == place, blocks[k], 0) for k in range(4)).astype(LOW)
            for place in range(4)
        ]
    )
    mine = rows_of(flat, ordered[:, :size_z])
    far = send(mine, flip("x", 1))
    gate = yield mine
    far = gated(far, gate)

    pieces = [(units, size_x // units), (1, size_y), (4, size_z)]
    both = assembled(me, mine, far, [ordered[:, size_z:]] if out_rows else [], pieces)
    far = send(with_extra(both), flip("core", 1))
    yield both
    rows = both.shape[0]
    if extra_rows:
        extra = added(extra, far[rows:])
        far = far[:rows]
    yield both, far, extra


def rows_at(start, size):
    return pl.ds(pl.multiple_of(start, size), size)


def joint_plan(places, along_x, along_y, mats):
    query, key, value, vectors = mats
    pairs = []
    for ky in range(4):
        y = places[4 + ky]
        for kx in range(4):
            x = places[kx]
            shard, half = (x // 2) * 4 + y, x % 2
            source = along_x[kx].at[ky]
            pairs.append(
                (source.at[pl.ds(0, 64)], query.at[rows_at(shard * 128 + half * 64, 64)])
            )
            pairs.append(
                (source.at[pl.ds(64, 32)], value.at[rows_at(shard * 128 + half * 32, 32)])
            )
        for p in range(2):
            shard = (places[12] ^ p) * 4 + y
            source, at = along_y[ky], p * 208
            pairs.append((source.at[pl.ds(at, 128)], key.at[rows_at(shard * 128, 128)]))
            pairs.append((source.at[pl.ds(at + 128, 64)], value.at[rows_at(shard * 128 + 64, 64)]))
            pairs.append(
                (
                    source.at[pl.ds(at + 192, 16), pl.ds(0, 128)],
                    vectors.at[:, rows_at(shard * 128, 128)],
                )
            )
    return pairs


def joint_sent_plan(places, raw, parts):
    query, key, value = parts
    pairs = []
    for ky in range(4):
        y = places[4 + ky]
        for kx in range(4):
            x = places[kx]
            start = ((x // 2) * 4 + y) * 128 + (x % 2) * 64
            pairs.append((query.at[rows_at(start, 64)], raw[0 + kx // 2].at[kx % 2, ky]))
        for p in range(2):
            shard = (places[12] ^ p) * 4 + y
            pairs.append((key.at[rows_at(shard * 128, 128)], raw[2 + ky // 2].at[ky % 2, p]))
            for kz in range(4):
                start = shard * 128 + places[8 + kz] * 32
                pairs.append((value.at[rows_at(start, 32)], raw[4 + kz // 2].at[kz % 2, ky, p]))
    return pairs


def up_plan(places, at_x, at_y, at_z, mats):
    up, down_one, down_two = mats
    pairs = []
    for ky in range(4):
        y = places[4 + ky]
        for kx in range(4):
            x = places[kx]
            start = ((x // 2) * 4 + y) * 128 + (x % 2) * 64
            for j in range(3):
                source = at_x(kx).at[ky, pl.ds(64 * j, 64)]
                pairs.append((source, up.at[j, rows_at(start, 64)]))
        for p in range(2):
            shard = (places[12] ^ p) * 4 + y
            source = at_y(ky).at[p]
            pairs.append((source.at[pl.ds(0, 128)], up.at[3, rows_at(shard * 128, 128)]))
            pairs.append((source.at[pl.ds(128, 256)], down_one.at[rows_at(shard * 256, 256)]))
            for kz in range(4):
                start = shard * 256 + places[8 + kz] * 64
                source = at_z(kz).at[ky, p, pl.ds(0, 64)]
                pairs.append((source, down_two.at[rows_at(start, 64)]))
    return pairs


def up_kind(index):
    index %= 24
    if index < 12:
        return index % 3
    return 3 if (index - 12) % 6 == 0 else None


def up_shard(places, index):
    ky, index = divmod(index, 24)
    return (places[12] ^ ((index - 12) // 6)) * 4 + places[4 + ky]


def out_plan(places, at_z, first, mat):
    pairs = []
    for ky in range(4):
        for kz in range(4):
            start = places[4 + ky] * 128 + places[8 + kz] * 32
            for p in range(2):
                source = at_z(kz).at[ky, p, pl.ds(first, 32)]
                pairs.append((source, mat.at[p, rows_at(start, 32)]))
    return pairs


def two_of(arrays):
    return lambda k: arrays[k // 2].at[k % 2]


def started(pairs, sems):
    all_of_them = [pltpu.make_async_copy(a, b, sems.at[i]) for i, (a, b) in enumerate(pairs)]
    for copy in all_of_them:
        copy.start()
    return all_of_them


def finished(all_of_them):
    for copy in all_of_them:
        copy.wait()


def turned(pairs):
    return [(b, a) for a, b in pairs]


def low_shape(*shape):
    return jax.ShapeDtypeStruct(shape, LOW)


def full_shape(*shape):
    return jax.ShapeDtypeStruct(shape, FULL)


SCALARS = pl.BlockSpec(memory_space=pltpu.SMEM)
INSIDE = pl.BlockSpec(memory_space=pltpu.VMEM)
OUTSIDE = pl.BlockSpec(memory_space=pl.ANY)


def call(kernel, in_specs, outs, scratch, length, args, grid=(), vmem=60):
    shapes, specs = [o[0] for o in outs], [o[1] for o in outs]
    moved = sum(a.size * a.dtype.itemsize for a in (*args, *shapes))
    return pl.pallas_call(
        kernel,
        grid=grid,
        out_shape=shapes,
        in_specs=in_specs,
        out_specs=specs,
        scratch_shapes=scratch,
        compiler_params=pltpu.CompilerParams(vmem_limit_bytes=vmem << 20),
        cost_estimate=pl.CostEstimate(
            flops=length * FLOPS_PER_US, bytes_accessed=moved, transcendentals=0
        ),
    )(*args)


def gelu_both(upward):
    square = upward * upward
    tangent = jnp.tanh(ROOT_TWO_PI * upward * (1.0 + CUBIC * square))
    half = 0.5 * (1.0 + tangent)
    slope = half + 0.5 * upward * (1.0 - tangent * tangent) * ROOT_TWO_PI * (
        1.0 + 3.0 * CUBIC * square
    )
    return upward * half, slope


def dot(a, b):
    return jnp.dot(a, b, preferred_element_type=FULL)


def dot_nt(a, b):
    return lax.dot_general(a, b, (((1,), (1,)), ((), ())), preferred_element_type=FULL)


def dot_tn(a, b):
    return lax.dot_general(a, b, (((0,), (0,)), ((), ())), preferred_element_type=FULL)


def unit_of(values):
    center = values - jnp.mean(values, axis=-1, keepdims=True)
    inverse = lax.rsqrt(jnp.mean(center * center, axis=-1, keepdims=True) + 1e-05)
    return center * inverse, inverse


def norm_backward(grad_out, unit, inverse, gain):
    scaled = grad_out * gain
    return inverse * (
        scaled
        - jnp.mean(scaled, axis=-1, keepdims=True)
        - unit * jnp.mean(scaled * unit, axis=-1, keepdims=True)
    )


def row_of(vectors, row):
    return vectors[row : row + 1, :].astype(FULL)


def own_columns(full, core, size):
    groups = full.shape[1] // (2 * size)
    first = jnp.concatenate(
        [full[:, (2 * g) * size : (2 * g + 1) * size] for g in range(groups)], axis=1
    )
    second = jnp.concatenate(
        [full[:, (2 * g + 1) * size : (2 * g + 2) * size] for g in range(groups)], axis=1
    )
    return jnp.where(core == 0, first, second)


def barred(lengths, block, first, height, span):
    shape = (height, span)
    rows = lax.broadcasted_iota(jnp.int32, shape, 0) + first
    keys = lax.broadcasted_iota(jnp.int32, shape, 1)
    opening = lengths[block, 0]
    filled = opening + lengths[block, 1]
    begin = jnp.where(rows < opening, 0, jnp.where(rows < filled, opening, rows))
    return jnp.where((keys <= rows) & (keys >= begin), 0.0, -1e30)


TILE = 128


def cast_kernel(
    places, weight, vector, expand, reduce, output, half, block, rest_half, rest_y,
    held, rest, wide, padded, sems,
):
    core, xl, z = places[13], places[14], places[15]

    def cols(which):
        return rows_at(which * 2 * COLS + core * COLS, COLS)

    first = [
        (weight.at[rows_at(xl * 64, 64), cols(0)], held.at[pl.ds(0, 64)]),
        (weight.at[rows_at(xl * 32, 32), cols(2)], held.at[pl.ds(64, 32)]),
        (weight.at[:, cols(1)], held.at[pl.ds(96, 128)]),
        (weight.at[pl.ds(64, 64), cols(2)], held.at[pl.ds(224, 64)]),
        (
            reduce.at[rows_at(core * 256 + z * 64, 64), pl.ds(COLS, COLS)],
            held.at[pl.ds(288, 64)],
        ),
        (output.at[rows_at(z * 32, 32)], wide),
    ]
    second = [(reduce.at[rows_at(core * 256, 256), pl.ds(0, COLS)], rest.at[pl.ds(320, 256)])]
    for s in range(8):
        j, right = s // 2, (s % 2) * 256
        at = rows_at(s * 512 + core * 256, 256)
        rows, size = (rows_at(xl * 64, 64), 64) if j < 3 else (pl.ds(0, 128), 128)
        second.append((expand.at[rows, at], rest.at[pl.ds(64 * j, size), pl.ds(right, 256)]))
    first = started(first, sems.at[pl.ds(0, 6)])
    second = started(second, sems.at[pl.ds(6, 9)])
    padded[...] = jnp.zeros_like(padded)
    padded[: vector.shape[0], : vector.shape[1]] = vector[...]
    block[192:208, :] = padded[...].astype(LOW)
    finished(first)
    half[...] = held[:96].astype(LOW)
    block[:192, :] = held[96:288].astype(LOW)
    block[208:272, :] = held[288:].astype(LOW)
    block[272:304, :] = wide[:, :COLS].astype(LOW)
    block[304:336, :] = wide[:, COLS:].astype(LOW)
    finished(second)
    rest_half[...] = rest[:192].astype(LOW)
    rest_y[...] = rest[192:].astype(LOW)


def cast(places, *arrays):
    outs = [low_shape(96, COLS), low_shape(336, COLS), low_shape(192, COLS), low_shape(384, COLS)]
    vmem = pltpu.VMEM
    return call(
        cast_kernel,
        [SCALARS, OUTSIDE, INSIDE, OUTSIDE, OUTSIDE, OUTSIDE],
        [(shape, INSIDE) for shape in outs],
        [vmem((352, COLS), FULL), vmem((576, COLS), FULL), vmem((32, 2 * COLS), FULL)]
        + [vmem((16, COLS), FULL), pltpu.SemaphoreType.DMA((15,))],
        3,
        (places, *arrays),
        vmem=60,
    )


def joint_kernel(places, own, other, *refs):
    along_x, along_y, refs = refs[:4], refs[4:8], refs[8:]
    normed, query, key, value, vectors, query_mat, key_mat, value_mat, sems = refs
    mats = (query_mat, key_mat, value_mat, vectors)
    finished(started(joint_plan(places, along_x, along_y, mats), sems))
    gain, shift = row_of(vectors, 0), row_of(vectors, 1)
    core = places[13]
    query_bias = own_columns(row_of(vectors, 2), core, COLS)
    value_bias = own_columns(row_of(vectors, 3), core, COLS)
    count = own.shape[0]
    for block, tokens in enumerate((own, other)):
        rows = pl.ds(block * count, count)
        unit, _ = unit_of(tokens[...].astype(FULL))
        low = (unit * gain + shift).astype(LOW)
        normed[rows, :] = low
        query[rows, :] = ((dot(low, query_mat[...]) + query_bias).astype(LOW) * 0.125).astype(LOW)
        key[rows, :] = dot(low, key_mat[...]).astype(LOW)
        value[rows, :] = (dot(low, value_mat[...]) + value_bias).astype(LOW)


def joint(places, own, other, along_x, along_y):
    count, width = own.shape
    rows = 2 * count
    mat, half = (low_shape(width, COLS), INSIDE), (low_shape(rows, COLS), INSIDE)
    return call(
        joint_kernel,
        [SCALARS, INSIDE, INSIDE] + [OUTSIDE] * 8,
        [(low_shape(rows, width), INSIDE), half, half, half]
        + [(low_shape(16, width), INSIDE), mat, mat, mat],
        [pltpu.SemaphoreType.DMA((56,))],
        8,
        (places, own, other, *along_x, *along_y),
        vmem=24,
    )


def two_by_two(values, lane):
    return jnp.concatenate([jnp.where(lane, values, 0), jnp.where(lane, 0, values)], axis=0)


def probabilities(stacked, keys, bar):
    scores = dot_nt(stacked, keys) + jnp.concatenate([bar, bar], axis=0)
    probs = jnp.exp(scores - jnp.max(scores, axis=-1, keepdims=True))
    return probs * (1.0 / jnp.sum(probs, axis=-1, keepdims=True))


def attention_kernel(block, lengths, query, key, value, attended, mask):
    count = query.shape[0]
    mask[...] = barred(lengths, block, 0, count, count)
    lane = lax.broadcasted_iota(jnp.int32, (count, TILE), 1) < HEAD_DIM
    for index in range(COLS // TILE):
        cols = pl.ds(index * TILE, TILE)
        probs = probabilities(two_by_two(query[:, cols], lane), key[:, cols], mask[...])
        out = dot(probs.astype(LOW), value[:, cols])
        attended[:, cols] = jnp.where(lane, out[:count], out[count:]).astype(LOW)


def attention(block, lengths, query, key, value):
    count = query.shape[0] // 2
    return call(
        lambda *refs: attention_kernel(block, *refs),
        [SCALARS] + [pl.BlockSpec((count, COLS), lambda i: (block, 0))] * 3,
        [(low_shape(count, COLS), INSIDE)],
        [pltpu.VMEM((count, count), FULL)],
        5,
        (lengths, query, key, value),
        grid=(1,),
        vmem=20,
    )[0]


def output_kernel(places, own, other, *refs):
    raw, (branch, out_mat, sems) = refs[:4], refs[4:]
    finished(started(out_plan(places, lambda k: raw[k], 64, out_mat), sems))
    count = own.shape[0]
    for block, attended in enumerate((own, other)):
        for half in range(2):
            branch[block * count : (block + 1) * count, half * COLS : (half + 1) * COLS] = dot(
                attended[...], out_mat[half]
            ).astype(LOW)


def output(places, own, other, raw):
    rows, local = 2 * own.shape[0], own.shape[1]
    return call(
        output_kernel,
        [SCALARS, INSIDE, INSIDE] + [OUTSIDE] * 4,
        [(low_shape(rows, 2 * COLS), INSIDE), (low_shape(2, local, COLS), INSIDE)],
        [pltpu.SemaphoreType.DMA((32,))],
        5,
        (places, own, other, *raw),
        vmem=14,
    )


def forward_backward_kernel(
    places, lengths, own, other, arriving_own, arriving_other, branch, branch_far, vectors, *refs
):
    raw, refs = refs[:12], refs[12:]
    sent, refs = refs[:6], refs[6:]
    (middle, layer_own, layer_other, normed_grad, bias_grad,
     up, down_one, down_two, up_grad, one_grad, two_grad,
     tokens, near, far, held, normed, arriving, layer_sum, normed_sum, active, up_low,
     row_sems, sems, sems_out) = refs
    count = own.shape[0]
    blocks = [pl.ds(0, count), pl.ds(count, count)]
    rows_in = []
    for block, (token, cotangent) in enumerate(((own, arriving_own), (other, arriving_other))):
        here, there = blocks[block], blocks[1 - block]
        pairs = [
            (token, tokens.at[here]),
            (branch.at[here], near.at[here]),
            (branch_far.at[there], far.at[here]),
            (cotangent, arriving.at[here]),
        ]
        rows_in.append(started(pairs, row_sems.at[pl.ds(4 * block, 4)]))
    views = [lambda k, a=axis: raw[4 * a + k] for axis in range(3)]
    plan = up_plan(places, *views, (up, down_one, down_two))
    copies = [pltpu.make_async_copy(a, b, sems.at[i]) for i, (a, b) in enumerate(plan)]
    kinds = [up_kind(index) for index in range(len(copies))]
    for wanted in (0, None, 1, 2, 3):
        for copy, kind in zip(copies, kinds):
            if kind == wanted:
                copy.start()
    gain, shift = row_of(vectors, 5), row_of(vectors, 6)
    rows_out = []
    for block, here in enumerate(blocks):
        finished(rows_in[block])
        summed = near[here, :].astype(FULL) + far[here, :].astype(FULL)
        value = tokens[here, :].astype(FULL) + summed + row_of(vectors, 4)
        held[here, :] = value
        rows_out += started([(held.at[here], middle.at[here])], row_sems.at[pl.ds(8 + block, 1)])
        unit, _ = unit_of(value)
        normed[here, :] = (unit * gain + shift).astype(LOW)
        slots = lax.broadcasted_iota(jnp.int32, value.shape, 0)
        live = slots < lengths[block, 0] + lengths[block, 1]
        arriving[here, :] = jnp.where(live, arriving[here, :], 0)
    core = places[13]
    biases = jnp.concatenate(
        [own_columns(row_of(vectors, 7 + k), core, 256) for k in range(4)], axis=0
    )
    finished(copies)
    views = [two_of(sent[2 * axis : 2 * axis + 2]) for axis in range(3)]
    plan = turned(up_plan(places, *views, (up_grad, one_grad, two_grad)))
    copies_out = [pltpu.make_async_copy(a, b, sems_out.at[i]) for i, (a, b) in enumerate(plan)]

    def of_chunk(j, action, list_of_copies):
        for index, (copy, kind) in enumerate(zip(list_of_copies, kinds)):
            if kind == j:
                action(copy)
            elif kind is None:

                @pl.when(up_shard(places, index) // 2 == j)
                def _(copy=copy):
                    action(copy)

    for j in range(up.shape[0]):
        hidden = pl.ds(j * COLS, COLS)
        upward = dot(normed[...], up[j]) + biases[j : j + 1]
        act, slope = gelu_both(upward)
        active[...] = act.astype(LOW)
        layer_one, layer_two = dot(active[...], down_one[hidden, :]), dot(active[...], down_two[hidden, :])
        grad = dot_nt(arriving[:, :COLS], down_one[hidden, :])
        grad += dot_nt(arriving[:, COLS:], down_two[hidden, :])
        low = (grad * slope).astype(LOW)
        up_low[...] = low
        bias_grad[j : j + 1, :] = jnp.sum(low.astype(FULL), axis=0, keepdims=True)
        normed_part = dot_nt(up_low[...], up[j])
        if j == 0:
            layer_sum[:, :COLS], layer_sum[:, COLS:] = layer_one, layer_two
            normed_sum[...] = normed_part
        else:
            layer_sum[:, :COLS] += layer_one
            layer_sum[:, COLS:] += layer_two
            normed_sum[...] += normed_part
        whole = dot_tn(active[...], arriving[...]).astype(LOW)
        one_grad[hidden, :] = whole[:, :COLS]
        two_grad[hidden, :] = whole[:, COLS:]
        up_grad[j] = dot_tn(normed[...], up_low[...]).astype(LOW)
        of_chunk(j, lambda copy: copy.start(), copies_out)
    layer_own[...] = held[:count, :] + layer_sum[:count, :] + row_of(vectors, 11)
    layer_other[...] = layer_sum[count:, :].astype(LOW)
    normed_grad[...] = normed_sum[...].astype(LOW)
    finished(rows_out)
    finished(copies_out)


def forward_backward(places, lengths, tokens, arriving, branch, branch_far, vectors, raw):
    count, width = tokens[0].shape
    rows, hidden = 2 * count, 4 * COLS
    sent = [low_shape(2, 4, 192, COLS), low_shape(2, 2, 384, COLS), low_shape(2, 4, 2, 64, COLS)]
    inside = [
        full_shape(count, width), low_shape(count, width), low_shape(rows, width),
        full_shape(4, COLS),
    ]
    vmem = pltpu.VMEM
    mats = [vmem((4, width, COLS), LOW), vmem((hidden, COLS), LOW), vmem((hidden, COLS), LOW)]
    low, full = vmem((rows, width), LOW), vmem((rows, width), FULL)
    return call(
        forward_backward_kernel,
        [SCALARS, SCALARS] + [OUTSIDE] * 6 + [INSIDE] + [OUTSIDE] * 12,
        [(s, OUTSIDE) for s in sent for _ in range(2)]
        + [(full_shape(rows, width), OUTSIDE)]
        + [(s, INSIDE) for s in inside],
        mats + mats + [low, low, low, full, low, low, full, full]
        + [vmem((rows, COLS), LOW), vmem((rows, COLS), LOW)]
        + [pltpu.SemaphoreType.DMA((n,)) for n in (10, 96, 96)],
        33,
        (places, lengths, *tokens, *arriving, branch, branch_far, vectors, *raw),
        vmem=50,
    )


def output_backward_kernel(
    places, lengths, arriving_own, arriving_other, middle, part, part_far, vectors, own, other,
    out_mat, sent_one, sent_two, middle_grad, attended_grad, sums,
    held, near, far, arriving, branch, out_grad, row_sems, sems,
):
    count = arriving_own.shape[0]
    blocks = [pl.ds(0, count), pl.ds(count, count)]
    rows_in = []
    for block, cotangent in enumerate((arriving_own, arriving_other)):
        here, there = blocks[block], blocks[1 - block]
        pairs = [
            (middle.at[here], held.at[here]),
            (part.at[here], near.at[here]),
            (part_far.at[there], far.at[here]),
            (cotangent, arriving.at[here]),
        ]
        rows_in.append(started(pairs, row_sems.at[pl.ds(4 * block, 4)]))
    gain = row_of(vectors, 5)
    for block, rows in enumerate(blocks):
        finished(rows_in[block])
        unit, inverse = unit_of(held[rows, :])
        grad = near[rows, :].astype(FULL) + far[rows, :].astype(FULL)
        slots = lax.broadcasted_iota(jnp.int32, grad.shape, 0)
        live = slots < lengths[block, 0] + lengths[block, 1]
        coming = jnp.where(live, arriving[rows, :].astype(FULL), 0.0)
        result = coming + norm_backward(grad, unit, inverse, gain)
        low = result.astype(LOW)
        branch[rows, :] = low
        if block == 0:
            middle_grad[...] = result
            sums[...] = jnp.zeros_like(sums)
            sums[0:1, :] = jnp.sum(low.astype(FULL), axis=0, keepdims=True)
            sums[1:2, :] = jnp.sum(grad * unit, axis=0, keepdims=True)
            sums[2:3, :] = jnp.sum(grad, axis=0, keepdims=True)
            sums[3:4, :] = jnp.sum(coming, axis=0, keepdims=True)
    whole = dot_tn(own[...], branch[:count, :]) + dot_tn(other[...], branch[count:, :])
    out_grad[0] = whole[:, :COLS].astype(LOW)
    out_grad[1] = whole[:, COLS:].astype(LOW)
    copies = started(turned(out_plan(places, two_of((sent_one, sent_two)), 0, out_grad)), sems)
    attended_grad[...] = (
        dot_nt(branch[:, :COLS], out_mat[0]) + dot_nt(branch[:, COLS:], out_mat[1])
    ).astype(LOW)
    finished(copies)


def output_backward(
    places, lengths, arriving, middle, part, part_far, vectors, attended, out_mat
):
    rows, width = middle.shape
    sent = (low_shape(2, 4, 2, 32, COLS), OUTSIDE)
    inside = [full_shape(rows // 2, width), low_shape(rows, COLS), full_shape(8, width)]
    low = pltpu.VMEM((rows, width), LOW)
    return call(
        output_backward_kernel,
        [SCALARS, SCALARS] + [OUTSIDE] * 5 + [INSIDE] * 4,
        [sent, sent] + [(s, INSIDE) for s in inside],
        [pltpu.VMEM((rows, width), FULL), low, low, low, low, pltpu.VMEM((2, COLS, COLS), LOW)]
        + [pltpu.SemaphoreType.DMA((8,)), pltpu.SemaphoreType.DMA((32,))],
        10,
        (places, lengths, *arriving, middle, part, part_far, vectors, *attended, out_mat),
        vmem=60,
    )


def attention_backward_kernel(
    block, lengths, query, key, value, grad_in, query_grad, key_grad, value_grad, sums, mask
):
    count = query.shape[0]
    mask[...] = barred(lengths, block, 0, count, count)
    lane = lax.broadcasted_iota(jnp.int32, (count, TILE), 1) < HEAD_DIM
    for index in range(COLS // TILE):
        cols = pl.ds(index * TILE, TILE)
        stacked, given = two_by_two(query[:, cols], lane), two_by_two(grad_in[:, cols], lane)
        probs = probabilities(stacked, key[:, cols], mask[...])
        weighted = probs * dot_nt(given, value[:, cols])
        grad = (weighted - probs * jnp.sum(weighted, axis=-1, keepdims=True)).astype(LOW)
        out = dot(grad, key[:, cols])
        query_grad[:, cols] = (jnp.where(lane, out[:count], out[count:]) * 0.125).astype(LOW)
        key_grad[:, cols] = dot_tn(grad, stacked).astype(LOW)
        value_grad[:, cols] = dot_tn(probs.astype(LOW), given).astype(LOW)
    sums[...] = jnp.zeros_like(sums)
    sums[0:1, :] = jnp.sum(query_grad[...].astype(FULL), axis=0, keepdims=True)
    sums[1:2, :] = jnp.sum(value_grad[...].astype(FULL), axis=0, keepdims=True)


def attention_backward(block, lengths, query, key, value, grad_in):
    count = query.shape[0] // 2
    vmem = pltpu.VMEM
    half = (low_shape(count, COLS), INSIDE)
    part = pl.BlockSpec((count, COLS), lambda i: (block, 0))
    return call(
        lambda *refs: attention_backward_kernel(block, *refs),
        [SCALARS] + [part] * 4,
        [half, half, half, (full_shape(8, COLS), INSIDE)],
        [vmem((count, count), FULL)],
        8,
        (lengths, query, key, value, grad_in),
        grid=(1,),
        vmem=20,
    )


def joint_grad_kernel(places, normed, *refs):
    grads, sent, (query_part, key_part, value_part, sems) = refs[:6], refs[6:12], refs[12:]
    parts = (query_part, key_part, value_part)
    count = grads[0].shape[0]
    sides = [jnp.concatenate([g[...] for g in grads[i : i + 3]], axis=1) for i in (0, 3)]
    whole = dot_tn(normed[:count, :], sides[0]) + dot_tn(normed[count:, :], sides[1])
    for index, part in enumerate(parts):
        part[...] = whole[:, index * COLS : (index + 1) * COLS].astype(LOW)
    finished(started(joint_sent_plan(places, sent, parts), sems))


def joint_grad_parts(places, normed, own, other):
    rows, width = normed.shape
    sent = [low_shape(2, 4, 64, COLS), low_shape(2, 2, 128, COLS), low_shape(2, 4, 2, 32, COLS)]
    return call(
        joint_grad_kernel,
        [SCALARS] + [INSIDE] * 7,
        [(s, OUTSIDE) for s in sent for _ in range(2)],
        [pltpu.VMEM((width, COLS), LOW)] * 3 + [pltpu.SemaphoreType.DMA((56,))],
        8,
        (places, normed, *own, *other),
        vmem=60,
    )


def joint_backward_kernel(*refs):
    own, other, mats, outs = refs[:3], refs[3:6], refs[6:9], refs[9:]
    for grads, out in zip((own, other), outs):
        whole = dot_nt(grads[0][...], mats[0][...])
        whole += dot_nt(grads[1][...], mats[1][...])
        whole += dot_nt(grads[2][...], mats[2][...])
        out[...] = whole.astype(out.dtype)


def joint_backward(own, other, mats):
    count, width = own[0].shape[0], mats[0].shape[0]
    return call(
        joint_backward_kernel,
        [INSIDE] * 9,
        [(full_shape(count, width), INSIDE), (low_shape(count, width), INSIDE)],
        [],
        6,
        (*own, *other, *mats),
        vmem=20,
    )


def input_kernel(
    places, tokens, part, part_far, middle_grad, vectors, two_sums, own_sums, other_sums, up_sums,
    input_grad, sums, rows,
):
    unit, inverse = unit_of(tokens[...].astype(FULL))
    grad = part[...] + part_far[...].astype(FULL)
    input_grad[...] = middle_grad[...] + norm_backward(grad, unit, inverse, row_of(vectors, 0))
    first = places[13] == 0

    def own_side(values):
        none = jnp.zeros_like(values)
        return jnp.concatenate(
            [jnp.where(first, values, none), jnp.where(first, none, values)], axis=1
        )

    rows[...] = jnp.zeros_like(rows)
    rows[0:1, :] = jnp.sum(grad * unit, axis=0, keepdims=True)
    rows[1:2, :] = jnp.sum(grad, axis=0, keepdims=True)
    for k in range(2):
        rows[2 + k : 3 + k, :] = own_side(own_sums[k : k + 1, :] + other_sums[k : k + 1, :])
    rows[4:7, :] = two_sums[0:3, :]
    for k in range(4):
        hidden = up_sums[k : k + 1, :]
        rows[7 + k : 8 + k, :] = jnp.concatenate(
            [own_side(hidden[:, :256]), own_side(hidden[:, 256:])], axis=1
        )
    rows[11:12, :] = two_sums[3:4, :]
    sums[:16, :] = rows[:, :COLS].astype(LOW)
    sums[16:, :] = rows[:, COLS:].astype(LOW)


def input_backward(places, *arrays):
    count, width = arrays[0].shape
    return call(
        input_kernel,
        [SCALARS] + [INSIDE] * 9,
        [(full_shape(count, width), INSIDE), (low_shape(32, COLS), INSIDE)],
        [pltpu.VMEM((16, width), FULL)],
        4,
        (places, *arrays),
        vmem=20,
    )


def adam_step(weight, first, second, grad, rate, decay):
    first_new = BETA_ONE * first + (1.0 - BETA_ONE) * grad
    second_new = BETA_TWO * second + (1.0 - BETA_TWO) * grad * grad
    mean_hat = first_new / (1.0 - BETA_ONE**STEP)
    square_hat = second_new / (1.0 - BETA_TWO**STEP)
    fresh = weight - rate * (mean_hat / (jnp.sqrt(square_hat) + ADAM_EPS) + decay * weight)
    return (first_new, second_new, fresh)


def adam_kernel(grad_of, rate, chunks, places, *refs):
    state, refs = refs[:3], refs[3:]
    grads, refs = refs[:-8], refs[-8:]
    outs, (held, results, sems_in, sems_out) = refs[:4], refs[4:]
    coming = [
        started([(a.at[at], held.at[(i, *at)]) for i, a in enumerate(state)], sems_in.at[n])
        for n, at in enumerate(chunks)
    ]
    going = []
    for n, at in enumerate(chunks):
        grad = grad_of(n, places, *grads)
        finished(coming[n])
        results[(0, *at)] = grad
        weight, first, second = (held[(i, *at)] for i in range(3))
        new = adam_step(weight, first, second, grad, rate, MATRIX_DECAY)
        for i, value in enumerate(new):
            results[(1 + i, *at)] = value
        going += started(
            [(results.at[(i, *at)], out.at[at]) for i, out in enumerate(outs)], sems_out.at[n]
        )
    finished(going)


def adam(grad_of, rate, chunks, state, grads, places):
    shape = state[0].shape
    return pl.pallas_call(
        lambda *refs: adam_kernel(grad_of, rate, chunks, *refs),
        grid=(1,),
        in_specs=[SCALARS]
        + [OUTSIDE] * 3
        + [pl.BlockSpec((g[1], COLS), lambda i, at=g[2]: (at, 0)) for g in grads],
        out_specs=[OUTSIDE] * 4,
        out_shape=[full_shape(*shape)] * 4,
        scratch_shapes=[pltpu.VMEM((3, *shape), FULL), pltpu.VMEM((4, *shape), FULL)]
        + [pltpu.SemaphoreType.DMA((len(chunks), 3)), pltpu.SemaphoreType.DMA((len(chunks), 4))],
        compiler_params=pltpu.CompilerParams(vmem_limit_bytes=24 << 20),
        cost_estimate=pl.CostEstimate(
            flops=6 * FLOPS_PER_US, bytes_accessed=30 * state[0].size, transcendentals=0
        ),
    )(places, *state, *(g[0] for g in grads))


def by_core(places, both, far):
    own = places[13] == 0
    both, far = both.astype(FULL), far.astype(FULL)
    return jnp.where(own, both, far), jnp.where(own, far, both)


def columns_of(width, count):
    return [(slice(None), slice(n * width, (n + 1) * width)) for n in range(count)]


def rows_each(height, count):
    return [(slice(n * height, (n + 1) * height), slice(None)) for n in range(count)]


def adam_joint(places, state, sums):
    def grad_of(n, places, both, far):
        rows = slice(128 * n, 128 * (n + 1))
        return jnp.concatenate(by_core(places, both[rows, :], far[rows, :]), axis=1)

    grads = [(a, 384, 0) for a in sums]
    return adam(grad_of, MATRIX_RATE, columns_of(2 * COLS, 3), state, grads, places)


def adam_expand(places, state, sums):
    def grad_of(n, places, both, far):
        rows = slice(128 * n, 128 * (n + 1))
        zero, one = by_core(places, both[rows, :], far[rows, :])
        return jnp.concatenate(
            [zero[:, :256], one[:, :256], zero[:, 256:], one[:, 256:]], axis=1
        )

    grads = [(a, 512, 0) for a in sums]
    return adam(grad_of, MATRIX_RATE, columns_of(2 * COLS, 4), state, grads, places)


def adam_reduce(places, state, sums):
    def grad_of(n, places, left, right, far_left, far_right):
        rows = slice(128 * (n % 2), 128 * (n % 2 + 1))
        own = places[13] == n // 2
        return jnp.concatenate(
            [
                jnp.where(own, left[rows, :].astype(FULL), far_left[rows, :].astype(FULL)),
                jnp.where(own, right[rows, :].astype(FULL), far_right[rows, :].astype(FULL)),
            ],
            axis=1,
        )

    grads = [(a, 256, at) for a in sums for at in (2, 3)]
    return adam(grad_of, MATRIX_RATE, rows_each(128, 4), state, grads, places)


def adam_output(places, state, sums):
    def grad_of(n, places, *grads):
        both, far = grads[n], grads[2 + n]

        def rows(a):
            return jnp.concatenate(
                [
                    jnp.concatenate([a[64 * q : 64 * q + 32, :], a[64 * q + 32 : 64 * q + 64, :]], axis=1)
                    for q in (0, 1)
                ]
            ).astype(FULL)

        return jnp.where(places[13] == places[12], rows(both), rows(far))

    grads = [(a, 128, at) for a in sums for at in (3, 4)]
    return adam(grad_of, OUTPUT_RATE, rows_each(64, 2), state, grads, places)


def per_device(
    tokens,
    cotangent,
    lengths,
    joint_weight,
    joint_first,
    joint_second,
    output_weight,
    output_first,
    output_second,
    expand_weight,
    expand_first,
    expand_second,
    reduce_weight,
    reduce_first,
    reduce_second,
    vector_weight,
    vector_first,
    vector_second,
):
    me = coordinates()
    places = places_of(me)
    across = flip("core", 1)

    half, block, rest_half, rest_y = cast(
        places, joint_weight, vector_weight, expand_weight, reduce_weight, output_weight
    )
    joint_x, joint_y, along_x, along_y, along_z, far = gather_first(
        places, half, block, rest_half, rest_y, [send(a, across) for a in (lengths, tokens, cotangent)]
    )
    tokens, cotangent = (tokens, far[1]), (cotangent, far[2])
    lengths = jnp.concatenate([lengths, far[0]])

    normed_one, query, key, value, vectors, *joint_mats = joint(
        places, *tokens, joint_x, joint_y
    )
    along_z.append(send(after(along_z[1], query), turn("z", 1)))
    along_y.append(send(after(along_y[0], query), turn("y", 1)))
    along_y.append(send(after(along_y[1], query), turn("y", 1)))
    own = attention(0, lengths, after(query, along_y[1], *along_z[1:3]), key, value)
    along_x.append(send(after(along_x[1], own), turn("x", 1)))
    other = attention(1, lengths, after(query, along_x[1]), key, value)
    attended = (own, other)
    branch, out_mat = output(places, own, after(other, *along_x[2:], *along_y[2:]), along_z)
    branch_far = send(branch, across)
    *sent, middle, layer_own, layer_other, normed_two_part, up_bias_grad = forward_backward(
        places, lengths, tokens, cotangent, branch, branch_far, vectors,
        [*along_x, *along_y, *along_z],
    )
    part_far = send(normed_two_part, across)
    layer_out = (layer_own + send(layer_other, across).astype(FULL)).astype(LOW)

    out_one, out_two, middle_grad, attended_grad, two_sums = output_backward(
        places, lengths, cotangent, middle, normed_two_part, part_far, vectors, attended, out_mat
    )
    rest = total(me, sent, 0, 3, 0)
    next(rest)
    out_far = send(out_two, turn("z", 1))
    *own_grads, own_sums = attention_backward(0, lengths, query, key, value, attended_grad)
    *other_grads, other_sums = attention_backward(1, lengths, query, key, value, attended_grad)
    mark = rest.send(other_grads[0])
    sent = joint_grad_parts(places, after(normed_one, mark), own_grads, other_grads)
    joint_rows = total(me, sent, 32, 1, 32)
    next(joint_rows)
    mark = rest.send((sent[0], None, None))
    (out_near,) = added_all([[(out_one, 1), (after(out_far, mark), 1)]])
    out_near = out_near.reshape(out_one.shape[1:])
    out_again = send(out_near, turn("z", 0))
    part_own, part_other = joint_backward(
        (after(own_grads[0], out_near), *own_grads[1:]), other_grads, joint_mats
    )
    part_far = send(part_other, across)
    mark = joint_rows.send(part_own)
    mark = rest.send(mark)
    input_grad, vector_local = input_backward(
        places, tokens[0], after(part_own, mark), part_far, middle_grad, vectors, two_sums,
        own_sums, other_sums, up_bias_grad,
    )
    (out_along,) = added_all(
        [[(out_one, 0), (out_far, 0), (after(out_again, vector_local), 0)]]
    )
    out_along = out_along.reshape(out_one.shape[1:])

    mark = joint_rows.send((vector_local, vector_local, out_along))
    for turn_number in range(4):
        mark = rest.send((mark, layer_out) if turn_number == 1 else mark)
        mark = joint_rows.send(mark)
    mark = rest.send(mark)
    mark = joint_rows.send(mark)
    mark = joint_rows.send(mark)
    mark = rest.send(mark)
    mark = joint_rows.send(mark)
    one, two, extra = next(joint_rows)
    joint_state = adam_joint(
        places, (joint_weight, joint_first, joint_second), (after(one, mark), two)
    )
    output_state = adam_output(
        places, (output_weight, output_first, output_second), (after(one, mark), two)
    )
    one, two, _ = next(rest)
    one = after(one, joint_state[0], output_state[0])
    expand = adam_expand(places, (expand_weight, expand_first, expand_second), (one, two))
    reduce = adam_reduce(places, (reduce_weight, reduce_first, reduce_second), (one, two))
    vector_grad = lax.dynamic_slice(
        jnp.concatenate([extra[:12], extra[16:28]], axis=1).astype(FULL),
        (0, 128 * lax.axis_index("shard")),
        (12, 128),
    )
    vector_state = (vector_grad,) + adam_step(
        vector_weight, vector_first, vector_second, vector_grad, VECTOR_RATE, 0.0
    )
    states = zip(joint_state, output_state, expand, reduce, vector_state)
    return (layer_out, input_grad, *(a for kind in states for a in kind))


def solution(mesh):
    rows, columns, split = P("shard", None), P(None, "shard"), P(("wide", "shard"), None)
    state = (rows, rows, rows, rows, columns)
    return jax.shard_map(
        per_device,
        mesh=mesh,
        in_specs=(split, split, split) + (rows,) * 12 + (columns,) * 3,
        out_specs=(split, split) + state * 4,
        check_vma=False,
    )
```

```python
import jax
import jax.numpy as jnp
from jax import lax
from jax.experimental import pallas as pl
from jax.experimental.pallas import tpu as pltpu
from jax.sharding import PartitionSpec as P

HEAD_DIM = 64
STEP = 10


ROOT_TWO_PI = 0.7978845608028654
CUBIC = 0.044715
BETA_ONE = 0.9
BETA_TWO = 0.999
ADAM_EPS = 1e-08
MATRIX_RATE = 0.03
OUTPUT_RATE = 0.1
VECTOR_RATE = 0.2
MATRIX_DECAY = 0.1

LOW = jnp.bfloat16
FULL = jnp.float32
AXES = ("wide", "shard")
SIZES = (4, 2, 2, 2, 4)
COLS = 512
FLOPS_PER_US = 1_150_000_000


def coordinates():
    wide, shard = lax.axis_index("wide"), lax.axis_index("shard")
    z, xl, core = wide // 4, (wide // 2) % 2, wide % 2
    xh, y = shard // 4, shard % 4
    return {"z": z, "x": 2 * xh + xl, "y": y, "xl": xl, "xh": xh, "core": core}


def route(partner):
    pairs = []
    for source in range(128):
        rest, places = source, []
        for size in reversed(SIZES):
            places.append(rest % size)
            rest //= size
        y, xh, core, xl, z = places
        target = partner({"z": z, "x": 2 * xh + xl, "y": y, "core": core})
        flat = 0
        for place, size in zip(
            (target["z"], target["x"] % 2, target["core"], target["x"] // 2, target["y"]), SIZES
        ):
            flat = flat * size + place
        pairs.append((source, flat))
    return pairs


def flip(axis, bits):
    return route(lambda at: {**at, axis: at[axis] ^ bits})


def turn(axis, step):
    return route(lambda at: {**at, axis: at[axis] ^ (1 if (at["core"] + step) % 2 == 0 else 3)})


def send(value, pairs):
    return lax.ppermute(value, AXES, pairs)


def added(*terms):
    return sum(term.astype(FULL) for term in terms).astype(LOW)


def orders(me, axis):
    here = me[axis]
    one = jnp.where(me["core"] == 0, 1, 3)
    return [here, here ^ one, here ^ (4 - one), here ^ 2]


def places_of(me):
    return jnp.stack(
        orders(me, "x")
        + orders(me, "y")
        + orders(me, "z")
        + [me["xh"], me["core"], me["xl"], me["z"]]
    ).astype(jnp.int32)


def after(value, *others):
    return lax.optimization_barrier((value, *others))[0]


def rows_of(*parts):
    return jnp.concatenate([p.reshape(-1, COLS) for p in parts])


def main_phase(block, axis, gate, late=False):
    first, second = send(block, turn(axis, 0)), send(gated(block, gate if late else None), turn(axis, 1))
    return [block, first, second, send(after(first, gate), turn(axis, 1))]


def pack_kernel(places, block, other, half, second, first, again):
    for out in (first, again):
        out[:208, :] = block[:208, :]
        out[208:416, :] = other[:208, :]
    again[416:512, :] = half[...]
    again[512:608, :] = second[...]
    own = places[13] == places[12]
    for p, held in enumerate((block, other)):
        at = 416 + 96 * p
        first[at : at + 64, :] = held[208:272, :]
        rows = slice(272 + 32 * p, 304 + 32 * p)
        first[at + 64 : at + 96, :] = jnp.where(own, block[rows, :], other[rows, :])


def pack(places, *arrays):
    return call(
        pack_kernel,
        [SCALARS] + [INSIDE] * 4,
        [(low_shape(608, COLS), INSIDE)] * 2,
        [],
        1,
        (places, *arrays),
        vmem=8,
    )


def gather_first(places, half, block, rest_half, rest_y, exchanged):
    size = half.shape[0]
    other, second, *early = lax.optimization_barrier(
        (send(block, flip("x", 3)), send(half, turn("y", 0)), *exchanged[:2])
    )
    own_y, both = pack(places, block, other, half, second)
    first_y, second_y = send(own_y, turn("y", 0)), send(both, turn("y", 1))
    rest_other = send(after(rest_y, other), flip("x", 3))
    first_y, second_y, rest_other, *late = lax.optimization_barrier(
        (first_y, second_y, rest_other, *exchanged[2:])
    )
    plane = rows_of(half, second, second_y[416:]).reshape(4, size, COLS)
    first_x, second_x = send(plane, turn("x", 0)), send(plane, turn("x", 1))
    third_y = send(rows_of(first_y[:416], own_y[416:], first_y[416:]), turn("y", 1))
    rest_near = send(after(rest_half, first_y), turn("y", 0))
    first_x, second_x, third_y, rest_near = lax.optimization_barrier(
        (first_x, second_x, third_y, rest_near)
    )
    third_x = send(first_x, turn("x", 1))
    here = rows_of(rest_half, rest_near)
    there = send(here, turn("y", 1))
    plane_z = rows_of(own_y[416:], first_y[416:], third_y[416:]).reshape(4, 2, 96, COLS)
    pair_y = jnp.stack([rest_y, rest_other])
    along_z = [plane_z, send(plane_z, turn("z", 0)), send(plane_z, turn("z", 1))]
    along_y = [pair_y, send(after(pair_y, third_y), turn("y", 0))]
    third_x, there = lax.optimization_barrier((third_x, there))
    plane_x = rows_of(here, there).reshape(4, -1, COLS)
    along_x = [plane_x, send(plane_x, turn("x", 0)), send(plane_x, turn("x", 1))]
    joint_x = [plane, first_x, second_x, third_x]
    joint_y = [own_y, first_y, second_y, third_y]
    return joint_x, joint_y, along_x, along_y, along_z, early + late


def added_all(sums, steps=2):
    terms, specs, outs, out_specs = [], [], [], []
    for group in sums:
        rows = min(a.size for a, _ in group) // COLS
        rows = rows // 2 if len(group) == 2 else rows
        for array, which in group:
            terms.append(array.reshape(-1, COLS))
            specs.append(
                pl.BlockSpec((rows // steps, COLS), lambda i, at=which * steps: (at + i, 0))
            )
        outs.append(low_shape(rows, COLS))
        out_specs.append(pl.BlockSpec((rows // steps, COLS), lambda i: (i, 0)))

    def kernel(*refs):
        at = 0
        for group, out in zip(sums, refs[len(terms) :]):
            out[...] = added(*(ref[...] for ref in refs[at : at + len(group)]))
            at += len(group)

    return pl.pallas_call(
        kernel,
        grid=(steps,),
        in_specs=specs,
        out_specs=out_specs,
        out_shape=outs,
        compiler_params=pltpu.CompilerParams(vmem_limit_bytes=12 << 20),
        cost_estimate=pl.CostEstimate(
            flops=3 * FLOPS_PER_US, bytes_accessed=6 * sum(o.size for o in outs), transcendentals=0
        ),
    )(*terms)


def assembled(me, mine, far, behind, pieces):
    behind = [a.reshape(-1, COLS) for a in behind]
    rows = 2 * mine.shape[0] + sum(a.shape[0] for a in behind)

    def kernel(right, mine, far, *refs):
        behind, out = refs[:-1], refs[-1]
        first = right[0] == 0
        source = target = 0
        for count, size in pieces:
            for _ in range(count):
                a, b = mine[source : source + size, :], far[source : source + size, :]
                out[target : target + size, :] = jnp.where(first, a, b)
                out[target + size : target + 2 * size, :] = jnp.where(first, b, a)
                source, target = source + size, target + 2 * size
        for part in behind:
            out[target : target + part.shape[0], :] = part[...]
            target += part.shape[0]

    return pl.pallas_call(
        kernel,
        out_shape=low_shape(rows, COLS),
        in_specs=[pl.BlockSpec(memory_space=pltpu.SMEM)]
        + [pl.BlockSpec(memory_space=pltpu.VMEM)] * (2 + len(behind)),
        out_specs=pl.BlockSpec(memory_space=pltpu.VMEM),
        compiler_params=pltpu.CompilerParams(vmem_limit_bytes=8 << 20),
        cost_estimate=pl.CostEstimate(
            flops=FLOPS_PER_US, bytes_accessed=4 * rows * COLS, transcendentals=0
        ),
    )(me["xl"].reshape(1).astype(jnp.int32), mine, far, *behind)


def gated(value, gate):
    return value if gate is None else after(value, *(gate if isinstance(gate, tuple) else (gate,)))


def total(me, raw, out_rows, units, extra_rows):
    axes = "xyz"
    parts = [raw[:2], raw[2:4], raw[4:]]
    far = [send(away, turn(axis, 1)) for (_, away), axis in zip(parts, axes)]
    gate = yield
    far = list(far if gate is None else lax.optimization_barrier((*far, gate))[:-1])
    keeps = [keep for keep, _ in parts]
    near = added_all([[(k, 1), (f, 1)] for k, f in zip(keeps, far)])
    near = lax.optimization_barrier([n.reshape(k.shape[1:]) for n, k in zip(near, keeps)])
    again = [send(n, turn(axis, 0)) for n, axis in zip(near, axes)]
    gate, extra, out = yield near[2]
    again = lax.optimization_barrier((*again, gate))[:-1]
    along = added_all([[(k, 0), (f, 0), (a, 0)] for k, f, a in zip(keeps, far, again)])
    along_x, along_y, along_z = lax.optimization_barrier(
        [a.reshape(k.shape[1:]) for a, k in zip(along, keeps)]
    )
    if out_rows:
        along_z = jnp.concatenate([along_z, out], axis=2)
    size_x, size_y = along_x.shape[1], along_y.shape[1] // 2
    size_z = (along_z.shape[2] - out_rows) // 2

    def with_extra(*parts):
        return rows_of(*parts, extra) if extra_rows else rows_of(*parts)

    def split(rows, *sizes):
        at, parts = 0, []
        for size in sizes:
            parts.append(rows[at : at + size])
            at += size
        return parts

    plane = jnp.concatenate([along_x, along_z.reshape(4, -1, COLS)], axis=1)
    size = plane.shape[1]
    far = send(with_extra(plane[2:]), turn("y", 1))
    gate = yield plane
    far, kept = gated(far, gate), plane[:2]
    near = added(kept[1], far[size : 2 * size])
    if extra_rows:
        extra = added(extra, far[2 * size :])
    again = send(with_extra(near), turn("y", 0))
    gate = yield near
    again = gated(again, gate)
    plane = added(kept[0], far[:size], again[:size])
    if extra_rows:
        extra = added(extra, again[size:])
    half, pair = plane[:size_x], plane[size_x:].reshape(2, 2 * size_z + out_rows, COLS)
    out = pair[:, 2 * size_z :].reshape(-1, COLS)
    pieces = jnp.concatenate(
        [along_y.reshape(4, size_y, COLS), pair[:, : 2 * size_z].reshape(4, size_z, COLS)], axis=1
    )
    size = size_y + size_z
    pieces = [
        lax.dynamic_index_in_dim(pieces, ((k // 2) ^ me["xh"]) * 2 + k % 2, 0, keepdims=False)
        for k in orders(me, "x")
    ]
    far = send(with_extra(pieces[2], pieces[3], out), turn("x", 1))
    gate = yield plane
    far = gated(far, gate)
    first, second, far_out, far_extra = split(far, size, size, 2 * out_rows, extra_rows)
    sums = added(rows_of(pieces[1], out), rows_of(second, far_out))
    if extra_rows:
        extra = added(extra, far_extra)
    again = send(with_extra(sums), turn("x", 0))
    gate = yield sums
    near, out, far_extra = split(gated(again, gate), size, 2 * out_rows, extra_rows)
    sums = rows_of(added(pieces[0], first, near), added(sums[size:], out))
    if extra_rows:
        extra = added(extra, far_extra)
    flat, block = rows_of(half, sums[:size_y]), sums[size_y:]
    size, size_block = flat.shape[0], block.shape[0]
    far = send(with_extra(flat, block), turn("z", 0))
    gate = yield sums
    sums, other, far_extra = split(gated(far, gate), size, size_block, extra_rows)
    flat = added(flat, sums)
    if extra_rows:
        extra = added(extra, far_extra)
    blocks = rows_of(block, other)
    far = send(with_extra(flat, blocks), turn("z", 1))
    gate = yield flat
    sums, other, far_extra = split(gated(far, gate), size, 2 * size_block, extra_rows)
    flat = added(flat, sums)
    if extra_rows:
        extra = added(extra, far_extra)
    blocks = rows_of(blocks, other).reshape(4, size_block, COLS)
    where = orders(me, "z")
    ordered = jnp.stack(
        [
            sum(jnp.where(where[k] == place, blocks[k], 0) for k in range(4)).astype(LOW)
            for place in range(4)
        ]
    )
    mine = rows_of(flat, ordered[:, :size_z])
    far = send(mine, flip("x", 1))
    gate = yield mine
    far = gated(far, gate)

    pieces = [(units, size_x // units), (1, size_y), (4, size_z)]
    both = assembled(me, mine, far, [ordered[:, size_z:]] if out_rows else [], pieces)
    far = send(with_extra(both), flip("core", 1))
    yield both
    rows = both.shape[0]
    if extra_rows:
        extra = added(extra, far[rows:])
        far = far[:rows]
    yield both, far, extra


def rows_at(start, size):
    return pl.ds(pl.multiple_of(start, size), size)


def joint_plan(places, along_x, along_y, mats):
    query, key, value, vectors = mats
    pairs = []
    for ky in range(4):
        y = places[4 + ky]
        for kx in range(4):
            x = places[kx]
            shard, half = (x // 2) * 4 + y, x % 2
            source = along_x[kx].at[ky]
            pairs.append(
                (source.at[pl.ds(0, 64)], query.at[rows_at(shard * 128 + half * 64, 64)])
            )
            pairs.append(
                (source.at[pl.ds(64, 32)], value.at[rows_at(shard * 128 + half * 32, 32)])
            )
        for p in range(2):
            shard = (places[12] ^ p) * 4 + y
            source, at = along_y[ky], p * 208
            pairs.append((source.at[pl.ds(at, 128)], key.at[rows_at(shard * 128, 128)]))
            pairs.append((source.at[pl.ds(at + 128, 64)], value.at[rows_at(shard * 128 + 64, 64)]))
            pairs.append(
                (
                    source.at[pl.ds(at + 192, 16), pl.ds(0, 128)],
                    vectors.at[:, rows_at(shard * 128, 128)],
                )
            )
    return pairs


def joint_sent_plan(places, raw, parts):
    query, key, value = parts
    pairs = []
    for ky in range(4):
        y = places[4 + ky]
        for kx in range(4):
            x = places[kx]
            start = ((x // 2) * 4 + y) * 128 + (x % 2) * 64
            pairs.append((query.at[rows_at(start, 64)], raw[0 + kx // 2].at[kx % 2, ky]))
        for p in range(2):
            shard = (places[12] ^ p) * 4 + y
            pairs.append((key.at[rows_at(shard * 128, 128)], raw[2 + ky // 2].at[ky % 2, p]))
            for kz in range(4):
                start = shard * 128 + places[8 + kz] * 32
                pairs.append((value.at[rows_at(start, 32)], raw[4 + kz // 2].at[kz % 2, ky, p]))
    return pairs


def up_plan(places, at_x, at_y, at_z, mats):
    up, down_one, down_two = mats
    pairs = []
    for ky in range(4):
        y = places[4 + ky]
        for kx in range(4):
            x = places[kx]
            start = ((x // 2) * 4 + y) * 128 + (x % 2) * 64
            for j in range(3):
                source = at_x(kx).at[ky, pl.ds(64 * j, 64)]
                pairs.append((source, up.at[j, rows_at(start, 64)]))
        for p in range(2):
            shard = (places[12] ^ p) * 4 + y
            source = at_y(ky).at[p]
            pairs.append((source.at[pl.ds(0, 128)], up.at[3, rows_at(shard * 128, 128)]))
            pairs.append((source.at[pl.ds(128, 256)], down_one.at[rows_at(shard * 256, 256)]))
            for kz in range(4):
                start = shard * 256 + places[8 + kz] * 64
                source = at_z(kz).at[ky, p, pl.ds(0, 64)]
                pairs.append((source, down_two.at[rows_at(start, 64)]))
    return pairs


def up_kind(index):
    index %= 24
    if index < 12:
        return index % 3
    return 3 if (index - 12) % 6 == 0 else None


def up_shard(places, index):
    ky, index = divmod(index, 24)
    return (places[12] ^ ((index - 12) // 6)) * 4 + places[4 + ky]


def out_plan(places, at_z, first, mat):
    pairs = []
    for ky in range(4):
        for kz in range(4):
            start = places[4 + ky] * 128 + places[8 + kz] * 32
            for p in range(2):
                source = at_z(kz).at[ky, p, pl.ds(first, 32)]
                pairs.append((source, mat.at[p, rows_at(start, 32)]))
    return pairs


def two_of(arrays):
    return lambda k: arrays[k // 2].at[k % 2]


def started(pairs, sems):
    all_of_them = [pltpu.make_async_copy(a, b, sems.at[i]) for i, (a, b) in enumerate(pairs)]
    for copy in all_of_them:
        copy.start()
    return all_of_them


def finished(all_of_them):
    for copy in all_of_them:
        copy.wait()


def turned(pairs):
    return [(b, a) for a, b in pairs]


def low_shape(*shape):
    return jax.ShapeDtypeStruct(shape, LOW)


def full_shape(*shape):
    return jax.ShapeDtypeStruct(shape, FULL)


SCALARS = pl.BlockSpec(memory_space=pltpu.SMEM)
INSIDE = pl.BlockSpec(memory_space=pltpu.VMEM)
OUTSIDE = pl.BlockSpec(memory_space=pl.ANY)
FAR_OUTSIDE = pl.BlockSpec(memory_space=pltpu.HBM)


def call(kernel, in_specs, outs, scratch, length, args, grid=(), vmem=60):
    shapes, specs = [o[0] for o in outs], [o[1] for o in outs]
    moved = sum(a.size * a.dtype.itemsize for a in (*args, *shapes))
    return pl.pallas_call(
        kernel,
        grid=grid,
        out_shape=shapes,
        in_specs=in_specs,
        out_specs=specs,
        scratch_shapes=scratch,
        compiler_params=pltpu.CompilerParams(vmem_limit_bytes=vmem << 20),
        cost_estimate=pl.CostEstimate(
            flops=length * FLOPS_PER_US, bytes_accessed=moved, transcendentals=0
        ),
    )(*args)


def gelu_both(upward):
    square = upward * upward
    tangent = jnp.tanh(ROOT_TWO_PI * upward * (1.0 + CUBIC * square))
    half = 0.5 * (1.0 + tangent)
    slope = half + 0.5 * upward * (1.0 - tangent * tangent) * ROOT_TWO_PI * (
        1.0 + 3.0 * CUBIC * square
    )
    return upward * half, slope


def dot(a, b):
    return jnp.dot(a, b, preferred_element_type=FULL)


def dot_nt(a, b):
    return lax.dot_general(a, b, (((1,), (1,)), ((), ())), preferred_element_type=FULL)


def dot_tn(a, b):
    return lax.dot_general(a, b, (((0,), (0,)), ((), ())), preferred_element_type=FULL)


def unit_of(values):
    center = values - jnp.mean(values, axis=-1, keepdims=True)
    inverse = lax.rsqrt(jnp.mean(center * center, axis=-1, keepdims=True) + 1e-05)
    return center * inverse, inverse


def norm_backward(grad_out, unit, inverse, gain):
    scaled = grad_out * gain
    return inverse * (
        scaled
        - jnp.mean(scaled, axis=-1, keepdims=True)
        - unit * jnp.mean(scaled * unit, axis=-1, keepdims=True)
    )


def row_of(vectors, row):
    return vectors[row : row + 1, :].astype(FULL)


def own_columns(full, core, size):
    groups = full.shape[1] // (2 * size)
    first = jnp.concatenate(
        [full[:, (2 * g) * size : (2 * g + 1) * size] for g in range(groups)], axis=1
    )
    second = jnp.concatenate(
        [full[:, (2 * g + 1) * size : (2 * g + 2) * size] for g in range(groups)], axis=1
    )
    return jnp.where(core == 0, first, second)


def barred(lengths, block, first, height, span):
    shape = (height, span)
    rows = lax.broadcasted_iota(jnp.int32, shape, 0) + first
    keys = lax.broadcasted_iota(jnp.int32, shape, 1)
    opening = lengths[block, 0]
    filled = opening + lengths[block, 1]
    begin = jnp.where(rows < opening, 0, jnp.where(rows < filled, opening, rows))
    return jnp.where((keys <= rows) & (keys >= begin), 0.0, -1e30)


TILE = 128


def cast_kernel(
    places, weight, vector, expand, reduce, output, half, block, rest_half, rest_y,
    held, rest, wide, padded, sems,
):
    core, xl, z = places[13], places[14], places[15]

    def cols(which):
        return rows_at(which * 2 * COLS + core * COLS, COLS)

    first = [
        (weight.at[rows_at(xl * 64, 64), cols(0)], held.at[pl.ds(0, 64)]),
        (weight.at[rows_at(xl * 32, 32), cols(2)], held.at[pl.ds(64, 32)]),
        (weight.at[:, cols(1)], held.at[pl.ds(96, 128)]),
        (weight.at[pl.ds(64, 64), cols(2)], held.at[pl.ds(224, 64)]),
        (
            reduce.at[rows_at(core * 256 + z * 64, 64), pl.ds(COLS, COLS)],
            held.at[pl.ds(288, 64)],
        ),
        (output.at[rows_at(z * 32, 32)], wide),
    ]
    second = [(reduce.at[rows_at(core * 256, 256), pl.ds(0, COLS)], rest.at[pl.ds(320, 256)])]
    for s in range(8):
        j, right = s // 2, (s % 2) * 256
        at = rows_at(s * 512 + core * 256, 256)
        rows, size = (rows_at(xl * 64, 64), 64) if j < 3 else (pl.ds(0, 128), 128)
        second.append((expand.at[rows, at], rest.at[pl.ds(64 * j, size), pl.ds(right, 256)]))
    first = started(first, sems.at[pl.ds(0, 6)])
    second = started(second, sems.at[pl.ds(6, 9)])
    padded[...] = jnp.zeros_like(padded)
    padded[: vector.shape[0], : vector.shape[1]] = vector[...]
    block[192:208, :] = padded[...].astype(LOW)
    finished(first)
    half[...] = held[:96].astype(LOW)
    block[:192, :] = held[96:288].astype(LOW)
    block[208:272, :] = held[288:].astype(LOW)
    block[272:304, :] = wide[:, :COLS].astype(LOW)
    block[304:336, :] = wide[:, COLS:].astype(LOW)
    finished(second)
    rest_half[...] = rest[:192].astype(LOW)
    rest_y[...] = rest[192:].astype(LOW)


def cast(places, *arrays):
    outs = [low_shape(96, COLS), low_shape(336, COLS), low_shape(192, COLS), low_shape(384, COLS)]
    vmem = pltpu.VMEM
    return call(
        cast_kernel,
        [SCALARS, OUTSIDE, INSIDE, OUTSIDE, OUTSIDE, OUTSIDE],
        [(shape, INSIDE) for shape in outs],
        [vmem((352, COLS), FULL), vmem((576, COLS), FULL), vmem((32, 2 * COLS), FULL)]
        + [vmem((16, COLS), FULL), pltpu.SemaphoreType.DMA((15,))],
        3,
        (places, *arrays),
        vmem=60,
    )


def joint_kernel(places, own, other, *refs):
    along_x, along_y, refs = refs[:4], refs[4:8], refs[8:]
    normed, query, key, value, vectors, query_mat, key_mat, value_mat, sems = refs
    mats = (query_mat, key_mat, value_mat, vectors)
    finished(started(joint_plan(places, along_x, along_y, mats), sems))
    gain, shift = row_of(vectors, 0), row_of(vectors, 1)
    core = places[13]
    query_bias = own_columns(row_of(vectors, 2), core, COLS)
    value_bias = own_columns(row_of(vectors, 3), core, COLS)
    count = own.shape[0]
    for block, tokens in enumerate((own, other)):
        rows = pl.ds(block * count, count)
        unit, _ = unit_of(tokens[...].astype(FULL))
        low = (unit * gain + shift).astype(LOW)
        normed[rows, :] = low
        query[rows, :] = ((dot(low, query_mat[...]) + query_bias).astype(LOW) * 0.125).astype(LOW)
        key[rows, :] = dot(low, key_mat[...]).astype(LOW)
        value[rows, :] = (dot(low, value_mat[...]) + value_bias).astype(LOW)


def joint(places, own, other, along_x, along_y):
    count, width = own.shape
    rows = 2 * count
    mat, half = (low_shape(width, COLS), INSIDE), (low_shape(rows, COLS), INSIDE)
    return call(
        joint_kernel,
        [SCALARS, INSIDE, INSIDE] + [OUTSIDE] * 8,
        [(low_shape(rows, width), INSIDE), half, half, half]
        + [(low_shape(16, width), INSIDE), mat, mat, mat],
        [pltpu.SemaphoreType.DMA((56,))],
        8,
        (places, own, other, *along_x, *along_y),
        vmem=24,
    )


def two_by_two(values, lane):
    return jnp.concatenate([jnp.where(lane, values, 0), jnp.where(lane, 0, values)], axis=0)


def probabilities(stacked, keys, bar):
    scores = dot_nt(stacked, keys) + jnp.concatenate([bar, bar], axis=0)
    probs = jnp.exp(scores - jnp.max(scores, axis=-1, keepdims=True))
    return probs * (1.0 / jnp.sum(probs, axis=-1, keepdims=True))


def attention_kernel(block, lengths, query, key, value, attended, mask):
    count = query.shape[0]
    mask[...] = barred(lengths, block, 0, count, count)
    lane = lax.broadcasted_iota(jnp.int32, (count, TILE), 1) < HEAD_DIM
    for index in range(COLS // TILE):
        cols = pl.ds(index * TILE, TILE)
        probs = probabilities(two_by_two(query[:, cols], lane), key[:, cols], mask[...])
        out = dot(probs.astype(LOW), value[:, cols])
        attended[:, cols] = jnp.where(lane, out[:count], out[count:]).astype(LOW)


def attention(block, lengths, query, key, value):
    count = query.shape[0] // 2
    return call(
        lambda *refs: attention_kernel(block, *refs),
        [SCALARS] + [pl.BlockSpec((count, COLS), lambda i: (block, 0))] * 3,
        [(low_shape(count, COLS), INSIDE)],
        [pltpu.VMEM((count, count), FULL)],
        5,
        (lengths, query, key, value),
        grid=(1,),
        vmem=20,
    )[0]


def output_kernel(places, own, other, *refs):
    raw, (branch, out_mat, sems) = refs[:4], refs[4:]
    finished(started(out_plan(places, lambda k: raw[k], 64, out_mat), sems))
    count = own.shape[0]
    for block, attended in enumerate((own, other)):
        for half in range(2):
            branch[block * count : (block + 1) * count, half * COLS : (half + 1) * COLS] = dot(
                attended[...], out_mat[half]
            ).astype(LOW)


def output(places, own, other, raw):
    rows, local = 2 * own.shape[0], own.shape[1]
    return call(
        output_kernel,
        [SCALARS, INSIDE, INSIDE] + [OUTSIDE] * 4,
        [(low_shape(rows, 2 * COLS), INSIDE), (low_shape(2, local, COLS), INSIDE)],
        [pltpu.SemaphoreType.DMA((32,))],
        5,
        (places, own, other, *raw),
        vmem=14,
    )


def forward_backward_kernel(
    places, lengths, own, other, arriving_own, arriving_other, branch, branch_far, vectors, *refs
):
    raw, refs = refs[:12], refs[12:]
    sent, refs = refs[:6], refs[6:]
    (middle, layer_own, layer_other, normed_grad, bias_grad,
     up, down_one, down_two, up_grad, one_grad, two_grad,
     tokens, near, far, held, normed, arriving, layer_sum, normed_sum, active, up_low,
     row_sems, sems, sems_out) = refs
    count = own.shape[0]
    blocks = [pl.ds(0, count), pl.ds(count, count)]
    rows_in = []
    for block, (token, cotangent) in enumerate(((own, arriving_own), (other, arriving_other))):
        here, there = blocks[block], blocks[1 - block]
        pairs = [
            (token, tokens.at[here]),
            (branch.at[here], near.at[here]),
            (branch_far.at[there], far.at[here]),
            (cotangent, arriving.at[here]),
        ]
        rows_in.append(started(pairs, row_sems.at[pl.ds(4 * block, 4)]))
    views = [lambda k, a=axis: raw[4 * a + k] for axis in range(3)]
    plan = up_plan(places, *views, (up, down_one, down_two))
    copies = [pltpu.make_async_copy(a, b, sems.at[i]) for i, (a, b) in enumerate(plan)]
    kinds = [up_kind(index) for index in range(len(copies))]
    for wanted in (0, None, 1, 2, 3):
        for copy, kind in zip(copies, kinds):
            if kind == wanted:
                copy.start()
    gain, shift = row_of(vectors, 5), row_of(vectors, 6)
    rows_out = []
    for block, here in enumerate(blocks):
        finished(rows_in[block])
        summed = near[here, :].astype(FULL) + far[here, :].astype(FULL)
        value = tokens[here, :].astype(FULL) + summed + row_of(vectors, 4)
        held[here, :] = value
        rows_out += started([(held.at[here], middle.at[here])], row_sems.at[pl.ds(8 + block, 1)])
        unit, _ = unit_of(value)
        normed[here, :] = (unit * gain + shift).astype(LOW)
        slots = lax.broadcasted_iota(jnp.int32, value.shape, 0)
        live = slots < lengths[block, 0] + lengths[block, 1]
        arriving[here, :] = jnp.where(live, arriving[here, :], 0)
    core = places[13]
    biases = jnp.concatenate(
        [own_columns(row_of(vectors, 7 + k), core, 256) for k in range(4)], axis=0
    )
    finished(copies)
    views = [two_of(sent[2 * axis : 2 * axis + 2]) for axis in range(3)]
    plan = turned(up_plan(places, *views, (up_grad, one_grad, two_grad)))
    copies_out = [pltpu.make_async_copy(a, b, sems_out.at[i]) for i, (a, b) in enumerate(plan)]

    def of_chunk(j, action, list_of_copies):
        for index, (copy, kind) in enumerate(zip(list_of_copies, kinds)):
            if kind == j:
                action(copy)
            elif kind is None:

                @pl.when(up_shard(places, index) // 2 == j)
                def _(copy=copy):
                    action(copy)

    for j in range(up.shape[0]):
        hidden = pl.ds(j * COLS, COLS)
        upward = dot(normed[...], up[j]) + biases[j : j + 1]
        act, slope = gelu_both(upward)
        active[...] = act.astype(LOW)
        layer_one, layer_two = dot(active[...], down_one[hidden, :]), dot(active[...], down_two[hidden, :])
        grad = dot_nt(arriving[:, :COLS], down_one[hidden, :])
        grad += dot_nt(arriving[:, COLS:], down_two[hidden, :])
        low = (grad * slope).astype(LOW)
        up_low[...] = low
        bias_grad[j : j + 1, :] = jnp.sum(low.astype(FULL), axis=0, keepdims=True)
        normed_part = dot_nt(up_low[...], up[j])
        if j == 0:
            layer_sum[:, :COLS], layer_sum[:, COLS:] = layer_one, layer_two
            normed_sum[...] = normed_part
        else:
            layer_sum[:, :COLS] += layer_one
            layer_sum[:, COLS:] += layer_two
            normed_sum[...] += normed_part
        whole = dot_tn(active[...], arriving[...]).astype(LOW)
        one_grad[hidden, :] = whole[:, :COLS]
        two_grad[hidden, :] = whole[:, COLS:]
        up_grad[j] = dot_tn(normed[...], up_low[...]).astype(LOW)
        of_chunk(j, lambda copy: copy.start(), copies_out)
    layer_own[...] = held[:count, :] + layer_sum[:count, :] + row_of(vectors, 11)
    layer_other[...] = layer_sum[count:, :].astype(LOW)
    normed_grad[...] = normed_sum[...].astype(LOW)
    finished(rows_out)
    finished(copies_out)


def forward_backward(places, lengths, tokens, arriving, branch, branch_far, vectors, raw):
    count, width = tokens[0].shape
    rows, hidden = 2 * count, 4 * COLS
    sent = [low_shape(2, 4, 192, COLS), low_shape(2, 2, 384, COLS), low_shape(2, 4, 2, 64, COLS)]
    inside = [
        full_shape(count, width), low_shape(count, width), low_shape(rows, width),
        full_shape(4, COLS),
    ]
    vmem = pltpu.VMEM
    mats = [vmem((4, width, COLS), LOW), vmem((hidden, COLS), LOW), vmem((hidden, COLS), LOW)]
    low, full = vmem((rows, width), LOW), vmem((rows, width), FULL)
    return call(
        forward_backward_kernel,
        [SCALARS, SCALARS] + [OUTSIDE] * 6 + [INSIDE] + [OUTSIDE] * 12,
        [(s, OUTSIDE) for s in sent for _ in range(2)]
        + [(full_shape(rows, width), OUTSIDE)]
        + [(s, INSIDE) for s in inside],
        mats + mats + [low, low, low, full, low, low, full, full]
        + [vmem((rows, COLS), LOW), vmem((rows, COLS), LOW)]
        + [pltpu.SemaphoreType.DMA((n,)) for n in (10, 96, 96)],
        33,
        (places, lengths, *tokens, *arriving, branch, branch_far, vectors, *raw),
        vmem=50,
    )


def output_backward_kernel(
    places, lengths, arriving_own, arriving_other, middle, part, part_far, vectors, own, other,
    out_mat, sent_one, sent_two, middle_grad, attended_grad, sums,
    held, near, far, arriving, branch, out_grad, attended, weights, row_sems, sems,
):
    count = arriving_own.shape[0]
    blocks = [pl.ds(0, count), pl.ds(count, count)]
    rows_in = []
    for block, cotangent in enumerate((arriving_own, arriving_other)):
        here, there = blocks[block], blocks[1 - block]
        pairs = [
            (middle.at[here], held.at[here]),
            (part.at[here], near.at[here]),
            (part_far.at[there], far.at[here]),
            (cotangent, arriving.at[here]),
        ]
        rows_in.append(started(pairs, row_sems.at[pl.ds(4 * block, 4)]))
    pairs = [(own, attended.at[blocks[0]]), (other, attended.at[blocks[1]]), (out_mat, weights)]
    later = started(pairs, row_sems.at[pl.ds(8, 3)])
    gain = row_of(vectors, 5)
    for block, rows in enumerate(blocks):
        finished(rows_in[block])
        unit, inverse = unit_of(held[rows, :])
        grad = near[rows, :].astype(FULL) + far[rows, :].astype(FULL)
        slots = lax.broadcasted_iota(jnp.int32, grad.shape, 0)
        live = slots < lengths[block, 0] + lengths[block, 1]
        coming = jnp.where(live, arriving[rows, :].astype(FULL), 0.0)
        result = coming + norm_backward(grad, unit, inverse, gain)
        low = result.astype(LOW)
        branch[rows, :] = low
        if block == 0:
            middle_grad[...] = result
            sums[...] = jnp.zeros_like(sums)
            sums[0:1, :] = jnp.sum(low.astype(FULL), axis=0, keepdims=True)
            sums[1:2, :] = jnp.sum(grad * unit, axis=0, keepdims=True)
            sums[2:3, :] = jnp.sum(grad, axis=0, keepdims=True)
            sums[3:4, :] = jnp.sum(coming, axis=0, keepdims=True)
    finished(later)
    whole = dot_tn(attended[...], branch[...])
    out_grad[0] = whole[:, :COLS].astype(LOW)
    out_grad[1] = whole[:, COLS:].astype(LOW)
    copies = started(turned(out_plan(places, two_of((sent_one, sent_two)), 0, out_grad)), sems)
    attended_grad[...] = (
        dot_nt(branch[:, :COLS], weights[0]) + dot_nt(branch[:, COLS:], weights[1])
    ).astype(LOW)
    finished(copies)


def output_backward(
    places, lengths, arriving, middle, part, part_far, vectors, attended, out_mat
):
    rows, width = middle.shape
    sent = (low_shape(2, 4, 2, 32, COLS), OUTSIDE)
    inside = [full_shape(rows // 2, width), low_shape(rows, COLS), full_shape(8, width)]
    low = pltpu.VMEM((rows, width), LOW)
    return call(
        output_backward_kernel,
        [SCALARS, SCALARS] + [FAR_OUTSIDE] * 5 + [INSIDE] + [FAR_OUTSIDE] * 3,
        [sent, sent] + [(s, INSIDE) for s in inside],
        [pltpu.VMEM((rows, width), FULL), low, low, low, low, pltpu.VMEM((2, COLS, COLS), LOW)]
        + [pltpu.VMEM((rows, COLS), LOW), pltpu.VMEM((2, COLS, COLS), LOW)]
        + [pltpu.SemaphoreType.DMA((11,)), pltpu.SemaphoreType.DMA((32,))],
        10,
        (places, lengths, *arriving, middle, part, part_far, vectors, *attended, out_mat),
        vmem=54,
    )


def attention_backward_kernel(
    block, lengths, query, key, value, grad_in, query_grad, key_grad, value_grad, sums, mask
):
    count = query.shape[0]
    mask[...] = barred(lengths, block, 0, count, count)
    lane = lax.broadcasted_iota(jnp.int32, (count, TILE), 1) < HEAD_DIM
    for index in range(COLS // TILE):
        cols = pl.ds(index * TILE, TILE)
        stacked, given = two_by_two(query[:, cols], lane), two_by_two(grad_in[:, cols], lane)
        probs = probabilities(stacked, key[:, cols], mask[...])
        weighted = probs * dot_nt(given, value[:, cols])
        grad = (weighted - probs * jnp.sum(weighted, axis=-1, keepdims=True)).astype(LOW)
        out = dot(grad, key[:, cols])
        query_grad[:, cols] = (jnp.where(lane, out[:count], out[count:]) * 0.125).astype(LOW)
        key_grad[:, cols] = dot_tn(grad, stacked).astype(LOW)
        value_grad[:, cols] = dot_tn(probs.astype(LOW), given).astype(LOW)
    sums[...] = jnp.zeros_like(sums)
    sums[0:1, :] = jnp.sum(query_grad[...].astype(FULL), axis=0, keepdims=True)
    sums[1:2, :] = jnp.sum(value_grad[...].astype(FULL), axis=0, keepdims=True)


def attention_backward(block, lengths, query, key, value, grad_in):
    count = query.shape[0] // 2
    vmem = pltpu.VMEM
    half = (low_shape(count, COLS), INSIDE)
    part = pl.BlockSpec((count, COLS), lambda i: (block, 0))
    return call(
        lambda *refs: attention_backward_kernel(block, *refs),
        [SCALARS] + [part] * 4,
        [half, half, half, (full_shape(8, COLS), INSIDE)],
        [vmem((count, count), FULL)],
        8,
        (lengths, query, key, value, grad_in),
        grid=(1,),
        vmem=20,
    )


def joint_grad_kernel(places, normed, *refs):
    grads, sent, (query_part, key_part, value_part, sems) = refs[:6], refs[6:12], refs[12:]
    parts = (query_part, key_part, value_part)
    count = grads[0].shape[0]
    sides = [jnp.concatenate([g[...] for g in grads[i : i + 3]], axis=1) for i in (0, 3)]
    whole = dot_tn(normed[:count, :], sides[0]) + dot_tn(normed[count:, :], sides[1])
    for index, part in enumerate(parts):
        part[...] = whole[:, index * COLS : (index + 1) * COLS].astype(LOW)
    finished(started(joint_sent_plan(places, sent, parts), sems))


def joint_grad_parts(places, normed, own, other):
    rows, width = normed.shape
    sent = [low_shape(2, 4, 64, COLS), low_shape(2, 2, 128, COLS), low_shape(2, 4, 2, 32, COLS)]
    return call(
        joint_grad_kernel,
        [SCALARS] + [INSIDE] * 7,
        [(s, OUTSIDE) for s in sent for _ in range(2)],
        [pltpu.VMEM((width, COLS), LOW)] * 3 + [pltpu.SemaphoreType.DMA((56,))],
        8,
        (places, normed, *own, *other),
        vmem=60,
    )


def joint_backward_kernel(*refs):
    own, other, mats, outs = refs[:3], refs[3:6], refs[6:9], refs[9:]
    for grads, out in zip((own, other), outs):
        whole = dot_nt(grads[0][...], mats[0][...])
        whole += dot_nt(grads[1][...], mats[1][...])
        whole += dot_nt(grads[2][...], mats[2][...])
        out[...] = whole.astype(out.dtype)


def joint_backward(own, other, mats):
    count, width = own[0].shape[0], mats[0].shape[0]
    return call(
        joint_backward_kernel,
        [INSIDE] * 9,
        [(full_shape(count, width), INSIDE), (low_shape(count, width), INSIDE)],
        [],
        6,
        (*own, *other, *mats),
        vmem=20,
    )


def input_kernel(
    places, tokens, part, part_far, middle_grad, vectors, two_sums, own_sums, other_sums, up_sums,
    input_grad, sums, rows,
):
    unit, inverse = unit_of(tokens[...].astype(FULL))
    grad = part[...] + part_far[...].astype(FULL)
    input_grad[...] = middle_grad[...] + norm_backward(grad, unit, inverse, row_of(vectors, 0))
    first = places[13] == 0

    def own_side(values):
        none = jnp.zeros_like(values)
        return jnp.concatenate(
            [jnp.where(first, values, none), jnp.where(first, none, values)], axis=1
        )

    rows[...] = jnp.zeros_like(rows)
    rows[0:1, :] = jnp.sum(grad * unit, axis=0, keepdims=True)
    rows[1:2, :] = jnp.sum(grad, axis=0, keepdims=True)
    for k in range(2):
        rows[2 + k : 3 + k, :] = own_side(own_sums[k : k + 1, :] + other_sums[k : k + 1, :])
    rows[4:7, :] = two_sums[0:3, :]
    for k in range(4):
        hidden = up_sums[k : k + 1, :]
        rows[7 + k : 8 + k, :] = jnp.concatenate(
            [own_side(hidden[:, :256]), own_side(hidden[:, 256:])], axis=1
        )
    rows[11:12, :] = two_sums[3:4, :]
    sums[:16, :] = rows[:, :COLS].astype(LOW)
    sums[16:, :] = rows[:, COLS:].astype(LOW)


def input_backward(places, *arrays):
    count, width = arrays[0].shape
    return call(
        input_kernel,
        [SCALARS] + [INSIDE] * 9,
        [(full_shape(count, width), INSIDE), (low_shape(32, COLS), INSIDE)],
        [pltpu.VMEM((16, width), FULL)],
        4,
        (places, *arrays),
        vmem=20,
    )


def adam_step(weight, first, second, grad, rate, decay):
    first_new = BETA_ONE * first + (1.0 - BETA_ONE) * grad
    second_new = BETA_TWO * second + (1.0 - BETA_TWO) * grad * grad
    mean_hat = first_new / (1.0 - BETA_ONE**STEP)
    square_hat = second_new / (1.0 - BETA_TWO**STEP)
    fresh = weight - rate * (mean_hat / (jnp.sqrt(square_hat) + ADAM_EPS) + decay * weight)
    return (first_new, second_new, fresh)


def adam_kernel(grad_of, rate, chunks, places, *refs):
    state, refs = refs[:3], refs[3:]
    grads, refs = refs[:-8], refs[-8:]
    outs, (held, results, sems_in, sems_out) = refs[:4], refs[4:]
    coming = [
        started([(a.at[at], held.at[(i, *at)]) for i, a in enumerate(state)], sems_in.at[n])
        for n, at in enumerate(chunks)
    ]
    going = []
    for n, at in enumerate(chunks):
        grad = grad_of(n, places, *grads)
        finished(coming[n])
        results[(0, *at)] = grad
        weight, first, second = (held[(i, *at)] for i in range(3))
        new = adam_step(weight, first, second, grad, rate, MATRIX_DECAY)
        for i, value in enumerate(new):
            results[(1 + i, *at)] = value
        going += started(
            [(results.at[(i, *at)], out.at[at]) for i, out in enumerate(outs)], sems_out.at[n]
        )
    finished(going)


def adam(grad_of, rate, chunks, state, grads, places):
    shape = state[0].shape
    return pl.pallas_call(
        lambda *refs: adam_kernel(grad_of, rate, chunks, *refs),
        grid=(1,),
        in_specs=[SCALARS]
        + [OUTSIDE] * 3
        + [pl.BlockSpec((g[1], COLS), lambda i, at=g[2]: (at, 0)) for g in grads],
        out_specs=[OUTSIDE] * 4,
        out_shape=[full_shape(*shape)] * 4,
        scratch_shapes=[pltpu.VMEM((3, *shape), FULL), pltpu.VMEM((4, *shape), FULL)]
        + [pltpu.SemaphoreType.DMA((len(chunks), 3)), pltpu.SemaphoreType.DMA((len(chunks), 4))],
        compiler_params=pltpu.CompilerParams(vmem_limit_bytes=24 << 20),
        cost_estimate=pl.CostEstimate(
            flops=6 * FLOPS_PER_US, bytes_accessed=30 * state[0].size, transcendentals=0
        ),
    )(places, *state, *(g[0] for g in grads))


def by_core(places, both, far):
    own = places[13] == 0
    both, far = both.astype(FULL), far.astype(FULL)
    return jnp.where(own, both, far), jnp.where(own, far, both)


def columns_of(width, count):
    return [(slice(None), slice(n * width, (n + 1) * width)) for n in range(count)]


def rows_each(height, count):
    return [(slice(n * height, (n + 1) * height), slice(None)) for n in range(count)]


def adam_joint(places, state, sums):
    def grad_of(n, places, both, far):
        rows = slice(128 * n, 128 * (n + 1))
        return jnp.concatenate(by_core(places, both[rows, :], far[rows, :]), axis=1)

    grads = [(a, 384, 0) for a in sums]
    return adam(grad_of, MATRIX_RATE, columns_of(2 * COLS, 3), state, grads, places)


def adam_expand(places, state, sums):
    def grad_of(n, places, both, far):
        rows = slice(128 * n, 128 * (n + 1))
        zero, one = by_core(places, both[rows, :], far[rows, :])
        return jnp.concatenate(
            [zero[:, :256], one[:, :256], zero[:, 256:], one[:, 256:]], axis=1
        )

    grads = [(a, 512, 0) for a in sums]
    return adam(grad_of, MATRIX_RATE, columns_of(2 * COLS, 4), state, grads, places)


def adam_reduce(places, state, sums):
    def grad_of(n, places, left, right, far_left, far_right):
        rows = slice(128 * (n % 2), 128 * (n % 2 + 1))
        own = places[13] == n // 2
        return jnp.concatenate(
            [
                jnp.where(own, left[rows, :].astype(FULL), far_left[rows, :].astype(FULL)),
                jnp.where(own, right[rows, :].astype(FULL), far_right[rows, :].astype(FULL)),
            ],
            axis=1,
        )

    grads = [(a, 256, at) for a in sums for at in (2, 3)]
    return adam(grad_of, MATRIX_RATE, rows_each(128, 4), state, grads, places)


def adam_output(places, state, sums):
    def grad_of(n, places, *grads):
        both, far = grads[n], grads[2 + n]

        def rows(a):
            return jnp.concatenate(
                [
                    jnp.concatenate([a[64 * q : 64 * q + 32, :], a[64 * q + 32 : 64 * q + 64, :]], axis=1)
                    for q in (0, 1)
                ]
            ).astype(FULL)

        return jnp.where(places[13] == places[12], rows(both), rows(far))

    grads = [(a, 128, at) for a in sums for at in (3, 4)]
    return adam(grad_of, OUTPUT_RATE, rows_each(64, 2), state, grads, places)


def per_device(
    tokens,
    cotangent,
    lengths,
    joint_weight,
    joint_first,
    joint_second,
    output_weight,
    output_first,
    output_second,
    expand_weight,
    expand_first,
    expand_second,
    reduce_weight,
    reduce_first,
    reduce_second,
    vector_weight,
    vector_first,
    vector_second,
):
    me = coordinates()
    places = places_of(me)
    across = flip("core", 1)

    half, block, rest_half, rest_y = cast(
        places, joint_weight, vector_weight, expand_weight, reduce_weight, output_weight
    )
    joint_x, joint_y, along_x, along_y, along_z, far = gather_first(
        places, half, block, rest_half, rest_y, [send(a, across) for a in (lengths, tokens, cotangent)]
    )
    tokens, cotangent = (tokens, far[1]), (cotangent, far[2])
    lengths = jnp.concatenate([lengths, far[0]])

    normed_one, query, key, value, vectors, *joint_mats = joint(
        places, *tokens, joint_x, joint_y
    )
    along_z.append(send(after(along_z[1], query), turn("z", 1)))
    along_y.append(send(after(along_y[0], query), turn("y", 1)))
    along_y.append(send(after(along_y[1], query), turn("y", 1)))
    own = attention(0, lengths, after(query, along_y[1], *along_z[1:3]), key, value)
    along_x.append(send(after(along_x[1], own), turn("x", 1)))
    other = attention(1, lengths, after(query, along_x[1]), key, value)
    attended = (own, other)
    branch, out_mat = output(places, own, after(other, *along_x[2:], *along_y[2:]), along_z)
    branch_far = send(branch, across)
    *sent, middle, layer_own, layer_other, normed_two_part, up_bias_grad = forward_backward(
        places, lengths, tokens, cotangent, branch, branch_far, vectors,
        [*along_x, *along_y, *along_z],
    )
    part_far = send(normed_two_part, across)
    layer_out = (layer_own + send(layer_other, across).astype(FULL)).astype(LOW)

    out_one, out_two, middle_grad, attended_grad, two_sums = output_backward(
        places, lengths, cotangent, middle, normed_two_part, part_far, vectors, attended, out_mat
    )
    sent[5] = after(sent[5], attended_grad)
    rest = total(me, sent, 0, 3, 0)
    next(rest)
    out_far = send(out_two, turn("z", 1))
    *own_grads, own_sums = attention_backward(0, lengths, query, key, value, attended_grad)
    *other_grads, other_sums = attention_backward(1, lengths, query, key, value, attended_grad)
    mark = rest.send(other_grads[0])
    sent = joint_grad_parts(places, after(normed_one, mark), own_grads, other_grads)
    joint_rows = total(me, sent, 32, 1, 32)
    next(joint_rows)
    mark = rest.send((sent[0], None, None))
    part_own, part_other = joint_backward(
        (after(own_grads[0], mark), *own_grads[1:]), other_grads, joint_mats
    )
    part_far = send(part_other, across)
    (out_near,) = added_all([[(out_one, 1), (after(out_far, part_own), 1)]])
    out_near = out_near.reshape(out_one.shape[1:])
    out_again = send(out_near, turn("z", 0))
    mark = joint_rows.send(part_own)
    mark = rest.send(mark)
    input_grad, vector_local = input_backward(
        places, tokens[0], after(part_own, mark), part_far, middle_grad, vectors, two_sums,
        own_sums, other_sums, up_bias_grad,
    )
    (out_along,) = added_all(
        [[(out_one, 0), (out_far, 0), (after(out_again, vector_local), 0)]]
    )
    out_along = out_along.reshape(out_one.shape[1:])

    mark = joint_rows.send((vector_local, vector_local, out_along))
    for turn_number in range(4):
        mark = rest.send((mark, layer_out) if turn_number == 1 else mark)
        mark = joint_rows.send(mark)
    mark = rest.send(mark)
    mark = joint_rows.send(mark)
    mark = joint_rows.send(mark)
    mark = rest.send(mark)
    mark = joint_rows.send(mark)
    one, two, extra = next(joint_rows)
    joint_state = adam_joint(
        places, (joint_weight, joint_first, joint_second), (after(one, mark), two)
    )
    output_state = adam_output(
        places, (output_weight, output_first, output_second), (after(one, mark), two)
    )
    one, two, _ = next(rest)
    one = after(one, joint_state[0], output_state[0])
    expand = adam_expand(places, (expand_weight, expand_first, expand_second), (one, two))
    reduce = adam_reduce(places, (reduce_weight, reduce_first, reduce_second), (one, two))
    vector_grad = lax.dynamic_slice(
        jnp.concatenate([extra[:12], extra[16:28]], axis=1).astype(FULL),
        (0, 128 * lax.axis_index("shard")),
        (12, 128),
    )
    vector_state = (vector_grad,) + adam_step(
        vector_weight, vector_first, vector_second, vector_grad, VECTOR_RATE, 0.0
    )
    states = zip(joint_state, output_state, expand, reduce, vector_state)
    return (layer_out, input_grad, *(a for kind in states for a in kind))


def solution(mesh):
    rows, columns, split = P("shard", None), P(None, "shard"), P(("wide", "shard"), None)
    state = (rows, rows, rows, rows, columns)
    return jax.shard_map(
        per_device,
        mesh=mesh,
        in_specs=(split, split, split) + (rows,) * 12 + (columns,) * 3,
        out_specs=(split, split) + state * 4,
        check_vma=False,
    )
```

```python
import jax
import jax.numpy as jnp
from jax import lax
from jax.experimental import pallas as pl
from jax.experimental.pallas import tpu as pltpu
from jax.sharding import PartitionSpec as P

HEAD_DIM = 64
STEP = 10


ROOT_TWO_PI = 0.7978845608028654
CUBIC = 0.044715
BETA_ONE = 0.9
BETA_TWO = 0.999
ADAM_EPS = 1e-08
MATRIX_RATE = 0.03
OUTPUT_RATE = 0.1
VECTOR_RATE = 0.2
MATRIX_DECAY = 0.1

LOW = jnp.bfloat16
FULL = jnp.float32
AXES = ("wide", "shard")
SIZES = (4, 2, 2, 2, 4)
COLS = 512
FLOPS_PER_US = 1_150_000_000


def coordinates():
    wide, shard = lax.axis_index("wide"), lax.axis_index("shard")
    z, xl, core = wide // 4, (wide // 2) % 2, wide % 2
    xh, y = shard // 4, shard % 4
    return {"z": z, "x": 2 * xh + xl, "y": y, "xl": xl, "xh": xh, "core": core}


def route(partner):
    pairs = []
    for source in range(128):
        rest, places = source, []
        for size in reversed(SIZES):
            places.append(rest % size)
            rest //= size
        y, xh, core, xl, z = places
        target = partner({"z": z, "x": 2 * xh + xl, "y": y, "core": core})
        flat = 0
        for place, size in zip(
            (target["z"], target["x"] % 2, target["core"], target["x"] // 2, target["y"]), SIZES
        ):
            flat = flat * size + place
        pairs.append((source, flat))
    return pairs


def flip(axis, bits):
    return route(lambda at: {**at, axis: at[axis] ^ bits})


def turn(axis, step):
    return route(lambda at: {**at, axis: at[axis] ^ (1 if (at["core"] + step) % 2 == 0 else 3)})


def send(value, pairs):
    return lax.ppermute(value, AXES, pairs)


def added(*terms):
    return sum(term.astype(FULL) for term in terms).astype(LOW)


def orders(me, axis):
    here = me[axis]
    one = jnp.where(me["core"] == 0, 1, 3)
    return [here, here ^ one, here ^ (4 - one), here ^ 2]


def places_of(me):
    return jnp.stack(
        orders(me, "x")
        + orders(me, "y")
        + orders(me, "z")
        + [me["xh"], me["core"], me["xl"], me["z"]]
    ).astype(jnp.int32)


def after(value, *others):
    return lax.optimization_barrier((value, *others))[0]


def rows_of(*parts):
    return jnp.concatenate([p.reshape(-1, COLS) for p in parts])


def main_phase(block, axis, gate, late=False):
    first, second = send(block, turn(axis, 0)), send(gated(block, gate if late else None), turn(axis, 1))
    return [block, first, second, send(after(first, gate), turn(axis, 1))]


def pack_kernel(places, block, other, half, second, first, again):
    for out in (first, again):
        out[:208, :] = block[:208, :]
        out[208:416, :] = other[:208, :]
    again[416:512, :] = half[...]
    again[512:608, :] = second[...]
    own = places[13] == places[12]
    for p, held in enumerate((block, other)):
        at = 416 + 96 * p
        first[at : at + 64, :] = held[208:272, :]
        rows = slice(272 + 32 * p, 304 + 32 * p)
        first[at + 64 : at + 96, :] = jnp.where(own, block[rows, :], other[rows, :])


def pack(places, *arrays):
    return call(
        pack_kernel,
        [SCALARS] + [INSIDE] * 4,
        [(low_shape(608, COLS), INSIDE)] * 2,
        [],
        1,
        (places, *arrays),
        vmem=8,
    )


def gather_first(places, half, block, rest_half, rest_y, exchanged):
    size = half.shape[0]
    other, second, *early = lax.optimization_barrier(
        (send(block, flip("x", 3)), send(half, turn("y", 0)), *exchanged[:2])
    )
    own_y, both = pack(places, block, other, half, second)
    first_y, second_y = send(own_y, turn("y", 0)), send(both, turn("y", 1))
    rest_other = send(after(rest_y, other), flip("x", 3))
    first_y, second_y, rest_other, *late = lax.optimization_barrier(
        (first_y, second_y, rest_other, *exchanged[2:])
    )
    plane = rows_of(half, second, second_y[416:]).reshape(4, size, COLS)
    first_x, second_x = send(plane, turn("x", 0)), send(plane, turn("x", 1))
    third_y = send(rows_of(first_y[:416], own_y[416:], first_y[416:]), turn("y", 1))
    rest_near = send(after(rest_half, first_y), turn("y", 0))
    first_x, second_x, third_y, rest_near = lax.optimization_barrier(
        (first_x, second_x, third_y, rest_near)
    )
    third_x = send(first_x, turn("x", 1))
    here = rows_of(rest_half, rest_near)
    there = send(here, turn("y", 1))
    plane_z = rows_of(own_y[416:], first_y[416:], third_y[416:]).reshape(4, 2, 96, COLS)
    pair_y = jnp.stack([rest_y, rest_other])
    along_z = [plane_z, send(plane_z, turn("z", 0)), send(plane_z, turn("z", 1))]
    along_y = [pair_y, send(after(pair_y, third_y), turn("y", 0))]
    third_x, there = lax.optimization_barrier((third_x, there))
    plane_x = rows_of(here, there).reshape(4, -1, COLS)
    along_x = [plane_x, send(plane_x, turn("x", 0)), send(plane_x, turn("x", 1))]
    joint_x = [plane, first_x, second_x, third_x]
    joint_y = [own_y, first_y, second_y, third_y]
    return joint_x, joint_y, along_x, along_y, along_z, early + late


def added_all(sums, steps=2):
    terms, specs, outs, out_specs = [], [], [], []
    for group in sums:
        rows = min(a.size for a, _ in group) // COLS
        rows = rows // 2 if len(group) == 2 else rows
        for array, which in group:
            terms.append(array.reshape(-1, COLS))
            specs.append(
                pl.BlockSpec((rows // steps, COLS), lambda i, at=which * steps: (at + i, 0))
            )
        outs.append(low_shape(rows, COLS))
        out_specs.append(pl.BlockSpec((rows // steps, COLS), lambda i: (i, 0)))

    def kernel(*refs):
        at = 0
        for group, out in zip(sums, refs[len(terms) :]):
            out[...] = added(*(ref[...] for ref in refs[at : at + len(group)]))
            at += len(group)

    return pl.pallas_call(
        kernel,
        grid=(steps,),
        in_specs=specs,
        out_specs=out_specs,
        out_shape=outs,
        compiler_params=pltpu.CompilerParams(vmem_limit_bytes=12 << 20),
        cost_estimate=pl.CostEstimate(
            flops=3 * FLOPS_PER_US, bytes_accessed=6 * sum(o.size for o in outs), transcendentals=0
        ),
    )(*terms)


def assembled(me, mine, far, behind, pieces):
    behind = [a.reshape(-1, COLS) for a in behind]
    rows = 2 * mine.shape[0] + sum(a.shape[0] for a in behind)

    def kernel(right, mine, far, *refs):
        behind, out = refs[:-1], refs[-1]
        first = right[0] == 0
        source = target = 0
        for count, size in pieces:
            for _ in range(count):
                a, b = mine[source : source + size, :], far[source : source + size, :]
                out[target : target + size, :] = jnp.where(first, a, b)
                out[target + size : target + 2 * size, :] = jnp.where(first, b, a)
                source, target = source + size, target + 2 * size
        for part in behind:
            out[target : target + part.shape[0], :] = part[...]
            target += part.shape[0]

    return pl.pallas_call(
        kernel,
        out_shape=low_shape(rows, COLS),
        in_specs=[pl.BlockSpec(memory_space=pltpu.SMEM)]
        + [pl.BlockSpec(memory_space=pltpu.VMEM)] * (2 + len(behind)),
        out_specs=pl.BlockSpec(memory_space=pltpu.VMEM),
        compiler_params=pltpu.CompilerParams(vmem_limit_bytes=8 << 20),
        cost_estimate=pl.CostEstimate(
            flops=FLOPS_PER_US, bytes_accessed=4 * rows * COLS, transcendentals=0
        ),
    )(me["xl"].reshape(1).astype(jnp.int32), mine, far, *behind)


def gated(value, gate):
    return value if gate is None else after(value, *(gate if isinstance(gate, tuple) else (gate,)))


def total(me, raw, out_rows, units, extra_rows):
    axes = "xyz"
    parts = [raw[:2], raw[2:4], raw[4:]]
    far = [send(away, turn(axis, 1)) for (_, away), axis in zip(parts, axes)]
    gate = yield
    far = list(far if gate is None else lax.optimization_barrier((*far, gate))[:-1])
    keeps = [keep for keep, _ in parts]
    near = added_all([[(k, 1), (f, 1)] for k, f in zip(keeps, far)])
    near = lax.optimization_barrier([n.reshape(k.shape[1:]) for n, k in zip(near, keeps)])
    again = [send(n, turn(axis, 0)) for n, axis in zip(near, axes)]
    gate, extra, out = yield near[2]
    again = lax.optimization_barrier((*again, gate))[:-1]
    along = added_all([[(k, 0), (f, 0), (a, 0)] for k, f, a in zip(keeps, far, again)])
    along_x, along_y, along_z = lax.optimization_barrier(
        [a.reshape(k.shape[1:]) for a, k in zip(along, keeps)]
    )
    if out_rows:
        along_z = jnp.concatenate([along_z, out], axis=2)
    size_x, size_y = along_x.shape[1], along_y.shape[1] // 2
    size_z = (along_z.shape[2] - out_rows) // 2

    def with_extra(*parts):
        return rows_of(*parts, extra) if extra_rows else rows_of(*parts)

    def split(rows, *sizes):
        at, parts = 0, []
        for size in sizes:
            parts.append(rows[at : at + size])
            at += size
        return parts

    plane = jnp.concatenate([along_x, along_z.reshape(4, -1, COLS)], axis=1)
    size = plane.shape[1]
    far = send(with_extra(plane[2:]), turn("y", 1))
    gate = yield plane
    far, kept = gated(far, gate), plane[:2]
    near = added(kept[1], far[size : 2 * size])
    if extra_rows:
        extra = added(extra, far[2 * size :])
    again = send(with_extra(near), turn("y", 0))
    gate = yield near
    again = gated(again, gate)
    plane = added(kept[0], far[:size], again[:size])
    if extra_rows:
        extra = added(extra, again[size:])
    half, pair = plane[:size_x], plane[size_x:].reshape(2, 2 * size_z + out_rows, COLS)
    out = pair[:, 2 * size_z :].reshape(-1, COLS)
    pieces = jnp.concatenate(
        [along_y.reshape(4, size_y, COLS), pair[:, : 2 * size_z].reshape(4, size_z, COLS)], axis=1
    )
    size = size_y + size_z
    pieces = [
        lax.dynamic_index_in_dim(pieces, ((k // 2) ^ me["xh"]) * 2 + k % 2, 0, keepdims=False)
        for k in orders(me, "x")
    ]
    far = send(with_extra(pieces[2], pieces[3], out), turn("x", 1))
    gate = yield plane
    far = gated(far, gate)
    first, second, far_out, far_extra = split(far, size, size, 2 * out_rows, extra_rows)
    sums = added(rows_of(pieces[1], out), rows_of(second, far_out))
    if extra_rows:
        extra = added(extra, far_extra)
    again = send(with_extra(sums), turn("x", 0))
    gate = yield sums
    near, out, far_extra = split(gated(again, gate), size, 2 * out_rows, extra_rows)
    sums = rows_of(added(pieces[0], first, near), added(sums[size:], out))
    if extra_rows:
        extra = added(extra, far_extra)
    flat, block = rows_of(half, sums[:size_y]), sums[size_y:]
    size, size_block = flat.shape[0], block.shape[0]
    far = send(with_extra(flat, block), turn("z", 0))
    gate = yield sums
    sums, other, far_extra = split(gated(far, gate), size, size_block, extra_rows)
    flat = added(flat, sums)
    if extra_rows:
        extra = added(extra, far_extra)
    blocks = rows_of(block, other)
    far = send(with_extra(flat, blocks), turn("z", 1))
    gate = yield flat
    sums, other, far_extra = split(gated(far, gate), size, 2 * size_block, extra_rows)
    flat = added(flat, sums)
    if extra_rows:
        extra = added(extra, far_extra)
    blocks = rows_of(blocks, other).reshape(4, size_block, COLS)
    where = orders(me, "z")
    ordered = jnp.stack(
        [
            sum(jnp.where(where[k] == place, blocks[k], 0) for k in range(4)).astype(LOW)
            for place in range(4)
        ]
    )
    mine = rows_of(flat, ordered[:, :size_z])
    far = send(mine, flip("x", 1))
    gate = yield mine
    far = gated(far, gate)

    pieces = [(units, size_x // units), (1, size_y), (4, size_z)]
    both = assembled(me, mine, far, [ordered[:, size_z:]] if out_rows else [], pieces)
    far = send(with_extra(both), flip("core", 1))
    yield both
    rows = both.shape[0]
    if extra_rows:
        extra = added(extra, far[rows:])
        far = far[:rows]
    yield both, far, extra


def rows_at(start, size):
    return pl.ds(pl.multiple_of(start, size), size)


def joint_plan(places, along_x, along_y, mats):
    query, key, value, vectors = mats
    pairs = []
    for ky in range(4):
        y = places[4 + ky]
        for kx in range(4):
            x = places[kx]
            shard, half = (x // 2) * 4 + y, x % 2
            source = along_x[kx].at[ky]
            pairs.append(
                (source.at[pl.ds(0, 64)], query.at[rows_at(shard * 128 + half * 64, 64)])
            )
            pairs.append(
                (source.at[pl.ds(64, 32)], value.at[rows_at(shard * 128 + half * 32, 32)])
            )
        for p in range(2):
            shard = (places[12] ^ p) * 4 + y
            source, at = along_y[ky], p * 208
            pairs.append((source.at[pl.ds(at, 128)], key.at[rows_at(shard * 128, 128)]))
            pairs.append((source.at[pl.ds(at + 128, 64)], value.at[rows_at(shard * 128 + 64, 64)]))
            pairs.append(
                (
                    source.at[pl.ds(at + 192, 16), pl.ds(0, 128)],
                    vectors.at[:, rows_at(shard * 128, 128)],
                )
            )
    return pairs


def joint_sent_plan(places, raw, parts):
    query, key, value = parts
    pairs = []
    for ky in range(4):
        y = places[4 + ky]
        for kx in range(4):
            x = places[kx]
            start = ((x // 2) * 4 + y) * 128 + (x % 2) * 64
            pairs.append((query.at[rows_at(start, 64)], raw[0 + kx // 2].at[kx % 2, ky]))
        for p in range(2):
            shard = (places[12] ^ p) * 4 + y
            pairs.append((key.at[rows_at(shard * 128, 128)], raw[2 + ky // 2].at[ky % 2, p]))
            for kz in range(4):
                start = shard * 128 + places[8 + kz] * 32
                pairs.append((value.at[rows_at(start, 32)], raw[4 + kz // 2].at[kz % 2, ky, p]))
    return pairs


def up_plan(places, at_x, at_y, at_z, mats):
    up, down_one, down_two = mats
    pairs = []
    for ky in range(4):
        y = places[4 + ky]
        for kx in range(4):
            x = places[kx]
            start = ((x // 2) * 4 + y) * 128 + (x % 2) * 64
            for j in range(3):
                source = at_x(kx).at[ky, pl.ds(64 * j, 64)]
                pairs.append((source, up.at[j, rows_at(start, 64)]))
        for p in range(2):
            shard = (places[12] ^ p) * 4 + y
            source = at_y(ky).at[p]
            pairs.append((source.at[pl.ds(0, 128)], up.at[3, rows_at(shard * 128, 128)]))
            pairs.append((source.at[pl.ds(128, 256)], down_one.at[rows_at(shard * 256, 256)]))
            for kz in range(4):
                start = shard * 256 + places[8 + kz] * 64
                source = at_z(kz).at[ky, p, pl.ds(0, 64)]
                pairs.append((source, down_two.at[rows_at(start, 64)]))
    return pairs


def up_kind(index):
    index %= 24
    if index < 12:
        return index % 3
    return 3 if (index - 12) % 6 == 0 else None


def up_shard(places, index):
    ky, index = divmod(index, 24)
    return (places[12] ^ ((index - 12) // 6)) * 4 + places[4 + ky]


def out_plan(places, at_z, first, mat):
    pairs = []
    for ky in range(4):
        for kz in range(4):
            start = places[4 + ky] * 128 + places[8 + kz] * 32
            for p in range(2):
                source = at_z(kz).at[ky, p, pl.ds(first, 32)]
                pairs.append((source, mat.at[p, rows_at(start, 32)]))
    return pairs


def two_of(arrays):
    return lambda k: arrays[k // 2].at[k % 2]


def started(pairs, sems):
    all_of_them = [pltpu.make_async_copy(a, b, sems.at[i]) for i, (a, b) in enumerate(pairs)]
    for copy in all_of_them:
        copy.start()
    return all_of_them


def finished(all_of_them):
    for copy in all_of_them:
        copy.wait()


def turned(pairs):
    return [(b, a) for a, b in pairs]


def low_shape(*shape):
    return jax.ShapeDtypeStruct(shape, LOW)


def full_shape(*shape):
    return jax.ShapeDtypeStruct(shape, FULL)


SCALARS = pl.BlockSpec(memory_space=pltpu.SMEM)
INSIDE = pl.BlockSpec(memory_space=pltpu.VMEM)
OUTSIDE = pl.BlockSpec(memory_space=pl.ANY)
FAR_OUTSIDE = pl.BlockSpec(memory_space=pltpu.HBM)


def call(kernel, in_specs, outs, scratch, length, args, grid=(), vmem=60):
    shapes, specs = [o[0] for o in outs], [o[1] for o in outs]
    moved = sum(a.size * a.dtype.itemsize for a in (*args, *shapes))
    return pl.pallas_call(
        kernel,
        grid=grid,
        out_shape=shapes,
        in_specs=in_specs,
        out_specs=specs,
        scratch_shapes=scratch,
        compiler_params=pltpu.CompilerParams(vmem_limit_bytes=vmem << 20),
        cost_estimate=pl.CostEstimate(
            flops=length * FLOPS_PER_US, bytes_accessed=moved, transcendentals=0
        ),
    )(*args)


def gelu_both(upward):
    square = upward * upward
    tangent = jnp.tanh(ROOT_TWO_PI * upward * (1.0 + CUBIC * square))
    half = 0.5 * (1.0 + tangent)
    slope = half + 0.5 * upward * (1.0 - tangent * tangent) * ROOT_TWO_PI * (
        1.0 + 3.0 * CUBIC * square
    )
    return upward * half, slope


def dot(a, b):
    return jnp.dot(a, b, preferred_element_type=FULL)


def dot_nt(a, b):
    return lax.dot_general(a, b, (((1,), (1,)), ((), ())), preferred_element_type=FULL)


def dot_tn(a, b):
    return lax.dot_general(a, b, (((0,), (0,)), ((), ())), preferred_element_type=FULL)


def unit_of(values):
    center = values - jnp.mean(values, axis=-1, keepdims=True)
    inverse = lax.rsqrt(jnp.mean(center * center, axis=-1, keepdims=True) + 1e-05)
    return center * inverse, inverse


def norm_backward(grad_out, unit, inverse, gain):
    scaled = grad_out * gain
    return inverse * (
        scaled
        - jnp.mean(scaled, axis=-1, keepdims=True)
        - unit * jnp.mean(scaled * unit, axis=-1, keepdims=True)
    )


def row_of(vectors, row):
    return vectors[row : row + 1, :].astype(FULL)


def own_columns(full, core, size):
    groups = full.shape[1] // (2 * size)
    first = jnp.concatenate(
        [full[:, (2 * g) * size : (2 * g + 1) * size] for g in range(groups)], axis=1
    )
    second = jnp.concatenate(
        [full[:, (2 * g + 1) * size : (2 * g + 2) * size] for g in range(groups)], axis=1
    )
    return jnp.where(core == 0, first, second)


def barred(lengths, block, first, height, span):
    shape = (height, span)
    rows = lax.broadcasted_iota(jnp.int32, shape, 0) + first
    keys = lax.broadcasted_iota(jnp.int32, shape, 1)
    opening = lengths[block, 0]
    filled = opening + lengths[block, 1]
    begin = jnp.where(rows < opening, 0, jnp.where(rows < filled, opening, rows))
    return jnp.where((keys <= rows) & (keys >= begin), 0.0, -1e30)


TILE = 128


def cast_kernel(
    places, weight, vector, expand, reduce, output, half, block, rest_half, rest_y,
    held, rest, wide, padded, sems,
):
    core, xl, z = places[13], places[14], places[15]

    def cols(which):
        return rows_at(which * 2 * COLS + core * COLS, COLS)

    first = [
        (weight.at[rows_at(xl * 64, 64), cols(0)], held.at[pl.ds(0, 64)]),
        (weight.at[rows_at(xl * 32, 32), cols(2)], held.at[pl.ds(64, 32)]),
        (weight.at[:, cols(1)], held.at[pl.ds(96, 128)]),
        (weight.at[pl.ds(64, 64), cols(2)], held.at[pl.ds(224, 64)]),
        (
            reduce.at[rows_at(core * 256 + z * 64, 64), pl.ds(COLS, COLS)],
            held.at[pl.ds(288, 64)],
        ),
        (output.at[rows_at(z * 32, 32)], wide),
    ]
    second = [(reduce.at[rows_at(core * 256, 256), pl.ds(0, COLS)], rest.at[pl.ds(320, 256)])]
    for s in range(8):
        j, right = s // 2, (s % 2) * 256
        at = rows_at(s * 512 + core * 256, 256)
        rows, size = (rows_at(xl * 64, 64), 64) if j < 3 else (pl.ds(0, 128), 128)
        second.append((expand.at[rows, at], rest.at[pl.ds(64 * j, size), pl.ds(right, 256)]))
    first = started(first, sems.at[pl.ds(0, 6)])
    second = started(second, sems.at[pl.ds(6, 9)])
    padded[...] = jnp.zeros_like(padded)
    padded[: vector.shape[0], : vector.shape[1]] = vector[...]
    block[192:208, :] = padded[...].astype(LOW)
    finished(first)
    half[...] = held[:96].astype(LOW)
    block[:192, :] = held[96:288].astype(LOW)
    block[208:272, :] = held[288:].astype(LOW)
    block[272:304, :] = wide[:, :COLS].astype(LOW)
    block[304:336, :] = wide[:, COLS:].astype(LOW)
    finished(second)
    rest_half[...] = rest[:192].astype(LOW)
    rest_y[...] = rest[192:].astype(LOW)


def cast(places, *arrays):
    outs = [low_shape(96, COLS), low_shape(336, COLS), low_shape(192, COLS), low_shape(384, COLS)]
    vmem = pltpu.VMEM
    return call(
        cast_kernel,
        [SCALARS, OUTSIDE, INSIDE, OUTSIDE, OUTSIDE, OUTSIDE],
        [(shape, INSIDE) for shape in outs],
        [vmem((352, COLS), FULL), vmem((576, COLS), FULL), vmem((32, 2 * COLS), FULL)]
        + [vmem((16, COLS), FULL), pltpu.SemaphoreType.DMA((15,))],
        3,
        (places, *arrays),
        vmem=60,
    )


def joint_kernel(places, own, other, *refs):
    along_x, along_y, refs = refs[:4], refs[4:8], refs[8:]
    normed, query, key, value, vectors, query_mat, key_mat, value_mat, sems = refs
    mats = (query_mat, key_mat, value_mat, vectors)
    finished(started(joint_plan(places, along_x, along_y, mats), sems))
    gain, shift = row_of(vectors, 0), row_of(vectors, 1)
    core = places[13]
    query_bias = own_columns(row_of(vectors, 2), core, COLS)
    value_bias = own_columns(row_of(vectors, 3), core, COLS)
    count = own.shape[0]
    for block, tokens in enumerate((own, other)):
        rows = pl.ds(block * count, count)
        unit, _ = unit_of(tokens[...].astype(FULL))
        low = (unit * gain + shift).astype(LOW)
        normed[rows, :] = low
        query[rows, :] = ((dot(low, query_mat[...]) + query_bias).astype(LOW) * 0.125).astype(LOW)
        key[rows, :] = dot(low, key_mat[...]).astype(LOW)
        value[rows, :] = (dot(low, value_mat[...]) + value_bias).astype(LOW)


def joint(places, own, other, along_x, along_y):
    count, width = own.shape
    rows = 2 * count
    mat, half = (low_shape(width, COLS), INSIDE), (low_shape(rows, COLS), INSIDE)
    return call(
        joint_kernel,
        [SCALARS, INSIDE, INSIDE] + [OUTSIDE] * 8,
        [(low_shape(rows, width), INSIDE), half, half, half]
        + [(low_shape(16, width), INSIDE), mat, mat, mat],
        [pltpu.SemaphoreType.DMA((56,))],
        8,
        (places, own, other, *along_x, *along_y),
        vmem=24,
    )


def two_by_two(values, lane):
    return jnp.concatenate([jnp.where(lane, values, 0), jnp.where(lane, 0, values)], axis=0)


def probabilities(stacked, keys, bar):
    scores = dot_nt(stacked, keys) + jnp.concatenate([bar, bar], axis=0)
    probs = jnp.exp(scores - jnp.max(scores, axis=-1, keepdims=True))
    return probs * (1.0 / jnp.sum(probs, axis=-1, keepdims=True))


def attention_kernel(block, lengths, query, key, value, attended, mask):
    count = query.shape[0]
    mask[...] = barred(lengths, block, 0, count, count)
    lane = lax.broadcasted_iota(jnp.int32, (count, TILE), 1) < HEAD_DIM
    for index in range(COLS // TILE):
        cols = pl.ds(index * TILE, TILE)
        probs = probabilities(two_by_two(query[:, cols], lane), key[:, cols], mask[...])
        out = dot(probs.astype(LOW), value[:, cols])
        attended[:, cols] = jnp.where(lane, out[:count], out[count:]).astype(LOW)


def attention(block, lengths, query, key, value):
    count = query.shape[0] // 2
    return call(
        lambda *refs: attention_kernel(block, *refs),
        [SCALARS] + [pl.BlockSpec((count, COLS), lambda i: (block, 0))] * 3,
        [(low_shape(count, COLS), INSIDE)],
        [pltpu.VMEM((count, count), FULL)],
        5,
        (lengths, query, key, value),
        grid=(1,),
        vmem=20,
    )[0]


def output_kernel(places, own, other, *refs):
    raw, (branch, out_mat, sems) = refs[:4], refs[4:]
    finished(started(out_plan(places, lambda k: raw[k], 64, out_mat), sems))
    count = own.shape[0]
    for block, attended in enumerate((own, other)):
        for half in range(2):
            branch[block * count : (block + 1) * count, half * COLS : (half + 1) * COLS] = dot(
                attended[...], out_mat[half]
            ).astype(LOW)


def output(places, own, other, raw):
    rows, local = 2 * own.shape[0], own.shape[1]
    return call(
        output_kernel,
        [SCALARS, INSIDE, INSIDE] + [OUTSIDE] * 4,
        [(low_shape(rows, 2 * COLS), INSIDE), (low_shape(2, local, COLS), INSIDE)],
        [pltpu.SemaphoreType.DMA((32,))],
        5,
        (places, own, other, *raw),
        vmem=14,
    )


def forward_backward_kernel(
    places, lengths, own, other, arriving_own, arriving_other, branch, branch_far, vectors, *refs
):
    raw, refs = refs[:12], refs[12:]
    sent, refs = refs[:6], refs[6:]
    (middle, layer_own, layer_other, normed_grad, bias_grad,
     up, down_one, down_two, up_grad, one_grad, two_grad,
     tokens, near, far, held, normed, arriving, layer_sum, normed_sum, active, up_low,
     row_sems, sems, sems_out) = refs
    count = own.shape[0]
    blocks = [pl.ds(0, count), pl.ds(count, count)]
    rows_in = []
    for block, (token, cotangent) in enumerate(((own, arriving_own), (other, arriving_other))):
        here, there = blocks[block], blocks[1 - block]
        pairs = [
            (token, tokens.at[here]),
            (branch.at[here], near.at[here]),
            (branch_far.at[there], far.at[here]),
            (cotangent, arriving.at[here]),
        ]
        rows_in.append(started(pairs, row_sems.at[pl.ds(4 * block, 4)]))
    views = [lambda k, a=axis: raw[4 * a + k] for axis in range(3)]
    plan = up_plan(places, *views, (up, down_one, down_two))
    copies = [pltpu.make_async_copy(a, b, sems.at[i]) for i, (a, b) in enumerate(plan)]
    kinds = [up_kind(index) for index in range(len(copies))]
    for wanted in (0, None, 1, 2, 3):
        for copy, kind in zip(copies, kinds):
            if kind == wanted:
                copy.start()
    gain, shift = row_of(vectors, 5), row_of(vectors, 6)
    rows_out = []
    for block, here in enumerate(blocks):
        finished(rows_in[block])
        summed = near[here, :].astype(FULL) + far[here, :].astype(FULL)
        value = tokens[here, :].astype(FULL) + summed + row_of(vectors, 4)
        held[here, :] = value
        rows_out += started([(held.at[here], middle.at[here])], row_sems.at[pl.ds(8 + block, 1)])
        unit, _ = unit_of(value)
        normed[here, :] = (unit * gain + shift).astype(LOW)
        slots = lax.broadcasted_iota(jnp.int32, value.shape, 0)
        live = slots < lengths[block, 0] + lengths[block, 1]
        arriving[here, :] = jnp.where(live, arriving[here, :], 0)
    core = places[13]
    biases = jnp.concatenate(
        [own_columns(row_of(vectors, 7 + k), core, 256) for k in range(4)], axis=0
    )
    finished(copies)
    views = [two_of(sent[2 * axis : 2 * axis + 2]) for axis in range(3)]
    plan = turned(up_plan(places, *views, (up_grad, one_grad, two_grad)))
    copies_out = [pltpu.make_async_copy(a, b, sems_out.at[i]) for i, (a, b) in enumerate(plan)]

    def of_chunk(j, action, list_of_copies):
        for index, (copy, kind) in enumerate(zip(list_of_copies, kinds)):
            if kind == j:
                action(copy)
            elif kind is None:

                @pl.when(up_shard(places, index) // 2 == j)
                def _(copy=copy):
                    action(copy)

    for j in range(up.shape[0]):
        hidden = pl.ds(j * COLS, COLS)
        upward = dot(normed[...], up[j]) + biases[j : j + 1]
        act, slope = gelu_both(upward)
        active[...] = act.astype(LOW)
        layer_one, layer_two = dot(active[...], down_one[hidden, :]), dot(active[...], down_two[hidden, :])
        grad = dot_nt(arriving[:, :COLS], down_one[hidden, :])
        grad += dot_nt(arriving[:, COLS:], down_two[hidden, :])
        low = (grad * slope).astype(LOW)
        up_low[...] = low
        bias_grad[j : j + 1, :] = jnp.sum(low.astype(FULL), axis=0, keepdims=True)
        normed_part = dot_nt(up_low[...], up[j])
        if j == 0:
            layer_sum[:, :COLS], layer_sum[:, COLS:] = layer_one, layer_two
            normed_sum[...] = normed_part
        else:
            layer_sum[:, :COLS] += layer_one
            layer_sum[:, COLS:] += layer_two
            normed_sum[...] += normed_part
        whole = dot_tn(active[...], arriving[...]).astype(LOW)
        one_grad[hidden, :] = whole[:, :COLS]
        two_grad[hidden, :] = whole[:, COLS:]
        up_grad[j] = dot_tn(normed[...], up_low[...]).astype(LOW)
        of_chunk(j, lambda copy: copy.start(), copies_out)
    layer_own[...] = held[:count, :] + layer_sum[:count, :] + row_of(vectors, 11)
    layer_other[...] = layer_sum[count:, :].astype(LOW)
    normed_grad[...] = normed_sum[...].astype(LOW)
    finished(rows_out)
    finished(copies_out)


def forward_backward(places, lengths, tokens, arriving, branch, branch_far, vectors, raw):
    count, width = tokens[0].shape
    rows, hidden = 2 * count, 4 * COLS
    sent = [low_shape(2, 4, 192, COLS), low_shape(2, 2, 384, COLS), low_shape(2, 4, 2, 64, COLS)]
    inside = [
        full_shape(count, width), low_shape(count, width), low_shape(rows, width),
        full_shape(4, COLS),
    ]
    vmem = pltpu.VMEM
    mats = [vmem((4, width, COLS), LOW), vmem((hidden, COLS), LOW), vmem((hidden, COLS), LOW)]
    low, full = vmem((rows, width), LOW), vmem((rows, width), FULL)
    return call(
        forward_backward_kernel,
        [SCALARS, SCALARS] + [OUTSIDE] * 6 + [INSIDE] + [OUTSIDE] * 12,
        [(s, OUTSIDE) for s in sent for _ in range(2)]
        + [(full_shape(rows, width), OUTSIDE)]
        + [(s, INSIDE) for s in inside],
        mats + mats + [low, low, low, full, low, low, full, full]
        + [vmem((rows, COLS), LOW), vmem((rows, COLS), LOW)]
        + [pltpu.SemaphoreType.DMA((n,)) for n in (10, 96, 96)],
        33,
        (places, lengths, *tokens, *arriving, branch, branch_far, vectors, *raw),
        vmem=50,
    )


def output_backward_kernel(
    places, lengths, arriving_own, arriving_other, middle, part, part_far, vectors, own, other,
    out_mat, sent_one, sent_two, middle_grad, attended_grad, sums,
    held, near, far, arriving, branch, out_grad, attended, weights, row_sems, sems,
):
    count = arriving_own.shape[0]
    blocks = [pl.ds(0, count), pl.ds(count, count)]
    rows_in = []
    for block, cotangent in enumerate((arriving_own, arriving_other)):
        here, there = blocks[block], blocks[1 - block]
        pairs = [
            (middle.at[here], held.at[here]),
            (part.at[here], near.at[here]),
            (part_far.at[there], far.at[here]),
            (cotangent, arriving.at[here]),
        ]
        rows_in.append(started(pairs, row_sems.at[pl.ds(4 * block, 4)]))
    pairs = [(own, attended.at[blocks[0]]), (other, attended.at[blocks[1]]), (out_mat, weights)]
    later = started(pairs, row_sems.at[pl.ds(8, 3)])
    gain = row_of(vectors, 5)
    for block, rows in enumerate(blocks):
        finished(rows_in[block])
        unit, inverse = unit_of(held[rows, :])
        grad = near[rows, :].astype(FULL) + far[rows, :].astype(FULL)
        slots = lax.broadcasted_iota(jnp.int32, grad.shape, 0)
        live = slots < lengths[block, 0] + lengths[block, 1]
        coming = jnp.where(live, arriving[rows, :].astype(FULL), 0.0)
        result = coming + norm_backward(grad, unit, inverse, gain)
        low = result.astype(LOW)
        branch[rows, :] = low
        if block == 0:
            middle_grad[...] = result
            sums[...] = jnp.zeros_like(sums)
            sums[0:1, :] = jnp.sum(low.astype(FULL), axis=0, keepdims=True)
            sums[1:2, :] = jnp.sum(grad * unit, axis=0, keepdims=True)
            sums[2:3, :] = jnp.sum(grad, axis=0, keepdims=True)
            sums[3:4, :] = jnp.sum(coming, axis=0, keepdims=True)
    finished(later)
    whole = dot_tn(attended[...], branch[...])
    out_grad[0] = whole[:, :COLS].astype(LOW)
    out_grad[1] = whole[:, COLS:].astype(LOW)
    copies = started(turned(out_plan(places, two_of((sent_one, sent_two)), 0, out_grad)), sems)
    attended_grad[...] = (
        dot_nt(branch[:, :COLS], weights[0]) + dot_nt(branch[:, COLS:], weights[1])
    ).astype(LOW)
    finished(copies)


def output_backward(
    places, lengths, arriving, middle, part, part_far, vectors, attended, out_mat
):
    rows, width = middle.shape
    sent = (low_shape(2, 4, 2, 32, COLS), OUTSIDE)
    inside = [full_shape(rows // 2, width), low_shape(rows, COLS), full_shape(8, width)]
    low = pltpu.VMEM((rows, width), LOW)
    return call(
        output_backward_kernel,
        [SCALARS, SCALARS] + [FAR_OUTSIDE] * 5 + [INSIDE] + [FAR_OUTSIDE] * 3,
        [sent, sent] + [(s, INSIDE) for s in inside],
        [pltpu.VMEM((rows, width), FULL), low, low, low, low, pltpu.VMEM((2, COLS, COLS), LOW)]
        + [pltpu.VMEM((rows, COLS), LOW), pltpu.VMEM((2, COLS, COLS), LOW)]
        + [pltpu.SemaphoreType.DMA((11,)), pltpu.SemaphoreType.DMA((32,))],
        10,
        (places, lengths, *arriving, middle, part, part_far, vectors, *attended, out_mat),
        vmem=54,
    )


def attention_backward_kernel(
    block, lengths, query, key, value, grad_in, query_grad, key_grad, value_grad, sums, mask
):
    count = query.shape[0]
    mask[...] = barred(lengths, block, 0, count, count)
    lane = lax.broadcasted_iota(jnp.int32, (count, TILE), 1) < HEAD_DIM
    for index in range(COLS // TILE):
        cols = pl.ds(index * TILE, TILE)
        stacked, given = two_by_two(query[:, cols], lane), two_by_two(grad_in[:, cols], lane)
        probs = probabilities(stacked, key[:, cols], mask[...])
        weighted = probs * dot_nt(given, value[:, cols])
        grad = (weighted - probs * jnp.sum(weighted, axis=-1, keepdims=True)).astype(LOW)
        out = dot(grad, key[:, cols])
        query_grad[:, cols] = (jnp.where(lane, out[:count], out[count:]) * 0.125).astype(LOW)
        key_grad[:, cols] = dot_tn(grad, stacked).astype(LOW)
        value_grad[:, cols] = dot_tn(probs.astype(LOW), given).astype(LOW)
    sums[...] = jnp.zeros_like(sums)
    sums[0:1, :] = jnp.sum(query_grad[...].astype(FULL), axis=0, keepdims=True)
    sums[1:2, :] = jnp.sum(value_grad[...].astype(FULL), axis=0, keepdims=True)


def attention_backward(block, lengths, query, key, value, grad_in):
    count = query.shape[0] // 2
    vmem = pltpu.VMEM
    half = (low_shape(count, COLS), INSIDE)
    part = pl.BlockSpec((count, COLS), lambda i: (block, 0))
    return call(
        lambda *refs: attention_backward_kernel(block, *refs),
        [SCALARS] + [part] * 4,
        [half, half, half, (full_shape(8, COLS), INSIDE)],
        [vmem((count, count), FULL)],
        8,
        (lengths, query, key, value, grad_in),
        grid=(1,),
        vmem=20,
    )


def joint_grad_kernel(places, normed, *refs):
    grads, sent, (query_part, key_part, value_part, sems) = refs[:6], refs[6:12], refs[12:]
    parts = (query_part, key_part, value_part)
    count = grads[0].shape[0]
    sides = [jnp.concatenate([g[...] for g in grads[i : i + 3]], axis=1) for i in (0, 3)]
    whole = dot_tn(normed[:count, :], sides[0]) + dot_tn(normed[count:, :], sides[1])
    for index, part in enumerate(parts):
        part[...] = whole[:, index * COLS : (index + 1) * COLS].astype(LOW)
    finished(started(joint_sent_plan(places, sent, parts), sems))


def joint_grad_parts(places, normed, own, other):
    rows, width = normed.shape
    sent = [low_shape(2, 4, 64, COLS), low_shape(2, 2, 128, COLS), low_shape(2, 4, 2, 32, COLS)]
    return call(
        joint_grad_kernel,
        [SCALARS] + [INSIDE] * 7,
        [(s, OUTSIDE) for s in sent for _ in range(2)],
        [pltpu.VMEM((width, COLS), LOW)] * 3 + [pltpu.SemaphoreType.DMA((56,))],
        8,
        (places, normed, *own, *other),
        vmem=44,
    )


def joint_backward_kernel(*refs):
    own, other, mats, outs = refs[:3], refs[3:6], refs[6:9], refs[9:]
    for grads, out in zip((own, other), outs):
        whole = dot_nt(grads[0][...], mats[0][...])
        whole += dot_nt(grads[1][...], mats[1][...])
        whole += dot_nt(grads[2][...], mats[2][...])
        out[...] = whole.astype(out.dtype)


def joint_backward(own, other, mats):
    count, width = own[0].shape[0], mats[0].shape[0]
    return call(
        joint_backward_kernel,
        [INSIDE] * 9,
        [(full_shape(count, width), INSIDE), (low_shape(count, width), INSIDE)],
        [],
        6,
        (*own, *other, *mats),
        vmem=20,
    )


def input_kernel(
    places, tokens, part, part_far, middle_grad, vectors, two_sums, own_sums, other_sums, up_sums,
    input_grad, sums, rows,
):
    unit, inverse = unit_of(tokens[...].astype(FULL))
    grad = part[...] + part_far[...].astype(FULL)
    input_grad[...] = middle_grad[...] + norm_backward(grad, unit, inverse, row_of(vectors, 0))
    first = places[13] == 0

    def own_side(values):
        none = jnp.zeros_like(values)
        return jnp.concatenate(
            [jnp.where(first, values, none), jnp.where(first, none, values)], axis=1
        )

    rows[...] = jnp.zeros_like(rows)
    rows[0:1, :] = jnp.sum(grad * unit, axis=0, keepdims=True)
    rows[1:2, :] = jnp.sum(grad, axis=0, keepdims=True)
    for k in range(2):
        rows[2 + k : 3 + k, :] = own_side(own_sums[k : k + 1, :] + other_sums[k : k + 1, :])
    rows[4:7, :] = two_sums[0:3, :]
    for k in range(4):
        hidden = up_sums[k : k + 1, :]
        rows[7 + k : 8 + k, :] = jnp.concatenate(
            [own_side(hidden[:, :256]), own_side(hidden[:, 256:])], axis=1
        )
    rows[11:12, :] = two_sums[3:4, :]
    sums[:16, :] = rows[:, :COLS].astype(LOW)
    sums[16:, :] = rows[:, COLS:].astype(LOW)


def input_backward(places, *arrays):
    count, width = arrays[0].shape
    return call(
        input_kernel,
        [SCALARS] + [INSIDE] * 9,
        [(full_shape(count, width), INSIDE), (low_shape(32, COLS), INSIDE)],
        [pltpu.VMEM((16, width), FULL)],
        4,
        (places, *arrays),
        vmem=20,
    )


def adam_step(weight, first, second, grad, rate, decay):
    first_new = BETA_ONE * first + (1.0 - BETA_ONE) * grad
    second_new = BETA_TWO * second + (1.0 - BETA_TWO) * grad * grad
    mean_hat = first_new / (1.0 - BETA_ONE**STEP)
    square_hat = second_new / (1.0 - BETA_TWO**STEP)
    fresh = weight - rate * (mean_hat / (jnp.sqrt(square_hat) + ADAM_EPS) + decay * weight)
    return (first_new, second_new, fresh)


def adam_kernel(grad_of, rate, chunks, places, *refs):
    state, refs = refs[:3], refs[3:]
    grads, refs = refs[:-8], refs[-8:]
    outs, (held, results, sems_in, sems_out) = refs[:4], refs[4:]
    coming = [
        started([(a.at[at], held.at[(i, *at)]) for i, a in enumerate(state)], sems_in.at[n])
        for n, at in enumerate(chunks)
    ]
    going = []
    for n, at in enumerate(chunks):
        grad = grad_of(n, places, *grads)
        finished(coming[n])
        results[(0, *at)] = grad
        weight, first, second = (held[(i, *at)] for i in range(3))
        new = adam_step(weight, first, second, grad, rate, MATRIX_DECAY)
        for i, value in enumerate(new):
            results[(1 + i, *at)] = value
        going += started(
            [(results.at[(i, *at)], out.at[at]) for i, out in enumerate(outs)], sems_out.at[n]
        )
    finished(going)


def adam(grad_of, rate, chunks, state, grads, places):
    shape = state[0].shape
    return pl.pallas_call(
        lambda *refs: adam_kernel(grad_of, rate, chunks, *refs),
        grid=(1,),
        in_specs=[SCALARS]
        + [OUTSIDE] * 3
        + [pl.BlockSpec((g[1], COLS), lambda i, at=g[2]: (at, 0)) for g in grads],
        out_specs=[OUTSIDE] * 4,
        out_shape=[full_shape(*shape)] * 4,
        scratch_shapes=[pltpu.VMEM((3, *shape), FULL), pltpu.VMEM((4, *shape), FULL)]
        + [pltpu.SemaphoreType.DMA((len(chunks), 3)), pltpu.SemaphoreType.DMA((len(chunks), 4))],
        compiler_params=pltpu.CompilerParams(vmem_limit_bytes=24 << 20),
        cost_estimate=pl.CostEstimate(
            flops=6 * FLOPS_PER_US, bytes_accessed=30 * state[0].size, transcendentals=0
        ),
    )(places, *state, *(g[0] for g in grads))


def by_core(places, both, far):
    own = places[13] == 0
    both, far = both.astype(FULL), far.astype(FULL)
    return jnp.where(own, both, far), jnp.where(own, far, both)


def columns_of(width, count):
    return [(slice(None), slice(n * width, (n + 1) * width)) for n in range(count)]


def rows_each(height, count):
    return [(slice(n * height, (n + 1) * height), slice(None)) for n in range(count)]


def adam_joint(places, state, sums):
    def grad_of(n, places, both, far):
        rows = slice(128 * n, 128 * (n + 1))
        return jnp.concatenate(by_core(places, both[rows, :], far[rows, :]), axis=1)

    grads = [(a, 384, 0) for a in sums]
    return adam(grad_of, MATRIX_RATE, columns_of(2 * COLS, 3), state, grads, places)


def adam_expand(places, state, sums):
    def grad_of(n, places, both, far):
        rows = slice(128 * n, 128 * (n + 1))
        zero, one = by_core(places, both[rows, :], far[rows, :])
        return jnp.concatenate(
            [zero[:, :256], one[:, :256], zero[:, 256:], one[:, 256:]], axis=1
        )

    grads = [(a, 512, 0) for a in sums]
    return adam(grad_of, MATRIX_RATE, columns_of(2 * COLS, 4), state, grads, places)


def adam_reduce(places, state, sums):
    def grad_of(n, places, left, right, far_left, far_right):
        rows = slice(128 * (n % 2), 128 * (n % 2 + 1))
        own = places[13] == n // 2
        return jnp.concatenate(
            [
                jnp.where(own, left[rows, :].astype(FULL), far_left[rows, :].astype(FULL)),
                jnp.where(own, right[rows, :].astype(FULL), far_right[rows, :].astype(FULL)),
            ],
            axis=1,
        )

    grads = [(a, 256, at) for a in sums for at in (2, 3)]
    return adam(grad_of, MATRIX_RATE, rows_each(128, 4), state, grads, places)


def adam_output(places, state, sums):
    def grad_of(n, places, *grads):
        both, far = grads[n], grads[2 + n]

        def rows(a):
            return jnp.concatenate(
                [
                    jnp.concatenate([a[64 * q : 64 * q + 32, :], a[64 * q + 32 : 64 * q + 64, :]], axis=1)
                    for q in (0, 1)
                ]
            ).astype(FULL)

        return jnp.where(places[13] == places[12], rows(both), rows(far))

    grads = [(a, 128, at) for a in sums for at in (3, 4)]
    return adam(grad_of, OUTPUT_RATE, rows_each(64, 2), state, grads, places)


def per_device(
    tokens,
    cotangent,
    lengths,
    joint_weight,
    joint_first,
    joint_second,
    output_weight,
    output_first,
    output_second,
    expand_weight,
    expand_first,
    expand_second,
    reduce_weight,
    reduce_first,
    reduce_second,
    vector_weight,
    vector_first,
    vector_second,
):
    me = coordinates()
    places = places_of(me)
    across = flip("core", 1)

    half, block, rest_half, rest_y = cast(
        places, joint_weight, vector_weight, expand_weight, reduce_weight, output_weight
    )
    joint_x, joint_y, along_x, along_y, along_z, far = gather_first(
        places, half, block, rest_half, rest_y, [send(a, across) for a in (lengths, tokens, cotangent)]
    )
    tokens, cotangent = (tokens, far[1]), (cotangent, far[2])
    lengths = jnp.concatenate([lengths, far[0]])

    normed_one, query, key, value, vectors, *joint_mats = joint(
        places, *tokens, joint_x, joint_y
    )
    along_z.append(send(after(along_z[1], query), turn("z", 1)))
    along_y.append(send(after(along_y[0], query), turn("y", 1)))
    along_y.append(send(after(along_y[1], query), turn("y", 1)))
    own = attention(0, lengths, after(query, along_y[1], *along_z[1:3]), key, value)
    along_x.append(send(after(along_x[1], own), turn("x", 1)))
    other = attention(1, lengths, after(query, along_x[1]), key, value)
    attended = (own, other)
    branch, out_mat = output(places, own, after(other, *along_x[2:], *along_y[2:]), along_z)
    branch_far = send(branch, across)
    *sent, middle, layer_own, layer_other, normed_two_part, up_bias_grad = forward_backward(
        places, lengths, tokens, cotangent, branch, branch_far, vectors,
        [*along_x, *along_y, *along_z],
    )
    part_far = send(normed_two_part, across)
    layer_far = send(layer_other, across)

    out_one, out_two, middle_grad, attended_grad, two_sums = output_backward(
        places, lengths, cotangent, middle, normed_two_part, part_far, vectors, attended, out_mat
    )
    sent[5] = after(sent[5], attended_grad)
    rest = total(me, sent, 0, 3, 0)
    next(rest)
    out_far = send(out_two, turn("z", 1))
    *own_grads, own_sums = attention_backward(0, lengths, query, key, value, attended_grad)
    *other_grads, other_sums = attention_backward(1, lengths, query, key, value, attended_grad)
    mark = rest.send(other_grads[0])
    sent = joint_grad_parts(places, after(normed_one, mark), own_grads, other_grads)
    joint_rows = total(me, sent, 32, 1, 32)
    next(joint_rows)
    mark = rest.send((sent[0], None, None))
    part_own, part_other = joint_backward(
        (after(own_grads[0], mark), *own_grads[1:]), other_grads, joint_mats
    )
    part_far = send(part_other, across)
    (out_near,) = added_all([[(out_one, 1), (after(out_far, part_own), 1)]])
    out_near = out_near.reshape(out_one.shape[1:])
    out_again = send(out_near, turn("z", 0))
    mark = joint_rows.send(part_own)
    mark = rest.send(mark)
    input_grad, vector_local = input_backward(
        places, tokens[0], after(part_own, mark), part_far, middle_grad, vectors, two_sums,
        own_sums, other_sums, up_bias_grad,
    )
    (out_along,) = added_all(
        [[(out_one, 0), (out_far, 0), (after(out_again, vector_local), 0)]]
    )
    out_along = out_along.reshape(out_one.shape[1:])

    mark = joint_rows.send((vector_local, vector_local, out_along))
    for turn_number in range(4):
        if turn_number == 2:
            layer_out = (after(layer_own, mark) + layer_far.astype(FULL)).astype(LOW)
            mark = (mark, layer_out)
        mark = rest.send(mark)
        mark = joint_rows.send(mark)
    mark = rest.send(mark)
    mark = joint_rows.send(mark)
    mark = joint_rows.send(mark)
    mark = rest.send(mark)
    mark = joint_rows.send(mark)
    one, two, extra = next(joint_rows)
    joint_state = adam_joint(
        places, (joint_weight, joint_first, joint_second), (after(one, mark), two)
    )
    output_state = adam_output(
        places, (output_weight, output_first, output_second), (after(one, mark), two)
    )
    one, two, _ = next(rest)
    one = after(one, joint_state[0], output_state[0])
    expand = adam_expand(places, (expand_weight, expand_first, expand_second), (one, two))
    reduce = adam_reduce(places, (reduce_weight, reduce_first, reduce_second), (one, two))
    vector_grad = lax.dynamic_slice(
        jnp.concatenate([extra[:12], extra[16:28]], axis=1).astype(FULL),
        (0, 128 * lax.axis_index("shard")),
        (12, 128),
    )
    vector_state = (vector_grad,) + adam_step(
        vector_weight, vector_first, vector_second, vector_grad, VECTOR_RATE, 0.0
    )
    states = zip(joint_state, output_state, expand, reduce, vector_state)
    return (layer_out, input_grad, *(a for kind in states for a in kind))


def solution(mesh):
    rows, columns, split = P("shard", None), P(None, "shard"), P(("wide", "shard"), None)
    state = (rows, rows, rows, rows, columns)
    return jax.shard_map(
        per_device,
        mesh=mesh,
        in_specs=(split, split, split) + (rows,) * 12 + (columns,) * 3,
        out_specs=(split, split) + state * 4,
        check_vma=False,
    )
```

```python
import jax
import jax.numpy as jnp
from jax import lax
from jax.experimental import pallas as pl
from jax.experimental.pallas import tpu as pltpu
from jax.sharding import PartitionSpec as P

HEAD_DIM = 64
STEP = 10


ROOT_TWO_PI = 0.7978845608028654
CUBIC = 0.044715
BETA_ONE = 0.9
BETA_TWO = 0.999
ADAM_EPS = 1e-08
MATRIX_RATE = 0.03
OUTPUT_RATE = 0.1
VECTOR_RATE = 0.2
MATRIX_DECAY = 0.1

LOW = jnp.bfloat16
FULL = jnp.float32
AXES = ("wide", "shard")
SIZES = (4, 2, 2, 2, 4)
COLS = 512
FLOPS_PER_US = 1_150_000_000


def coordinates():
    wide, shard = lax.axis_index("wide"), lax.axis_index("shard")
    z, xl, core = wide // 4, (wide // 2) % 2, wide % 2
    xh, y = shard // 4, shard % 4
    return {"z": z, "x": 2 * xh + xl, "y": y, "xl": xl, "xh": xh, "core": core}


def route(partner):
    pairs = []
    for source in range(128):
        rest, places = source, []
        for size in reversed(SIZES):
            places.append(rest % size)
            rest //= size
        y, xh, core, xl, z = places
        target = partner({"z": z, "x": 2 * xh + xl, "y": y, "core": core})
        flat = 0
        for place, size in zip(
            (target["z"], target["x"] % 2, target["core"], target["x"] // 2, target["y"]), SIZES
        ):
            flat = flat * size + place
        pairs.append((source, flat))
    return pairs


def flip(axis, bits):
    return route(lambda at: {**at, axis: at[axis] ^ bits})


def turn(axis, step):
    return route(lambda at: {**at, axis: at[axis] ^ (1 if (at["core"] + step) % 2 == 0 else 3)})


def send(value, pairs):
    return lax.ppermute(value, AXES, pairs)


def added(*terms):
    return sum(term.astype(FULL) for term in terms).astype(LOW)


def orders(me, axis):
    here = me[axis]
    one = jnp.where(me["core"] == 0, 1, 3)
    return [here, here ^ one, here ^ (4 - one), here ^ 2]


def places_of(me):
    return jnp.stack(
        orders(me, "x")
        + orders(me, "y")
        + orders(me, "z")
        + [me["xh"], me["core"], me["xl"], me["z"]]
    ).astype(jnp.int32)


def after(value, *others):
    return lax.optimization_barrier((value, *others))[0]


def rows_of(*parts):
    return jnp.concatenate([p.reshape(-1, COLS) for p in parts])


def main_phase(block, axis, gate, late=False):
    first, second = send(block, turn(axis, 0)), send(gated(block, gate if late else None), turn(axis, 1))
    return [block, first, second, send(after(first, gate), turn(axis, 1))]


def pack_kernel(places, block, other, half, second, first, again):
    for out in (first, again):
        out[:208, :] = block[:208, :]
        out[208:416, :] = other[:208, :]
    again[416:512, :] = half[...]
    again[512:608, :] = second[...]
    own = places[13] == places[12]
    for p, held in enumerate((block, other)):
        at = 416 + 96 * p
        first[at : at + 64, :] = held[208:272, :]
        rows = slice(272 + 32 * p, 304 + 32 * p)
        first[at + 64 : at + 96, :] = jnp.where(own, block[rows, :], other[rows, :])


def pack(places, *arrays):
    return call(
        pack_kernel,
        [SCALARS] + [INSIDE] * 4,
        [(low_shape(608, COLS), INSIDE)] * 2,
        [],
        1,
        (places, *arrays),
        vmem=8,
    )


def gather_first(places, half, block, rest_half, rest_y, exchanged):
    size = half.shape[0]
    other, second, *early = lax.optimization_barrier(
        (send(block, flip("x", 3)), send(half, turn("y", 0)), *exchanged[:2])
    )
    own_y, both = pack(places, block, other, half, second)
    first_y, second_y = send(own_y, turn("y", 0)), send(both, turn("y", 1))
    rest_other = send(after(rest_y, other), flip("x", 3))
    first_y, second_y, rest_other, *late = lax.optimization_barrier(
        (first_y, second_y, rest_other, *exchanged[2:])
    )
    plane = rows_of(half, second, second_y[416:]).reshape(4, size, COLS)
    first_x, second_x = send(plane, turn("x", 0)), send(plane, turn("x", 1))
    third_y = send(rows_of(first_y[:416], own_y[416:], first_y[416:]), turn("y", 1))
    rest_near = send(after(rest_half, first_y), turn("y", 0))
    first_x, second_x, third_y, rest_near = lax.optimization_barrier(
        (first_x, second_x, third_y, rest_near)
    )
    third_x = send(first_x, turn("x", 1))
    here = rows_of(rest_half, rest_near)
    there = send(here, turn("y", 1))
    plane_z = rows_of(own_y[416:], first_y[416:], third_y[416:]).reshape(4, 2, 96, COLS)
    pair_y = jnp.stack([rest_y, rest_other])
    along_z = [plane_z, send(plane_z, turn("z", 0)), send(plane_z, turn("z", 1))]
    along_y = [pair_y, send(after(pair_y, third_y), turn("y", 0))]
    third_x, there = lax.optimization_barrier((third_x, there))
    plane_x = rows_of(here, there).reshape(4, -1, COLS)
    along_x = [plane_x, send(plane_x, turn("x", 0)), send(plane_x, turn("x", 1))]
    joint_x = [plane, first_x, second_x, third_x]
    joint_y = [own_y, first_y, second_y, third_y]
    return joint_x, joint_y, along_x, along_y, along_z, early + late


def added_all(sums, steps=2):
    terms, specs, outs, out_specs = [], [], [], []
    for group in sums:
        rows = min(a.size for a, _ in group) // COLS
        rows = rows // 2 if len(group) == 2 else rows
        for array, which in group:
            terms.append(array.reshape(-1, COLS))
            specs.append(
                pl.BlockSpec((rows // steps, COLS), lambda i, at=which * steps: (at + i, 0))
            )
        outs.append(low_shape(rows, COLS))
        out_specs.append(pl.BlockSpec((rows // steps, COLS), lambda i: (i, 0)))

    def kernel(*refs):
        at = 0
        for group, out in zip(sums, refs[len(terms) :]):
            out[...] = added(*(ref[...] for ref in refs[at : at + len(group)]))
            at += len(group)

    return pl.pallas_call(
        kernel,
        grid=(steps,),
        in_specs=specs,
        out_specs=out_specs,
        out_shape=outs,
        compiler_params=pltpu.CompilerParams(vmem_limit_bytes=12 << 20),
        cost_estimate=pl.CostEstimate(
            flops=3 * FLOPS_PER_US, bytes_accessed=6 * sum(o.size for o in outs), transcendentals=0
        ),
    )(*terms)


def assembled(me, mine, far, behind, pieces):
    behind = [a.reshape(-1, COLS) for a in behind]
    rows = 2 * mine.shape[0] + sum(a.shape[0] for a in behind)

    def kernel(right, mine, far, *refs):
        behind, out = refs[:-1], refs[-1]
        first = right[0] == 0
        source = target = 0
        for count, size in pieces:
            for _ in range(count):
                a, b = mine[source : source + size, :], far[source : source + size, :]
                out[target : target + size, :] = jnp.where(first, a, b)
                out[target + size : target + 2 * size, :] = jnp.where(first, b, a)
                source, target = source + size, target + 2 * size
        for part in behind:
            out[target : target + part.shape[0], :] = part[...]
            target += part.shape[0]

    return pl.pallas_call(
        kernel,
        out_shape=low_shape(rows, COLS),
        in_specs=[pl.BlockSpec(memory_space=pltpu.SMEM)]
        + [pl.BlockSpec(memory_space=pltpu.VMEM)] * (2 + len(behind)),
        out_specs=pl.BlockSpec(memory_space=pltpu.VMEM),
        compiler_params=pltpu.CompilerParams(vmem_limit_bytes=8 << 20),
        cost_estimate=pl.CostEstimate(
            flops=FLOPS_PER_US, bytes_accessed=4 * rows * COLS, transcendentals=0
        ),
    )(me["xl"].reshape(1).astype(jnp.int32), mine, far, *behind)


def gated(value, gate):
    return value if gate is None else after(value, *(gate if isinstance(gate, tuple) else (gate,)))


def total(me, raw, out_rows, units, extra_rows):
    axes = "xyz"
    parts = [raw[:2], raw[2:4], raw[4:]]
    far = [send(away, turn(axis, 1)) for (_, away), axis in zip(parts, axes)]
    gate = yield
    far = list(far if gate is None else lax.optimization_barrier((*far, gate))[:-1])
    keeps = [keep for keep, _ in parts]
    near = added_all([[(k, 1), (f, 1)] for k, f in zip(keeps, far)])
    near = lax.optimization_barrier([n.reshape(k.shape[1:]) for n, k in zip(near, keeps)])
    again = [send(n, turn(axis, 0)) for n, axis in zip(near, axes)]
    gate, extra, out = yield near[2]
    again = lax.optimization_barrier((*again, gate))[:-1]
    along = added_all([[(k, 0), (f, 0), (a, 0)] for k, f, a in zip(keeps, far, again)])
    along_x, along_y, along_z = lax.optimization_barrier(
        [a.reshape(k.shape[1:]) for a, k in zip(along, keeps)]
    )
    if out_rows:
        along_z = jnp.concatenate([along_z, out], axis=2)
    size_x, size_y = along_x.shape[1], along_y.shape[1] // 2
    size_z = (along_z.shape[2] - out_rows) // 2

    def with_extra(*parts):
        return rows_of(*parts, extra) if extra_rows else rows_of(*parts)

    def split(rows, *sizes):
        at, parts = 0, []
        for size in sizes:
            parts.append(rows[at : at + size])
            at += size
        return parts

    plane = jnp.concatenate([along_x, along_z.reshape(4, -1, COLS)], axis=1)
    size = plane.shape[1]
    far = send(with_extra(plane[2:]), turn("y", 1))
    gate = yield plane
    far, kept = gated(far, gate), plane[:2]
    near = added(kept[1], far[size : 2 * size])
    if extra_rows:
        extra = added(extra, far[2 * size :])
    again = send(with_extra(near), turn("y", 0))
    gate = yield near
    again = gated(again, gate)
    plane = added(kept[0], far[:size], again[:size])
    if extra_rows:
        extra = added(extra, again[size:])
    half, pair = plane[:size_x], plane[size_x:].reshape(2, 2 * size_z + out_rows, COLS)
    out = pair[:, 2 * size_z :].reshape(-1, COLS)
    pieces = jnp.concatenate(
        [along_y.reshape(4, size_y, COLS), pair[:, : 2 * size_z].reshape(4, size_z, COLS)], axis=1
    )
    size = size_y + size_z
    pieces = [
        lax.dynamic_index_in_dim(pieces, ((k // 2) ^ me["xh"]) * 2 + k % 2, 0, keepdims=False)
        for k in orders(me, "x")
    ]
    far = send(with_extra(pieces[2], pieces[3], out), turn("x", 1))
    gate = yield plane
    far = gated(far, gate)
    first, second, far_out, far_extra = split(far, size, size, 2 * out_rows, extra_rows)
    sums = added(rows_of(pieces[1], out), rows_of(second, far_out))
    if extra_rows:
        extra = added(extra, far_extra)
    again = send(with_extra(sums), turn("x", 0))
    gate = yield sums
    near, out, far_extra = split(gated(again, gate), size, 2 * out_rows, extra_rows)
    sums = rows_of(added(pieces[0], first, near), added(sums[size:], out))
    if extra_rows:
        extra = added(extra, far_extra)
    flat, block = rows_of(half, sums[:size_y]), sums[size_y:]
    size, size_block = flat.shape[0], block.shape[0]
    far = send(with_extra(flat, block), turn("z", 0))
    gate = yield sums
    sums, other, far_extra = split(gated(far, gate), size, size_block, extra_rows)
    flat = added(flat, sums)
    if extra_rows:
        extra = added(extra, far_extra)
    blocks = rows_of(block, other)
    far = send(with_extra(flat, blocks), turn("z", 1))
    gate = yield flat
    sums, other, far_extra = split(gated(far, gate), size, 2 * size_block, extra_rows)
    flat = added(flat, sums)
    if extra_rows:
        extra = added(extra, far_extra)
    blocks = rows_of(blocks, other).reshape(4, size_block, COLS)
    where = orders(me, "z")
    ordered = jnp.stack(
        [
            sum(jnp.where(where[k] == place, blocks[k], 0) for k in range(4)).astype(LOW)
            for place in range(4)
        ]
    )
    mine = rows_of(flat, ordered[:, :size_z])
    far = send(mine, flip("x", 1))
    gate = yield mine
    far = gated(far, gate)

    pieces = [(units, size_x // units), (1, size_y), (4, size_z)]
    both = assembled(me, mine, far, [ordered[:, size_z:]] if out_rows else [], pieces)
    far = send(with_extra(both), flip("core", 1))
    yield both
    rows = both.shape[0]
    if extra_rows:
        extra = added(extra, far[rows:])
        far = far[:rows]
    yield both, far, extra


def rows_at(start, size):
    return pl.ds(pl.multiple_of(start, size), size)


def joint_plan(places, along_x, along_y, mats):
    query, key, value, vectors = mats
    pairs = []
    for ky in range(4):
        y = places[4 + ky]
        for kx in range(4):
            x = places[kx]
            shard, half = (x // 2) * 4 + y, x % 2
            source = along_x[kx].at[ky]
            pairs.append(
                (source.at[pl.ds(0, 64)], query.at[rows_at(shard * 128 + half * 64, 64)])
            )
            pairs.append(
                (source.at[pl.ds(64, 32)], value.at[rows_at(shard * 128 + half * 32, 32)])
            )
        for p in range(2):
            shard = (places[12] ^ p) * 4 + y
            source, at = along_y[ky], p * 208
            pairs.append((source.at[pl.ds(at, 128)], key.at[rows_at(shard * 128, 128)]))
            pairs.append((source.at[pl.ds(at + 128, 64)], value.at[rows_at(shard * 128 + 64, 64)]))
            pairs.append(
                (
                    source.at[pl.ds(at + 192, 16), pl.ds(0, 128)],
                    vectors.at[:, rows_at(shard * 128, 128)],
                )
            )
    return pairs


def joint_sent_plan(places, raw, parts):
    query, key, value = parts
    pairs = []
    for ky in range(4):
        y = places[4 + ky]
        for kx in range(4):
            x = places[kx]
            start = ((x // 2) * 4 + y) * 128 + (x % 2) * 64
            pairs.append((query.at[rows_at(start, 64)], raw[0 + kx // 2].at[kx % 2, ky]))
        for p in range(2):
            shard = (places[12] ^ p) * 4 + y
            pairs.append((key.at[rows_at(shard * 128, 128)], raw[2 + ky // 2].at[ky % 2, p]))
            for kz in range(4):
                start = shard * 128 + places[8 + kz] * 32
                pairs.append((value.at[rows_at(start, 32)], raw[4 + kz // 2].at[kz % 2, ky, p]))
    return pairs


def up_plan(places, at_x, at_y, at_z, mats):
    up, down_one, down_two = mats
    pairs = []
    for ky in range(4):
        y = places[4 + ky]
        for kx in range(4):
            x = places[kx]
            start = ((x // 2) * 4 + y) * 128 + (x % 2) * 64
            for j in range(3):
                source = at_x(kx).at[ky, pl.ds(64 * j, 64)]
                pairs.append((source, up.at[j, rows_at(start, 64)]))
        for p in range(2):
            shard = (places[12] ^ p) * 4 + y
            source = at_y(ky).at[p]
            pairs.append((source.at[pl.ds(0, 128)], up.at[3, rows_at(shard * 128, 128)]))
            pairs.append((source.at[pl.ds(128, 256)], down_one.at[rows_at(shard * 256, 256)]))
            for kz in range(4):
                start = shard * 256 + places[8 + kz] * 64
                source = at_z(kz).at[ky, p, pl.ds(0, 64)]
                pairs.append((source, down_two.at[rows_at(start, 64)]))
    return pairs


def up_kind(index):
    index %= 24
    if index < 12:
        return index % 3
    return 3 if (index - 12) % 6 == 0 else None


def up_shard(places, index):
    ky, index = divmod(index, 24)
    return (places[12] ^ ((index - 12) // 6)) * 4 + places[4 + ky]


def out_plan(places, at_z, first, mat):
    pairs = []
    for ky in range(4):
        for kz in range(4):
            start = places[4 + ky] * 128 + places[8 + kz] * 32
            for p in range(2):
                source = at_z(kz).at[ky, p, pl.ds(first, 32)]
                pairs.append((source, mat.at[p, rows_at(start, 32)]))
    return pairs


def two_of(arrays):
    return lambda k: arrays[k // 2].at[k % 2]


def started(pairs, sems):
    all_of_them = [pltpu.make_async_copy(a, b, sems.at[i]) for i, (a, b) in enumerate(pairs)]
    for copy in all_of_them:
        copy.start()
    return all_of_them


def finished(all_of_them):
    for copy in all_of_them:
        copy.wait()


def turned(pairs):
    return [(b, a) for a, b in pairs]


def low_shape(*shape):
    return jax.ShapeDtypeStruct(shape, LOW)


def full_shape(*shape):
    return jax.ShapeDtypeStruct(shape, FULL)


SCALARS = pl.BlockSpec(memory_space=pltpu.SMEM)
INSIDE = pl.BlockSpec(memory_space=pltpu.VMEM)
OUTSIDE = pl.BlockSpec(memory_space=pl.ANY)
FAR_OUTSIDE = pl.BlockSpec(memory_space=pltpu.HBM)


def call(kernel, in_specs, outs, scratch, length, args, grid=(), vmem=60):
    shapes, specs = [o[0] for o in outs], [o[1] for o in outs]
    moved = sum(a.size * a.dtype.itemsize for a in (*args, *shapes))
    return pl.pallas_call(
        kernel,
        grid=grid,
        out_shape=shapes,
        in_specs=in_specs,
        out_specs=specs,
        scratch_shapes=scratch,
        compiler_params=pltpu.CompilerParams(vmem_limit_bytes=vmem << 20),
        cost_estimate=pl.CostEstimate(
            flops=length * FLOPS_PER_US, bytes_accessed=moved, transcendentals=0
        ),
    )(*args)


def gelu_both(upward):
    square = upward * upward
    tangent = jnp.tanh(ROOT_TWO_PI * upward * (1.0 + CUBIC * square))
    half = 0.5 * (1.0 + tangent)
    slope = half + 0.5 * upward * (1.0 - tangent * tangent) * ROOT_TWO_PI * (
        1.0 + 3.0 * CUBIC * square
    )
    return upward * half, slope


def dot(a, b):
    return jnp.dot(a, b, preferred_element_type=FULL)


def dot_nt(a, b):
    return lax.dot_general(a, b, (((1,), (1,)), ((), ())), preferred_element_type=FULL)


def dot_tn(a, b):
    return lax.dot_general(a, b, (((0,), (0,)), ((), ())), preferred_element_type=FULL)


def unit_of(values):
    center = values - jnp.mean(values, axis=-1, keepdims=True)
    inverse = lax.rsqrt(jnp.mean(center * center, axis=-1, keepdims=True) + 1e-05)
    return center * inverse, inverse


def norm_backward(grad_out, unit, inverse, gain):
    scaled = grad_out * gain
    return inverse * (
        scaled
        - jnp.mean(scaled, axis=-1, keepdims=True)
        - unit * jnp.mean(scaled * unit, axis=-1, keepdims=True)
    )


def row_of(vectors, row):
    return vectors[row : row + 1, :].astype(FULL)


def own_columns(full, core, size):
    groups = full.shape[1] // (2 * size)
    first = jnp.concatenate(
        [full[:, (2 * g) * size : (2 * g + 1) * size] for g in range(groups)], axis=1
    )
    second = jnp.concatenate(
        [full[:, (2 * g + 1) * size : (2 * g + 2) * size] for g in range(groups)], axis=1
    )
    return jnp.where(core == 0, first, second)


def barred(lengths, block, first, height, span):
    shape = (height, span)
    rows = lax.broadcasted_iota(jnp.int32, shape, 0) + first
    keys = lax.broadcasted_iota(jnp.int32, shape, 1)
    opening = lengths[block, 0]
    filled = opening + lengths[block, 1]
    begin = jnp.where(rows < opening, 0, jnp.where(rows < filled, opening, rows))
    return jnp.where((keys <= rows) & (keys >= begin), 0.0, -1e30)


TILE = 128


def cast_kernel(
    places, weight, vector, expand, reduce, output, half, block, rest_half, rest_y,
    held, rest, wide, padded, sems,
):
    core, xl, z = places[13], places[14], places[15]

    def cols(which):
        return rows_at(which * 2 * COLS + core * COLS, COLS)

    first = [
        (weight.at[rows_at(xl * 64, 64), cols(0)], held.at[pl.ds(0, 64)]),
        (weight.at[rows_at(xl * 32, 32), cols(2)], held.at[pl.ds(64, 32)]),
        (weight.at[:, cols(1)], held.at[pl.ds(96, 128)]),
        (weight.at[pl.ds(64, 64), cols(2)], held.at[pl.ds(224, 64)]),
        (
            reduce.at[rows_at(core * 256 + z * 64, 64), pl.ds(COLS, COLS)],
            held.at[pl.ds(288, 64)],
        ),
        (output.at[rows_at(z * 32, 32)], wide),
    ]
    second = [(reduce.at[rows_at(core * 256, 256), pl.ds(0, COLS)], rest.at[pl.ds(320, 256)])]
    for s in range(8):
        j, right = s // 2, (s % 2) * 256
        at = rows_at(s * 512 + core * 256, 256)
        rows, size = (rows_at(xl * 64, 64), 64) if j < 3 else (pl.ds(0, 128), 128)
        second.append((expand.at[rows, at], rest.at[pl.ds(64 * j, size), pl.ds(right, 256)]))
    first = started(first, sems.at[pl.ds(0, 6)])
    second = started(second, sems.at[pl.ds(6, 9)])
    padded[...] = jnp.zeros_like(padded)
    padded[: vector.shape[0], : vector.shape[1]] = vector[...]
    block[192:208, :] = padded[...].astype(LOW)
    finished(first)
    half[...] = held[:96].astype(LOW)
    block[:192, :] = held[96:288].astype(LOW)
    block[208:272, :] = held[288:].astype(LOW)
    block[272:304, :] = wide[:, :COLS].astype(LOW)
    block[304:336, :] = wide[:, COLS:].astype(LOW)
    finished(second)
    rest_half[...] = rest[:192].astype(LOW)
    rest_y[...] = rest[192:].astype(LOW)


def cast(places, *arrays):
    outs = [low_shape(96, COLS), low_shape(336, COLS), low_shape(192, COLS), low_shape(384, COLS)]
    vmem = pltpu.VMEM
    return call(
        cast_kernel,
        [SCALARS, OUTSIDE, INSIDE, OUTSIDE, OUTSIDE, OUTSIDE],
        [(shape, INSIDE) for shape in outs],
        [vmem((352, COLS), FULL), vmem((576, COLS), FULL), vmem((32, 2 * COLS), FULL)]
        + [vmem((16, COLS), FULL), pltpu.SemaphoreType.DMA((15,))],
        3,
        (places, *arrays),
        vmem=60,
    )


def joint_kernel(places, own, other, *refs):
    along_x, along_y, refs = refs[:4], refs[4:8], refs[8:]
    normed, query, key, value, vectors, query_mat, key_mat, value_mat, sems = refs
    mats = (query_mat, key_mat, value_mat, vectors)
    finished(started(joint_plan(places, along_x, along_y, mats), sems))
    gain, shift = row_of(vectors, 0), row_of(vectors, 1)
    core = places[13]
    query_bias = own_columns(row_of(vectors, 2), core, COLS)
    value_bias = own_columns(row_of(vectors, 3), core, COLS)
    count = own.shape[0]
    for block, tokens in enumerate((own, other)):
        rows = pl.ds(block * count, count)
        unit, _ = unit_of(tokens[...].astype(FULL))
        low = (unit * gain + shift).astype(LOW)
        normed[rows, :] = low
        query[rows, :] = ((dot(low, query_mat[...]) + query_bias).astype(LOW) * 0.125).astype(LOW)
        key[rows, :] = dot(low, key_mat[...]).astype(LOW)
        value[rows, :] = (dot(low, value_mat[...]) + value_bias).astype(LOW)


def joint(places, own, other, along_x, along_y):
    count, width = own.shape
    rows = 2 * count
    mat, half = (low_shape(width, COLS), INSIDE), (low_shape(rows, COLS), INSIDE)
    return call(
        joint_kernel,
        [SCALARS, INSIDE, INSIDE] + [OUTSIDE] * 8,
        [(low_shape(rows, width), INSIDE), half, half, half]
        + [(low_shape(16, width), INSIDE), mat, mat, mat],
        [pltpu.SemaphoreType.DMA((56,))],
        8,
        (places, own, other, *along_x, *along_y),
        vmem=24,
    )


def two_by_two(values, lane):
    return jnp.concatenate([jnp.where(lane, values, 0), jnp.where(lane, 0, values)], axis=0)


def probabilities(stacked, keys, bar):
    scores = dot_nt(stacked, keys) + jnp.concatenate([bar, bar], axis=0)
    probs = jnp.exp(scores - jnp.max(scores, axis=-1, keepdims=True))
    return probs * (1.0 / jnp.sum(probs, axis=-1, keepdims=True))


def attention_kernel(block, lengths, query, key, value, attended, mask):
    count = query.shape[0]
    mask[...] = barred(lengths, block, 0, count, count)
    lane = lax.broadcasted_iota(jnp.int32, (count, TILE), 1) < HEAD_DIM
    for index in range(COLS // TILE):
        cols = pl.ds(index * TILE, TILE)
        probs = probabilities(two_by_two(query[:, cols], lane), key[:, cols], mask[...])
        out = dot(probs.astype(LOW), value[:, cols])
        attended[:, cols] = jnp.where(lane, out[:count], out[count:]).astype(LOW)


def attention(block, lengths, query, key, value):
    count = query.shape[0] // 2
    return call(
        lambda *refs: attention_kernel(block, *refs),
        [SCALARS] + [pl.BlockSpec((count, COLS), lambda i: (block, 0))] * 3,
        [(low_shape(count, COLS), INSIDE)],
        [pltpu.VMEM((count, count), FULL)],
        5,
        (lengths, query, key, value),
        grid=(1,),
        vmem=20,
    )[0]


def output_kernel(places, own, other, *refs):
    raw, (branch, out_mat, sems) = refs[:4], refs[4:]
    finished(started(out_plan(places, lambda k: raw[k], 64, out_mat), sems))
    count = own.shape[0]
    for block, attended in enumerate((own, other)):
        for half in range(2):
            branch[block * count : (block + 1) * count, half * COLS : (half + 1) * COLS] = dot(
                attended[...], out_mat[half]
            ).astype(LOW)


def output(places, own, other, raw):
    rows, local = 2 * own.shape[0], own.shape[1]
    return call(
        output_kernel,
        [SCALARS, INSIDE, INSIDE] + [OUTSIDE] * 4,
        [(low_shape(rows, 2 * COLS), INSIDE), (low_shape(2, local, COLS), INSIDE)],
        [pltpu.SemaphoreType.DMA((32,))],
        5,
        (places, own, other, *raw),
        vmem=14,
    )


def forward_backward_kernel(
    places, lengths, own, other, arriving_own, arriving_other, branch, branch_far, vectors, *refs
):
    raw, refs = refs[:12], refs[12:]
    sent, refs = refs[:6], refs[6:]
    (middle, layer_own, layer_other, normed_grad, bias_grad,
     up, down_one, down_two, up_grad, one_grad, two_grad,
     tokens, near, far, held, normed, arriving, layer_sum, normed_sum, active, up_low,
     row_sems, sems, sems_out) = refs
    count = own.shape[0]
    blocks = [pl.ds(0, count), pl.ds(count, count)]
    rows_in = []
    for block, (token, cotangent) in enumerate(((own, arriving_own), (other, arriving_other))):
        here, there = blocks[block], blocks[1 - block]
        pairs = [
            (token, tokens.at[here]),
            (branch.at[here], near.at[here]),
            (branch_far.at[there], far.at[here]),
            (cotangent, arriving.at[here]),
        ]
        rows_in.append(started(pairs, row_sems.at[pl.ds(4 * block, 4)]))
    views = [lambda k, a=axis: raw[4 * a + k] for axis in range(3)]
    plan = up_plan(places, *views, (up, down_one, down_two))
    copies = [pltpu.make_async_copy(a, b, sems.at[i]) for i, (a, b) in enumerate(plan)]
    kinds = [up_kind(index) for index in range(len(copies))]
    for wanted in (0, None, 1, 2, 3):
        for copy, kind in zip(copies, kinds):
            if kind == wanted:
                copy.start()
    gain, shift = row_of(vectors, 5), row_of(vectors, 6)
    rows_out = []
    for block, here in enumerate(blocks):
        finished(rows_in[block])
        summed = near[here, :].astype(FULL) + far[here, :].astype(FULL)
        value = tokens[here, :].astype(FULL) + summed + row_of(vectors, 4)
        held[here, :] = value
        rows_out += started([(held.at[here], middle.at[here])], row_sems.at[pl.ds(8 + block, 1)])
        unit, _ = unit_of(value)
        normed[here, :] = (unit * gain + shift).astype(LOW)
        slots = lax.broadcasted_iota(jnp.int32, value.shape, 0)
        live = slots < lengths[block, 0] + lengths[block, 1]
        arriving[here, :] = jnp.where(live, arriving[here, :], 0)
    core = places[13]
    biases = jnp.concatenate(
        [own_columns(row_of(vectors, 7 + k), core, 256) for k in range(4)], axis=0
    )
    finished(copies)
    views = [two_of(sent[2 * axis : 2 * axis + 2]) for axis in range(3)]
    plan = turned(up_plan(places, *views, (up_grad, one_grad, two_grad)))
    copies_out = [pltpu.make_async_copy(a, b, sems_out.at[i]) for i, (a, b) in enumerate(plan)]

    def of_chunk(j, action, list_of_copies):
        for index, (copy, kind) in enumerate(zip(list_of_copies, kinds)):
            if kind == j:
                action(copy)
            elif kind is None:

                @pl.when(up_shard(places, index) // 2 == j)
                def _(copy=copy):
                    action(copy)

    for j in range(up.shape[0]):
        hidden = pl.ds(j * COLS, COLS)
        upward = dot(normed[...], up[j]) + biases[j : j + 1]
        act, slope = gelu_both(upward)
        active[...] = act.astype(LOW)
        layer_one, layer_two = dot(active[...], down_one[hidden, :]), dot(active[...], down_two[hidden, :])
        grad = dot_nt(arriving[:, :COLS], down_one[hidden, :])
        grad += dot_nt(arriving[:, COLS:], down_two[hidden, :])
        low = (grad * slope).astype(LOW)
        up_low[...] = low
        bias_grad[j : j + 1, :] = jnp.sum(low.astype(FULL), axis=0, keepdims=True)
        normed_part = dot_nt(up_low[...], up[j])
        if j == 0:
            layer_sum[:, :COLS], layer_sum[:, COLS:] = layer_one, layer_two
            normed_sum[...] = normed_part
        else:
            layer_sum[:, :COLS] += layer_one
            layer_sum[:, COLS:] += layer_two
            normed_sum[...] += normed_part
        whole = dot_tn(active[...], arriving[...]).astype(LOW)
        one_grad[hidden, :] = whole[:, :COLS]
        two_grad[hidden, :] = whole[:, COLS:]
        up_grad[j] = dot_tn(normed[...], up_low[...]).astype(LOW)
        of_chunk(j, lambda copy: copy.start(), copies_out)
    layer_own[...] = held[:count, :] + layer_sum[:count, :] + row_of(vectors, 11)
    layer_other[...] = layer_sum[count:, :].astype(LOW)
    normed_grad[...] = normed_sum[...].astype(LOW)
    finished(rows_out)
    finished(copies_out)


def forward_backward(places, lengths, tokens, arriving, branch, branch_far, vectors, raw):
    count, width = tokens[0].shape
    rows, hidden = 2 * count, 4 * COLS
    sent = [low_shape(2, 4, 192, COLS), low_shape(2, 2, 384, COLS), low_shape(2, 4, 2, 64, COLS)]
    inside = [
        full_shape(count, width), low_shape(count, width), low_shape(rows, width),
        full_shape(4, COLS),
    ]
    vmem = pltpu.VMEM
    mats = [vmem((4, width, COLS), LOW), vmem((hidden, COLS), LOW), vmem((hidden, COLS), LOW)]
    low, full = vmem((rows, width), LOW), vmem((rows, width), FULL)
    return call(
        forward_backward_kernel,
        [SCALARS, SCALARS] + [OUTSIDE] * 6 + [INSIDE] + [OUTSIDE] * 12,
        [(s, OUTSIDE) for s in sent for _ in range(2)]
        + [(full_shape(rows, width), OUTSIDE)]
        + [(s, INSIDE) for s in inside],
        mats + mats + [low, low, low, full, low, low, full, full]
        + [vmem((rows, COLS), LOW), vmem((rows, COLS), LOW)]
        + [pltpu.SemaphoreType.DMA((n,)) for n in (10, 96, 96)],
        33,
        (places, lengths, *tokens, *arriving, branch, branch_far, vectors, *raw),
        vmem=46,
    )


def output_backward_kernel(
    places, lengths, arriving_own, arriving_other, middle, part, part_far, vectors, own, other,
    out_mat, sent_one, sent_two, middle_grad, attended_grad, sums,
    held, near, far, arriving, branch, out_grad, attended, weights, row_sems, sems,
):
    count = arriving_own.shape[0]
    blocks = [pl.ds(0, count), pl.ds(count, count)]
    rows_in = []
    for block, cotangent in enumerate((arriving_own, arriving_other)):
        here, there = blocks[block], blocks[1 - block]
        pairs = [
            (middle.at[here], held.at[here]),
            (part.at[here], near.at[here]),
            (part_far.at[there], far.at[here]),
            (cotangent, arriving.at[here]),
        ]
        rows_in.append(started(pairs, row_sems.at[pl.ds(4 * block, 4)]))
    pairs = [(own, attended.at[blocks[0]]), (other, attended.at[blocks[1]]), (out_mat, weights)]
    later = started(pairs, row_sems.at[pl.ds(8, 3)])
    gain = row_of(vectors, 5)
    for block, rows in enumerate(blocks):
        finished(rows_in[block])
        unit, inverse = unit_of(held[rows, :])
        grad = near[rows, :].astype(FULL) + far[rows, :].astype(FULL)
        slots = lax.broadcasted_iota(jnp.int32, grad.shape, 0)
        live = slots < lengths[block, 0] + lengths[block, 1]
        coming = jnp.where(live, arriving[rows, :].astype(FULL), 0.0)
        result = coming + norm_backward(grad, unit, inverse, gain)
        low = result.astype(LOW)
        branch[rows, :] = low
        if block == 0:
            middle_grad[...] = result
            sums[...] = jnp.zeros_like(sums)
            sums[0:1, :] = jnp.sum(low.astype(FULL), axis=0, keepdims=True)
            sums[1:2, :] = jnp.sum(grad * unit, axis=0, keepdims=True)
            sums[2:3, :] = jnp.sum(grad, axis=0, keepdims=True)
            sums[3:4, :] = jnp.sum(coming, axis=0, keepdims=True)
    finished(later)
    whole = dot_tn(attended[...], branch[...])
    out_grad[0] = whole[:, :COLS].astype(LOW)
    out_grad[1] = whole[:, COLS:].astype(LOW)
    copies = started(turned(out_plan(places, two_of((sent_one, sent_two)), 0, out_grad)), sems)
    attended_grad[...] = (
        dot_nt(branch[:, :COLS], weights[0]) + dot_nt(branch[:, COLS:], weights[1])
    ).astype(LOW)
    finished(copies)


def output_backward(
    places, lengths, arriving, middle, part, part_far, vectors, attended, out_mat
):
    rows, width = middle.shape
    sent = (low_shape(2, 4, 2, 32, COLS), OUTSIDE)
    inside = [full_shape(rows // 2, width), low_shape(rows, COLS), full_shape(8, width)]
    low = pltpu.VMEM((rows, width), LOW)
    return call(
        output_backward_kernel,
        [SCALARS, SCALARS] + [FAR_OUTSIDE] * 5 + [INSIDE] + [FAR_OUTSIDE] * 3,
        [sent, sent] + [(s, INSIDE) for s in inside],
        [pltpu.VMEM((rows, width), FULL), low, low, low, low, pltpu.VMEM((2, COLS, COLS), LOW)]
        + [pltpu.VMEM((rows, COLS), LOW), pltpu.VMEM((2, COLS, COLS), LOW)]
        + [pltpu.SemaphoreType.DMA((11,)), pltpu.SemaphoreType.DMA((32,))],
        10,
        (places, lengths, *arriving, middle, part, part_far, vectors, *attended, out_mat),
        vmem=54,
    )


def attention_backward_kernel(
    block, lengths, query, key, value, grad_in, query_grad, key_grad, value_grad, sums, mask
):
    count = query.shape[0]
    mask[...] = barred(lengths, block, 0, count, count)
    lane = lax.broadcasted_iota(jnp.int32, (count, TILE), 1) < HEAD_DIM
    for index in range(COLS // TILE):
        cols = pl.ds(index * TILE, TILE)
        stacked, given = two_by_two(query[:, cols], lane), two_by_two(grad_in[:, cols], lane)
        probs = probabilities(stacked, key[:, cols], mask[...])
        weighted = probs * dot_nt(given, value[:, cols])
        grad = (weighted - probs * jnp.sum(weighted, axis=-1, keepdims=True)).astype(LOW)
        out = dot(grad, key[:, cols])
        query_grad[:, cols] = (jnp.where(lane, out[:count], out[count:]) * 0.125).astype(LOW)
        key_grad[:, cols] = dot_tn(grad, stacked).astype(LOW)
        value_grad[:, cols] = dot_tn(probs.astype(LOW), given).astype(LOW)
    sums[...] = jnp.zeros_like(sums)
    sums[0:1, :] = jnp.sum(query_grad[...].astype(FULL), axis=0, keepdims=True)
    sums[1:2, :] = jnp.sum(value_grad[...].astype(FULL), axis=0, keepdims=True)


def attention_backward(block, lengths, query, key, value, grad_in):
    count = query.shape[0] // 2
    vmem = pltpu.VMEM
    half = (low_shape(count, COLS), INSIDE)
    part = pl.BlockSpec((count, COLS), lambda i: (block, 0))
    return call(
        lambda *refs: attention_backward_kernel(block, *refs),
        [SCALARS] + [part] * 4,
        [half, half, half, (full_shape(8, COLS), INSIDE)],
        [vmem((count, count), FULL)],
        8,
        (lengths, query, key, value, grad_in),
        grid=(1,),
        vmem=20,
    )


def joint_grad_kernel(places, normed, *refs):
    grads, sent, (query_part, key_part, value_part, sems) = refs[:6], refs[6:12], refs[12:]
    parts = (query_part, key_part, value_part)
    count = grads[0].shape[0]
    sides = [jnp.concatenate([g[...] for g in grads[i : i + 3]], axis=1) for i in (0, 3)]
    whole = dot_tn(normed[:count, :], sides[0]) + dot_tn(normed[count:, :], sides[1])
    for index, part in enumerate(parts):
        part[...] = whole[:, index * COLS : (index + 1) * COLS].astype(LOW)
    finished(started(joint_sent_plan(places, sent, parts), sems))


def joint_grad_parts(places, normed, own, other):
    rows, width = normed.shape
    sent = [low_shape(2, 4, 64, COLS), low_shape(2, 2, 128, COLS), low_shape(2, 4, 2, 32, COLS)]
    return call(
        joint_grad_kernel,
        [SCALARS] + [INSIDE] * 7,
        [(s, OUTSIDE) for s in sent for _ in range(2)],
        [pltpu.VMEM((width, COLS), LOW)] * 3 + [pltpu.SemaphoreType.DMA((56,))],
        8,
        (places, normed, *own, *other),
        vmem=44,
    )


def joint_backward_kernel(*refs):
    own, other, mats, outs = refs[:3], refs[3:6], refs[6:9], refs[9:]
    for grads, out in zip((own, other), outs):
        whole = dot_nt(grads[0][...], mats[0][...])
        whole += dot_nt(grads[1][...], mats[1][...])
        whole += dot_nt(grads[2][...], mats[2][...])
        out[...] = whole.astype(out.dtype)


def joint_backward(own, other, mats):
    count, width = own[0].shape[0], mats[0].shape[0]
    return call(
        joint_backward_kernel,
        [INSIDE] * 9,
        [(full_shape(count, width), INSIDE), (low_shape(count, width), INSIDE)],
        [],
        6,
        (*own, *other, *mats),
        vmem=20,
    )


def input_kernel(
    places, tokens, part, part_far, middle_grad, vectors, two_sums, own_sums, other_sums, up_sums,
    input_grad, sums, rows,
):
    unit, inverse = unit_of(tokens[...].astype(FULL))
    grad = part[...] + part_far[...].astype(FULL)
    input_grad[...] = middle_grad[...] + norm_backward(grad, unit, inverse, row_of(vectors, 0))
    first = places[13] == 0

    def own_side(values):
        none = jnp.zeros_like(values)
        return jnp.concatenate(
            [jnp.where(first, values, none), jnp.where(first, none, values)], axis=1
        )

    rows[...] = jnp.zeros_like(rows)
    rows[0:1, :] = jnp.sum(grad * unit, axis=0, keepdims=True)
    rows[1:2, :] = jnp.sum(grad, axis=0, keepdims=True)
    for k in range(2):
        rows[2 + k : 3 + k, :] = own_side(own_sums[k : k + 1, :] + other_sums[k : k + 1, :])
    rows[4:7, :] = two_sums[0:3, :]
    for k in range(4):
        hidden = up_sums[k : k + 1, :]
        rows[7 + k : 8 + k, :] = jnp.concatenate(
            [own_side(hidden[:, :256]), own_side(hidden[:, 256:])], axis=1
        )
    rows[11:12, :] = two_sums[3:4, :]
    sums[:16, :] = rows[:, :COLS].astype(LOW)
    sums[16:, :] = rows[:, COLS:].astype(LOW)


def input_backward(places, *arrays):
    count, width = arrays[0].shape
    return call(
        input_kernel,
        [SCALARS] + [INSIDE] * 9,
        [(full_shape(count, width), INSIDE), (low_shape(32, COLS), INSIDE)],
        [pltpu.VMEM((16, width), FULL)],
        4,
        (places, *arrays),
        vmem=20,
    )


def adam_step(weight, first, second, grad, rate, decay):
    first_new = BETA_ONE * first + (1.0 - BETA_ONE) * grad
    second_new = BETA_TWO * second + (1.0 - BETA_TWO) * grad * grad
    mean_hat = first_new / (1.0 - BETA_ONE**STEP)
    square_hat = second_new / (1.0 - BETA_TWO**STEP)
    fresh = weight - rate * (mean_hat / (jnp.sqrt(square_hat) + ADAM_EPS) + decay * weight)
    return (first_new, second_new, fresh)


def adam_kernel(grad_of, rate, chunks, places, *refs):
    state, refs = refs[:3], refs[3:]
    grads, refs = refs[:-8], refs[-8:]
    outs, (held, results, sems_in, sems_out) = refs[:4], refs[4:]
    coming = [
        started([(a.at[at], held.at[(i, *at)]) for i, a in enumerate(state)], sems_in.at[n])
        for n, at in enumerate(chunks)
    ]
    going = []
    for n, at in enumerate(chunks):
        grad = grad_of(n, places, *grads)
        finished(coming[n])
        results[(0, *at)] = grad
        weight, first, second = (held[(i, *at)] for i in range(3))
        new = adam_step(weight, first, second, grad, rate, MATRIX_DECAY)
        for i, value in enumerate(new):
            results[(1 + i, *at)] = value
        going += started(
            [(results.at[(i, *at)], out.at[at]) for i, out in enumerate(outs)], sems_out.at[n]
        )
    finished(going)


def adam(grad_of, rate, chunks, state, grads, places):
    shape = state[0].shape
    return pl.pallas_call(
        lambda *refs: adam_kernel(grad_of, rate, chunks, *refs),
        grid=(1,),
        in_specs=[SCALARS]
        + [OUTSIDE] * 3
        + [pl.BlockSpec((g[1], COLS), lambda i, at=g[2]: (at, 0)) for g in grads],
        out_specs=[OUTSIDE] * 4,
        out_shape=[full_shape(*shape)] * 4,
        scratch_shapes=[pltpu.VMEM((3, *shape), FULL), pltpu.VMEM((4, *shape), FULL)]
        + [pltpu.SemaphoreType.DMA((len(chunks), 3)), pltpu.SemaphoreType.DMA((len(chunks), 4))],
        compiler_params=pltpu.CompilerParams(vmem_limit_bytes=24 << 20),
        cost_estimate=pl.CostEstimate(
            flops=6 * FLOPS_PER_US, bytes_accessed=30 * state[0].size, transcendentals=0
        ),
    )(places, *state, *(g[0] for g in grads))


def by_core(places, both, far):
    own = places[13] == 0
    both, far = both.astype(FULL), far.astype(FULL)
    return jnp.where(own, both, far), jnp.where(own, far, both)


def columns_of(width, count):
    return [(slice(None), slice(n * width, (n + 1) * width)) for n in range(count)]


def rows_each(height, count):
    return [(slice(n * height, (n + 1) * height), slice(None)) for n in range(count)]


def adam_joint(places, state, sums):
    def grad_of(n, places, both, far):
        rows = slice(128 * n, 128 * (n + 1))
        return jnp.concatenate(by_core(places, both[rows, :], far[rows, :]), axis=1)

    grads = [(a, 384, 0) for a in sums]
    return adam(grad_of, MATRIX_RATE, columns_of(2 * COLS, 3), state, grads, places)


def adam_expand(places, state, sums):
    def grad_of(n, places, both, far):
        rows = slice(128 * n, 128 * (n + 1))
        zero, one = by_core(places, both[rows, :], far[rows, :])
        return jnp.concatenate(
            [zero[:, :256], one[:, :256], zero[:, 256:], one[:, 256:]], axis=1
        )

    grads = [(a, 512, 0) for a in sums]
    return adam(grad_of, MATRIX_RATE, columns_of(2 * COLS, 4), state, grads, places)


def adam_reduce(places, state, sums):
    def grad_of(n, places, left, right, far_left, far_right):
        rows = slice(128 * (n % 2), 128 * (n % 2 + 1))
        own = places[13] == n // 2
        return jnp.concatenate(
            [
                jnp.where(own, left[rows, :].astype(FULL), far_left[rows, :].astype(FULL)),
                jnp.where(own, right[rows, :].astype(FULL), far_right[rows, :].astype(FULL)),
            ],
            axis=1,
        )

    grads = [(a, 256, at) for a in sums for at in (2, 3)]
    return adam(grad_of, MATRIX_RATE, rows_each(128, 4), state, grads, places)


def adam_output(places, state, sums):
    def grad_of(n, places, *grads):
        both, far = grads[n], grads[2 + n]

        def rows(a):
            return jnp.concatenate(
                [
                    jnp.concatenate([a[64 * q : 64 * q + 32, :], a[64 * q + 32 : 64 * q + 64, :]], axis=1)
                    for q in (0, 1)
                ]
            ).astype(FULL)

        return jnp.where(places[13] == places[12], rows(both), rows(far))

    grads = [(a, 128, at) for a in sums for at in (3, 4)]
    return adam(grad_of, OUTPUT_RATE, rows_each(64, 2), state, grads, places)


def per_device(
    tokens,
    cotangent,
    lengths,
    joint_weight,
    joint_first,
    joint_second,
    output_weight,
    output_first,
    output_second,
    expand_weight,
    expand_first,
    expand_second,
    reduce_weight,
    reduce_first,
    reduce_second,
    vector_weight,
    vector_first,
    vector_second,
):
    me = coordinates()
    places = places_of(me)
    across = flip("core", 1)

    half, block, rest_half, rest_y = cast(
        places, joint_weight, vector_weight, expand_weight, reduce_weight, output_weight
    )
    joint_x, joint_y, along_x, along_y, along_z, far = gather_first(
        places, half, block, rest_half, rest_y, [send(a, across) for a in (lengths, tokens, cotangent)]
    )
    tokens, cotangent = (tokens, far[1]), (cotangent, far[2])
    lengths = jnp.concatenate([lengths, far[0]])

    normed_one, query, key, value, vectors, *joint_mats = joint(
        places, *tokens, joint_x, joint_y
    )
    along_z.append(send(after(along_z[1], query), turn("z", 1)))
    along_y.append(send(after(along_y[0], query), turn("y", 1)))
    along_y.append(send(after(along_y[1], query), turn("y", 1)))
    own = attention(0, lengths, after(query, along_y[1], *along_z[1:3]), key, value)
    along_x.append(send(after(along_x[1], own), turn("x", 1)))
    other = attention(1, lengths, after(query, along_x[1]), key, value)
    attended = (own, other)
    branch, out_mat = output(places, own, after(other, *along_x[2:], *along_y[2:]), along_z)
    branch_far = send(branch, across)
    *sent, middle, layer_own, layer_other, normed_two_part, up_bias_grad = forward_backward(
        places, lengths, tokens, cotangent, branch, branch_far, vectors,
        [*along_x, *along_y, *along_z],
    )
    part_far = send(normed_two_part, across)
    layer_far = send(layer_other, across)

    out_one, out_two, middle_grad, attended_grad, two_sums = output_backward(
        places, lengths, cotangent, middle, normed_two_part, part_far, vectors, attended, out_mat
    )
    sent[5] = after(sent[5], attended_grad)
    rest = total(me, sent, 0, 3, 0)
    next(rest)
    out_far = send(out_two, turn("z", 1))
    *own_grads, own_sums = attention_backward(0, lengths, query, key, value, attended_grad)
    *other_grads, other_sums = attention_backward(1, lengths, query, key, value, attended_grad)
    mark = rest.send(other_grads[0])
    sent = joint_grad_parts(places, after(normed_one, mark), own_grads, other_grads)
    joint_rows = total(me, sent, 32, 1, 32)
    next(joint_rows)
    mark = rest.send((sent[0], None, None))
    part_own, part_other = joint_backward(
        (after(own_grads[0], mark), *own_grads[1:]), other_grads, joint_mats
    )
    part_far = send(part_other, across)
    (out_near,) = added_all([[(out_one, 1), (after(out_far, part_own), 1)]])
    out_near = out_near.reshape(out_one.shape[1:])
    out_again = send(out_near, turn("z", 0))
    mark = joint_rows.send(part_own)
    mark = rest.send(mark)
    input_grad, vector_local = input_backward(
        places, tokens[0], after(part_own, mark), part_far, middle_grad, vectors, two_sums,
        own_sums, other_sums, up_bias_grad,
    )
    (out_along,) = added_all(
        [[(out_one, 0), (out_far, 0), (after(out_again, vector_local), 0)]]
    )
    out_along = out_along.reshape(out_one.shape[1:])

    mark = joint_rows.send((vector_local, vector_local, out_along))
    for turn_number in range(4):
        if turn_number == 2:
            layer_out = (after(layer_own, mark) + layer_far.astype(FULL)).astype(LOW)
            mark = (mark, layer_out)
        mark = rest.send(mark)
        mark = joint_rows.send(mark)
    mark = rest.send(mark)
    mark = joint_rows.send(mark)
    mark = joint_rows.send(mark)
    mark = rest.send(mark)
    mark = joint_rows.send(mark)
    one, two, extra = next(joint_rows)
    joint_state = adam_joint(
        places, (joint_weight, joint_first, joint_second), (after(one, mark), two)
    )
    output_state = adam_output(
        places, (output_weight, output_first, output_second), (after(one, mark), two)
    )
    one, two, _ = next(rest)
    one = after(one, joint_state[0], output_state[0])
    expand = adam_expand(places, (expand_weight, expand_first, expand_second), (one, two))
    reduce = adam_reduce(places, (reduce_weight, reduce_first, reduce_second), (one, two))
    vector_grad = lax.dynamic_slice(
        jnp.concatenate([extra[:12], extra[16:28]], axis=1).astype(FULL),
        (0, 128 * lax.axis_index("shard")),
        (12, 128),
    )
    vector_state = (vector_grad,) + adam_step(
        vector_weight, vector_first, vector_second, vector_grad, VECTOR_RATE, 0.0
    )
    states = zip(joint_state, output_state, expand, reduce, vector_state)
    return (layer_out, input_grad, *(a for kind in states for a in kind))


def solution(mesh):
    rows, columns, split = P("shard", None), P(None, "shard"), P(("wide", "shard"), None)
    state = (rows, rows, rows, rows, columns)
    return jax.shard_map(
        per_device,
        mesh=mesh,
        in_specs=(split, split, split) + (rows,) * 12 + (columns,) * 3,
        out_specs=(split, split) + state * 4,
        check_vma=False,
    )
```
